32 devices in a mesh: tile: 8 (over z, y), opt: 4 (over x, core).
Axes of the slice: x: 2, y: 2, z: 4, core: 2. Of those that a mesh axis runs over, the one named last changes fastest.
Arguments:
- inputs: bfloat16 [4, 16, 24, 24, 800], P('opt', 'tile'), may hold values from -6 to 6
- cotangent: bfloat16 [4, 16, 24, 24, 800], P('opt', 'tile'), may hold values from -6 to 6
- master: float32 [16, 800, 400], P('opt', 'tile'), may hold values from -0.21875 to 0.21875
- moment_one: float32 [16, 800, 400], P('opt', 'tile'), may hold values from -512 to 512
- moment_two: float32 [16, 800, 400], P('opt', 'tile'), may hold values from 9216 to 36864
- left_basis: float32 [16, 800, 800], P('opt', None, 'tile'), as said below
- column_basis: float32 [16, 400, 400], P('opt'), as said below
- small_params: float32 [57, 800], replicated
- small_first: float32 [57, 800], replicated, may hold values from -512 to 512
- small_second: float32 [57, 800], replicated, may hold values from 9216 to 36864
- land_mask: int32 [16, 24, 24], P('tile'), may hold values 0 or 1
- tile_count: int32 [8], replicated, may hold values from 1 to 2, as said below
- neighbours: int32 [16, 8], P('tile'), may hold values from -1 to 15, as said below
- block_order: int32 [16], replicated, may hold values from 0 to 15, each once
- cell_weight: int32 [4], replicated, may hold values from 1024 to 8192
- step_count: int32 [1], replicated, may hold values from 1 to 4
Outputs:
- block_output: bfloat16 [4, 16, 24, 24, 800], P('opt', 'tile')
- input_grad: float32 [4, 16, 24, 24, 800], P('opt', 'tile')
- new_master: float32 [16, 800, 400], P('opt', 'tile')
- new_master_low: bfloat16 [16, 800, 400], P('opt', 'tile')
- new_moment_one: float32 [16, 800, 400], P('opt', 'tile')
- new_moment_two: float32 [16, 800, 400], P('opt', 'tile')
- new_small: float32 [57, 800], replicated
- new_small_first: float32 [57, 800], replicated
- new_small_second: float32 [57, 800], replicated
The draws below stay inside these ranges and needn't reach their ends.
Inputs may be any that keep to these rules, and one draw needn't show every extreme that they name: `tile_count`: every entry is at least 1 and at most 2; some index has exactly 2. `neighbours`: entries are -1 or a live slot; empty slots have only -1; if slot a names slot b in one direction, b names a in the opposite direction. Each left_basis[s] is orthogonal. Each column_basis[s] is orthogonal.
All inputs are finite; a program needn't handle non-finite values. No bound on the sum of `land_mask` on one device may be relied on, other than what follows from the above.
Results may differ from the reference program's by a relative error of at most 0.007.
The reference program's roundings to bfloat16 on the way count: a program that leaves them out, or rounds other values in their place, can miss the bound.
Values may be sent and summed in bfloat16 or wider, within the bound.
A program may use at most 192 MiB of HBM per device.

```python
import math
import jax
import jax.numpy as jnp
from jax import lax

D = 800
G = 16
S = 24
CAP = 2
BW = 400
BATCH = 4
SLOTS = 16
NBLK = 16
GRID_W = 8
TOTAL_CELLS = 36864
N_TILE = 8


def ocean_tile_layout(key):
    base_key = jax.random.fold_in(key, 11)
    count_key = jax.random.fold_in(base_key, 0)
    score_key = jax.random.fold_in(base_key, 2)
    counts = jax.random.randint(count_key, (N_TILE,), 1, CAP + 1)
    counts = jnp.where(jnp.arange(N_TILE) == N_TILE - 1, CAP, counts).astype(jnp.int32)
    ocean_total = jnp.sum(counts)
    position = jnp.arange(SLOTS, dtype=jnp.int32)
    scores = jax.random.randint(score_key, (SLOTS,), 0, SLOTS) * SLOTS + position
    scores = jnp.where(position >= SLOTS - 2, position - SLOTS, scores)
    ranking = jnp.argsort(jnp.argsort(scores))
    ocean_grid = ranking < ocean_total
    raster_order = jnp.argsort(jnp.where(ocean_grid, position, SLOTS + position)).astype(jnp.int32)
    offsets = jnp.cumsum(counts) - counts
    device = position // CAP
    within = position % CAP
    alive_slot = within < counts[device]
    grid_cell = jnp.where(alive_slot, raster_order[jnp.clip(offsets[device] + within, 0, SLOTS - 1)], -1)
    slot_owner = jnp.full((SLOTS,), -1, jnp.int32).at[jnp.where(alive_slot, grid_cell, SLOTS)].set(position, mode='drop')
    grid_row = grid_cell // GRID_W
    grid_col = grid_cell % GRID_W
    row_steps = jnp.array([-1, -1, -1, 0, 0, 1, 1, 1], jnp.int32)
    col_steps = jnp.array([-1, 0, 1, -1, 1, -1, 0, 1], jnp.int32)
    next_row = grid_row[:, None] + row_steps[None, :]
    next_col = grid_col[:, None] + col_steps[None, :]
    inside = alive_slot[:, None] & (next_row >= 0) & (next_row < SLOTS // GRID_W) & (next_col >= 0) & (next_col < GRID_W)
    target = jnp.clip(next_row * GRID_W + next_col, 0, SLOTS - 1)
    linked = jnp.where(inside, slot_owner[target], -1)
    return (counts, linked.astype(jnp.int32))


def draw_tile_count(key, part):
    return ocean_tile_layout(key)[0]


def draw_neighbours(key, part):
    return ocean_tile_layout(key)[1]


def basis(key, dimension, block_total):
    sign_key, shuffle_key = jax.random.split(key)
    sign_flip = (jax.random.randint(sign_key, (block_total, dimension, 1), 0, 2) * 2 - 1).astype(jnp.float32)

    def shuffle_one(one_key):
        return jax.random.permutation(one_key, dimension)
    shuffles = jax.vmap(shuffle_one)(jax.random.split(shuffle_key, block_total))
    positions = jnp.arange(dimension, dtype=jnp.int32)
    product = (2 * positions[None, :, None] + 1) * (2 * shuffles[:, None, :] + 1) % (8 * dimension)
    angles = product.astype(jnp.float32) * (math.pi / (4 * dimension))
    entries = jnp.cos(angles)
    return sign_flip * entries * math.sqrt(2.0 / dimension)


def draw_left_basis(key, part):
    return basis(jax.random.fold_in(key, 21), D, NBLK)


def draw_column_basis(key, part):
    return basis(jax.random.fold_in(key, 31), BW, NBLK)


def draw_small_params(key, part):
    tap_key, rest_key, gain_key = jax.random.split(jax.random.fold_in(key, 5), 3)
    taps = jax.random.normal(tap_key, (49, D), jnp.float32) / 7.0
    rest = jax.random.uniform(rest_key, (7, D), jnp.float32, -0.5, 0.5)
    gain = 1.0 + jax.random.uniform(gain_key, (1, D), jnp.float32, -0.4, 0.4)
    return jnp.concatenate([taps, rest[0:1], gain, rest[1:7]], 0)


def touch_ends(result, key, smallest, top_value):
    place = [jax.random.randint(jax.random.fold_in(key, axis), (), 0, length) for axis, length in enumerate(result.shape)]
    widest = result.shape.index(max(result.shape))
    next_to = place[:widest] + [(place[widest] + 1) % result.shape[widest]] + place[widest + 1:]
    return result.at[tuple(place)].set(smallest).at[tuple(next_to)].set(top_value)


def level_of(key, shape, pieces, least, largest):
    loudness = 1.0
    for dim, parts in pieces:
        steps = jax.random.uniform(jax.random.fold_in(jax.random.fold_in(key, 6), dim), (parts,), jnp.float32, least / len(pieces), largest / len(pieces))
        loudness = loudness * jnp.repeat(jnp.exp(steps), shape[dim] // parts).reshape((-1,) + (1,) * (len(shape) - 1 - dim))
    return loudness


def noise(stream_key, shape, width, bound, cuts=(), held_as=jnp.bfloat16):
    values = jax.random.normal(stream_key, shape, jnp.float32) * width
    if len(cuts) > 0:
        values = level_of(stream_key, shape, cuts, -0.22, 0.18) * values
    return jnp.clip(values, min=-bound, max=bound).astype(held_as)


def setup_inputs(seed: int = 0) -> dict:
    key_list = jax.random.split(jax.random.key(seed), 17)
    inputs = noise(key_list[0], (BATCH, SLOTS, S, S, D), 1.0, 6.0, ((0, 4), (1, 8)))
    cotangent = noise(key_list[1], (BATCH, SLOTS, S, S, D), 1.0, 6.0, ((0, 4), (1, 8)))
    master = noise(key_list[2], (NBLK, D, BW), D ** -0.5, 0.21875, ((0, 4), (1, 8)), jnp.float32)
    moment_one = noise(key_list[3], (NBLK, D, BW), (0.5 * TOTAL_CELLS ** 0.5), 512.0, ((0, 4), (1, 8)), jnp.float32)
    moment_two = jnp.clip(jnp.exp(math.log(36864.0) - 1.3862944 * jax.random.uniform(key_list[4], (NBLK, D, BW), jnp.float32) ** level_of(key_list[4], (NBLK, D, BW), ((0, 4), (1, 8)), -0.2, 0.2)), 9216.0, 36864.0)
    left_basis = draw_left_basis(jax.random.fold_in(key_list[16], 71), 0)
    column_basis = draw_column_basis(jax.random.fold_in(key_list[16], 71), 0)
    small_params = draw_small_params(jax.random.fold_in(key_list[16], 71), 0)
    small_first = noise(key_list[8], (57, D), (0.5 * TOTAL_CELLS ** 0.5), 512.0, (), jnp.float32)
    small_second = jnp.clip(jnp.exp(jax.random.uniform(key_list[9], (57, D), jnp.float32, math.log(9216.0), math.log(36864.0))), 9216.0, 36864.0)
    land_mask = touch_ends((jax.random.randint(key_list[10], (SLOTS, S, S), 0, 8) < 7).astype(jnp.int32), jax.random.fold_in(key_list[10], 1), 0, 1)
    tile_count = draw_tile_count(jax.random.fold_in(key_list[16], 71), 0)
    neighbours = draw_neighbours(jax.random.fold_in(key_list[16], 71), 0)
    block_order = jax.random.permutation(key_list[13], NBLK).astype(jnp.int32)
    cell_weight = touch_ends(jax.random.randint(key_list[14], (BATCH,), 1024, 8193), jax.random.fold_in(key_list[14], 1), 1024, 8192).astype(jnp.int32)
    step_count = jax.random.randint(key_list[15], (1,), 1, 5).astype(jnp.int32)
    return {"inputs": inputs, "cotangent": cotangent, "master": master, "moment_one": moment_one, "moment_two": moment_two, "left_basis": left_basis, "column_basis": column_basis, "small_params": small_params, "small_first": small_first, "small_second": small_second, "land_mask": land_mask, "tile_count": tile_count, "neighbours": neighbours, "block_order": block_order, "cell_weight": cell_weight, "step_count": step_count}


highest_precision = lax.Precision.HIGHEST
epsilon = 1e-05
adam_eps = 1e-08
decay_rate = 0.5
small_rate = 0.05

@jax.custom_vjp
def low(v):
    return lax.optimization_barrier(v.astype(jnp.bfloat16)).astype(jnp.float32)

@jax.custom_vjp
def low_back(v):
    return v

def low_keep(v):
    return (low(v), None)

def low_pass(kept, grad):
    return (grad,)

def back_keep(v):
    return (v, None)

def back_low(kept, grad):
    return (low(grad),)
low.defvjp(low_keep, low_pass)
low_back.defvjp(back_keep, back_low)

def edge_rims(field_in):
    return (field_in[:, :3], field_in[:, -3:], field_in[:, :, :3], field_in[:, :, -3:])

def assemble(own_tiles, upper_rim, lower_rim, left_rim, right_rim, neighbours):
    total_rows = upper_rim.shape[0]
    side_len = own_tiles.shape[1]

    def take_rim(source, column):
        extended = jnp.concatenate([source, jnp.zeros((1,) + source.shape[1:], source.dtype)], 0)
        chosen = jnp.where(neighbours[:, column] < 0, total_rows, neighbours[:, column]).astype(jnp.int32)
        return jnp.take(extended, chosen, axis=0)
    top_band = jnp.concatenate([take_rim(lower_rim, 0)[:, :, side_len - 3:], take_rim(lower_rim, 1), take_rim(lower_rim, 2)[:, :, :3]], 2)
    mid_band = jnp.concatenate([take_rim(right_rim, 3), own_tiles, take_rim(left_rim, 4)], 2)
    bottom_band = jnp.concatenate([take_rim(upper_rim, 5)[:, :, side_len - 3:], take_rim(upper_rim, 6), take_rim(upper_rim, 7)[:, :, :3]], 2)
    return jnp.concatenate([top_band, mid_band, bottom_band], 1)

def depthwise(padded, kernel):
    side_len = padded.shape[1] - 6
    summed = jnp.zeros(padded.shape[:1] + (side_len, side_len, padded.shape[3]), jnp.float32)
    for tap_index in range(49):
        tap_row = tap_index // 7
        tap_col = tap_index % 7
        summed = summed + kernel[tap_index] * padded[:, tap_row:tap_row + side_len, tap_col:tap_col + side_len].astype(jnp.float32)
    return summed

def block_forward(field_in, w_first, w_second, small, neighbours, ocean_mask):
    channels = field_in.shape[3]
    cell_count = field_in.shape[0] * field_in.shape[1] * field_in.shape[2]
    masked = ocean_mask[..., None] * field_in
    upper_rim, lower_rim, left_rim, right_rim = edge_rims(masked)
    padded = assemble(masked, upper_rim, lower_rim, left_rim, right_rim, neighbours)
    conv_out = depthwise(padded, small[:49]) + small[49]
    grouped = conv_out.reshape(cell_count, G, channels // G)
    weight_cells = ocean_mask.reshape(cell_count, 1, 1)
    counted = jnp.sum(ocean_mask) * (channels // G)
    group_mean = lax.optimization_barrier(jnp.sum(weight_cells * grouped, axis=(0, 2))) / counted
    centered = grouped - group_mean[:, None]
    variance = lax.optimization_barrier(jnp.sum(weight_cells * centered * centered, axis=(0, 2))) / counted
    normed = (centered * lax.rsqrt(variance + epsilon)[:, None]).reshape(cell_count, channels)
    shaped = low(normed * small[50] + small[51])
    pre_act = low_back(jnp.dot(shaped, low(w_first), precision=highest_precision) + small[53:57].reshape(-1))
    activation = low(jax.nn.gelu(pre_act))
    branch = low_back(jnp.dot(activation, low(w_second), precision=highest_precision) + small[52])
    return ocean_mask[..., None] * (field_in + branch.reshape(field_in.shape))

def reference(inputs, cotangent, master, moment_one, moment_two, left_basis, column_basis, small_params, small_first, small_second, land_mask, tile_count, neighbours, block_order, cell_weight, step_count):
    block_total = master.shape[0]
    half_count = block_total // 2
    channels = master.shape[1]
    block_cols = master.shape[2]
    inverse = jnp.argsort(block_order).astype(jnp.int32)
    by_block = jnp.take(master, inverse, axis=0)
    w_first = by_block[:half_count].transpose(1, 0, 2).reshape(channels, half_count * block_cols)
    w_second = by_block[half_count:].transpose(0, 2, 1).reshape(half_count * block_cols, channels)
    slot_count = land_mask.shape[0]
    per_dev = slot_count // tile_count.shape[0]
    slot_index = jnp.arange(slot_count, dtype=jnp.int32)
    occupied_slot = (slot_index % per_dev < tile_count[slot_index // per_dev]).astype(jnp.float32)
    ocean_mask = land_mask.astype(jnp.float32) * occupied_slot[:, None, None]
    counts = cell_weight.astype(jnp.float32)
    sample_weight = counts * counts.shape[0] / jnp.sum(counts)

    def forward(first_matrix, second_mat, small, field_in):
        return block_forward(field_in, first_matrix, second_mat, small, neighbours, ocean_mask)

    def one_sample(totals, sample_item):
        field_in, back_in, factor = sample_item
        output, pullback = jax.vjp(forward, w_first, w_second, small_params, field_in.astype(jnp.float32))
        gradients = pullback(factor * back_in.astype(jnp.float32))
        new_totals = (totals[0] + gradients[0], totals[1] + gradients[1], totals[2] + gradients[2])
        return (new_totals, (output.astype(jnp.bfloat16), gradients[3]))
    start = (jnp.zeros(w_first.shape, jnp.float32), jnp.zeros(w_second.shape, jnp.float32), jnp.zeros(small_params.shape, jnp.float32))
    totals, outputs = lax.scan(one_sample, start, (inputs, cotangent, sample_weight))
    d_first, d_second, d_small = totals
    block_output, input_grad = outputs
    grad_blocks = jnp.concatenate([d_first.reshape(channels, half_count, block_cols).transpose(1, 0, 2), d_second.reshape(half_count, block_cols, channels).transpose(0, 2, 1)], 0)
    slot_grads = jnp.take(grad_blocks, block_order, axis=0)
    rotated_gradient = jnp.einsum('sdk,sdw->skw', left_basis, slot_grads, precision=highest_precision)
    rotated_gradient = jnp.einsum('cnh,cha->cna', rotated_gradient, column_basis, precision=highest_precision)
    correction = 1.0 - jnp.power(jnp.float32(decay_rate), step_count[0].astype(jnp.float32))
    first_new = decay_rate * moment_one + (1.0 - decay_rate) * rotated_gradient
    second_new = decay_rate * moment_two + (1.0 - decay_rate) * rotated_gradient * rotated_gradient
    step_direction = first_new / correction / (jnp.sqrt(second_new / correction) + adam_eps)
    turned_update = jnp.einsum('fda,fua->fdu', step_direction, column_basis, precision=highest_precision)
    change = jnp.einsum('sdk,skw->sdw', left_basis, turned_update, precision=highest_precision)
    new_master = master - 0.5 / math.sqrt(channels) * change
    small_one = decay_rate * small_first + (1.0 - decay_rate) * d_small
    small_two = decay_rate * small_second + (1.0 - decay_rate) * d_small * d_small
    new_small = small_params - small_rate * (small_one / correction) / (jnp.sqrt(small_two / correction) + adam_eps)
    return (block_output, input_grad, new_master, new_master.astype(jnp.bfloat16), first_new, second_new, new_small, small_one, small_two)
```

```python
import math

import jax
import jax.numpy as jnp
from jax import lax
from jax.experimental import pallas as pl
from jax.experimental.pallas import tpu as pltpu
from jax.sharding import PartitionSpec as P

GROUPS = 16
LANES = 128
RIM = 3
PITCH = 40
BF = jnp.bfloat16
F32 = jnp.float32

highest = lax.Precision.HIGHEST
epsilon = 1e-05
adam_eps = 1e-08
decay_rate = 0.5
small_rate = 0.05
ROOT = 0.7978845608028654
CUBE = 0.044715


class Grid:
    def __init__(self, n_tile, n_opt):
        b = 4 if n_tile % 16 == 0 else 2
        self.n_tile, self.n_opt = n_tile, n_opt
        self.size = {"a": n_tile // b, "b": b, "x": n_opt // 2, "c": 2}
        self.stride = {"a": b * n_opt, "b": n_opt, "x": 2, "c": 1}

    def own(self):
        t, o = lax.axis_index("tile"), lax.axis_index("opt")
        b = self.size["b"]
        return {"a": t // b, "b": t % b, "x": o // 2, "c": o % 2}

    def swap(self, value, dim, k, keep=None):
        total = self.n_tile * self.n_opt
        pairs = []
        for d in range(total):
            at = d // self.stride[dim] % self.size[dim]
            to = d + ((at ^ k) - at) * self.stride[dim]
            pairs.append((d, to))
        return lax.ppermute(value, ("tile", "opt"), pairs)

    def tile_swap(self, value, k, sends=None, takes=None):
        pairs = []
        for t in range(self.n_tile):
            u = t ^ k
            if (sends is None or t < sends) and (takes is None or u < takes):
                for o in range(self.n_opt):
                    pairs.append((t * self.n_opt + o, u * self.n_opt + o))
        return lax.ppermute(value, ("tile", "opt"), pairs)

    def total(self, value, dims):
        for dim in dims:
            k = 1
            while k < self.size[dim]:
                value = value + self.swap(value, dim, k)
                k *= 2
        return value

    def gather(self, value, dim):
        return jnp.stack([value] + [self.swap(value, dim, k) for k in range(1, self.size[dim])])


def natural(rel, own, size):
    return jnp.concatenate([lax.dynamic_slice_in_dim(rel, j ^ own, 1, 0) for j in range(size)], 0)


def store_rims(src, outs, slot, side):
    outs[slot, 0] = src[pl.ds(0, RIM * side), :].astype(BF)
    outs[slot, 1] = src[pl.ds((side - RIM) * side, RIM * side), :].astype(BF)
    for e in range(RIM):
        rows = pl.ds(e * side, side)
        outs[slot, 2, rows] = src[pl.ds(e, side, stride=side), :].astype(BF)
        outs[slot, 3, rows] = src[pl.ds(side - RIM + e, side, stride=side), :].astype(BF)


def send_out(chunk, own, rims, outs, sems, n_chunk):
    for k in range(len(outs)):

        @pl.when(chunk ^ own == k)
        def _():
            pltpu.make_async_copy(rims.at[chunk], outs[k], sems.at[chunk]).start()

    @pl.when(chunk == n_chunk - 1)
    def _():
        for c in range(n_chunk):
            pltpu.make_async_copy(rims.at[c], outs[0], sems.at[c]).wait()


def rims_of_input(inputs, mask_lanes, own_tile, n_tile):
    slots, side, _, channels = inputs.shape
    n_chunk = -(-channels // LANES)

    def kernel(own_ref, x_ref, m_ref, *rest):
        outs, (cells, rims, sems) = rest[:n_tile], rest[n_tile:]
        chunk = pl.program_id(0)
        for s in range(slots):
            for i in range(side):
                cells[pl.ds(i * side, side), :] = (
                    x_ref[s, i].astype(F32) * m_ref[s, pl.ds(i * side, side), :]
                )
            store_rims(cells, rims.at[chunk], s, side)
        send_out(chunk, own_ref[0], rims, outs, sems, n_chunk)

    piece = (slots, 4, RIM * side, LANES)
    return pl.pallas_call(
        kernel,
        grid_spec=pltpu.PrefetchScalarGridSpec(
            num_scalar_prefetch=1,
            grid=(n_chunk,),
            in_specs=[
                pl.BlockSpec((slots, side, side, LANES), lambda c, _: (0, 0, 0, c)),
                pl.BlockSpec((slots, side * side, LANES), lambda c, _: (0, 0, 0)),
            ],
            out_specs=[pl.BlockSpec(memory_space=pl.ANY)] * n_tile,
            scratch_shapes=[
                pltpu.VMEM((side * side, LANES), F32),
                pltpu.VMEM((n_chunk,) + piece, BF),
                pltpu.SemaphoreType.DMA((n_chunk,)),
            ],
        ),
        out_shape=[jax.ShapeDtypeStruct(piece, BF)] * n_tile,
        compiler_params=pltpu.CompilerParams(vmem_limit_bytes=32 << 20),
        name="rims_of_input",
    )(own_tile, inputs, mask_lanes)


def pick_halos(pieces, neighbours_rel, own_tile, side):
    n_tile = len(pieces)
    slots = pieces[0].shape[0]
    band = RIM * side

    def kernel(own_ref, nbr_ref, *rest):
        takes, outs, (held, sems) = rest[:n_tile], rest[n_tile : 2 * n_tile], rest[2 * n_tile :]
        own = own_ref[0]
        copies = [pltpu.make_async_copy(takes[k], held.at[k], sems.at[k]) for k in range(n_tile)]
        for c in copies:
            c.start()
        for c in copies:
            c.wait()
        for k in range(n_tile):
            for s in range(slots):

                def rim(direction, which):
                    slot = nbr_ref[(k * slots + s) * 8 + direction]
                    at = jnp.maximum(slot, 0)
                    value = held[(at // slots) ^ own, at % slots, which].astype(F32)
                    return jnp.where(slot >= 0, value, 0.0)

                for to, (direction, which) in enumerate(((1, 1), (6, 0), (3, 3), (4, 2))):
                    outs[k][s, to] = rim(direction, which).astype(BF)
                for corner, (direction, which, first) in enumerate(
                    ((0, 1, side - RIM), (2, 1, 0), (5, 0, side - RIM), (7, 0, 0))
                ):
                    value = rim(direction, which)
                    rows = [value[e * side + first : e * side + first + RIM] for e in range(RIM)]
                    rows.append(jnp.zeros((16 - RIM * RIM, LANES), F32))
                    outs[k][s, 4, pl.ds(16 * corner, 16)] = jnp.concatenate(rows, 0).astype(BF)
                outs[k][s, 4, pl.ds(64, band - 64)] = jnp.zeros((band - 64, LANES), BF)

    return pl.pallas_call(
        kernel,
        grid_spec=pltpu.PrefetchScalarGridSpec(
            num_scalar_prefetch=2,
            grid=(1,),
            in_specs=[pl.BlockSpec(memory_space=pl.ANY)] * n_tile,
            out_specs=[pl.BlockSpec((slots, 5, band, LANES), lambda i, *_: (0, 0, 0, 0))] * n_tile,
            scratch_shapes=[
                pltpu.VMEM((n_tile, slots, 4, band, LANES), BF),
                pltpu.SemaphoreType.DMA((n_tile,)),
            ],
        ),
        out_shape=[jax.ShapeDtypeStruct((slots, 5, band, LANES), BF)] * n_tile,
        compiler_params=pltpu.CompilerParams(vmem_limit_bytes=32 << 20),
        name="pick_halos",
    )(own_tile, neighbours_rel, *pieces)


def exchange_halos(grid, rims, neighbours_rel, own_tile, side, n_chunk):
    arrived = [rims[0]] + [
        grid.tile_swap(rims[k], k, takes=n_chunk) for k in range(1, grid.n_tile)
    ]
    halos = pick_halos(arrived, neighbours_rel, own_tile, side)
    return [halos[0]] + [grid.tile_swap(halos[k], k, sends=n_chunk) for k in range(1, grid.n_tile)]


def fill_halo(pad, halo, side):
    last = side + RIM
    up, down, left, right, corner = (halo(k) for k in range(5))
    for e in range(RIM):
        rows = slice(e * side, e * side + side)
        pad[pl.ds(e * PITCH + 8, side), :] = up[rows]
        pad[pl.ds((last + e) * PITCH + 8, side), :] = down[rows]
        pad[pl.ds(RIM * PITCH + 8 - RIM + e, side, stride=PITCH), :] = left[rows]
        pad[pl.ds(RIM * PITCH + 8 + side + e, side, stride=PITCH), :] = right[rows]
    places = ((0, 8 - RIM), (0, 8 + side), (last, 8 - RIM), (last, 8 + side))
    for k, (row, col) in enumerate(places):
        for e in range(RIM):
            at = 16 * k + RIM * e
            pad[pl.ds((row + e) * PITCH + col, RIM), :] = corner[at : at + RIM]


def conv_pass(pad, side, weight, emit):
    for block in range(side // 8):
        sums = [None] * side
        for b in range(7):
            taps = [weight(a, b) for a in range(7)]
            for r in range(side + 2 * RIM):
                cells = pad[pl.ds(r * PITCH + 8 - RIM + b + 8 * block, 8), :]
                for a in range(7):
                    i = r - a
                    if 0 <= i < side:
                        term = taps[a] * cells
                        sums[i] = term if sums[i] is None else sums[i] + term
        emit(block, sums)


def load_halos(first, halos, held, sems):
    @pl.when(first)
    def _():
        copies = [pltpu.make_async_copy(h, held.at[k], sems.at[k]) for k, h in enumerate(halos)]
        for c in copies:
            c.start()
        for c in copies:
            c.wait()


def conv_cost(n_chunk, slots, side, nbytes):
    return pl.CostEstimate(
        flops=n_chunk * slots * side * side * LANES * 98 * 100, bytes_accessed=nbytes, transcendentals=0
    )


def conv_forward(inputs, mask_lanes, halos, taps, own_tile):
    slots, side, _, channels = inputs.shape
    n_chunk = -(-channels // LANES)
    n_tile = len(halos)

    def kernel(own_ref, x_ref, m_ref, w_ref, *rest):
        given, (o_ref, s_ref), (pad, held, sems) = rest[:n_tile], rest[n_tile : n_tile + 2], rest[n_tile + 2 :]
        chunk, slot = pl.program_id(0), pl.program_id(1)
        load_halos((chunk == 0) & (slot == 0), given, held, sems)
        for i in range(side):
            pad[pl.ds((i + RIM) * PITCH + 8, side), :] = (
                x_ref[0, i].astype(F32) * m_ref[0, pl.ds(i * side, side), :]
            )
        fill_halo(pad, lambda k: held[chunk ^ own_ref[0], slot, k].astype(F32), side)
        bias = w_ref[49]
        totals = [jnp.zeros((8, LANES), F32), jnp.zeros((8, LANES), F32)]

        def emit(block, sums):
            for i in range(side):
                value = sums[i] + bias
                rows = pl.ds(i * side + 8 * block, 8)
                o_ref[0, rows, :] = value
                weighted = m_ref[0, rows, :] * value
                totals[0] = totals[0] + weighted
                totals[1] = totals[1] + weighted * value

        conv_pass(pad, side, lambda a, b: w_ref[7 * a + b], emit)
        s_ref[0, 0], s_ref[0, 1] = totals

    cells = side * side
    return pl.pallas_call(
        kernel,
        grid_spec=pltpu.PrefetchScalarGridSpec(
            num_scalar_prefetch=1,
            grid=(n_chunk, slots),
            in_specs=[
                pl.BlockSpec((1, side, side, LANES), lambda c, s, _: (s, 0, 0, c)),
                pl.BlockSpec((1, cells, LANES), lambda c, s, _: (s, 0, 0)),
                pl.BlockSpec((50, 8, LANES), lambda c, s, _: (0, 0, c)),
            ]
            + [pl.BlockSpec(memory_space=pl.ANY)] * n_tile,
            out_specs=[
                pl.BlockSpec((1, cells, LANES), lambda c, s, _: (s, 0, c)),
                pl.BlockSpec((1, 2, 8, LANES), lambda c, s, _: (s, 0, 0, c)),
            ],
            scratch_shapes=[
                pltpu.VMEM(((side + 2 * RIM) * PITCH, LANES), F32),
                pltpu.VMEM((n_tile,) + halos[0].shape, BF),
                pltpu.SemaphoreType.DMA((n_tile,)),
            ],
        ),
        out_shape=[
            jax.ShapeDtypeStruct((slots, cells, channels), F32),
            jax.ShapeDtypeStruct((slots, 2, 8, channels), F32),
        ],
        cost_estimate=conv_cost(n_chunk, slots, side, 10 << 20),
        compiler_params=pltpu.CompilerParams(vmem_limit_bytes=32 << 20),
        name="conv_forward",
    )(own_tile, inputs, mask_lanes, taps, *halos)


def conv_gradient(d_shaped, conv_out, mask_lanes, coefs, own_tile, n_tile, side):
    slots, cells, channels = d_shaped.shape
    n_chunk = -(-channels // LANES)

    def kernel(own_ref, d_ref, v_ref, m_ref, c_ref, o_ref, *rest):
        outs, (held, rims, sems) = rest[:n_tile], rest[n_tile:]
        chunk = pl.program_id(0)
        one, two, three = c_ref[0, :1], c_ref[1, :1], c_ref[2, :1]
        for s in range(slots):
            value = d_ref[s] * one - m_ref[s] * (two + three * v_ref[s])
            o_ref[s] = value
            held[...] = value
            store_rims(held, rims.at[chunk], s, side)
        send_out(chunk, own_ref[0], rims, outs, sems, n_chunk)

    piece = (slots, 4, RIM * side, LANES)
    block = pl.BlockSpec((slots, cells, LANES), lambda c, _: (0, 0, c))
    return pl.pallas_call(
        kernel,
        grid_spec=pltpu.PrefetchScalarGridSpec(
            num_scalar_prefetch=1,
            grid=(n_chunk,),
            in_specs=[
                block,
                block,
                pl.BlockSpec((slots, cells, LANES), lambda c, _: (0, 0, 0)),
                pl.BlockSpec((3, 8, LANES), lambda c, _: (0, 0, c)),
            ],
            out_specs=[block] + [pl.BlockSpec(memory_space=pl.ANY)] * n_tile,
            scratch_shapes=[
                pltpu.VMEM((cells, LANES), F32),
                pltpu.VMEM((n_chunk,) + piece, BF),
                pltpu.SemaphoreType.DMA((n_chunk,)),
            ],
        ),
        out_shape=[jax.ShapeDtypeStruct((slots, cells, channels), F32)]
        + [jax.ShapeDtypeStruct(piece, BF)] * n_tile,
        compiler_params=pltpu.CompilerParams(vmem_limit_bytes=32 << 20),
        name="conv_gradient",
    )(own_tile, d_shaped, conv_out, mask_lanes, coefs)


def tap_gradient(inputs, mask_lanes, halos, d_conv, own_tile):
    slots, side, _, channels = inputs.shape
    n_chunk = -(-channels // LANES)
    n_tile = len(halos)
    cells = side * side

    def kernel(own_ref, x_ref, m_ref, d_ref, *rest):
        given, o_ref, (pad, held, sums, sems) = rest[:n_tile], rest[n_tile], rest[n_tile + 1 :]
        chunk, slot = pl.program_id(0), pl.program_id(1)
        load_halos((chunk == 0) & (slot == 0), given, held, sems)
        for i in range(side):
            pad[pl.ds((i + RIM) * PITCH + 8, side), :] = (
                x_ref[0, i].astype(F32) * m_ref[0, pl.ds(i * side, side), :]
            )
        fill_halo(pad, lambda k: held[chunk ^ own_ref[0], slot, k].astype(F32), side)

        @pl.when(slot == 0)
        def _():
            sums[...] = jnp.zeros_like(sums)

        for block in range(side // 8):
            grads = [d_ref[0, pl.ds(i * side + 8 * block, 8), :] for i in range(side)]
            total = grads[0]
            for i in range(1, side):
                total = total + grads[i]
            sums[49] += total
            for b in range(7):
                taps = [None] * 7
                for r in range(side + 2 * RIM):
                    window = pad[pl.ds(r * PITCH + 8 - RIM + b + 8 * block, 8), :]
                    for a in range(7):
                        i = r - a
                        if 0 <= i < side:
                            term = window * grads[i]
                            taps[a] = term if taps[a] is None else taps[a] + term
                for a in range(7):
                    sums[7 * a + b] += taps[a]

        @pl.when(slot == slots - 1)
        def _():
            o_ref[...] = jnp.sum(sums[...], axis=1)

    return pl.pallas_call(
        kernel,
        grid_spec=pltpu.PrefetchScalarGridSpec(
            num_scalar_prefetch=1,
            grid=(n_chunk, slots),
            in_specs=[
                pl.BlockSpec((1, side, side, LANES), lambda c, s, _: (s, 0, 0, c)),
                pl.BlockSpec((1, cells, LANES), lambda c, s, _: (s, 0, 0)),
                pl.BlockSpec((1, cells, LANES), lambda c, s, _: (s, 0, c)),
            ]
            + [pl.BlockSpec(memory_space=pl.ANY)] * n_tile,
            out_specs=pl.BlockSpec((50, LANES), lambda c, s, _: (0, c)),
            scratch_shapes=[
                pltpu.VMEM(((side + 2 * RIM) * PITCH, LANES), F32),
                pltpu.VMEM((n_tile,) + halos[0].shape, BF),
                pltpu.VMEM((50, 8, LANES), F32),
                pltpu.SemaphoreType.DMA((n_tile,)),
            ],
        ),
        out_shape=jax.ShapeDtypeStruct((50, channels), F32),
        cost_estimate=conv_cost(n_chunk, slots, side, 10 << 20),
        compiler_params=pltpu.CompilerParams(vmem_limit_bytes=32 << 20),
        name="tap_gradient",
    )(own_tile, inputs, mask_lanes, d_conv, *halos)


def conv_backward(d_conv, halos, cotangent, mask_lanes, taps, weight_lanes, own_tile):
    slots, side, _, channels = cotangent.shape
    n_chunk = -(-channels // LANES)
    n_tile = len(halos)
    cells = side * side

    def kernel(own_ref, d_ref, g_ref, m_ref, w_ref, l_ref, *rest):
        given, o_ref, (pad, held, sems) = rest[:n_tile], rest[n_tile], rest[n_tile + 1 :]
        chunk, slot = pl.program_id(0), pl.program_id(1)
        load_halos((chunk == 0) & (slot == 0), given, held, sems)
        for i in range(side):
            pad[pl.ds((i + RIM) * PITCH + 8, side), :] = d_ref[0, pl.ds(i * side, side), :]
        fill_halo(pad, lambda k: held[chunk ^ own_ref[0], slot, k].astype(F32), side)
        weight = l_ref[...]

        def emit(block, sums):
            for i in range(side):
                rows = pl.ds(i * side + 8 * block, 8)
                scaled = weight * g_ref[0, i, pl.ds(8 * block, 8), :].astype(F32)
                o_ref[0, rows, :] = m_ref[0, rows, :] * (scaled + sums[i])

        conv_pass(pad, side, lambda a, b: w_ref[7 * (6 - a) + 6 - b], emit)

    return pl.pallas_call(
        kernel,
        grid_spec=pltpu.PrefetchScalarGridSpec(
            num_scalar_prefetch=1,
            grid=(n_chunk, slots),
            in_specs=[
                pl.BlockSpec((1, cells, LANES), lambda c, s, _: (s, 0, c)),
                pl.BlockSpec((1, side, side, LANES), lambda c, s, _: (s, 0, 0, c)),
                pl.BlockSpec((1, cells, LANES), lambda c, s, _: (s, 0, 0)),
                pl.BlockSpec((50, 8, LANES), lambda c, s, _: (0, 0, c)),
                pl.BlockSpec((8, LANES), lambda c, s, _: (0, 0)),
            ]
            + [pl.BlockSpec(memory_space=pl.ANY)] * n_tile,
            out_specs=pl.BlockSpec((1, cells, LANES), lambda c, s, _: (s, 0, c)),
            scratch_shapes=[
                pltpu.VMEM(((side + 2 * RIM) * PITCH, LANES), F32),
                pltpu.VMEM((n_tile,) + halos[0].shape, BF),
                pltpu.SemaphoreType.DMA((n_tile,)),
            ],
        ),
        out_shape=jax.ShapeDtypeStruct((slots, cells, channels), F32),
        cost_estimate=conv_cost(n_chunk, slots, side, 12 << 20),
        compiler_params=pltpu.CompilerParams(vmem_limit_bytes=32 << 20),
        name="conv_backward",
    )(own_tile, d_conv, cotangent, mask_lanes, taps, weight_lanes, *halos)


def spread_lanes(value, parts, width):
    rows, channels = value.shape
    run = channels // parts
    if run == width:
        return value
    gap = jnp.zeros((rows, width - run), value.dtype)
    pieces = []
    for t in range(parts):
        pieces += [value[:, t * run : (t + 1) * run], gap]
    return jnp.concatenate(pieces, 1)


def close_lanes(value, parts, run):
    width = value.shape[1] // parts
    if run == width:
        return value
    return jnp.concatenate([value[:, t * width : t * width + run] for t in range(parts)], 1)


def arrange(body, args, specs, rows, channels, parts, width, name):
    step = 3 * LANES if rows % (3 * LANES) == 0 else LANES

    def kernel(*refs):
        given, (gap_ref, turned_ref, sum_ref) = refs[: len(args)], refs[len(args) :]
        low = body(*given).astype(BF)
        value = low.astype(F32)
        gap_ref[...] = spread_lanes(value, parts, width).astype(BF)
        turned_ref[...] = value.T.astype(BF)

        @pl.when(pl.program_id(0) == 0)
        def _():
            sum_ref[...] = jnp.zeros_like(sum_ref)

        sum_ref[...] += jnp.sum(value, axis=0, keepdims=True)

    return pl.pallas_call(
        kernel,
        grid=(rows // step,),
        in_specs=specs(step),
        out_specs=[
            pl.BlockSpec((step, parts * width), lambda i: (i, 0)),
            pl.BlockSpec((channels, step), lambda i: (0, i)),
            pl.BlockSpec((1, channels), lambda i: (0, 0)),
        ],
        out_shape=[
            jax.ShapeDtypeStruct((rows, parts * width), BF),
            jax.ShapeDtypeStruct((channels, rows), BF),
            jax.ShapeDtypeStruct((1, channels), F32),
        ],
        compiler_params=pltpu.CompilerParams(vmem_limit_bytes=48 << 20),
        name=name,
    )(*args)


def feed_forward(inverse, place, shaped, shaped_t, d_branch, d_branch_t, hidden_bias, weights, grid, run, piece_rows):
    rows, depth = shaped.shape
    channels = shaped_t.shape[0]
    half, _, cols = hidden_bias.shape
    pairs = len(weights)
    n_tile = grid.n_tile
    width = depth // n_tile
    side_b, side_a, side_x = grid.size["b"], grid.size["a"], grid.size["x"]
    per_owner = 2 * pairs
    tile_rows = 3 * LANES if rows % (3 * LANES) == 0 else LANES
    flat = [w for pair in weights for w in pair]

    def kernel(inv_ref, place_ref, s_ref, st_ref, d_ref, dt_ref, hb_ref, *rest):
        given = rest[: 2 * pairs]
        branch_ref, ds_ref, keep_ref, send_ref, bias_ref = rest[2 * pairs : 2 * pairs + 5]
        packed, first, second, act, dpre, grads, sems, out_sems = rest[2 * pairs + 5 :]
        step = pl.program_id(0)
        own_a, own_b, own_x, own_c = (place_ref[i] for i in range(4))

        def where(slot):
            owner, inside = slot // per_owner, slot % per_owner
            return (owner // 2) ^ own_x, (owner % 2) ^ own_c, inside // 2, inside % 2

        def fetch(h, buffer):
            for which in range(2):
                rel_x, rel_c, pair, _ = where(inv_ref[h + which * half])
                for m in range(pairs):
                    for c in range(2):

                        @pl.when((pair == m) & (rel_c == c))
                        def _():
                            for t in range(n_tile):
                                rel_a, rel_b = (t // side_b) ^ own_a, (t % side_b) ^ own_b
                                if m % 2 == 0:
                                    at = (rel_b * side_x + rel_x) * side_a + rel_a
                                else:
                                    at = (rel_x * side_b + rel_b) * side_a + rel_a
                                pltpu.make_async_copy(
                                    given[2 * m + c].at[at],
                                    packed.at[buffer, which, pl.ds(t * width, width)],
                                    sems.at[buffer, which, t],
                                ).start()

        @pl.when(step == 0)
        def _():
            fetch(0, 0)
            grads[:, :, pl.ds(channels, grads.shape[2] - channels), :] = jnp.zeros(
                (2, grads.shape[1], grads.shape[2] - channels, 2 * cols), BF
            )

        @pl.when(step + 1 < half)
        def _():
            fetch(step + 1, (step + 1) % 2)

        now = step % 2
        slots = [where(inv_ref[step + which * half]) for which in range(2)]
        for which, held in enumerate((first, second)):
            for t in range(n_tile):
                pltpu.make_async_copy(
                    given[0].at[0], packed.at[now, which, pl.ds(t * width, width)], sems.at[now, which, t]
                ).wait()
            for parity in range(2):

                @pl.when(slots[which][3] == parity)
                def _():
                    held[...] = packed[now, which, :, parity * cols : (parity + 1) * cols]

        hidden = hb_ref[0]
        total = jnp.zeros((1, cols), F32)
        across = (((1,), (1,)), ((), ()))
        for i in range(rows // tile_rows):
            at = pl.ds(i * tile_rows, tile_rows)
            pre = jnp.dot(s_ref[at, :], first[...], preferred_element_type=F32) + hidden
            d_act = jnp.dot(d_ref[at, :], second[...], preferred_element_type=F32)
            square = pre * pre
            bend = jnp.tanh(ROOT * pre * (1.0 + CUBE * square))
            half_up = 0.5 * (1.0 + bend)
            low = (pre * half_up).astype(BF)
            slope = half_up + (0.5 * ROOT) * pre * (1.0 - bend * bend) * (1.0 + (3.0 * CUBE) * square)
            back = (d_act * slope).astype(BF)
            act[at, :] = low
            dpre[at, :] = back
            total = total + jnp.sum(back.astype(F32), axis=0, keepdims=True)
            out_add = lax.dot_general(low, second[...], across, preferred_element_type=F32)
            in_add = lax.dot_general(back, first[...], across, preferred_element_type=F32)

            @pl.when(step == 0)
            def _():
                branch_ref[at, :] = out_add
                ds_ref[at, :] = in_add

            @pl.when(step > 0)
            def _():
                branch_ref[at, :] += out_add
                ds_ref[at, :] += in_add

        bias_ref[0] = total
        for which, (left, right) in enumerate(((st_ref, dpre), (dt_ref, act))):
            rel_x, rel_c, pair, half_of_pair = slots[which]
            value = jnp.dot(left[...], right[...], preferred_element_type=F32).astype(BF)
            for parity in range(2):

                @pl.when(half_of_pair == parity)
                def _():
                    grads[rel_c, rel_x * pairs + pair, pl.ds(0, channels), parity * cols : (parity + 1) * cols] = value

        @pl.when(step == half - 1)
        def _():
            copies = []
            for c, out in enumerate((keep_ref, send_ref)):
                copies.append(pltpu.make_async_copy(grads.at[c], out, out_sems.at[c]))
            for c in copies:
                c.start()
            for c in copies:
                c.wait()

    whole = lambda *shape: pl.BlockSpec(shape, lambda h, *_: (0,) * len(shape))
    grad_shape = (side_x * pairs, piece_rows * n_tile, 2 * cols)
    return pl.pallas_call(
        kernel,
        grid_spec=pltpu.PrefetchScalarGridSpec(
            num_scalar_prefetch=2,
            grid=(half,),
            in_specs=[
                whole(rows, depth),
                whole(channels, rows),
                whole(rows, depth),
                whole(channels, rows),
                pl.BlockSpec((1, 1, cols), lambda h, *_: (h, 0, 0)),
            ]
            + [pl.BlockSpec(memory_space=pl.ANY)] * len(flat),
            out_specs=[
                whole(rows, depth),
                whole(rows, depth),
                pl.BlockSpec(memory_space=pl.ANY),
                pl.BlockSpec(memory_space=pl.ANY),
                pl.BlockSpec((1, 1, cols), lambda h, *_: (h, 0, 0)),
            ],
            scratch_shapes=[
                pltpu.VMEM((2, 2, depth, 2 * cols), BF),
                pltpu.VMEM((depth, cols), BF),
                pltpu.VMEM((depth, cols), BF),
                pltpu.VMEM((rows, cols), BF),
                pltpu.VMEM((rows, cols), BF),
                pltpu.VMEM((2,) + grad_shape, BF),
                pltpu.SemaphoreType.DMA((2, 2, n_tile)),
                pltpu.SemaphoreType.DMA((2,)),
            ],
        ),
        out_shape=[
            jax.ShapeDtypeStruct((rows, depth), F32),
            jax.ShapeDtypeStruct((rows, depth), F32),
            jax.ShapeDtypeStruct(grad_shape, BF),
            jax.ShapeDtypeStruct(grad_shape, BF),
            jax.ShapeDtypeStruct((half, 1, cols), F32),
        ],
        cost_estimate=pl.CostEstimate(
            flops=12 * rows * channels * half * cols, bytes_accessed=40 << 20, transcendentals=rows * half * cols
        ),
        compiler_params=pltpu.CompilerParams(vmem_limit_bytes=63 << 20),
        name="feed_forward",
    )(inverse, place, shaped, shaped_t, d_branch, d_branch_t, hidden_bias, *flat)


def close_out(branch, d_shaped, inputs, conv_out, mask_lanes, out_bias, parts, run):
    rows, channels = inputs.shape
    depth = branch.shape[1]
    step = 3 * LANES if rows % (3 * LANES) == 0 else LANES

    def kernel(b_ref, d_ref, x_ref, v_ref, m_ref, o_ref, out_ref, ds_ref, sum_ref):
        branch_here = close_lanes(b_ref[...], parts, run) + o_ref[...]
        out_ref[...] = (m_ref[:, :1] * (x_ref[...].astype(F32) + branch_here)).astype(BF)
        grads = close_lanes(d_ref[...], parts, run)
        ds_ref[...] = grads

        @pl.when(pl.program_id(0) == 0)
        def _():
            sum_ref[...] = jnp.zeros_like(sum_ref)

        sum_ref[0] += jnp.sum(grads, axis=0, keepdims=True)
        sum_ref[1] += jnp.sum(grads * v_ref[...], axis=0, keepdims=True)

    line = lambda n: pl.BlockSpec((step, n), lambda i: (i, 0))
    return pl.pallas_call(
        kernel,
        grid=(rows // step,),
        in_specs=[
            line(depth),
            line(depth),
            line(channels),
            line(channels),
            line(LANES),
            pl.BlockSpec((1, channels), lambda i: (0, 0)),
        ],
        out_specs=[line(channels), line(channels), pl.BlockSpec((2, 1, channels), lambda i: (0, 0, 0))],
        out_shape=[
            jax.ShapeDtypeStruct((rows, channels), BF),
            jax.ShapeDtypeStruct((rows, channels), F32),
            jax.ShapeDtypeStruct((2, 1, channels), F32),
        ],
        compiler_params=pltpu.CompilerParams(vmem_limit_bytes=60 << 20),
        name="close_out",
    )(branch, d_shaped, inputs, conv_out, mask_lanes, out_bias)


def up_to(value, unit):
    return -(-value // unit) * unit


def pack_pairs(value):
    slots, rows, cols = value.shape
    return value.reshape(slots // 2, 2, rows, cols).transpose(0, 2, 1, 3).reshape(slots // 2, rows, 2 * cols)


def unpack_pairs(value):
    pairs, rows, cols = value.shape
    return value.reshape(pairs, rows, 2, cols // 2).transpose(0, 2, 1, 3).reshape(2 * pairs, rows, cols // 2)


def gather_weights(grid, packed):
    gathered = []
    for m in range(packed.shape[0]):
        value = packed[m]
        for dim in ("a", "x", "b") if m % 2 == 0 else ("a", "b", "x"):
            value = grid.gather(value, dim)
        value = value.reshape((-1,) + packed.shape[1:])
        gathered.append((value, grid.swap(value, "c", 1)))
    return gathered


def add_up(parts):
    total = parts[0].astype(F32)
    for part in parts[1:]:
        total = total + part.astype(F32)
    return total.astype(BF)


def take(value, index, axis):
    return lax.dynamic_index_in_dim(value, index, axis, keepdims=False)


def reduce_gradients(grid, own, keep, send, pairs):
    size = grid.size
    whole, cols = keep.shape[1:]
    piece = whole // grid.n_tile
    both = add_up([keep, grid.swap(send, "c", 1)]).reshape(size["x"], pairs, size["b"], size["a"] * piece, cols)
    results = []
    for m in range(pairs):
        value = both[:, m]
        for dim in ("x", "b") if m % 2 == 0 else ("b", "x"):
            if dim == "x":
                value = add_up([value[0]] + [grid.swap(value[k], "x", k) for k in range(1, size["x"])])
            else:
                axis = value.ndim - 3
                others = [
                    grid.swap(take(value, own["b"] ^ k, axis), "b", k) for k in range(1, size["b"])
                ]
                value = add_up([take(value, own["b"], axis)] + others)
        value = value.reshape(size["a"], piece, cols)
        others = [grid.swap(take(value, own["a"] ^ k, 0), "a", k) for k in range(1, size["a"])]
        results.append(add_up([take(value, own["a"], 0)] + others))
    return results


def gather_gradients(grid, own, pieces):
    wholes = []
    for value in pieces:
        value = natural(grid.gather(value, "a"), own["a"], grid.size["a"])
        value = value.reshape((-1,) + value.shape[2:])
        value = natural(grid.gather(value, "b"), own["b"], grid.size["b"])
        wholes.append(value.reshape((-1,) + value.shape[2:]))
    return jnp.stack(wholes)


def per_device(
    grid,
    inputs,
    cotangent,
    master,
    moment_one,
    moment_two,
    left_basis,
    column_basis,
    small_params,
    small_first,
    small_second,
    land_mask,
    tile_count,
    neighbours,
    block_order,
    cell_weight,
    step_count,
):
    own = grid.own()
    position = lax.axis_index("tile")
    sample = lax.axis_index("opt")
    own_tile = jnp.reshape(position, (1,)).astype(jnp.int32)
    inputs, cotangent = inputs[0], cotangent[0]
    slots, side, _, channels = inputs.shape
    cells = side * side
    rows = slots * cells
    n_tile = grid.n_tile
    n_chunk = -(-channels // LANES)
    per_group = channels // GROUPS
    per_owner, run, cols = master.shape
    pairs = per_owner // 2
    block_total = block_order.shape[0]
    half = block_total // 2
    width = up_to(run, 16)

    live = (jnp.arange(slots) < tile_count[position]).astype(F32)
    mask = (land_mask.astype(F32) * live[:, None, None]).reshape(slots, cells)
    mask_lanes = jnp.broadcast_to(mask[:, :, None], (slots, cells, LANES))
    flat_mask = mask_lanes.reshape(rows, LANES)
    taps = jnp.broadcast_to(small_params[:50, None, :], (50, 8, channels))
    neighbours_rel = jnp.stack(
        [neighbours] + [grid.tile_swap(neighbours, k) for k in range(1, n_tile)]
    ).reshape(-1)

    low_master = jnp.pad(pack_pairs(master.astype(BF)), ((0, 0), (0, width - run), (0, 0)))
    rims = rims_of_input(inputs, mask_lanes, own_tile, n_tile)
    halos = exchange_halos(grid, rims, neighbours_rel, own_tile, side, n_chunk)
    weights = gather_weights(grid, low_master)

    weights_float = cell_weight.astype(F32)
    sample_weight = weights_float[sample] * weights_float.shape[0] / jnp.sum(weights_float)
    weight_lanes = jnp.broadcast_to(sample_weight, (8, LANES))
    weight_row = jnp.broadcast_to(sample_weight, (1, LANES))
    flat_cotangent = cotangent.reshape(rows, channels)

    def d_branch_body(g_ref, m_ref, w_ref):
        return m_ref[:, :1] * (w_ref[:, :1] * g_ref[...].astype(F32))

    d_branch, d_branch_t, d_out_bias = arrange(
        d_branch_body,
        (flat_cotangent, flat_mask, weight_row),
        lambda step: [
            pl.BlockSpec((step, channels), lambda i: (i, 0)),
            pl.BlockSpec((step, LANES), lambda i: (i, 0)),
            pl.BlockSpec((1, LANES), lambda i: (0, 0)),
        ],
        rows,
        channels,
        n_tile,
        width,
        "arrange_d_branch",
    )
    low_left = left_basis.astype(BF).reshape(per_owner, n_tile, run, run)
    left_rel = [take(low_left, position, 1)] + [
        grid.tile_swap(take(low_left, position ^ k, 1), k) for k in range(1, n_tile)
    ]
    left_rows = jnp.concatenate(left_rel, 2)

    conv_out, sums = conv_forward(inputs, mask_lanes, halos, taps, own_tile)
    sums = jnp.sum(sums, axis=(0, 2))
    occupied = jnp.broadcast_to(jnp.sum(mask), (1, channels))
    sums = grid.total(jnp.concatenate([sums, occupied], 0), ("b", "a"))
    counted = sums[2, 0] * per_group
    by_group = sums[:2].reshape(2, GROUPS, per_group).sum(2)
    group_mean = by_group[0] / counted
    variance = by_group[1] / counted - group_mean * group_mean
    inv_std = jnp.repeat(lax.rsqrt(variance + epsilon), per_group)
    mean = jnp.repeat(group_mean, per_group)
    gain, shift = small_params[50], small_params[51]
    norm_coefs = jnp.stack([inv_std, mean * inv_std, gain, shift])

    def shaped_body(v_ref, c_ref):
        normed = v_ref[...] * c_ref[0:1] - c_ref[1:2]
        return normed * c_ref[2:3] + c_ref[3:4]

    flat_conv = conv_out.reshape(rows, channels)
    shaped, shaped_t, _ = arrange(
        shaped_body,
        (flat_conv, norm_coefs),
        lambda step: [
            pl.BlockSpec((step, channels), lambda i: (i, 0)),
            pl.BlockSpec((4, channels), lambda i: (0, 0)),
        ],
        rows,
        channels,
        n_tile,
        width,
        "arrange_shaped",
    )

    block_ids = jnp.arange(block_total, dtype=jnp.int32)
    inverse = jnp.sum(
        jnp.where(block_order[None, :] == block_ids[:, None], block_ids[None, :], 0), axis=1
    ).astype(jnp.int32)
    place = jnp.stack([own["a"], own["b"], own["x"], own["c"]]).astype(jnp.int32)
    hidden_bias = small_params[53:57].reshape(half, 1, cols)
    piece_rows = up_to(channels // n_tile, 8)
    branch, d_shaped, grads_keep, grads_send, d_hidden = feed_forward(
        inverse, place, shaped, shaped_t, d_branch, d_branch_t, hidden_bias, weights, grid, run, piece_rows
    )
    block_output, d_shaped, d_sums = close_out(
        branch, d_shaped, inputs.reshape(rows, channels), flat_conv, flat_mask, small_params[52:53], n_tile, run
    )
    pieces = reduce_gradients(grid, own, grads_keep, grads_send, pairs)

    d_shift = d_sums[0, 0]
    d_gain = inv_std * (d_sums[1, 0] - mean * d_shift)
    parts = grid.total(jnp.stack([gain * d_shift, gain * d_gain]), ("b", "a"))
    parts = jnp.repeat(parts.reshape(2, GROUPS, per_group).sum(2) / counted, per_group, axis=1)
    grad_coefs = jnp.stack(
        [
            inv_std * gain,
            inv_std * (parts[0] - mean * inv_std * parts[1]),
            inv_std * inv_std * parts[1],
        ]
    )
    d_conv, *grad_rims = conv_gradient(
        d_shaped.reshape(slots, cells, channels),
        conv_out,
        mask_lanes,
        jnp.broadcast_to(grad_coefs[:, None, :], (3, 8, channels)),
        own_tile,
        n_tile,
        side,
    )
    grad_halos = exchange_halos(grid, grad_rims, neighbours_rel, own_tile, side, n_chunk)
    d_taps = tap_gradient(inputs, mask_lanes, halos, d_conv, own_tile)
    input_grad = conv_backward(d_conv, grad_halos, cotangent, mask_lanes, taps, weight_lanes, own_tile)

    correction = 1.0 - jnp.power(F32(decay_rate), step_count[0].astype(F32))
    d_small = jnp.concatenate(
        [d_taps, d_gain[None], d_shift[None], d_out_bias, d_hidden.reshape(4, channels)], 0
    )
    d_small = grid.total(d_small, ("c", "x", "b", "a"))
    small_one = decay_rate * small_first + (1.0 - decay_rate) * d_small
    small_two = decay_rate * small_second + (1.0 - decay_rate) * d_small * d_small
    new_small = small_params - small_rate * (small_one / correction) / (
        jnp.sqrt(small_two / correction) + adam_eps
    )

    owned = unpack_pairs(gather_gradients(grid, own, pieces)[:, :channels])
    rotated = jnp.einsum("bdk,bdw->bkw", left_basis, owned.astype(F32), precision=highest)
    rotated = jnp.einsum("bkw,bwv->bkv", rotated, column_basis, precision=highest)
    first_new = decay_rate * moment_one + (1.0 - decay_rate) * rotated
    second_new = decay_rate * moment_two + (1.0 - decay_rate) * rotated * rotated
    direction = first_new / correction / (jnp.sqrt(second_new / correction) + adam_eps)
    turned = jnp.einsum("bkv,bwv->bkw", direction, column_basis, precision=highest).astype(BF)
    turned = grid.gather(grid.gather(pack_pairs(turned), "a"), "b")
    turned = turned.transpose(2, 1, 0, 3, 4).reshape(pairs, n_tile * run, 2 * cols)
    change = jnp.einsum("bdk,bkw->bdw", left_rows, unpack_pairs(turned), preferred_element_type=F32)
    new_master = master - 0.5 / math.sqrt(channels) * change
    return (
        block_output.reshape((1,) + inputs.shape),
        input_grad.reshape((1,) + inputs.shape),
        new_master,
        new_master.astype(BF),
        first_new,
        second_new,
        new_small,
        small_one,
        small_two,
    )


def solution(mesh):
    grid = Grid(mesh.shape["tile"], mesh.shape["opt"])

    def step(*args):
        return per_device(grid, *args)

    return jax.shard_map(
        step,
        mesh=mesh,
        in_specs=(
            P("opt", "tile", None, None, None),
            P("opt", "tile", None, None, None),
            P("opt", "tile", None),
            P("opt", "tile", None),
            P("opt", "tile", None),
            P("opt", None, "tile"),
            P("opt", None, None),
            P(),
            P(),
            P(),
            P("tile", None, None),
            P(),
            P("tile", None),
            P(),
            P(),
            P(),
        ),
        out_specs=(
            P("opt", "tile", None, None, None),
            P("opt", "tile", None, None, None),
            P("opt", "tile", None),
            P("opt", "tile", None),
            P("opt", "tile", None),
            P("opt", "tile", None),
            P(),
            P(),
            P(),
        ),
        check_vma=False,
    )
```

```python
import math

import jax
import jax.numpy as jnp
from jax import lax
from jax.experimental import pallas as pl
from jax.experimental.pallas import tpu as pltpu
from jax.sharding import PartitionSpec as P

GROUPS = 16
LANES = 128
RIM = 3
PITCH = 40
BF = jnp.bfloat16
F32 = jnp.float32

highest = lax.Precision.HIGHEST
epsilon = 1e-05
adam_eps = 1e-08
decay_rate = 0.5
small_rate = 0.05
ROOT = 0.7978845608028654
CUBE = 0.044715


class Grid:
    def __init__(self, n_tile, n_opt):
        b = 4 if n_tile % 16 == 0 else 2
        self.n_tile, self.n_opt = n_tile, n_opt
        self.size = {"a": n_tile // b, "b": b, "x": n_opt // 2, "c": 2}

    def own(self):
        t, o = lax.axis_index("tile"), lax.axis_index("opt")
        b = self.size["b"]
        return {"a": t // b, "b": t % b, "x": o // 2, "c": o % 2}

    def at(self, place):
        return place["a"] * self.size["b"] + place["b"], place["x"] * 2 + place["c"]

    def partners(self, dims):
        own = self.own()
        found = []
        for dim in dims:
            if dim == "tile":
                t, o = self.at(own)
                found += [(t ^ k, o) for k in range(1, self.n_tile)]
            else:
                found += [self.beside(own, dim, k) for k in range(1, self.size[dim])]
        return found

    def beside(self, own, dim, k):
        return self.at({**own, dim: own[dim] ^ k})


def meet(devices):
    barrier = pltpu.get_barrier_semaphore()
    for device in devices:
        pl.semaphore_signal(barrier, inc=1, device_id=device, device_id_type=pl.DeviceIdType.MESH)
    pl.semaphore_wait(barrier, len(devices))


class Copies:
    def __init__(self, send_sems, recv_sems):
        self.sems = send_sems, recv_sems
        self.used = 0

    def make(self, src, dst, device):
        i = self.used
        self.used += 1
        return pltpu.make_async_remote_copy(
            src_ref=src,
            dst_ref=dst,
            send_sem=self.sems[0].at[i],
            recv_sem=self.sems[1].at[i],
            device_id=device,
            device_id_type=pl.DeviceIdType.MESH,
        )

    def start(self, src, dst, device):
        copy = self.make(src, dst, device)
        copy.start()
        return copy


def remote_params(number, mib):
    return pltpu.CompilerParams(collective_id=number, has_side_effects=True, vmem_limit_bytes=mib << 20)


def add_rows(target, sources, rows, step=16):
    @pl.loop(0, rows // step)
    def _(i):
        at = pl.ds(pl.multiple_of(i * step, step), step)
        total = target[at, :].astype(F32)
        for source in sources:
            total = total + source[at, :].astype(F32)
        target[at, :] = total.astype(BF)


def store_rims(src, outs, slot, side):
    outs[0, slot, 0] = src[pl.ds(0, RIM * side), :].astype(BF)
    outs[0, slot, 1] = src[pl.ds((side - RIM) * side, RIM * side), :].astype(BF)
    for e in range(RIM):
        rows = pl.ds(e * side, side)
        outs[0, slot, 2, rows] = src[pl.ds(e, side, stride=side), :].astype(BF)
        outs[0, slot, 3, rows] = src[pl.ds(side - RIM + e, side, stride=side), :].astype(BF)


def rims_of_input(inputs, mask_lanes):
    slots, side, _, channels = inputs.shape
    n_chunk = -(-channels // LANES)

    def kernel(x_ref, m_ref, o_ref, cells):
        for s in range(slots):
            for i in range(side):
                cells[pl.ds(i * side, side), :] = (
                    x_ref[s, i].astype(F32) * m_ref[s, pl.ds(i * side, side), :]
                )
            store_rims(cells, o_ref, s, side)

    return pl.pallas_call(
        kernel,
        grid=(n_chunk,),
        in_specs=[
            pl.BlockSpec((slots, side, side, LANES), lambda c: (0, 0, 0, c)),
            pl.BlockSpec((slots, side * side, LANES), lambda c: (0, 0, 0)),
        ],
        out_specs=pl.BlockSpec((1, slots, 4, RIM * side, LANES), lambda c: (c, 0, 0, 0, 0)),
        out_shape=jax.ShapeDtypeStruct((n_chunk, slots, 4, RIM * side, LANES), BF),
        scratch_shapes=[pltpu.VMEM((side * side, LANES), F32)],
        compiler_params=pltpu.CompilerParams(vmem_limit_bytes=32 << 20),
        name="rims_of_input",
    )(inputs, mask_lanes)


class HaloExchange:
    def __init__(self, grid, n_chunk, slots, side):
        self.grid, self.n_chunk, self.slots, self.side = grid, n_chunk, slots, side
        self.count = 2 * (grid.n_tile - 1)

    def scratch(self):
        n, s, band = self.grid.n_tile, self.slots, RIM * self.side
        return [
            pltpu.VMEM((n, s, 4, band, LANES), BF),
            pltpu.VMEM((n, s, 5, band, LANES), BF),
            pltpu.SemaphoreType.DMA((2,)),
        ]

    def halo_shape(self):
        return jax.ShapeDtypeStruct((self.n_chunk, self.slots, 5, RIM * self.side, LANES), BF)

    def send_rims(self, copies, rims, arrived, local):
        t, o = self.grid.at(self.grid.own())
        self.t, self.o = t, o
        self.first = []
        for k in range(1, self.grid.n_tile):
            to = t ^ k
            source = jnp.minimum(to, self.n_chunk - 1)
            copy = copies.make(rims.at[source], arrived.at[t], (to, o))
            self.first.append((to, copy))

            @pl.when(to < self.n_chunk)
            def _():
                copy.start()

        own = pltpu.make_async_copy(rims.at[jnp.minimum(t, self.n_chunk - 1)], arrived.at[t], local.at[0])
        own.start()
        self.own_copy = own

    def pick_and_send(self, copies, arrived, picked, halos, local, neighbours):
        grid, slots, side = self.grid, self.slots, self.side
        t, o = self.t, self.o
        self.own_copy.wait()
        for _, copy in self.first:

            @pl.when(t < self.n_chunk)
            def _():
                copy.wait_recv()

        @pl.when(t < self.n_chunk)
        def _():
            @pl.loop(0, grid.n_tile * slots)
            def _(d):
                def rim(direction, which):
                    slot = neighbours(d, direction)
                    at = jnp.maximum(slot, 0)
                    value = arrived[at // slots, at % slots, which].astype(F32)
                    return jnp.where(slot >= 0, value, 0.0)

                to_tile, to_slot = d // slots, d % slots
                for to, (direction, which) in enumerate(((1, 1), (6, 0), (3, 3), (4, 2))):
                    picked[to_tile, to_slot, to] = rim(direction, which).astype(BF)
                rows = []
                for direction, which, first in ((0, 1, side - RIM), (2, 1, 0), (5, 0, side - RIM), (7, 0, 0)):
                    value = rim(direction, which)
                    rows += [value[e * side + first : e * side + first + RIM] for e in range(RIM)]
                    rows.append(jnp.zeros((16 - RIM * RIM, LANES), F32))
                rows.append(jnp.zeros((RIM * side - 64, LANES), F32))
                picked[to_tile, to_slot, 4] = jnp.concatenate(rows, 0).astype(BF)

        own_chunk = jnp.minimum(t, self.n_chunk - 1)
        self.second = []
        for k in range(1, grid.n_tile):
            to = t ^ k
            copy = copies.make(picked.at[to], halos.at[own_chunk], (to, o))
            self.second.append((to, copy))

            @pl.when(t < self.n_chunk)
            def _():
                copy.start()

        self.back_copy = pltpu.make_async_copy(picked.at[t], halos.at[own_chunk], local.at[1])

        @pl.when(t < self.n_chunk)
        def _():
            self.back_copy.start()

    def finish(self):
        t = self.t

        @pl.when(t < self.n_chunk)
        def _():
            self.back_copy.wait()

        for to, copy in self.first:

            @pl.when(to < self.n_chunk)
            def _():
                copy.wait_send()

        for to, copy in self.second:

            @pl.when(to < self.n_chunk)
            def _():
                copy.wait_recv()

            @pl.when(t < self.n_chunk)
            def _():
                copy.wait_send()


class WeightGather:
    def __init__(self, grid, pairs, width):
        self.grid, self.pairs, self.width = grid, pairs, width
        self.count = pairs * (grid.n_tile * grid.n_opt - 1)

    def run(self, copies, packed, gathered, local):
        grid, width = self.grid, self.width
        own = grid.own()

        def place(m, rel):
            t, o = grid.at({d: own[d] ^ rel.get(d, 0) for d in own})
            return gathered.at[m, o, pl.ds(pl.multiple_of(t * width, width), width)]

        keeps = []
        known = []
        for m in range(self.pairs):
            keep = pltpu.make_async_copy(packed.at[m], place(m, {}), local.at[m])
            keep.start()
            keeps.append(keep)
            known.append([({}, None)])
        arrived = set()
        for stage in range(4):
            for m in range(self.pairs):
                order = ("a", "x", "b", "c") if m % 2 == 0 else ("a", "b", "x", "c")
                dim = order[stage]
                fresh = []
                for k in range(1, grid.size[dim]):
                    for rel, got in known[m]:
                        if got is not None and id(got) not in arrived:
                            got.wait_recv()
                            arrived.add(id(got))
                        source = packed.at[m] if not rel else place(m, rel)
                        copy = copies.start(source, place(m, rel), grid.beside(own, dim, k))
                        fresh.append(({**rel, dim: k}, copy))
                known[m] = known[m] + fresh
            yield stage
        for m in range(self.pairs):
            keeps[m].wait()
            for _, got in known[m]:
                if got is not None:
                    if id(got) not in arrived:
                        got.wait_recv()
                    got.wait_send()
        yield 4


def exchange_forward(grid, rims, packed, neighbours):
    n_chunk, slots, _, band, _ = rims.shape
    pairs, width, cols = packed.shape
    n_tile = grid.n_tile
    halo = HaloExchange(grid, n_chunk, slots, band // RIM)
    gather = WeightGather(grid, pairs, width)
    total = halo.count + gather.count + n_tile - 1

    def kernel(r_ref, p_ref, n_ref, halo_ref, w_ref, nbr_ref, arrived, picked, local, table, send, recv, locals_w, locals_n):
        own = grid.own()
        t, o = grid.at(own)
        meet(grid.partners(("tile", "x", "c")))
        copies = Copies(send, recv)
        tables = [copies.start(n_ref, nbr_ref.at[t], (t ^ k, o)) for k in range(1, n_tile)]
        keep = pltpu.make_async_copy(n_ref, nbr_ref.at[t], locals_n.at[0])
        keep.start()
        halo.send_rims(copies, r_ref, arrived, local)
        weights = gather.run(copies, p_ref, w_ref, locals_w)
        next(weights)
        keep.wait()
        for copy in tables:
            copy.wait()
        load = pltpu.make_async_copy(nbr_ref, table, locals_n.at[1])
        load.start()
        load.wait()
        halo.pick_and_send(
            copies, arrived, picked, halo_ref, local, lambda d, k: table[d // slots, d % slots, k]
        )
        for _ in weights:
            pass
        halo.finish()

    any_space = pl.BlockSpec(memory_space=pl.ANY)
    return pl.pallas_call(
        kernel,
        in_specs=[any_space] * 3,
        out_specs=[any_space] * 3,
        out_shape=[
            halo.halo_shape(),
            jax.ShapeDtypeStruct((pairs, grid.n_opt, n_tile * width, cols), BF),
            jax.ShapeDtypeStruct((n_tile,) + neighbours.shape, jnp.int32),
        ],
        scratch_shapes=halo.scratch()
        + [
            pltpu.SMEM((n_tile,) + neighbours.shape, jnp.int32),
            pltpu.SemaphoreType.DMA((total,)),
            pltpu.SemaphoreType.DMA((total,)),
            pltpu.SemaphoreType.DMA((pairs,)),
            pltpu.SemaphoreType.DMA((2,)),
        ],
        compiler_params=remote_params(1, 32),
        name="exchange_forward",
    )(rims, packed, neighbours)


def exchange_backward(grid, rims, grads, neighbours):
    n_chunk, slots, _, band, _ = rims.shape
    n_tile = grid.n_tile
    side_a, side_b, side_x = grid.size["a"], grid.size["b"], grid.size["x"]
    _, blocks, rows, cols = grads.shape
    pairs = blocks // side_x
    part = rows // side_b
    halo = HaloExchange(grid, n_chunk, slots, band // RIM)
    total = halo.count + blocks + pairs * ((side_x - 1) + (side_b - 1)) + pairs * side_x * (side_b - 1)

    def kernel(r_ref, g_ref, n_ref, halo_ref, o_ref, arrived, picked, local, here, core, far, across, send, recv, load_sems):
        own = grid.own()
        own_x, own_b = own["x"], own["b"]
        meet(grid.partners(("tile", "x", "c")))
        copies = Copies(send, recv)
        halo.send_rims(copies, r_ref, arrived, local)
        loads, cores = [], []
        order = []
        for m in range(pairs):
            order += [(k, m) for k in range(1, side_x)] if m % 2 == 0 else []
        order += [(k, m) for m in range(pairs) for k in range(side_x) if (k, m) not in order]
        index = lambda k, m: (own_x ^ k) * pairs + m
        for i, (k, m) in enumerate(order):
            at = index(k, m)
            cores.append(copies.start(g_ref.at[1 - own["c"], at], core.at[at], grid.beside(own, "c", 1)))
            load = pltpu.make_async_copy(g_ref.at[own["c"], at], here.at[at], load_sems.at[i])
            load.start()
            loads.append(load)
        sent_x = {m: [] for m in range(pairs)}
        sent_b = {m: [] for m in range(pairs)}
        rows_of = lambda b: pl.ds(pl.multiple_of(b * part, 16), part)

        def send_b(m, k):
            for j in range(1, side_b):
                to = grid.beside(own, "b", j)
                at = index(k, m)
                sent_b[m].append(
                    (k, copies.start(here.at[at, rows_of(own_b ^ j)], across.at[j - 1, at], to))
                )

        def send_x(m, k):
            at = index(k, m)
            to = grid.beside(own, "x", k)
            if m % 2 == 0:
                sent_x[m].append(copies.start(here.at[at], far.at[k - 1, m], to))
            else:
                sent_x[m].append(
                    copies.start(here.at[at, rows_of(own_b)], far.at[k - 1, m, pl.ds(0, part)], to)
                )

        for i, (k, m) in enumerate(order):
            loads[i].wait()
            cores[i].wait_recv()
            at = index(k, m)
            add_rows(here.at[at], [core.at[at]], rows)
            if m % 2 == 1:
                send_b(m, k)
            elif k > 0:
                send_x(m, k)
        halo.pick_and_send(
            copies, arrived, picked, halo_ref, local, lambda d, k: n_ref[d // slots, d % slots, k]
        )
        for m in range(pairs):
            if m % 2 == 1:
                for k, copy in sent_b[m]:
                    copy.wait()
                for k in [*range(1, side_x), 0]:
                    at = index(k, m)
                    add_rows(here.at[at, rows_of(own_b)], [across.at[j, at] for j in range(side_b - 1)], part)
                    if k > 0:
                        send_x(m, k)
            else:
                for copy in sent_x[m]:
                    copy.wait()
                add_rows(here.at[index(0, m)], [far.at[j, m] for j in range(side_x - 1)], rows)
                send_b(m, 0)
        for m in range(pairs):
            at = index(0, m)
            if m % 2 == 1:
                for copy in sent_x[m]:
                    copy.wait()
                sources = [far.at[j, m, pl.ds(0, part)] for j in range(side_x - 1)]
            else:
                for _, copy in sent_b[m]:
                    copy.wait()
                sources = [across.at[j, at] for j in range(side_b - 1)]
            add_rows(here.at[at, rows_of(own_b)], sources, part)
        outs = []
        for m in range(pairs):
            out = pltpu.make_async_copy(here.at[index(0, m), rows_of(own_b)], o_ref.at[m], load_sems.at[m])
            out.start()
            outs.append(out)
        halo.finish()
        for copy in cores:
            copy.wait_send()
        for out in outs:
            out.wait()

    any_space = pl.BlockSpec(memory_space=pl.ANY)
    return pl.pallas_call(
        kernel,
        in_specs=[any_space, any_space, pl.BlockSpec(memory_space=pltpu.SMEM)],
        out_specs=[any_space] * 2,
        out_shape=[halo.halo_shape(), jax.ShapeDtypeStruct((pairs, part, cols), BF)],
        scratch_shapes=halo.scratch()
        + [
            pltpu.VMEM((blocks, rows, cols), BF),
            pltpu.VMEM((blocks, rows, cols), BF),
            pltpu.VMEM((side_x - 1, pairs, rows, cols), BF),
            pltpu.VMEM((side_b - 1, blocks, part, cols), BF),
            pltpu.SemaphoreType.DMA((total,)),
            pltpu.SemaphoreType.DMA((total,)),
            pltpu.SemaphoreType.DMA((blocks,)),
        ],
        compiler_params=remote_params(2, 56),
        name="exchange_backward",
    )(rims, grads, neighbours)


def finish_gradients(grid, partial, small):
    pairs, part, cols = partial.shape
    side_a, side_b = grid.size["a"], grid.size["b"]
    piece = part // side_a
    steps = [(dim, 1 << i) for dim in ("c", "x", "b", "a") for i in range((grid.size[dim] - 1).bit_length())]
    total = pairs * 2 * (side_a - 1) + pairs * side_a * (side_b - 1) + len(steps)

    def kernel(p_ref, s_ref, o_ref, t_ref, mine, got, sums, send, recv, load_sems):
        own = grid.own()
        meet(grid.partners(("a", "b", "x", "c")))
        copies = Copies(send, recv)
        rows_of = lambda a: pl.ds(pl.multiple_of(a * piece, 16), piece)
        place = lambda a, b: pl.ds(pl.multiple_of((b * side_a + a) * piece, 16), piece)
        firsts, loads = [], []
        for m in range(pairs):
            firsts.append(
                [
                    copies.start(p_ref.at[m, rows_of(own["a"] ^ k)], got.at[m, k - 1], grid.beside(own, "a", k))
                    for k in range(1, side_a)
                ]
            )
            load = pltpu.make_async_copy(p_ref.at[m, rows_of(own["a"])], mine.at[m], load_sems.at[m])
            load.start()
            loads.append(load)
        t_ref[...] = s_ref[...]
        small_copies = []

        def small_step(i):
            dim, k = steps[i]
            copy = copies.start(t_ref, sums.at[i], grid.beside(own, dim, k))
            copy.wait()
            t_ref[...] = t_ref[...] + sums[i]

        small_step(0)
        seconds, thirds, keeps = [], [], []
        for m in range(pairs):
            loads[m].wait()
            for copy in firsts[m]:
                copy.wait()
            add_rows(mine.at[m], [got.at[m, k] for k in range(side_a - 1)], piece)
            keep = pltpu.make_async_copy(mine.at[m], o_ref.at[m, place(own["a"], own["b"])], load_sems.at[m])
            keep.start()
            keeps.append(keep)
            to = o_ref.at[m, place(own["a"], own["b"])]
            seconds.append(
                [(k, copies.start(mine.at[m], to, grid.beside(own, "a", k))) for k in range(1, side_a)]
            )
            thirds += [copies.start(mine.at[m], to, grid.beside(own, "b", j)) for j in range(1, side_b)]
        for i in range(1, len(steps)):
            small_step(i)
        for m in range(pairs):
            for k, copy in seconds[m]:
                copy.wait_recv()
                at = o_ref.at[m, place(own["a"] ^ k, own["b"])]
                thirds += [copies.start(at, at, grid.beside(own, "b", j)) for j in range(1, side_b)]
        for m in range(pairs):
            keeps[m].wait()
            for _, copy in seconds[m]:
                copy.wait_send()
        for copy in thirds:
            copy.wait()

    any_space = pl.BlockSpec(memory_space=pl.ANY)
    whole = pl.BlockSpec(memory_space=pltpu.VMEM)
    return pl.pallas_call(
        kernel,
        in_specs=[any_space, whole],
        out_specs=[any_space, whole],
        out_shape=[
            jax.ShapeDtypeStruct((pairs, side_b * part, cols), BF),
            jax.ShapeDtypeStruct(small.shape, F32),
        ],
        scratch_shapes=[
            pltpu.VMEM((pairs, piece, cols), BF),
            pltpu.VMEM((pairs, side_a - 1, piece, cols), BF),
            pltpu.VMEM((len(steps),) + small.shape, F32),
            pltpu.SemaphoreType.DMA((total,)),
            pltpu.SemaphoreType.DMA((total,)),
            pltpu.SemaphoreType.DMA((pairs,)),
        ],
        compiler_params=remote_params(3, 32),
        name="finish_gradients",
    )(partial, small)


def scatter_change(grid, change):
    pairs, rows, cols = change.shape
    side_a, side_b = grid.size["a"], grid.size["b"]
    part = rows // side_b
    piece = part // side_a
    total = pairs * ((side_b - 1) + (side_a - 1))

    def kernel(c_ref, o_ref, mine, from_b, from_a, send, recv, load_sems):
        own = grid.own()
        meet(grid.partners(("a", "b")))
        copies = Copies(send, recv)
        half = lambda b: pl.ds(pl.multiple_of(b * part, 16), part)
        rows_of = lambda a: pl.ds(pl.multiple_of(a * piece, 16), piece)
        firsts, loads = [], []
        for m in range(pairs):
            firsts.append(
                [
                    copies.start(c_ref.at[m, half(own["b"] ^ k)], from_b.at[k - 1, m], grid.beside(own, "b", k))
                    for k in range(1, side_b)
                ]
            )
            load = pltpu.make_async_copy(c_ref.at[m, half(own["b"])], mine.at[m], load_sems.at[m])
            load.start()
            loads.append(load)
        seconds = []
        for m in range(pairs):
            loads[m].wait()
            for copy in firsts[m]:
                copy.wait()
            add_rows(mine.at[m], [from_b.at[k, m] for k in range(side_b - 1)], part)
            seconds.append(
                [
                    copies.start(mine.at[m, rows_of(own["a"] ^ k)], from_a.at[k - 1, m], grid.beside(own, "a", k))
                    for k in range(1, side_a)
                ]
            )
        for m in range(pairs):
            for copy in seconds[m]:
                copy.wait()
            here = mine.at[m, rows_of(own["a"])]
            total_here = here[...].astype(F32)
            for k in range(side_a - 1):
                total_here = total_here + from_a[k, m].astype(F32)
            o_ref[m] = total_here

    any_space = pl.BlockSpec(memory_space=pl.ANY)
    return pl.pallas_call(
        kernel,
        in_specs=[any_space],
        out_specs=pl.BlockSpec(memory_space=pltpu.VMEM),
        out_shape=jax.ShapeDtypeStruct((pairs, piece, cols), F32),
        scratch_shapes=[
            pltpu.VMEM((pairs, part, cols), BF),
            pltpu.VMEM((side_b - 1, pairs, part, cols), BF),
            pltpu.VMEM((side_a - 1, pairs, piece, cols), BF),
            pltpu.SemaphoreType.DMA((total,)),
            pltpu.SemaphoreType.DMA((total,)),
            pltpu.SemaphoreType.DMA((pairs,)),
        ],
        compiler_params=remote_params(4, 40),
        name="scatter_change",
    )(change)


def tile_total(grid, value, number):
    n_tile = grid.n_tile

    def kernel(v_ref, o_ref, got, send, recv):
        t, o = grid.at(grid.own())
        meet(grid.partners(("tile",)))
        copies = Copies(send, recv)
        got[t] = v_ref[...]
        sent = [copies.start(v_ref, got.at[t], (t ^ k, o)) for k in range(1, n_tile)]
        for copy in sent:
            copy.wait()
        total = got[0]
        for i in range(1, n_tile):
            total = total + got[i]
        o_ref[...] = total

    whole = pl.BlockSpec(memory_space=pltpu.VMEM)
    return pl.pallas_call(
        kernel,
        in_specs=[whole],
        out_specs=whole,
        out_shape=jax.ShapeDtypeStruct(value.shape, F32),
        scratch_shapes=[
            pltpu.VMEM((n_tile,) + value.shape, F32),
            pltpu.SemaphoreType.DMA((n_tile - 1,)),
            pltpu.SemaphoreType.DMA((n_tile - 1,)),
        ],
        compiler_params=remote_params(number, 16),
        name="tile_total",
    )(value)


def fill_halo(pad, halo, side):
    last = side + RIM
    up, down, left, right, corner = (halo(k) for k in range(5))
    for e in range(RIM):
        rows = slice(e * side, e * side + side)
        pad[pl.ds(e * PITCH + 8, side), :] = up[rows]
        pad[pl.ds((last + e) * PITCH + 8, side), :] = down[rows]
        pad[pl.ds(RIM * PITCH + 8 - RIM + e, side, stride=PITCH), :] = left[rows]
        pad[pl.ds(RIM * PITCH + 8 + side + e, side, stride=PITCH), :] = right[rows]
    places = ((0, 8 - RIM), (0, 8 + side), (last, 8 - RIM), (last, 8 + side))
    for k, (row, col) in enumerate(places):
        for e in range(RIM):
            at = 16 * k + RIM * e
            pad[pl.ds((row + e) * PITCH + col, RIM), :] = corner[at : at + RIM]


def conv_pass(pad, side, weight, emit):
    for block in range(side // 8):
        sums = [None] * side
        for b in range(7):
            taps = [weight(a, b) for a in range(7)]
            for r in range(side + 2 * RIM):
                cells = pad[pl.ds(r * PITCH + 8 - RIM + b + 8 * block, 8), :]
                for a in range(7):
                    i = r - a
                    if 0 <= i < side:
                        term = taps[a] * cells
                        sums[i] = term if sums[i] is None else sums[i] + term
        emit(block, sums)


def halo_block(halos):
    return pl.BlockSpec((1, 1) + halos.shape[2:], lambda c, s: (c, s, 0, 0, 0))


def conv_cost(n_chunk, slots, side, nbytes):
    return pl.CostEstimate(
        flops=n_chunk * slots * side * side * LANES * 98 * 100, bytes_accessed=nbytes, transcendentals=0
    )


def conv_forward(inputs, mask_lanes, halos, taps):
    slots, side, _, channels = inputs.shape
    n_chunk = halos.shape[0]

    def kernel(x_ref, m_ref, w_ref, h_ref, o_ref, s_ref, pad):
        for i in range(side):
            pad[pl.ds((i + RIM) * PITCH + 8, side), :] = (
                x_ref[0, i].astype(F32) * m_ref[0, pl.ds(i * side, side), :]
            )
        fill_halo(pad, lambda k: h_ref[0, 0, k].astype(F32), side)
        bias = w_ref[49]
        totals = [jnp.zeros((8, LANES), F32), jnp.zeros((8, LANES), F32)]

        def emit(block, sums):
            for i in range(side):
                value = sums[i] + bias
                rows = pl.ds(i * side + 8 * block, 8)
                o_ref[0, rows, :] = value
                weighted = m_ref[0, rows, :] * value
                totals[0] = totals[0] + weighted
                totals[1] = totals[1] + weighted * value

        conv_pass(pad, side, lambda a, b: w_ref[7 * a + b], emit)
        s_ref[0, 0], s_ref[0, 1] = totals

    cells = side * side
    return pl.pallas_call(
        kernel,
        grid=(n_chunk, slots),
        in_specs=[
            pl.BlockSpec((1, side, side, LANES), lambda c, s: (s, 0, 0, c)),
            pl.BlockSpec((1, cells, LANES), lambda c, s: (s, 0, 0)),
            pl.BlockSpec((50, 8, LANES), lambda c, s: (0, 0, c)),
            halo_block(halos),
        ],
        out_specs=[
            pl.BlockSpec((1, cells, LANES), lambda c, s: (s, 0, c)),
            pl.BlockSpec((1, 2, 8, LANES), lambda c, s: (s, 0, 0, c)),
        ],
        scratch_shapes=[pltpu.VMEM(((side + 2 * RIM) * PITCH, LANES), F32)],
        out_shape=[
            jax.ShapeDtypeStruct((slots, cells, channels), F32),
            jax.ShapeDtypeStruct((slots, 2, 8, channels), F32),
        ],
        cost_estimate=conv_cost(n_chunk, slots, side, 10 << 20),
        compiler_params=pltpu.CompilerParams(vmem_limit_bytes=32 << 20),
        name="conv_forward",
    )(inputs, mask_lanes, taps, halos)


def conv_gradient(d_shaped, conv_out, mask_lanes, coefs, side):
    slots, cells, channels = d_shaped.shape
    n_chunk = -(-channels // LANES)

    def kernel(d_ref, v_ref, m_ref, c_ref, o_ref, r_ref, held):
        one, two, three = c_ref[0, :1], c_ref[1, :1], c_ref[2, :1]
        for s in range(slots):
            value = d_ref[s] * one - m_ref[s] * (two + three * v_ref[s])
            o_ref[s] = value
            held[...] = value
            store_rims(held, r_ref, s, side)

    piece = (slots, 4, RIM * side, LANES)
    block = pl.BlockSpec((slots, cells, LANES), lambda c: (0, 0, c))
    return pl.pallas_call(
        kernel,
        grid=(n_chunk,),
        in_specs=[
            block,
            block,
            pl.BlockSpec((slots, cells, LANES), lambda c: (0, 0, 0)),
            pl.BlockSpec((3, 8, LANES), lambda c: (0, 0, c)),
        ],
        out_specs=[block, pl.BlockSpec((1,) + piece, lambda c: (c, 0, 0, 0, 0))],
        scratch_shapes=[pltpu.VMEM((cells, LANES), F32)],
        out_shape=[
            jax.ShapeDtypeStruct((slots, cells, channels), F32),
            jax.ShapeDtypeStruct((n_chunk,) + piece, BF),
        ],
        compiler_params=pltpu.CompilerParams(vmem_limit_bytes=32 << 20),
        name="conv_gradient",
    )(d_shaped, conv_out, mask_lanes, coefs)


def tap_gradient(inputs, mask_lanes, halos, d_conv):
    slots, side, _, channels = inputs.shape
    n_chunk = halos.shape[0]
    cells = side * side

    def kernel(x_ref, m_ref, d_ref, h_ref, o_ref, pad, sums):
        slot = pl.program_id(1)
        for i in range(side):
            pad[pl.ds((i + RIM) * PITCH + 8, side), :] = (
                x_ref[0, i].astype(F32) * m_ref[0, pl.ds(i * side, side), :]
            )
        fill_halo(pad, lambda k: h_ref[0, 0, k].astype(F32), side)

        @pl.when(slot == 0)
        def _():
            sums[...] = jnp.zeros_like(sums)

        for block in range(side // 8):
            grads = [d_ref[0, pl.ds(i * side + 8 * block, 8), :] for i in range(side)]
            total = grads[0]
            for i in range(1, side):
                total = total + grads[i]
            sums[49] += total
            for b in range(7):
                taps = [None] * 7
                for r in range(side + 2 * RIM):
                    window = pad[pl.ds(r * PITCH + 8 - RIM + b + 8 * block, 8), :]
                    for a in range(7):
                        i = r - a
                        if 0 <= i < side:
                            term = window * grads[i]
                            taps[a] = term if taps[a] is None else taps[a] + term
                for a in range(7):
                    sums[7 * a + b] += taps[a]

        @pl.when(slot == slots - 1)
        def _():
            o_ref[...] = jnp.sum(sums[...], axis=1)

    return pl.pallas_call(
        kernel,
        grid=(n_chunk, slots),
        in_specs=[
            pl.BlockSpec((1, side, side, LANES), lambda c, s: (s, 0, 0, c)),
            pl.BlockSpec((1, cells, LANES), lambda c, s: (s, 0, 0)),
            pl.BlockSpec((1, cells, LANES), lambda c, s: (s, 0, c)),
            halo_block(halos),
        ],
        out_specs=pl.BlockSpec((50, LANES), lambda c, s: (0, c)),
        scratch_shapes=[
            pltpu.VMEM(((side + 2 * RIM) * PITCH, LANES), F32),
            pltpu.VMEM((50, 8, LANES), F32),
        ],
        out_shape=jax.ShapeDtypeStruct((50, channels), F32),
        cost_estimate=conv_cost(n_chunk, slots, side, 10 << 20),
        compiler_params=pltpu.CompilerParams(vmem_limit_bytes=32 << 20),
        name="tap_gradient",
    )(inputs, mask_lanes, d_conv, halos)


def conv_backward(d_conv, halos, cotangent, mask_lanes, taps, weight_lanes):
    slots, side, _, channels = cotangent.shape
    n_chunk = halos.shape[0]
    cells = side * side

    def kernel(d_ref, g_ref, m_ref, w_ref, l_ref, h_ref, o_ref, pad):
        for i in range(side):
            pad[pl.ds((i + RIM) * PITCH + 8, side), :] = d_ref[0, pl.ds(i * side, side), :]
        fill_halo(pad, lambda k: h_ref[0, 0, k].astype(F32), side)
        weight = l_ref[...]

        def emit(block, sums):
            for i in range(side):
                rows = pl.ds(i * side + 8 * block, 8)
                scaled = weight * g_ref[0, i, pl.ds(8 * block, 8), :].astype(F32)
                o_ref[0, rows, :] = m_ref[0, rows, :] * (scaled + sums[i])

        conv_pass(pad, side, lambda a, b: w_ref[7 * (6 - a) + 6 - b], emit)

    return pl.pallas_call(
        kernel,
        grid=(n_chunk, slots),
        in_specs=[
            pl.BlockSpec((1, cells, LANES), lambda c, s: (s, 0, c)),
            pl.BlockSpec((1, side, side, LANES), lambda c, s: (s, 0, 0, c)),
            pl.BlockSpec((1, cells, LANES), lambda c, s: (s, 0, 0)),
            pl.BlockSpec((50, 8, LANES), lambda c, s: (0, 0, c)),
            pl.BlockSpec((8, LANES), lambda c, s: (0, 0)),
            halo_block(halos),
        ],
        out_specs=pl.BlockSpec((1, cells, LANES), lambda c, s: (s, 0, c)),
        scratch_shapes=[pltpu.VMEM(((side + 2 * RIM) * PITCH, LANES), F32)],
        out_shape=jax.ShapeDtypeStruct((slots, cells, channels), F32),
        cost_estimate=conv_cost(n_chunk, slots, side, 12 << 20),
        compiler_params=pltpu.CompilerParams(vmem_limit_bytes=32 << 20),
        name="conv_backward",
    )(d_conv, cotangent, mask_lanes, taps, weight_lanes, halos)


def spread_lanes(value, parts, width):
    rows, channels = value.shape
    run = channels // parts
    if run == width:
        return value
    gap = jnp.zeros((rows, width - run), value.dtype)
    pieces = []
    for t in range(parts):
        pieces += [value[:, t * run : (t + 1) * run], gap]
    return jnp.concatenate(pieces, 1)


def close_lanes(value, parts, run):
    width = value.shape[1] // parts
    if run == width:
        return value
    return jnp.concatenate([value[:, t * width : t * width + run] for t in range(parts)], 1)


def arrange(body, args, specs, rows, channels, parts, width, name):
    step = 3 * LANES if rows % (3 * LANES) == 0 else LANES

    def kernel(*refs):
        given, (gap_ref, turned_ref, sum_ref) = refs[: len(args)], refs[len(args) :]
        low = body(*given).astype(BF)
        value = low.astype(F32)
        gap_ref[...] = spread_lanes(value, parts, width).astype(BF)
        turned_ref[...] = value.T.astype(BF)

        @pl.when(pl.program_id(0) == 0)
        def _():
            sum_ref[...] = jnp.zeros_like(sum_ref)

        sum_ref[...] += jnp.sum(value, axis=0, keepdims=True)

    return pl.pallas_call(
        kernel,
        grid=(rows // step,),
        in_specs=specs(step),
        out_specs=[
            pl.BlockSpec((step, parts * width), lambda i: (i, 0)),
            pl.BlockSpec((channels, step), lambda i: (0, i)),
            pl.BlockSpec((1, channels), lambda i: (0, 0)),
        ],
        out_shape=[
            jax.ShapeDtypeStruct((rows, parts * width), BF),
            jax.ShapeDtypeStruct((channels, rows), BF),
            jax.ShapeDtypeStruct((1, channels), F32),
        ],
        compiler_params=pltpu.CompilerParams(vmem_limit_bytes=48 << 20),
        name=name,
    )(*args)


def feed_forward(inverse, shaped, shaped_t, d_branch, d_branch_t, hidden_bias, weights, grad_rows):
    rows, depth = shaped.shape
    channels = shaped_t.shape[0]
    half, _, cols = hidden_bias.shape
    pairs, owners = weights.shape[:2]
    per_owner = 2 * pairs
    tile_rows = 3 * LANES if rows % (3 * LANES) == 0 else LANES

    def kernel(inv_ref, s_ref, st_ref, d_ref, dt_ref, hb_ref, w_ref, branch_ref, ds_ref, grad_ref, bias_ref, *scratch):
        packed, first, second, act, dpre, grads, sems, out_sem = scratch
        step = pl.program_id(0)

        def where(slot):
            owner, inside = slot // per_owner, slot % per_owner
            return owner, inside // 2, inside % 2

        def fetch(h, buffer):
            copies = []
            for which in range(2):
                owner, pair, _ = where(inv_ref[h + which * half])
                copies.append(
                    pltpu.make_async_copy(w_ref.at[pair, owner], packed.at[buffer, which], sems.at[buffer, which])
                )
            return copies

        @pl.when(step == 0)
        def _():
            for copy in fetch(0, 0):
                copy.start()
            if grad_rows > channels:
                rest = grad_rows - channels
                grads[:, :, pl.ds(channels, rest), :] = jnp.zeros(grads.shape[:2] + (rest, 2 * cols), BF)

        @pl.when(step + 1 < half)
        def _():
            for copy in fetch(step + 1, (step + 1) % 2):
                copy.start()

        now = step % 2
        slots = [where(inv_ref[step + which * half]) for which in range(2)]
        waits = fetch(step, now)
        for which, held in enumerate((first, second)):
            waits[which].wait()
            for parity in range(2):

                @pl.when(slots[which][2] == parity)
                def _():
                    held[...] = packed[now, which, :, parity * cols : (parity + 1) * cols]

        hidden = hb_ref[0]
        total = jnp.zeros((1, cols), F32)
        across = (((1,), (1,)), ((), ()))
        for i in range(rows // tile_rows):
            at = pl.ds(i * tile_rows, tile_rows)
            pre = jnp.dot(s_ref[at, :], first[...], preferred_element_type=F32) + hidden
            d_act = jnp.dot(d_ref[at, :], second[...], preferred_element_type=F32)
            square = pre * pre
            bend = jnp.tanh(ROOT * pre * (1.0 + CUBE * square))
            half_up = 0.5 * (1.0 + bend)
            low = (pre * half_up).astype(BF)
            slope = half_up + (0.5 * ROOT) * pre * (1.0 - bend * bend) * (1.0 + (3.0 * CUBE) * square)
            back = (d_act * slope).astype(BF)
            act[at, :] = low
            dpre[at, :] = back
            total = total + jnp.sum(back.astype(F32), axis=0, keepdims=True)
            out_add = lax.dot_general(low, second[...], across, preferred_element_type=F32)
            in_add = lax.dot_general(back, first[...], across, preferred_element_type=F32)

            @pl.when(step == 0)
            def _():
                branch_ref[at, :] = out_add
                ds_ref[at, :] = in_add

            @pl.when(step > 0)
            def _():
                branch_ref[at, :] += out_add
                ds_ref[at, :] += in_add

        bias_ref[0] = total
        for which, (left, right) in enumerate(((st_ref, dpre), (dt_ref, act))):
            owner, pair, half_of_pair = slots[which]
            value = jnp.dot(left[...], right[...], preferred_element_type=F32).astype(BF)
            for parity in range(2):

                @pl.when(half_of_pair == parity)
                def _():
                    at = (owner // 2) * pairs + pair
                    grads[owner % 2, at, pl.ds(0, channels), parity * cols : (parity + 1) * cols] = value

        @pl.when(step == half - 1)
        def _():
            out = pltpu.make_async_copy(grads, grad_ref, out_sem.at[0])
            out.start()
            out.wait()

    whole = lambda *shape: pl.BlockSpec(shape, lambda h, *_: (0,) * len(shape))
    line = pl.BlockSpec((1, 1, cols), lambda h, *_: (h, 0, 0))
    grad_shape = (2, owners // 2 * pairs, grad_rows, 2 * cols)
    return pl.pallas_call(
        kernel,
        grid_spec=pltpu.PrefetchScalarGridSpec(
            num_scalar_prefetch=1,
            grid=(half,),
            in_specs=[
                whole(rows, depth),
                whole(channels, rows),
                whole(rows, depth),
                whole(channels, rows),
                line,
                pl.BlockSpec(memory_space=pl.ANY),
            ],
            out_specs=[whole(rows, depth), whole(rows, depth), pl.BlockSpec(memory_space=pl.ANY), line],
            scratch_shapes=[
                pltpu.VMEM((2, 2, depth, 2 * cols), BF),
                pltpu.VMEM((depth, cols), BF),
                pltpu.VMEM((depth, cols), BF),
                pltpu.VMEM((rows, cols), BF),
                pltpu.VMEM((rows, cols), BF),
                pltpu.VMEM(grad_shape, BF),
                pltpu.SemaphoreType.DMA((2, 2)),
                pltpu.SemaphoreType.DMA((1,)),
            ],
        ),
        out_shape=[
            jax.ShapeDtypeStruct((rows, depth), F32),
            jax.ShapeDtypeStruct((rows, depth), F32),
            jax.ShapeDtypeStruct(grad_shape, BF),
            jax.ShapeDtypeStruct((half, 1, cols), F32),
        ],
        cost_estimate=pl.CostEstimate(
            flops=12 * rows * channels * half * cols, bytes_accessed=40 << 20, transcendentals=rows * half * cols
        ),
        compiler_params=pltpu.CompilerParams(vmem_limit_bytes=63 << 20),
        name="feed_forward",
    )(inverse, shaped, shaped_t, d_branch, d_branch_t, hidden_bias, weights)


def close_out(branch, d_shaped, inputs, conv_out, mask_lanes, out_bias, parts, run):
    rows, channels = inputs.shape
    depth = branch.shape[1]
    step = 3 * LANES if rows % (3 * LANES) == 0 else LANES

    def kernel(b_ref, d_ref, x_ref, v_ref, m_ref, o_ref, out_ref, ds_ref, sum_ref):
        branch_here = close_lanes(b_ref[...], parts, run) + o_ref[...]
        out_ref[...] = (m_ref[:, :1] * (x_ref[...].astype(F32) + branch_here)).astype(BF)
        grads = close_lanes(d_ref[...], parts, run)
        ds_ref[...] = grads

        @pl.when(pl.program_id(0) == 0)
        def _():
            sum_ref[...] = jnp.zeros_like(sum_ref)

        sum_ref[0] += jnp.sum(grads, axis=0, keepdims=True)
        sum_ref[1] += jnp.sum(grads * v_ref[...], axis=0, keepdims=True)

    line = lambda n: pl.BlockSpec((step, n), lambda i: (i, 0))
    return pl.pallas_call(
        kernel,
        grid=(rows // step,),
        in_specs=[
            line(depth),
            line(depth),
            line(channels),
            line(channels),
            line(LANES),
            pl.BlockSpec((1, channels), lambda i: (0, 0)),
        ],
        out_specs=[line(channels), line(channels), pl.BlockSpec((2, 1, channels), lambda i: (0, 0, 0))],
        out_shape=[
            jax.ShapeDtypeStruct((rows, channels), BF),
            jax.ShapeDtypeStruct((rows, channels), F32),
            jax.ShapeDtypeStruct((2, 1, channels), F32),
        ],
        compiler_params=pltpu.CompilerParams(vmem_limit_bytes=60 << 20),
        name="close_out",
    )(branch, d_shaped, inputs, conv_out, mask_lanes, out_bias)


def up_to(value, unit):
    return -(-value // unit) * unit


def pack_pairs(value):
    slots, rows, cols = value.shape
    return value.reshape(slots // 2, 2, rows, cols).transpose(0, 2, 1, 3).reshape(slots // 2, rows, 2 * cols)


def unpack_pairs(value):
    pairs, rows, cols = value.shape
    return value.reshape(pairs, rows, 2, cols // 2).transpose(0, 2, 1, 3).reshape(2 * pairs, rows, cols // 2)


def per_device(
    grid,
    inputs,
    cotangent,
    master,
    moment_one,
    moment_two,
    left_basis,
    column_basis,
    small_params,
    small_first,
    small_second,
    land_mask,
    tile_count,
    neighbours,
    block_order,
    cell_weight,
    step_count,
):
    position = lax.axis_index("tile")
    sample = lax.axis_index("opt")
    inputs, cotangent = inputs[0], cotangent[0]
    slots, side, _, channels = inputs.shape
    cells = side * side
    rows = slots * cells
    n_tile = grid.n_tile
    n_chunk = -(-channels // LANES)
    per_group = channels // GROUPS
    per_owner, run, cols = master.shape
    pairs = per_owner // 2
    block_total = block_order.shape[0]
    half = block_total // 2
    width = up_to(run, 16)

    live = (jnp.arange(slots) < tile_count[position]).astype(F32)
    mask = (land_mask.astype(F32) * live[:, None, None]).reshape(slots, cells)
    mask_lanes = jnp.broadcast_to(mask[:, :, None], (slots, cells, LANES))
    flat_mask = mask_lanes.reshape(rows, LANES)
    taps = jnp.broadcast_to(small_params[:50, None, :], (50, 8, channels))

    low_master = jnp.pad(pack_pairs(master.astype(BF)), ((0, 0), (0, width - run), (0, 0)))
    rims = rims_of_input(inputs, mask_lanes)
    halos, weights, all_neighbours = exchange_forward(grid, rims, low_master, neighbours)

    weights_float = cell_weight.astype(F32)
    sample_weight = weights_float[sample] * weights_float.shape[0] / jnp.sum(weights_float)
    weight_lanes = jnp.broadcast_to(sample_weight, (8, LANES))
    weight_row = jnp.broadcast_to(sample_weight, (1, LANES))
    flat_cotangent = cotangent.reshape(rows, channels)

    def d_branch_body(g_ref, m_ref, w_ref):
        return m_ref[:, :1] * (w_ref[:, :1] * g_ref[...].astype(F32))

    d_branch, d_branch_t, d_out_bias = arrange(
        d_branch_body,
        (flat_cotangent, flat_mask, weight_row),
        lambda step: [
            pl.BlockSpec((step, channels), lambda i: (i, 0)),
            pl.BlockSpec((step, LANES), lambda i: (i, 0)),
            pl.BlockSpec((1, LANES), lambda i: (0, 0)),
        ],
        rows,
        channels,
        n_tile,
        width,
        "arrange_d_branch",
    )
    conv_out, sums = conv_forward(inputs, mask_lanes, halos, taps)
    sums = jnp.sum(sums, axis=(0, 2))
    occupied = jnp.broadcast_to(jnp.sum(mask), (1, channels))
    sums = tile_total(grid, jnp.concatenate([sums, occupied], 0), 5)
    counted = sums[2, 0] * per_group
    by_group = sums[:2].reshape(2, GROUPS, per_group).sum(2)
    group_mean = by_group[0] / counted
    variance = by_group[1] / counted - group_mean * group_mean
    inv_std = jnp.repeat(lax.rsqrt(variance + epsilon), per_group)
    mean = jnp.repeat(group_mean, per_group)
    gain, shift = small_params[50], small_params[51]
    norm_coefs = jnp.stack([inv_std, mean * inv_std, gain, shift])

    def shaped_body(v_ref, c_ref):
        normed = v_ref[...] * c_ref[0:1] - c_ref[1:2]
        return normed * c_ref[2:3] + c_ref[3:4]

    flat_conv = conv_out.reshape(rows, channels)
    shaped, shaped_t, _ = arrange(
        shaped_body,
        (flat_conv, norm_coefs),
        lambda step: [
            pl.BlockSpec((step, channels), lambda i: (i, 0)),
            pl.BlockSpec((4, channels), lambda i: (0, 0)),
        ],
        rows,
        channels,
        n_tile,
        width,
        "arrange_shaped",
    )

    block_ids = jnp.arange(block_total, dtype=jnp.int32)
    inverse = jnp.sum(
        jnp.where(block_order[None, :] == block_ids[:, None], block_ids[None, :], 0), axis=1
    ).astype(jnp.int32)
    hidden_bias = small_params[53:57].reshape(half, 1, cols)
    branch, d_shaped, grads, d_hidden = feed_forward(
        inverse, shaped, shaped_t, d_branch, d_branch_t, hidden_bias, weights, n_tile * width
    )
    block_output, d_shaped, d_sums = close_out(
        branch, d_shaped, inputs.reshape(rows, channels), flat_conv, flat_mask, small_params[52:53], n_tile, run
    )

    d_shift = d_sums[0, 0]
    d_gain = inv_std * (d_sums[1, 0] - mean * d_shift)
    parts = tile_total(grid, jnp.stack([gain * d_shift, gain * d_gain]), 6)
    parts = jnp.repeat(parts.reshape(2, GROUPS, per_group).sum(2) / counted, per_group, axis=1)
    grad_coefs = jnp.stack(
        [
            inv_std * gain,
            inv_std * (parts[0] - mean * inv_std * parts[1]),
            inv_std * inv_std * parts[1],
        ]
    )
    d_conv, grad_rims = conv_gradient(
        d_shaped.reshape(slots, cells, channels),
        conv_out,
        mask_lanes,
        jnp.broadcast_to(grad_coefs[:, None, :], (3, 8, channels)),
        side,
    )
    grad_halos, partial = exchange_backward(grid, grad_rims, grads, all_neighbours)
    d_taps = tap_gradient(inputs, mask_lanes, halos, d_conv)
    input_grad = conv_backward(d_conv, grad_halos, cotangent, mask_lanes, taps, weight_lanes)

    correction = 1.0 - jnp.power(F32(decay_rate), step_count[0].astype(F32))
    d_small = jnp.concatenate(
        [d_taps, d_gain[None], d_shift[None], d_out_bias, d_hidden.reshape(4, channels)], 0
    )
    owned, d_small = finish_gradients(grid, partial, d_small)
    small_one = decay_rate * small_first + (1.0 - decay_rate) * d_small
    small_two = decay_rate * small_second + (1.0 - decay_rate) * d_small * d_small
    new_small = small_params - small_rate * (small_one / correction) / (
        jnp.sqrt(small_two / correction) + adam_eps
    )

    owned = unpack_pairs(owned[:, :channels])
    rotated = jnp.einsum("bdk,bdw->bkw", left_basis, owned.astype(F32), precision=highest)
    rotated = jnp.einsum("bkw,bwv->bkv", rotated, column_basis, precision=highest)
    first_new = decay_rate * moment_one + (1.0 - decay_rate) * rotated
    second_new = decay_rate * moment_two + (1.0 - decay_rate) * rotated * rotated
    direction = first_new / correction / (jnp.sqrt(second_new / correction) + adam_eps)
    turned = jnp.einsum("bkv,bwv->bkw", direction, column_basis, precision=highest)
    change = jnp.einsum("bdk,bkw->bdw", left_basis, turned, precision=highest)
    side_a, side_b = grid.size["a"], grid.size["b"]
    change = change.reshape(pairs, 2, side_a, side_b, run, cols).transpose(0, 3, 2, 4, 1, 5)
    change = jnp.pad(change.reshape(pairs, n_tile, run, 2 * cols).astype(BF), ((0, 0), (0, 0), (0, width - run), (0, 0)))
    change = scatter_change(grid, change.reshape(pairs, n_tile * width, 2 * cols))
    change = unpack_pairs(change[:, :run])
    new_master = master - 0.5 / math.sqrt(channels) * change
    return (
        block_output.reshape((1,) + inputs.shape),
        input_grad.reshape((1,) + inputs.shape),
        new_master,
        new_master.astype(BF),
        first_new,
        second_new,
        new_small,
        small_one,
        small_two,
    )


def solution(mesh):
    grid = Grid(mesh.shape["tile"], mesh.shape["opt"])

    def step(*args):
        return per_device(grid, *args)

    return jax.shard_map(
        step,
        mesh=mesh,
        in_specs=(
            P("opt", "tile", None, None, None),
            P("opt", "tile", None, None, None),
            P("opt", "tile", None),
            P("opt", "tile", None),
            P("opt", "tile", None),
            P("opt", None, "tile"),
            P("opt", None, None),
            P(),
            P(),
            P(),
            P("tile", None, None),
            P(),
            P("tile", None),
            P(),
            P(),
            P(),
        ),
        out_specs=(
            P("opt", "tile", None, None, None),
            P("opt", "tile", None, None, None),
            P("opt", "tile", None),
            P("opt", "tile", None),
            P("opt", "tile", None),
            P("opt", "tile", None),
            P(),
            P(),
            P(),
        ),
        check_vma=False,
    )
```

```python
import math

import jax
import jax.numpy as jnp
from jax import lax
from jax.experimental import pallas as pl
from jax.experimental.pallas import tpu as pltpu
from jax.sharding import PartitionSpec as P

GROUPS = 16
LANES = 128
RIM = 3
PITCH = 40
BF = jnp.bfloat16
F32 = jnp.float32

highest = lax.Precision.HIGHEST
epsilon = 1e-05
adam_eps = 1e-08
decay_rate = 0.5
small_rate = 0.05
ROOT = 0.7978845608028654
CUBE = 0.044715


class Grid:
    def __init__(self, n_tile, n_opt):
        b = 4 if n_tile % 16 == 0 else 2
        self.n_tile, self.n_opt = n_tile, n_opt
        self.size = {"a": n_tile // b, "b": b, "x": n_opt // 2, "c": 2}

    def own(self):
        t, o = lax.axis_index("tile"), lax.axis_index("opt")
        b = self.size["b"]
        return {"a": t // b, "b": t % b, "x": o // 2, "c": o % 2}

    def at(self, place):
        return place["a"] * self.size["b"] + place["b"], place["x"] * 2 + place["c"]

    def partners(self, dims):
        own = self.own()
        found = []
        for dim in dims:
            if dim == "tile":
                t, o = self.at(own)
                found += [(t ^ k, o) for k in range(1, self.n_tile)]
            else:
                found += [self.beside(own, dim, k) for k in range(1, self.size[dim])]
        return found

    def beside(self, own, dim, k):
        return self.at({**own, dim: own[dim] ^ k})


def meet(devices):
    barrier = pltpu.get_barrier_semaphore()
    for device in devices:
        pl.semaphore_signal(barrier, inc=1, device_id=device, device_id_type=pl.DeviceIdType.MESH)
    pl.semaphore_wait(barrier, len(devices))


class Copies:
    def __init__(self, send_sems, recv_sems):
        self.sems = send_sems, recv_sems
        self.used = 0

    def make(self, src, dst, device):
        i = self.used
        self.used += 1
        return pltpu.make_async_remote_copy(
            src_ref=src,
            dst_ref=dst,
            send_sem=self.sems[0].at[i],
            recv_sem=self.sems[1].at[i],
            device_id=device,
            device_id_type=pl.DeviceIdType.MESH,
        )

    def start(self, src, dst, device):
        copy = self.make(src, dst, device)
        copy.start()
        return copy


def remote_params(number, mib):
    return pltpu.CompilerParams(collective_id=number, has_side_effects=True, vmem_limit_bytes=mib << 20)


def add_rows(target, sources, rows, step=16):
    @pl.loop(0, rows // step)
    def _(i):
        at = pl.ds(pl.multiple_of(i * step, step), step)
        total = target[at, :].astype(F32)
        for source in sources:
            total = total + source[at, :].astype(F32)
        target[at, :] = total.astype(BF)


def store_rims(src, outs, slot, side):
    outs[0, slot, 0] = src[pl.ds(0, RIM * side), :].astype(BF)
    outs[0, slot, 1] = src[pl.ds((side - RIM) * side, RIM * side), :].astype(BF)
    for e in range(RIM):
        rows = pl.ds(e * side, side)
        outs[0, slot, 2, rows] = src[pl.ds(e, side, stride=side), :].astype(BF)
        outs[0, slot, 3, rows] = src[pl.ds(side - RIM + e, side, stride=side), :].astype(BF)


def rims_of_input(inputs, mask_lanes):
    slots, side, _, channels = inputs.shape
    n_chunk = -(-channels // LANES)

    def kernel(x_ref, m_ref, o_ref, cells):
        for s in range(slots):
            for i in range(side):
                cells[pl.ds(i * side, side), :] = (
                    x_ref[s, i].astype(F32) * m_ref[s, pl.ds(i * side, side), :]
                )
            store_rims(cells, o_ref, s, side)

    return pl.pallas_call(
        kernel,
        grid=(n_chunk,),
        in_specs=[
            pl.BlockSpec((slots, side, side, LANES), lambda c: (0, 0, 0, c)),
            pl.BlockSpec((slots, side * side, LANES), lambda c: (0, 0, 0)),
        ],
        out_specs=pl.BlockSpec((1, slots, 4, RIM * side, LANES), lambda c: (c, 0, 0, 0, 0)),
        out_shape=jax.ShapeDtypeStruct((n_chunk, slots, 4, RIM * side, LANES), BF),
        scratch_shapes=[pltpu.VMEM((side * side, LANES), F32)],
        compiler_params=pltpu.CompilerParams(vmem_limit_bytes=32 << 20),
        name="rims_of_input",
    )(inputs, mask_lanes)


class HaloExchange:
    def __init__(self, grid, n_chunk, slots, side):
        self.grid, self.n_chunk, self.slots, self.side = grid, n_chunk, slots, side
        self.count = 2 * (grid.n_tile - 1)

    def scratch(self):
        n, s, band = self.grid.n_tile, self.slots, RIM * self.side
        return [
            pltpu.VMEM((n, s, 4, band, LANES), BF),
            pltpu.VMEM((n, s, 5, band, LANES), BF),
            pltpu.SemaphoreType.DMA((2,)),
        ]

    def halo_shape(self):
        return jax.ShapeDtypeStruct((self.n_chunk, self.slots, 5, RIM * self.side, LANES), BF)

    def send_rims(self, copies, rims, arrived, local):
        t, o = self.grid.at(self.grid.own())
        self.t, self.o = t, o
        self.first = []
        for k in range(1, self.grid.n_tile):
            to = t ^ k
            source = jnp.minimum(to, self.n_chunk - 1)
            copy = copies.make(rims.at[source], arrived.at[t], (to, o))
            self.first.append((to, copy))

            @pl.when(to < self.n_chunk)
            def _():
                copy.start()

        own = pltpu.make_async_copy(rims.at[jnp.minimum(t, self.n_chunk - 1)], arrived.at[t], local.at[0])
        own.start()
        self.own_copy = own

    def pick_and_send(self, copies, arrived, picked, halos, local, neighbours):
        grid, slots, side = self.grid, self.slots, self.side
        t, o = self.t, self.o
        self.own_copy.wait()
        for _, copy in self.first:

            @pl.when(t < self.n_chunk)
            def _():
                copy.wait_recv()

        @pl.when(t < self.n_chunk)
        def _():
            @pl.loop(0, grid.n_tile * slots)
            def _(d):
                def rim(direction, which):
                    slot = neighbours(d, direction)
                    at = jnp.maximum(slot, 0)
                    value = arrived[at // slots, at % slots, which].astype(F32)
                    return jnp.where(slot >= 0, value, 0.0)

                to_tile, to_slot = d // slots, d % slots
                for to, (direction, which) in enumerate(((1, 1), (6, 0), (3, 3), (4, 2))):
                    picked[to_tile, to_slot, to] = rim(direction, which).astype(BF)
                rows = []
                for direction, which, first in ((0, 1, side - RIM), (2, 1, 0), (5, 0, side - RIM), (7, 0, 0)):
                    value = rim(direction, which)
                    rows += [value[e * side + first : e * side + first + RIM] for e in range(RIM)]
                    rows.append(jnp.zeros((16 - RIM * RIM, LANES), F32))
                rows.append(jnp.zeros((RIM * side - 64, LANES), F32))
                picked[to_tile, to_slot, 4] = jnp.concatenate(rows, 0).astype(BF)

        own_chunk = jnp.minimum(t, self.n_chunk - 1)
        self.second = []
        for k in range(1, grid.n_tile):
            to = t ^ k
            copy = copies.make(picked.at[to], halos.at[own_chunk], (to, o))
            self.second.append((to, copy))

            @pl.when(t < self.n_chunk)
            def _():
                copy.start()

        self.back_copy = pltpu.make_async_copy(picked.at[t], halos.at[own_chunk], local.at[1])

        @pl.when(t < self.n_chunk)
        def _():
            self.back_copy.start()

    def finish(self):
        t = self.t

        @pl.when(t < self.n_chunk)
        def _():
            self.back_copy.wait()

        for to, copy in self.first:

            @pl.when(to < self.n_chunk)
            def _():
                copy.wait_send()

        for to, copy in self.second:

            @pl.when(to < self.n_chunk)
            def _():
                copy.wait_recv()

            @pl.when(t < self.n_chunk)
            def _():
                copy.wait_send()


class WeightGather:
    def __init__(self, grid, pairs, width):
        self.grid, self.pairs, self.width = grid, pairs, width
        self.count = pairs * (grid.n_tile * grid.n_opt - 1)

    def run(self, copies, packed, gathered, local):
        grid, width = self.grid, self.width
        own = grid.own()

        def place(m, rel):
            t, o = grid.at({d: own[d] ^ rel.get(d, 0) for d in own})
            return gathered.at[m, o, pl.ds(pl.multiple_of(t * width, width), width)]

        keeps, started = [], []
        for m in range(self.pairs):
            keep = pltpu.make_async_copy(packed.at[m], place(m, {}), local.at[m])
            keep.start()
            keeps.append(keep)

        def forward(m, rel, dims):
            source = packed.at[m] if not rel else place(m, rel)
            fresh = []
            for dim in dims:
                for k in range(1, grid.size[dim]):
                    copy = copies.start(source, place(m, rel), grid.beside(own, dim, k))
                    fresh.append(({**rel, dim: k}, copy))
            started.extend(copy for _, copy in fresh)
            return fresh

        orders = [("a", "x", "b", "c") if m % 2 == 0 else ("a", "b", "x", "c") for m in range(self.pairs)]
        waves = {}

        def note(m, fresh, after):
            for rel, copy in fresh:
                level = sum(1 for d in rel if d != "c")
                wave = max(rel.get("a", 0) + level - ("a" in rel), after)
                waves.setdefault(wave, []).append((m, rel, copy))

        for m in range(self.pairs):
            note(m, forward(m, {}, orders[m]), 0)
        yield 0
        for wave in range(4 * sum(grid.size.values())):
            for m, rel, copy in sorted(waves.pop(wave, []), key=lambda e: "c" in e[1]):
                copy.wait_recv()
                last = max(orders[m].index(d) for d in rel)
                note(m, forward(m, rel, orders[m][last + 1 :]), wave + 1)
            if not waves:
                break
            yield wave
        for keep in keeps:
            keep.wait()
        for copy in started:
            copy.wait_send()
        yield -1


def exchange_forward(grid, rims, packed, neighbours):
    n_chunk, slots, _, band, _ = rims.shape
    pairs, width, cols = packed.shape
    n_tile = grid.n_tile
    halo = HaloExchange(grid, n_chunk, slots, band // RIM)
    gather = WeightGather(grid, pairs, width)
    total = halo.count + gather.count + n_tile - 1

    def kernel(r_ref, p_ref, n_ref, halo_ref, w_ref, nbr_ref, arrived, picked, local, table, send, recv, locals_w, locals_n):
        own = grid.own()
        t, o = grid.at(own)
        meet(grid.partners(("tile", "x", "c")))
        copies = Copies(send, recv)
        tables = [copies.start(n_ref, nbr_ref.at[t], (t ^ k, o)) for k in range(1, n_tile)]
        keep = pltpu.make_async_copy(n_ref, nbr_ref.at[t], locals_n.at[0])
        keep.start()
        halo.send_rims(copies, r_ref, arrived, local)
        weights = gather.run(copies, p_ref, w_ref, locals_w)
        next(weights)
        keep.wait()
        for copy in tables:
            copy.wait()
        load = pltpu.make_async_copy(nbr_ref, table, locals_n.at[1])
        load.start()
        load.wait()
        halo.pick_and_send(
            copies, arrived, picked, halo_ref, local, lambda d, k: table[d // slots, d % slots, k]
        )
        for _ in weights:
            pass
        halo.finish()

    any_space = pl.BlockSpec(memory_space=pl.ANY)
    return pl.pallas_call(
        kernel,
        in_specs=[any_space] * 3,
        out_specs=[any_space] * 3,
        out_shape=[
            halo.halo_shape(),
            jax.ShapeDtypeStruct((pairs, grid.n_opt, n_tile * width, cols), BF),
            jax.ShapeDtypeStruct((n_tile,) + neighbours.shape, jnp.int32),
        ],
        scratch_shapes=halo.scratch()
        + [
            pltpu.SMEM((n_tile,) + neighbours.shape, jnp.int32),
            pltpu.SemaphoreType.DMA((total,)),
            pltpu.SemaphoreType.DMA((total,)),
            pltpu.SemaphoreType.DMA((pairs,)),
            pltpu.SemaphoreType.DMA((2,)),
        ],
        compiler_params=remote_params(1, 32),
        name="exchange_forward",
    )(rims, packed, neighbours)


def exchange_backward(grid, rims, grads, neighbours):
    n_chunk, slots, _, band, _ = rims.shape
    n_tile = grid.n_tile
    side_a, side_b, side_x = grid.size["a"], grid.size["b"], grid.size["x"]
    _, blocks, rows, cols = grads.shape
    pairs = blocks // side_x
    part = rows // side_b
    halo = HaloExchange(grid, n_chunk, slots, band // RIM)
    total = halo.count + blocks + pairs * ((side_x - 1) + (side_b - 1)) + pairs * side_x * (side_b - 1)

    def kernel(r_ref, g_ref, n_ref, halo_ref, o_ref, arrived, picked, local, here, core, far, across, send, recv, load_sems):
        own = grid.own()
        own_x, own_b = own["x"], own["b"]
        meet(grid.partners(("tile", "x", "c")))
        copies = Copies(send, recv)
        halo.send_rims(copies, r_ref, arrived, local)
        loads, cores = [], []
        order = []
        for m in range(pairs):
            order += [(k, m) for k in range(1, side_x)] if m % 2 == 0 else []
        order += [(k, m) for m in range(pairs) for k in range(side_x) if (k, m) not in order]
        index = lambda k, m: (own_x ^ k) * pairs + m
        for i, (k, m) in enumerate(order):
            at = index(k, m)
            cores.append(copies.start(g_ref.at[1 - own["c"], at], core.at[at], grid.beside(own, "c", 1)))
            load = pltpu.make_async_copy(g_ref.at[own["c"], at], here.at[at], load_sems.at[i])
            load.start()
            loads.append(load)
        sent_x = {m: [] for m in range(pairs)}
        sent_b = {m: [] for m in range(pairs)}
        rows_of = lambda b: pl.ds(pl.multiple_of(b * part, 16), part)

        def send_b(m, k):
            for j in range(1, side_b):
                to = grid.beside(own, "b", j)
                at = index(k, m)
                sent_b[m].append(
                    (k, copies.start(here.at[at, rows_of(own_b ^ j)], across.at[j - 1, at], to))
                )

        def send_x(m, k):
            at = index(k, m)
            to = grid.beside(own, "x", k)
            if m % 2 == 0:
                sent_x[m].append(copies.start(here.at[at], far.at[k - 1, m], to))
            else:
                sent_x[m].append(
                    copies.start(here.at[at, rows_of(own_b)], far.at[k - 1, m, pl.ds(0, part)], to)
                )

        for i, (k, m) in enumerate(order):
            loads[i].wait()
            cores[i].wait_recv()
            at = index(k, m)
            add_rows(here.at[at], [core.at[at]], rows)
            if m % 2 == 1:
                send_b(m, k)
            elif k > 0:
                send_x(m, k)
        halo.pick_and_send(
            copies, arrived, picked, halo_ref, local, lambda d, k: n_ref[d // slots, d % slots, k]
        )
        for m in range(pairs):
            if m % 2 == 1:
                for k, copy in sent_b[m]:
                    copy.wait()
                for k in [*range(1, side_x), 0]:
                    at = index(k, m)
                    add_rows(here.at[at, rows_of(own_b)], [across.at[j, at] for j in range(side_b - 1)], part)
                    if k > 0:
                        send_x(m, k)
            else:
                for copy in sent_x[m]:
                    copy.wait()
                add_rows(here.at[index(0, m)], [far.at[j, m] for j in range(side_x - 1)], rows)
                send_b(m, 0)
        for m in range(pairs):
            at = index(0, m)
            if m % 2 == 1:
                for copy in sent_x[m]:
                    copy.wait()
                sources = [far.at[j, m, pl.ds(0, part)] for j in range(side_x - 1)]
            else:
                for _, copy in sent_b[m]:
                    copy.wait()
                sources = [across.at[j, at] for j in range(side_b - 1)]
            add_rows(here.at[at, rows_of(own_b)], sources, part)
        outs = []
        for m in range(pairs):
            out = pltpu.make_async_copy(here.at[index(0, m), rows_of(own_b)], o_ref.at[m], load_sems.at[m])
            out.start()
            outs.append(out)
        halo.finish()
        for copy in cores:
            copy.wait_send()
        for out in outs:
            out.wait()

    any_space = pl.BlockSpec(memory_space=pl.ANY)
    return pl.pallas_call(
        kernel,
        in_specs=[any_space, any_space, pl.BlockSpec(memory_space=pltpu.SMEM)],
        out_specs=[any_space] * 2,
        out_shape=[halo.halo_shape(), jax.ShapeDtypeStruct((pairs, part, cols), BF)],
        scratch_shapes=halo.scratch()
        + [
            pltpu.VMEM((blocks, rows, cols), BF),
            pltpu.VMEM((blocks, rows, cols), BF),
            pltpu.VMEM((side_x - 1, pairs, rows, cols), BF),
            pltpu.VMEM((side_b - 1, blocks, part, cols), BF),
            pltpu.SemaphoreType.DMA((total,)),
            pltpu.SemaphoreType.DMA((total,)),
            pltpu.SemaphoreType.DMA((blocks,)),
        ],
        compiler_params=remote_params(2, 56),
        name="exchange_backward",
    )(rims, grads, neighbours)


def finish_gradients(grid, partial, small):
    pairs, part, cols = partial.shape
    side_a, side_b = grid.size["a"], grid.size["b"]
    piece = part // side_a
    steps = [(dim, 1 << i) for dim in ("c", "x", "b", "a") for i in range((grid.size[dim] - 1).bit_length())]
    total = pairs * 2 * (side_a - 1) + pairs * side_a * (side_b - 1) + len(steps)

    def kernel(p_ref, s_ref, o_ref, t_ref, mine, got, sums, send, recv, load_sems):
        own = grid.own()
        meet(grid.partners(("a", "b", "x", "c")))
        copies = Copies(send, recv)
        rows_of = lambda a: pl.ds(pl.multiple_of(a * piece, 16), piece)
        place = lambda a, b: pl.ds(pl.multiple_of((b * side_a + a) * piece, 16), piece)
        firsts, loads = [], []
        for m in range(pairs):
            firsts.append(
                [
                    copies.start(p_ref.at[m, rows_of(own["a"] ^ k)], got.at[m, k - 1], grid.beside(own, "a", k))
                    for k in range(1, side_a)
                ]
            )
            load = pltpu.make_async_copy(p_ref.at[m, rows_of(own["a"])], mine.at[m], load_sems.at[m])
            load.start()
            loads.append(load)
        t_ref[...] = s_ref[...]
        small_copies = []

        def small_step(i):
            dim, k = steps[i]
            copy = copies.start(t_ref, sums.at[i], grid.beside(own, dim, k))
            copy.wait()
            t_ref[...] = t_ref[...] + sums[i]

        for i in range(len(steps)):
            small_step(i)
        seconds, thirds, keeps = [], [], []
        for m in range(pairs):
            loads[m].wait()
            for copy in firsts[m]:
                copy.wait()
            add_rows(mine.at[m], [got.at[m, k] for k in range(side_a - 1)], piece)
            keep = pltpu.make_async_copy(mine.at[m], o_ref.at[m, place(own["a"], own["b"])], load_sems.at[m])
            keep.start()
            keeps.append(keep)
            to = o_ref.at[m, place(own["a"], own["b"])]
            seconds.append(
                [(k, copies.start(mine.at[m], to, grid.beside(own, "a", k))) for k in range(1, side_a)]
            )
            thirds += [copies.start(mine.at[m], to, grid.beside(own, "b", j)) for j in range(1, side_b)]
        for m in range(pairs):
            for k, copy in seconds[m]:
                copy.wait_recv()
                at = o_ref.at[m, place(own["a"] ^ k, own["b"])]
                thirds += [copies.start(at, at, grid.beside(own, "b", j)) for j in range(1, side_b)]
        for m in range(pairs):
            keeps[m].wait()
            for _, copy in seconds[m]:
                copy.wait_send()
        for copy in thirds:
            copy.wait()

    any_space = pl.BlockSpec(memory_space=pl.ANY)
    whole = pl.BlockSpec(memory_space=pltpu.VMEM)
    return pl.pallas_call(
        kernel,
        in_specs=[any_space, whole],
        out_specs=[any_space, whole],
        out_shape=[
            jax.ShapeDtypeStruct((pairs, side_b * part, cols), BF),
            jax.ShapeDtypeStruct(small.shape, F32),
        ],
        scratch_shapes=[
            pltpu.VMEM((pairs, piece, cols), BF),
            pltpu.VMEM((pairs, side_a - 1, piece, cols), BF),
            pltpu.VMEM((len(steps),) + small.shape, F32),
            pltpu.SemaphoreType.DMA((total,)),
            pltpu.SemaphoreType.DMA((total,)),
            pltpu.SemaphoreType.DMA((pairs,)),
        ],
        compiler_params=remote_params(3, 32),
        name="finish_gradients",
    )(partial, small)


def scatter_change(grid, change):
    pairs, rows, cols = change.shape
    side_a, side_b = grid.size["a"], grid.size["b"]
    part = rows // side_b
    piece = part // side_a
    total = pairs * ((side_b - 1) + (side_a - 1))

    def kernel(c_ref, o_ref, mine, from_b, from_a, send, recv, load_sems):
        own = grid.own()
        meet(grid.partners(("a", "b")))
        copies = Copies(send, recv)
        half = lambda b: pl.ds(pl.multiple_of(b * part, 16), part)
        rows_of = lambda a: pl.ds(pl.multiple_of(a * piece, 16), piece)
        firsts, loads = [], []
        for m in range(pairs):
            firsts.append(
                [
                    copies.start(c_ref.at[m, half(own["b"] ^ k)], from_b.at[k - 1, m], grid.beside(own, "b", k))
                    for k in range(1, side_b)
                ]
            )
            load = pltpu.make_async_copy(c_ref.at[m, half(own["b"])], mine.at[m], load_sems.at[m])
            load.start()
            loads.append(load)
        seconds = []
        for m in range(pairs):
            loads[m].wait()
            for copy in firsts[m]:
                copy.wait()
            add_rows(mine.at[m], [from_b.at[k, m] for k in range(side_b - 1)], part)
            seconds.append(
                [
                    copies.start(mine.at[m, rows_of(own["a"] ^ k)], from_a.at[k - 1, m], grid.beside(own, "a", k))
                    for k in range(1, side_a)
                ]
            )
        for m in range(pairs):
            for copy in seconds[m]:
                copy.wait()
            here = mine.at[m, rows_of(own["a"])]
            total_here = here[...].astype(F32)
            for k in range(side_a - 1):
                total_here = total_here + from_a[k, m].astype(F32)
            o_ref[m] = total_here

    any_space = pl.BlockSpec(memory_space=pl.ANY)
    return pl.pallas_call(
        kernel,
        in_specs=[any_space],
        out_specs=pl.BlockSpec(memory_space=pltpu.VMEM),
        out_shape=jax.ShapeDtypeStruct((pairs, piece, cols), F32),
        scratch_shapes=[
            pltpu.VMEM((pairs, part, cols), BF),
            pltpu.VMEM((side_b - 1, pairs, part, cols), BF),
            pltpu.VMEM((side_a - 1, pairs, piece, cols), BF),
            pltpu.SemaphoreType.DMA((total,)),
            pltpu.SemaphoreType.DMA((total,)),
            pltpu.SemaphoreType.DMA((pairs,)),
        ],
        compiler_params=remote_params(4, 40),
        name="scatter_change",
    )(change)


def tile_total(grid, value, number):
    n_tile = grid.n_tile

    def kernel(v_ref, o_ref, got, send, recv):
        t, o = grid.at(grid.own())
        meet(grid.partners(("tile",)))
        copies = Copies(send, recv)
        got[t] = v_ref[...]
        sent = [copies.start(v_ref, got.at[t], (t ^ k, o)) for k in range(1, n_tile)]
        for copy in sent:
            copy.wait()
        total = got[0]
        for i in range(1, n_tile):
            total = total + got[i]
        o_ref[...] = total

    whole = pl.BlockSpec(memory_space=pltpu.VMEM)
    return pl.pallas_call(
        kernel,
        in_specs=[whole],
        out_specs=whole,
        out_shape=jax.ShapeDtypeStruct(value.shape, F32),
        scratch_shapes=[
            pltpu.VMEM((n_tile,) + value.shape, F32),
            pltpu.SemaphoreType.DMA((n_tile - 1,)),
            pltpu.SemaphoreType.DMA((n_tile - 1,)),
        ],
        compiler_params=remote_params(number, 16),
        name="tile_total",
    )(value)


def fill_halo(pad, halo, side):
    last = side + RIM
    up, down, left, right, corner = (halo(k) for k in range(5))
    for e in range(RIM):
        rows = slice(e * side, e * side + side)
        pad[pl.ds(e * PITCH + 8, side), :] = up[rows]
        pad[pl.ds((last + e) * PITCH + 8, side), :] = down[rows]
        pad[pl.ds(RIM * PITCH + 8 - RIM + e, side, stride=PITCH), :] = left[rows]
        pad[pl.ds(RIM * PITCH + 8 + side + e, side, stride=PITCH), :] = right[rows]
    places = ((0, 8 - RIM), (0, 8 + side), (last, 8 - RIM), (last, 8 + side))
    for k, (row, col) in enumerate(places):
        for e in range(RIM):
            at = 16 * k + RIM * e
            pad[pl.ds((row + e) * PITCH + col, RIM), :] = corner[at : at + RIM]


def conv_pass(pad, side, weight, emit):
    for block in range(side // 8):
        sums = [None] * side
        for b in range(7):
            taps = [weight(a, b) for a in range(7)]
            for r in range(side + 2 * RIM):
                cells = pad[pl.ds(r * PITCH + 8 - RIM + b + 8 * block, 8), :]
                for a in range(7):
                    i = r - a
                    if 0 <= i < side:
                        term = taps[a] * cells
                        sums[i] = term if sums[i] is None else sums[i] + term
        emit(block, sums)


def halo_block(halos):
    return pl.BlockSpec((1, 1) + halos.shape[2:], lambda c, s: (c, s, 0, 0, 0))


def conv_cost(n_chunk, slots, side, nbytes):
    return pl.CostEstimate(
        flops=n_chunk * slots * side * side * LANES * 98 * 100, bytes_accessed=nbytes, transcendentals=0
    )


def conv_forward(inputs, mask_lanes, halos, taps):
    slots, side, _, channels = inputs.shape
    n_chunk = halos.shape[0]

    def kernel(x_ref, m_ref, w_ref, h_ref, o_ref, s_ref, pad):
        for i in range(side):
            pad[pl.ds((i + RIM) * PITCH + 8, side), :] = (
                x_ref[0, i].astype(F32) * m_ref[0, pl.ds(i * side, side), :]
            )
        fill_halo(pad, lambda k: h_ref[0, 0, k].astype(F32), side)
        bias = w_ref[49]
        totals = [jnp.zeros((8, LANES), F32), jnp.zeros((8, LANES), F32)]

        def emit(block, sums):
            for i in range(side):
                value = sums[i] + bias
                rows = pl.ds(i * side + 8 * block, 8)
                o_ref[0, rows, :] = value
                weighted = m_ref[0, rows, :] * value
                totals[0] = totals[0] + weighted
                totals[1] = totals[1] + weighted * value

        conv_pass(pad, side, lambda a, b: w_ref[7 * a + b], emit)
        s_ref[0, 0], s_ref[0, 1] = totals

    cells = side * side
    return pl.pallas_call(
        kernel,
        grid=(n_chunk, slots),
        in_specs=[
            pl.BlockSpec((1, side, side, LANES), lambda c, s: (s, 0, 0, c)),
            pl.BlockSpec((1, cells, LANES), lambda c, s: (s, 0, 0)),
            pl.BlockSpec((50, 8, LANES), lambda c, s: (0, 0, c)),
            halo_block(halos),
        ],
        out_specs=[
            pl.BlockSpec((1, cells, LANES), lambda c, s: (s, 0, c)),
            pl.BlockSpec((1, 2, 8, LANES), lambda c, s: (s, 0, 0, c)),
        ],
        scratch_shapes=[pltpu.VMEM(((side + 2 * RIM) * PITCH, LANES), F32)],
        out_shape=[
            jax.ShapeDtypeStruct((slots, cells, channels), F32),
            jax.ShapeDtypeStruct((slots, 2, 8, channels), F32),
        ],
        cost_estimate=conv_cost(n_chunk, slots, side, 10 << 20),
        compiler_params=pltpu.CompilerParams(vmem_limit_bytes=32 << 20),
        name="conv_forward",
    )(inputs, mask_lanes, taps, halos)


def conv_gradient(d_shaped, conv_out, mask_lanes, coefs, side):
    slots, cells, channels = d_shaped.shape
    n_chunk = -(-channels // LANES)

    def kernel(d_ref, v_ref, m_ref, c_ref, o_ref, r_ref, held):
        one, two, three = c_ref[0, :1], c_ref[1, :1], c_ref[2, :1]
        for s in range(slots):
            value = d_ref[s] * one - m_ref[s] * (two + three * v_ref[s])
            o_ref[s] = value
            held[...] = value
            store_rims(held, r_ref, s, side)

    piece = (slots, 4, RIM * side, LANES)
    block = pl.BlockSpec((slots, cells, LANES), lambda c: (0, 0, c))
    return pl.pallas_call(
        kernel,
        grid=(n_chunk,),
        in_specs=[
            block,
            block,
            pl.BlockSpec((slots, cells, LANES), lambda c: (0, 0, 0)),
            pl.BlockSpec((3, 8, LANES), lambda c: (0, 0, c)),
        ],
        out_specs=[block, pl.BlockSpec((1,) + piece, lambda c: (c, 0, 0, 0, 0))],
        scratch_shapes=[pltpu.VMEM((cells, LANES), F32)],
        out_shape=[
            jax.ShapeDtypeStruct((slots, cells, channels), F32),
            jax.ShapeDtypeStruct((n_chunk,) + piece, BF),
        ],
        compiler_params=pltpu.CompilerParams(vmem_limit_bytes=32 << 20),
        name="conv_gradient",
    )(d_shaped, conv_out, mask_lanes, coefs)


def tap_gradient(inputs, mask_lanes, halos, d_conv):
    slots, side, _, channels = inputs.shape
    n_chunk = halos.shape[0]
    cells = side * side

    def kernel(x_ref, m_ref, d_ref, h_ref, o_ref, pad, sums):
        slot = pl.program_id(1)
        for i in range(side):
            pad[pl.ds((i + RIM) * PITCH + 8, side), :] = (
                x_ref[0, i].astype(F32) * m_ref[0, pl.ds(i * side, side), :]
            )
        fill_halo(pad, lambda k: h_ref[0, 0, k].astype(F32), side)

        @pl.when(slot == 0)
        def _():
            sums[...] = jnp.zeros_like(sums)

        for block in range(side // 8):
            grads = [d_ref[0, pl.ds(i * side + 8 * block, 8), :] for i in range(side)]
            total = grads[0]
            for i in range(1, side):
                total = total + grads[i]
            sums[49] += total
            for b in range(7):
                taps = [None] * 7
                for r in range(side + 2 * RIM):
                    window = pad[pl.ds(r * PITCH + 8 - RIM + b + 8 * block, 8), :]
                    for a in range(7):
                        i = r - a
                        if 0 <= i < side:
                            term = window * grads[i]
                            taps[a] = term if taps[a] is None else taps[a] + term
                for a in range(7):
                    sums[7 * a + b] += taps[a]

        @pl.when(slot == slots - 1)
        def _():
            o_ref[...] = jnp.sum(sums[...], axis=1)

    return pl.pallas_call(
        kernel,
        grid=(n_chunk, slots),
        in_specs=[
            pl.BlockSpec((1, side, side, LANES), lambda c, s: (s, 0, 0, c)),
            pl.BlockSpec((1, cells, LANES), lambda c, s: (s, 0, 0)),
            pl.BlockSpec((1, cells, LANES), lambda c, s: (s, 0, c)),
            halo_block(halos),
        ],
        out_specs=pl.BlockSpec((50, LANES), lambda c, s: (0, c)),
        scratch_shapes=[
            pltpu.VMEM(((side + 2 * RIM) * PITCH, LANES), F32),
            pltpu.VMEM((50, 8, LANES), F32),
        ],
        out_shape=jax.ShapeDtypeStruct((50, channels), F32),
        cost_estimate=conv_cost(n_chunk, slots, side, 10 << 20),
        compiler_params=pltpu.CompilerParams(vmem_limit_bytes=32 << 20),
        name="tap_gradient",
    )(inputs, mask_lanes, d_conv, halos)


def conv_backward(d_conv, halos, cotangent, mask_lanes, taps, weight_lanes):
    slots, side, _, channels = cotangent.shape
    n_chunk = halos.shape[0]
    cells = side * side

    def kernel(d_ref, g_ref, m_ref, w_ref, l_ref, h_ref, o_ref, pad):
        for i in range(side):
            pad[pl.ds((i + RIM) * PITCH + 8, side), :] = d_ref[0, pl.ds(i * side, side), :]
        fill_halo(pad, lambda k: h_ref[0, 0, k].astype(F32), side)
        weight = l_ref[...]

        def emit(block, sums):
            for i in range(side):
                rows = pl.ds(i * side + 8 * block, 8)
                scaled = weight * g_ref[0, i, pl.ds(8 * block, 8), :].astype(F32)
                o_ref[0, rows, :] = m_ref[0, rows, :] * (scaled + sums[i])

        conv_pass(pad, side, lambda a, b: w_ref[7 * (6 - a) + 6 - b], emit)

    return pl.pallas_call(
        kernel,
        grid=(n_chunk, slots),
        in_specs=[
            pl.BlockSpec((1, cells, LANES), lambda c, s: (s, 0, c)),
            pl.BlockSpec((1, side, side, LANES), lambda c, s: (s, 0, 0, c)),
            pl.BlockSpec((1, cells, LANES), lambda c, s: (s, 0, 0)),
            pl.BlockSpec((50, 8, LANES), lambda c, s: (0, 0, c)),
            pl.BlockSpec((8, LANES), lambda c, s: (0, 0)),
            halo_block(halos),
        ],
        out_specs=pl.BlockSpec((1, cells, LANES), lambda c, s: (s, 0, c)),
        scratch_shapes=[pltpu.VMEM(((side + 2 * RIM) * PITCH, LANES), F32)],
        out_shape=jax.ShapeDtypeStruct((slots, cells, channels), F32),
        cost_estimate=conv_cost(n_chunk, slots, side, 12 << 20),
        compiler_params=pltpu.CompilerParams(vmem_limit_bytes=32 << 20),
        name="conv_backward",
    )(d_conv, cotangent, mask_lanes, taps, weight_lanes, halos)


def spread_lanes(value, parts, width):
    rows, channels = value.shape
    run = channels // parts
    if run == width:
        return value
    gap = jnp.zeros((rows, width - run), value.dtype)
    pieces = []
    for t in range(parts):
        pieces += [value[:, t * run : (t + 1) * run], gap]
    return jnp.concatenate(pieces, 1)


def close_lanes(value, parts, run):
    width = value.shape[1] // parts
    if run == width:
        return value
    return jnp.concatenate([value[:, t * width : t * width + run] for t in range(parts)], 1)


def arrange(body, args, specs, rows, channels, parts, width, name):
    step = 3 * LANES if rows % (3 * LANES) == 0 else LANES

    def kernel(*refs):
        given, (gap_ref, turned_ref, sum_ref) = refs[: len(args)], refs[len(args) :]
        low = body(*given).astype(BF)
        value = low.astype(F32)
        gap_ref[...] = spread_lanes(value, parts, width).astype(BF)
        turned_ref[...] = value.T.astype(BF)

        @pl.when(pl.program_id(0) == 0)
        def _():
            sum_ref[...] = jnp.zeros_like(sum_ref)

        sum_ref[...] += jnp.sum(value, axis=0, keepdims=True)

    return pl.pallas_call(
        kernel,
        grid=(rows // step,),
        in_specs=specs(step),
        out_specs=[
            pl.BlockSpec((step, parts * width), lambda i: (i, 0)),
            pl.BlockSpec((channels, step), lambda i: (0, i)),
            pl.BlockSpec((1, channels), lambda i: (0, 0)),
        ],
        out_shape=[
            jax.ShapeDtypeStruct((rows, parts * width), BF),
            jax.ShapeDtypeStruct((channels, rows), BF),
            jax.ShapeDtypeStruct((1, channels), F32),
        ],
        compiler_params=pltpu.CompilerParams(vmem_limit_bytes=48 << 20),
        name=name,
    )(*args)


def feed_forward(inverse, shaped, shaped_t, d_branch, d_branch_t, hidden_bias, weights, grad_rows):
    rows, depth = shaped.shape
    channels = shaped_t.shape[0]
    half, _, cols = hidden_bias.shape
    pairs, owners = weights.shape[:2]
    per_owner = 2 * pairs
    tile_rows = 3 * LANES if rows % (3 * LANES) == 0 else LANES

    def kernel(inv_ref, s_ref, st_ref, d_ref, dt_ref, hb_ref, w_ref, branch_ref, ds_ref, grad_ref, bias_ref, *scratch):
        packed, first, second, act, dpre, grads, sems, out_sem = scratch
        step = pl.program_id(0)

        def where(slot):
            owner, inside = slot // per_owner, slot % per_owner
            return owner, inside // 2, inside % 2

        def fetch(h, buffer):
            copies = []
            for which in range(2):
                owner, pair, _ = where(inv_ref[h + which * half])
                copies.append(
                    pltpu.make_async_copy(w_ref.at[pair, owner], packed.at[buffer, which], sems.at[buffer, which])
                )
            return copies

        @pl.when(step == 0)
        def _():
            for copy in fetch(0, 0):
                copy.start()
            if grad_rows > channels:
                rest = grad_rows - channels
                grads[:, :, pl.ds(channels, rest), :] = jnp.zeros(grads.shape[:2] + (rest, 2 * cols), BF)

        @pl.when(step + 1 < half)
        def _():
            for copy in fetch(step + 1, (step + 1) % 2):
                copy.start()

        now = step % 2
        slots = [where(inv_ref[step + which * half]) for which in range(2)]
        waits = fetch(step, now)
        for which, held in enumerate((first, second)):
            waits[which].wait()
            for parity in range(2):

                @pl.when(slots[which][2] == parity)
                def _():
                    held[...] = packed[now, which, :, parity * cols : (parity + 1) * cols]

        hidden = hb_ref[0]
        total = jnp.zeros((1, cols), F32)
        across = (((1,), (1,)), ((), ()))
        for i in range(rows // tile_rows):
            at = pl.ds(i * tile_rows, tile_rows)
            pre = jnp.dot(s_ref[at, :], first[...], preferred_element_type=F32) + hidden
            d_act = jnp.dot(d_ref[at, :], second[...], preferred_element_type=F32)
            square = pre * pre
            bend = jnp.tanh(ROOT * pre * (1.0 + CUBE * square))
            half_up = 0.5 * (1.0 + bend)
            low = (pre * half_up).astype(BF)
            slope = half_up + (0.5 * ROOT) * pre * (1.0 - bend * bend) * (1.0 + (3.0 * CUBE) * square)
            back = (d_act * slope).astype(BF)
            act[at, :] = low
            dpre[at, :] = back
            total = total + jnp.sum(back.astype(F32), axis=0, keepdims=True)
            out_add = lax.dot_general(low, second[...], across, preferred_element_type=F32)
            in_add = lax.dot_general(back, first[...], across, preferred_element_type=F32)

            @pl.when(step == 0)
            def _():
                branch_ref[at, :] = out_add
                ds_ref[at, :] = in_add

            @pl.when(step > 0)
            def _():
                branch_ref[at, :] += out_add
                ds_ref[at, :] += in_add

        bias_ref[0] = total
        for which, (left, right) in enumerate(((st_ref, dpre), (dt_ref, act))):
            owner, pair, half_of_pair = slots[which]
            value = jnp.dot(left[...], right[...], preferred_element_type=F32).astype(BF)
            for parity in range(2):

                @pl.when(half_of_pair == parity)
                def _():
                    at = (owner // 2) * pairs + pair
                    grads[owner % 2, at, pl.ds(0, channels), parity * cols : (parity + 1) * cols] = value

        @pl.when(step == half - 1)
        def _():
            out = pltpu.make_async_copy(grads, grad_ref, out_sem.at[0])
            out.start()
            out.wait()

    whole = lambda *shape: pl.BlockSpec(shape, lambda h, *_: (0,) * len(shape))
    line = pl.BlockSpec((1, 1, cols), lambda h, *_: (h, 0, 0))
    grad_shape = (2, owners // 2 * pairs, grad_rows, 2 * cols)
    return pl.pallas_call(
        kernel,
        grid_spec=pltpu.PrefetchScalarGridSpec(
            num_scalar_prefetch=1,
            grid=(half,),
            in_specs=[
                whole(rows, depth),
                whole(channels, rows),
                whole(rows, depth),
                whole(channels, rows),
                line,
                pl.BlockSpec(memory_space=pl.ANY),
            ],
            out_specs=[whole(rows, depth), whole(rows, depth), pl.BlockSpec(memory_space=pl.ANY), line],
            scratch_shapes=[
                pltpu.VMEM((2, 2, depth, 2 * cols), BF),
                pltpu.VMEM((depth, cols), BF),
                pltpu.VMEM((depth, cols), BF),
                pltpu.VMEM((rows, cols), BF),
                pltpu.VMEM((rows, cols), BF),
                pltpu.VMEM(grad_shape, BF),
                pltpu.SemaphoreType.DMA((2, 2)),
                pltpu.SemaphoreType.DMA((1,)),
            ],
        ),
        out_shape=[
            jax.ShapeDtypeStruct((rows, depth), F32),
            jax.ShapeDtypeStruct((rows, depth), F32),
            jax.ShapeDtypeStruct(grad_shape, BF),
            jax.ShapeDtypeStruct((half, 1, cols), F32),
        ],
        cost_estimate=pl.CostEstimate(
            flops=12 * rows * channels * half * cols, bytes_accessed=40 << 20, transcendentals=rows * half * cols
        ),
        compiler_params=pltpu.CompilerParams(vmem_limit_bytes=63 << 20),
        name="feed_forward",
    )(inverse, shaped, shaped_t, d_branch, d_branch_t, hidden_bias, weights)


def close_out(branch, d_shaped, inputs, conv_out, mask_lanes, out_bias, parts, run):
    rows, channels = inputs.shape
    depth = branch.shape[1]
    step = 3 * LANES if rows % (3 * LANES) == 0 else LANES

    def kernel(b_ref, d_ref, x_ref, v_ref, m_ref, o_ref, out_ref, ds_ref, sum_ref):
        branch_here = close_lanes(b_ref[...], parts, run) + o_ref[...]
        out_ref[...] = (m_ref[:, :1] * (x_ref[...].astype(F32) + branch_here)).astype(BF)
        grads = close_lanes(d_ref[...], parts, run)
        ds_ref[...] = grads

        @pl.when(pl.program_id(0) == 0)
        def _():
            sum_ref[...] = jnp.zeros_like(sum_ref)

        sum_ref[0] += jnp.sum(grads, axis=0, keepdims=True)
        sum_ref[1] += jnp.sum(grads * v_ref[...], axis=0, keepdims=True)

    line = lambda n: pl.BlockSpec((step, n), lambda i: (i, 0))
    return pl.pallas_call(
        kernel,
        grid=(rows // step,),
        in_specs=[
            line(depth),
            line(depth),
            line(channels),
            line(channels),
            line(LANES),
            pl.BlockSpec((1, channels), lambda i: (0, 0)),
        ],
        out_specs=[line(channels), line(channels), pl.BlockSpec((2, 1, channels), lambda i: (0, 0, 0))],
        out_shape=[
            jax.ShapeDtypeStruct((rows, channels), BF),
            jax.ShapeDtypeStruct((rows, channels), F32),
            jax.ShapeDtypeStruct((2, 1, channels), F32),
        ],
        compiler_params=pltpu.CompilerParams(vmem_limit_bytes=60 << 20),
        name="close_out",
    )(branch, d_shaped, inputs, conv_out, mask_lanes, out_bias)


def halves(value):
    high = value.astype(BF)
    return high, (value - high.astype(F32)).astype(BF)


def product(left, right, contract):
    dims = (contract, ((), ()))
    total = None
    for i, a in enumerate(left):
        for j, b in enumerate(right):
            if i + j < 2:
                term = lax.dot_general(a, b, dims, preferred_element_type=F32)
                total = term if total is None else total + term
    return total


def rotate(owned, left_basis, column_basis, moment_one, moment_two, correction, grid, width):
    slots, channels, run = left_basis.shape
    cols = column_basis.shape[1]
    pairs = slots // 2
    side_a, side_b = grid.size["a"], grid.size["b"]
    n_tile = grid.n_tile

    def kernel(f_ref, g_ref, l_ref, c_ref, one_ref, two_ref, first_ref, second_ref, o_ref):
        factor = f_ref[0]
        changes = []
        for p in range(2):
            grad = g_ref[0, pl.ds(0, channels), p * cols : (p + 1) * cols]
            left = halves(l_ref[p])
            column = halves(c_ref[p])
            rotated = product(left, (grad,), ((0,), (0,)))
            rotated = product(halves(rotated), column, ((1,), (0,)))
            first = decay_rate * one_ref[p] + (1.0 - decay_rate) * rotated
            second = decay_rate * two_ref[p] + (1.0 - decay_rate) * rotated * rotated
            first_ref[p] = first
            second_ref[p] = second
            direction = first * factor / (jnp.sqrt(second * factor) + adam_eps)
            turned = product(halves(direction), column, ((1,), (1,)))
            changes.append(product(left, halves(turned), ((1,), (0,))))
        change = jnp.concatenate(changes, 1)
        gap = jnp.zeros((width - run, 2 * cols), F32)
        for t in range(n_tile):
            piece = jnp.concatenate([change[t * run : (t + 1) * run], gap], 0)
            place = (t % side_b) * side_a + t // side_b
            o_ref[0, pl.ds(place * width, width), :] = piece.astype(BF)

    pair = lambda *shape: pl.BlockSpec(shape, lambda m: (m,) + (0,) * (len(shape) - 1))
    return pl.pallas_call(
        kernel,
        grid=(pairs,),
        in_specs=[
            pl.BlockSpec(memory_space=pltpu.SMEM),
            pair(1, owned.shape[1], 2 * cols),
            pair(2, channels, run),
            pair(2, cols, cols),
            pair(2, run, cols),
            pair(2, run, cols),
        ],
        out_specs=[pair(2, run, cols), pair(2, run, cols), pair(1, n_tile * width, 2 * cols)],
        out_shape=[
            jax.ShapeDtypeStruct(moment_one.shape, F32),
            jax.ShapeDtypeStruct(moment_one.shape, F32),
            jax.ShapeDtypeStruct((pairs, n_tile * width, 2 * cols), BF),
        ],
        compiler_params=pltpu.CompilerParams(vmem_limit_bytes=60 << 20),
        name="rotate",
    )(1.0 / correction.reshape(1), owned, left_basis, column_basis, moment_one, moment_two)


def up_to(value, unit):
    return -(-value // unit) * unit


def pack_pairs(value):
    slots, rows, cols = value.shape
    return value.reshape(slots // 2, 2, rows, cols).transpose(0, 2, 1, 3).reshape(slots // 2, rows, 2 * cols)


def unpack_pairs(value):
    pairs, rows, cols = value.shape
    return value.reshape(pairs, rows, 2, cols // 2).transpose(0, 2, 1, 3).reshape(2 * pairs, rows, cols // 2)


def per_device(
    grid,
    inputs,
    cotangent,
    master,
    moment_one,
    moment_two,
    left_basis,
    column_basis,
    small_params,
    small_first,
    small_second,
    land_mask,
    tile_count,
    neighbours,
    block_order,
    cell_weight,
    step_count,
):
    position = lax.axis_index("tile")
    sample = lax.axis_index("opt")
    inputs, cotangent = inputs[0], cotangent[0]
    slots, side, _, channels = inputs.shape
    cells = side * side
    rows = slots * cells
    n_tile = grid.n_tile
    n_chunk = -(-channels // LANES)
    per_group = channels // GROUPS
    per_owner, run, cols = master.shape
    pairs = per_owner // 2
    block_total = block_order.shape[0]
    half = block_total // 2
    width = up_to(run, 16)

    live = (jnp.arange(slots) < tile_count[position]).astype(F32)
    mask = (land_mask.astype(F32) * live[:, None, None]).reshape(slots, cells)
    mask_lanes = jnp.broadcast_to(mask[:, :, None], (slots, cells, LANES))
    flat_mask = mask_lanes.reshape(rows, LANES)
    taps = jnp.broadcast_to(small_params[:50, None, :], (50, 8, channels))

    low_master = jnp.pad(pack_pairs(master.astype(BF)), ((0, 0), (0, width - run), (0, 0)))
    rims = rims_of_input(inputs, mask_lanes)
    halos, weights, all_neighbours = exchange_forward(grid, rims, low_master, neighbours)

    weights_float = cell_weight.astype(F32)
    sample_weight = weights_float[sample] * weights_float.shape[0] / jnp.sum(weights_float)
    weight_lanes = jnp.broadcast_to(sample_weight, (8, LANES))
    weight_row = jnp.broadcast_to(sample_weight, (1, LANES))
    flat_cotangent = cotangent.reshape(rows, channels)

    def d_branch_body(g_ref, m_ref, w_ref):
        return m_ref[:, :1] * (w_ref[:, :1] * g_ref[...].astype(F32))

    d_branch, d_branch_t, d_out_bias = arrange(
        d_branch_body,
        (flat_cotangent, flat_mask, weight_row),
        lambda step: [
            pl.BlockSpec((step, channels), lambda i: (i, 0)),
            pl.BlockSpec((step, LANES), lambda i: (i, 0)),
            pl.BlockSpec((1, LANES), lambda i: (0, 0)),
        ],
        rows,
        channels,
        n_tile,
        width,
        "arrange_d_branch",
    )
    conv_out, sums = conv_forward(inputs, mask_lanes, halos, taps)
    sums = jnp.sum(sums, axis=(0, 2))
    occupied = jnp.broadcast_to(jnp.sum(mask), (1, channels))
    sums = tile_total(grid, jnp.concatenate([sums, occupied], 0), 5)
    counted = sums[2, 0] * per_group
    by_group = sums[:2].reshape(2, GROUPS, per_group).sum(2)
    group_mean = by_group[0] / counted
    variance = by_group[1] / counted - group_mean * group_mean
    inv_std = jnp.repeat(lax.rsqrt(variance + epsilon), per_group)
    mean = jnp.repeat(group_mean, per_group)
    gain, shift = small_params[50], small_params[51]
    norm_coefs = jnp.stack([inv_std, mean * inv_std, gain, shift])

    def shaped_body(v_ref, c_ref):
        normed = v_ref[...] * c_ref[0:1] - c_ref[1:2]
        return normed * c_ref[2:3] + c_ref[3:4]

    flat_conv = conv_out.reshape(rows, channels)
    shaped, shaped_t, _ = arrange(
        shaped_body,
        (flat_conv, norm_coefs),
        lambda step: [
            pl.BlockSpec((step, channels), lambda i: (i, 0)),
            pl.BlockSpec((4, channels), lambda i: (0, 0)),
        ],
        rows,
        channels,
        n_tile,
        width,
        "arrange_shaped",
    )

    block_ids = jnp.arange(block_total, dtype=jnp.int32)
    inverse = jnp.sum(
        jnp.where(block_order[None, :] == block_ids[:, None], block_ids[None, :], 0), axis=1
    ).astype(jnp.int32)
    hidden_bias = small_params[53:57].reshape(half, 1, cols)
    branch, d_shaped, grads, d_hidden = feed_forward(
        inverse, shaped, shaped_t, d_branch, d_branch_t, hidden_bias, weights, n_tile * width
    )
    block_output, d_shaped, d_sums = close_out(
        branch, d_shaped, inputs.reshape(rows, channels), flat_conv, flat_mask, small_params[52:53], n_tile, run
    )

    d_shift = d_sums[0, 0]
    d_gain = inv_std * (d_sums[1, 0] - mean * d_shift)
    parts = tile_total(grid, jnp.stack([gain * d_shift, gain * d_gain]), 6)
    parts = jnp.repeat(parts.reshape(2, GROUPS, per_group).sum(2) / counted, per_group, axis=1)
    grad_coefs = jnp.stack(
        [
            inv_std * gain,
            inv_std * (parts[0] - mean * inv_std * parts[1]),
            inv_std * inv_std * parts[1],
        ]
    )
    d_conv, grad_rims = conv_gradient(
        d_shaped.reshape(slots, cells, channels),
        conv_out,
        mask_lanes,
        jnp.broadcast_to(grad_coefs[:, None, :], (3, 8, channels)),
        side,
    )
    grad_halos, partial = exchange_backward(grid, grad_rims, grads, all_neighbours)
    d_taps = tap_gradient(inputs, mask_lanes, halos, d_conv)
    input_grad = conv_backward(d_conv, grad_halos, cotangent, mask_lanes, taps, weight_lanes)

    correction = 1.0 - jnp.power(F32(decay_rate), step_count[0].astype(F32))
    d_small = jnp.concatenate(
        [d_taps, d_gain[None], d_shift[None], d_out_bias, d_hidden.reshape(4, channels)], 0
    )
    owned, d_small = finish_gradients(grid, partial, d_small)
    small_one = decay_rate * small_first + (1.0 - decay_rate) * d_small
    small_two = decay_rate * small_second + (1.0 - decay_rate) * d_small * d_small
    new_small = small_params - small_rate * (small_one / correction) / (
        jnp.sqrt(small_two / correction) + adam_eps
    )

    first_new, second_new, change = rotate(
        owned, left_basis, column_basis, moment_one, moment_two, correction, grid, width
    )
    change = unpack_pairs(scatter_change(grid, change)[:, :run])
    new_master = master - 0.5 / math.sqrt(channels) * change
    return (
        block_output.reshape((1,) + inputs.shape),
        input_grad.reshape((1,) + inputs.shape),
        new_master,
        new_master.astype(BF),
        first_new,
        second_new,
        new_small,
        small_one,
        small_two,
    )


def solution(mesh):
    grid = Grid(mesh.shape["tile"], mesh.shape["opt"])

    def step(*args):
        return per_device(grid, *args)

    return jax.shard_map(
        step,
        mesh=mesh,
        in_specs=(
            P("opt", "tile", None, None, None),
            P("opt", "tile", None, None, None),
            P("opt", "tile", None),
            P("opt", "tile", None),
            P("opt", "tile", None),
            P("opt", None, "tile"),
            P("opt", None, None),
            P(),
            P(),
            P(),
            P("tile", None, None),
            P(),
            P("tile", None),
            P(),
            P(),
            P(),
        ),
        out_specs=(
            P("opt", "tile", None, None, None),
            P("opt", "tile", None, None, None),
            P("opt", "tile", None),
            P("opt", "tile", None),
            P("opt", "tile", None),
            P("opt", "tile", None),
            P(),
            P(),
            P(),
        ),
        check_vma=False,
    )
```

```python
import math

import jax
import jax.numpy as jnp
from jax import lax
from jax.experimental import pallas as pl
from jax.experimental.pallas import tpu as pltpu
from jax.sharding import PartitionSpec as P

GROUPS = 16
LANES = 128
RIM = 3
PITCH = 40
BF = jnp.bfloat16
F32 = jnp.float32

highest = lax.Precision.HIGHEST
epsilon = 1e-05
adam_eps = 1e-08
decay_rate = 0.5
small_rate = 0.05
ROOT = 0.7978845608028654
CUBE = 0.044715


class Grid:
    def __init__(self, n_tile, n_opt):
        b = 4 if n_tile % 16 == 0 else 2
        self.n_tile, self.n_opt = n_tile, n_opt
        self.size = {"a": n_tile // b, "b": b, "x": n_opt // 2, "c": 2}

    def own(self):
        t, o = lax.axis_index("tile"), lax.axis_index("opt")
        b = self.size["b"]
        return {"a": t // b, "b": t % b, "x": o // 2, "c": o % 2}

    def at(self, place):
        return place["a"] * self.size["b"] + place["b"], place["x"] * 2 + place["c"]

    def partners(self, dims):
        own = self.own()
        found = []
        for dim in dims:
            if dim == "tile":
                t, o = self.at(own)
                found += [(t ^ k, o) for k in range(1, self.n_tile)]
            else:
                found += [self.beside(own, dim, k) for k in range(1, self.size[dim])]
        return found

    def beside(self, own, dim, k):
        return self.at({**own, dim: own[dim] ^ k})


def meet(devices):
    barrier = pltpu.get_barrier_semaphore()
    for device in devices:
        pl.semaphore_signal(barrier, inc=1, device_id=device, device_id_type=pl.DeviceIdType.MESH)
    pl.semaphore_wait(barrier, len(devices))


class Copies:
    def __init__(self, send_sems, recv_sems):
        self.sems = send_sems, recv_sems
        self.used = 0

    def make(self, src, dst, device):
        i = self.used
        self.used += 1
        return pltpu.make_async_remote_copy(
            src_ref=src,
            dst_ref=dst,
            send_sem=self.sems[0].at[i],
            recv_sem=self.sems[1].at[i],
            device_id=device,
            device_id_type=pl.DeviceIdType.MESH,
        )

    def start(self, src, dst, device):
        copy = self.make(src, dst, device)
        copy.start()
        return copy


def remote_params(number, mib):
    return pltpu.CompilerParams(collective_id=number, has_side_effects=True, vmem_limit_bytes=mib << 20)


def add_rows(target, sources, rows, step=16):
    @pl.loop(0, rows // step)
    def _(i):
        at = pl.ds(pl.multiple_of(i * step, step), step)
        total = target[at, :].astype(F32)
        for source in sources:
            total = total + source[at, :].astype(F32)
        target[at, :] = total.astype(BF)


def store_rims(src, outs, slot, side):
    outs[0, slot, 0] = src[pl.ds(0, RIM * side), :].astype(BF)
    outs[0, slot, 1] = src[pl.ds((side - RIM) * side, RIM * side), :].astype(BF)
    for e in range(RIM):
        rows = pl.ds(e * side, side)
        outs[0, slot, 2, rows] = src[pl.ds(e, side, stride=side), :].astype(BF)
        outs[0, slot, 3, rows] = src[pl.ds(side - RIM + e, side, stride=side), :].astype(BF)


def rims_of_input(inputs, mask_lanes):
    slots, side, _, channels = inputs.shape
    n_chunk = -(-channels // LANES)

    def kernel(x_ref, m_ref, o_ref, cells):
        for s in range(slots):
            for i in range(side):
                cells[pl.ds(i * side, side), :] = (
                    x_ref[s, i].astype(F32) * m_ref[s, pl.ds(i * side, side), :]
                )
            store_rims(cells, o_ref, s, side)

    return pl.pallas_call(
        kernel,
        grid=(n_chunk,),
        in_specs=[
            pl.BlockSpec((slots, side, side, LANES), lambda c: (0, 0, 0, c)),
            pl.BlockSpec((slots, side * side, LANES), lambda c: (0, 0, 0)),
        ],
        out_specs=pl.BlockSpec((1, slots, 4, RIM * side, LANES), lambda c: (c, 0, 0, 0, 0)),
        out_shape=jax.ShapeDtypeStruct((n_chunk, slots, 4, RIM * side, LANES), BF),
        scratch_shapes=[pltpu.VMEM((side * side, LANES), F32)],
        compiler_params=pltpu.CompilerParams(vmem_limit_bytes=32 << 20),
        name="rims_of_input",
    )(inputs, mask_lanes)


class HaloExchange:
    def __init__(self, grid, n_chunk, slots, side):
        self.grid, self.n_chunk, self.slots, self.side = grid, n_chunk, slots, side
        self.count = 2 * (grid.n_tile - 1)

    def scratch(self):
        n, s, band = self.grid.n_tile, self.slots, RIM * self.side
        return [
            pltpu.VMEM((n, s, 4, band, LANES), BF),
            pltpu.VMEM((n, s, 5, band, LANES), BF),
            pltpu.SemaphoreType.DMA((2,)),
        ]

    def halo_shape(self):
        return jax.ShapeDtypeStruct((self.n_chunk, self.slots, 5, RIM * self.side, LANES), BF)

    def plan(self, copies, rims, arrived, picked, halos, local):
        t, o = self.grid.at(self.grid.own())
        self.t, self.arrived, self.picked = t, arrived, picked
        own_chunk = jnp.minimum(t, self.n_chunk - 1)
        self.first, self.second = [], []
        for k in range(1, self.grid.n_tile):
            to = t ^ k
            source = jnp.minimum(to, self.n_chunk - 1)
            self.first.append((to, copies.make(rims.at[source], arrived.at[t], (to, o))))
            self.second.append((to, copies.make(picked.at[to], halos.at[own_chunk], (to, o))))
        self.own_copy = pltpu.make_async_copy(rims.at[own_chunk], arrived.at[t], local.at[0])
        self.back_copy = pltpu.make_async_copy(picked.at[t], halos.at[own_chunk], local.at[1])

    def send_rims(self):
        for to, copy in self.first:

            @pl.when(to < self.n_chunk)
            def _():
                copy.start()

        self.own_copy.start()

    def pick_and_send(self, neighbours):
        grid, slots, side = self.grid, self.slots, self.side
        t, arrived, picked = self.t, self.arrived, self.picked
        self.own_copy.wait()
        for _, copy in self.first:

            @pl.when(t < self.n_chunk)
            def _():
                copy.wait_recv()

        @pl.when(t < self.n_chunk)
        def _():
            @pl.loop(0, grid.n_tile * slots)
            def _(d):
                def rim(direction, which):
                    slot = neighbours(d, direction)
                    at = jnp.maximum(slot, 0)
                    value = arrived[at // slots, at % slots, which].astype(F32)
                    return jnp.where(slot >= 0, value, 0.0)

                to_tile, to_slot = d // slots, d % slots
                for to, (direction, which) in enumerate(((1, 1), (6, 0), (3, 3), (4, 2))):
                    picked[to_tile, to_slot, to] = rim(direction, which).astype(BF)
                rows = []
                for direction, which, first in ((0, 1, side - RIM), (2, 1, 0), (5, 0, side - RIM), (7, 0, 0)):
                    value = rim(direction, which)
                    rows += [value[e * side + first : e * side + first + RIM] for e in range(RIM)]
                    rows.append(jnp.zeros((16 - RIM * RIM, LANES), F32))
                rows.append(jnp.zeros((RIM * side - 64, LANES), F32))
                picked[to_tile, to_slot, 4] = jnp.concatenate(rows, 0).astype(BF)

        for _, copy in self.second:

            @pl.when(t < self.n_chunk)
            def _():
                copy.start()

        @pl.when(t < self.n_chunk)
        def _():
            self.back_copy.start()

    def finish(self):
        t = self.t

        @pl.when(t < self.n_chunk)
        def _():
            self.back_copy.wait()

        for to, copy in self.first:

            @pl.when(to < self.n_chunk)
            def _():
                copy.wait_send()

        for to, copy in self.second:

            @pl.when(to < self.n_chunk)
            def _():
                copy.wait_recv()

            @pl.when(t < self.n_chunk)
            def _():
                copy.wait_send()


class WeightGather:
    def __init__(self, grid, pairs, width):
        self.grid, self.pairs, self.width = grid, pairs, width
        self.count = pairs * (grid.n_tile * grid.n_opt - 1)

    def run(self, copies, packed, gathered, local):
        grid, width = self.grid, self.width
        own = grid.own()

        def place(m, rel):
            t, o = grid.at({d: own[d] ^ rel.get(d, 0) for d in own})
            return gathered.at[m, o, pl.ds(pl.multiple_of(t * width, width), width)]

        keeps, started = [], []
        for m in range(self.pairs):
            keep = pltpu.make_async_copy(packed.at[m], place(m, {}), local.at[m])
            keep.start()
            keeps.append(keep)

        def forward(m, rel, dims):
            source = packed.at[m] if not rel else place(m, rel)
            fresh = []
            for dim in dims:
                for k in range(1, grid.size[dim]):
                    copy = copies.start(source, place(m, rel), grid.beside(own, dim, k))
                    fresh.append(({**rel, dim: k}, copy))
            started.extend(copy for _, copy in fresh)
            return fresh

        orders = [("a", "x", "b", "c") if m % 2 == 0 else ("a", "b", "x", "c") for m in range(self.pairs)]
        waves = {}

        def note(m, fresh, after):
            for rel, copy in fresh:
                level = sum(1 for d in rel if d != "c")
                wave = max(rel.get("a", 0) + level - ("a" in rel), after)
                waves.setdefault(wave, []).append((m, rel, copy))

        for m in range(self.pairs):
            note(m, forward(m, {}, orders[m]), 0)
        yield 0
        for wave in range(4 * sum(grid.size.values())):
            for m, rel, copy in sorted(waves.pop(wave, []), key=lambda e: "c" in e[1]):
                copy.wait_recv()
                last = max(orders[m].index(d) for d in rel)
                note(m, forward(m, rel, orders[m][last + 1 :]), wave + 1)
            if not waves:
                break
            yield wave
        for keep in keeps:
            keep.wait()
        for copy in started:
            copy.wait_send()
        yield -1


def exchange_forward(grid, rims, packed, neighbours):
    n_chunk, slots, _, band, _ = rims.shape
    pairs, width, cols = packed.shape
    n_tile = grid.n_tile
    halo = HaloExchange(grid, n_chunk, slots, band // RIM)
    gather = WeightGather(grid, pairs, width)
    total = halo.count + gather.count + n_tile - 1

    def kernel(r_ref, p_ref, n_ref, halo_ref, w_ref, nbr_ref, arrived, picked, local, table, send, recv, locals_w, locals_n):
        own = grid.own()
        t, o = grid.at(own)
        meet(grid.partners(("tile", "x", "c")))
        copies = Copies(send, recv)
        tables = [copies.start(n_ref, nbr_ref.at[t], (t ^ k, o)) for k in range(1, n_tile)]
        keep = pltpu.make_async_copy(n_ref, nbr_ref.at[t], locals_n.at[0])
        keep.start()
        halo.plan(copies, r_ref, arrived, picked, halo_ref, local)
        halo.send_rims()
        weights = gather.run(copies, p_ref, w_ref, locals_w)
        next(weights)
        keep.wait()
        for copy in tables:
            copy.wait()
        load = pltpu.make_async_copy(nbr_ref, table, locals_n.at[1])
        load.start()
        load.wait()
        halo.pick_and_send(lambda d, k: table[d // slots, d % slots, k])
        for _ in weights:
            pass
        halo.finish()

    any_space = pl.BlockSpec(memory_space=pl.ANY)
    return pl.pallas_call(
        kernel,
        in_specs=[any_space] * 3,
        out_specs=[any_space] * 3,
        out_shape=[
            halo.halo_shape(),
            jax.ShapeDtypeStruct((pairs, grid.n_opt, n_tile * width, cols), BF),
            jax.ShapeDtypeStruct((n_tile,) + neighbours.shape, jnp.int32),
        ],
        scratch_shapes=halo.scratch()
        + [
            pltpu.SMEM((n_tile,) + neighbours.shape, jnp.int32),
            pltpu.SemaphoreType.DMA((total,)),
            pltpu.SemaphoreType.DMA((total,)),
            pltpu.SemaphoreType.DMA((pairs,)),
            pltpu.SemaphoreType.DMA((2,)),
        ],
        compiler_params=remote_params(1, 32),
        name="exchange_forward",
    )(rims, packed, neighbours)


def exchange_backward(grid, rims, grads, neighbours, inputs, mask_lanes, d_conv, halos):
    n_chunk, slots, _, band, _ = rims.shape
    side, channels = inputs.shape[1], inputs.shape[3]
    side_b, side_x = grid.size["b"], grid.size["x"]
    _, blocks, rows, cols = grads.shape
    pairs = blocks // side_x
    part = rows // side_b
    halo = HaloExchange(grid, n_chunk, slots, side)
    total = halo.count + blocks + pairs * side_x * (side_x - 1 + side_b - 1)
    last = n_chunk * slots - 1

    def kernel(
        r_ref, g_ref, n_ref, x_ref, m_ref, d_ref, h_ref, halo_ref, o_ref, tap_ref,
        arrived, picked, local, here, core, far, across, pad, sums, send, recv, load_sems,
    ):
        own = grid.own()
        own_x, own_b, own_c = own["x"], own["b"], own["c"]
        step = pl.program_id(0) * slots + pl.program_id(1)
        copies = Copies(send, recv)
        halo.plan(copies, r_ref, arrived, picked, halo_ref, local)
        order = [(k, m) for m in range(0, pairs, 2) for k in range(1, side_x)]
        order += [(k, m) for m in range(pairs) for k in range(side_x) if (k, m) not in order]
        index = lambda k, m: (own_x ^ k) * pairs + m
        rows_of = lambda b: pl.ds(pl.multiple_of(b * part, 16), part)
        cores, loads, to_x, to_b = [], [], {}, {}
        for i, (k, m) in enumerate(order):
            at = index(k, m)
            cores.append(copies.make(g_ref.at[1 - own_c, at], core.at[at], grid.beside(own, "c", 1)))
            loads.append(pltpu.make_async_copy(g_ref.at[own_c, at], here.at[at], load_sems.at[i]))
            if k > 0:
                to = grid.beside(own, "x", k)
                if m % 2 == 0:
                    to_x[k, m] = copies.make(here.at[at], far.at[k - 1, m], to)
                else:
                    to_x[k, m] = copies.make(here.at[at, rows_of(own_b)], far.at[k - 1, m, pl.ds(0, part)], to)
            if m % 2 == 1 or k == 0:
                to_b[k, m] = [
                    copies.make(here.at[at, rows_of(own_b ^ j)], across.at[j - 1, at], grid.beside(own, "b", j))
                    for j in range(1, side_b)
                ]

        def start(found):
            for copy in found:
                copy.start()

        def wait(found):
            for copy in found:
                copy.wait()

        @pl.when(step == 0)
        def _():
            meet(grid.partners(("tile", "x", "c")))
            halo.send_rims()
            start(cores)
            start(loads)

        add_taps(x_ref, m_ref, d_ref, h_ref, tap_ref, pad, sums, slots, side)

        for i, (k, m) in enumerate(order):

            @pl.when(step == min(last, 3 + 2 * i))
            def _():
                loads[i].wait()
                cores[i].wait()
                at = index(k, m)
                add_rows(here.at[at], [core.at[at]], rows)
                if m % 2 == 1:
                    start(to_b[k, m])
                elif k > 0:
                    to_x[k, m].start()

        @pl.when(step == last)
        def _():
            halo.pick_and_send(lambda d, k: n_ref[d // slots, d % slots, k])
            for m in range(pairs):
                others = range(1, side_x)
                if m % 2 == 1:
                    for k in [*others, 0]:
                        at = index(k, m)
                        wait(to_b[k, m])
                        add_rows(here.at[at, rows_of(own_b)], [across.at[j, at] for j in range(side_b - 1)], part)
                        if k > 0:
                            to_x[k, m].start()
                else:
                    wait(to_x[k, m] for k in others)
                    add_rows(here.at[index(0, m)], [far.at[k - 1, m] for k in others], rows)
                    start(to_b[0, m])
            outs = []
            for m in range(pairs):
                at = index(0, m)
                if m % 2 == 1:
                    wait(to_x[k, m] for k in range(1, side_x))
                    sources = [far.at[k - 1, m, pl.ds(0, part)] for k in range(1, side_x)]
                else:
                    wait(to_b[0, m])
                    sources = [across.at[j, at] for j in range(side_b - 1)]
                add_rows(here.at[at, rows_of(own_b)], sources, part)
                outs.append(pltpu.make_async_copy(here.at[at, rows_of(own_b)], o_ref.at[m], load_sems.at[m]))
                outs[-1].start()
            halo.finish()
            for out in outs:
                out.wait()

    any_space = pl.BlockSpec(memory_space=pl.ANY)
    cells = side * side
    return pl.pallas_call(
        kernel,
        grid=(n_chunk, slots),
        in_specs=[
            any_space,
            any_space,
            pl.BlockSpec(memory_space=pltpu.SMEM),
            pl.BlockSpec((1, side, side, LANES), lambda c, s: (s, 0, 0, c)),
            pl.BlockSpec((1, cells, LANES), lambda c, s: (s, 0, 0)),
            pl.BlockSpec((1, cells, LANES), lambda c, s: (s, 0, c)),
            halo_block(halos),
        ],
        out_specs=[any_space, any_space, pl.BlockSpec((50, LANES), lambda c, s: (0, c))],
        out_shape=[
            halo.halo_shape(),
            jax.ShapeDtypeStruct((pairs, part, cols), BF),
            jax.ShapeDtypeStruct((50, channels), F32),
        ],
        scratch_shapes=halo.scratch()
        + [
            pltpu.VMEM((blocks, rows, cols), BF),
            pltpu.VMEM((blocks, rows, cols), BF),
            pltpu.VMEM((side_x - 1, pairs, rows, cols), BF),
            pltpu.VMEM((side_b - 1, blocks, part, cols), BF),
            pltpu.VMEM(((side + 2 * RIM) * PITCH, LANES), F32),
            pltpu.VMEM((50, 8, LANES), F32),
            pltpu.SemaphoreType.DMA((total,)),
            pltpu.SemaphoreType.DMA((total,)),
            pltpu.SemaphoreType.DMA((blocks,)),
        ],
        compiler_params=remote_params(2, 60),
        name="exchange_backward",
    )(rims, grads, neighbours, inputs, mask_lanes, d_conv, halos)


def finish_gradients(grid, partial, small):
    pairs, part, cols = partial.shape
    side_a, side_b = grid.size["a"], grid.size["b"]
    piece = part // side_a
    steps = [(dim, 1 << i) for dim in ("c", "x", "b", "a") for i in range((grid.size[dim] - 1).bit_length())]
    total = pairs * 2 * (side_a - 1) + pairs * side_a * (side_b - 1) + len(steps)

    def kernel(p_ref, s_ref, o_ref, t_ref, mine, got, sums, send, recv, load_sems):
        own = grid.own()
        meet(grid.partners(("a", "b", "x", "c")))
        copies = Copies(send, recv)
        rows_of = lambda a: pl.ds(pl.multiple_of(a * piece, 16), piece)
        place = lambda a, b: pl.ds(pl.multiple_of((b * side_a + a) * piece, 16), piece)
        firsts, loads = [], []
        for m in range(pairs):
            firsts.append(
                [
                    copies.start(p_ref.at[m, rows_of(own["a"] ^ k)], got.at[m, k - 1], grid.beside(own, "a", k))
                    for k in range(1, side_a)
                ]
            )
            load = pltpu.make_async_copy(p_ref.at[m, rows_of(own["a"])], mine.at[m], load_sems.at[m])
            load.start()
            loads.append(load)
        t_ref[...] = s_ref[...]
        small_copies = []

        def small_step(i):
            dim, k = steps[i]
            copy = copies.start(t_ref, sums.at[i], grid.beside(own, dim, k))
            copy.wait()
            t_ref[...] = t_ref[...] + sums[i]

        for i in range(len(steps)):
            small_step(i)
        seconds, thirds, keeps = [], [], []
        for m in range(pairs):
            loads[m].wait()
            for copy in firsts[m]:
                copy.wait()
            add_rows(mine.at[m], [got.at[m, k] for k in range(side_a - 1)], piece)
            keep = pltpu.make_async_copy(mine.at[m], o_ref.at[m, place(own["a"], own["b"])], load_sems.at[m])
            keep.start()
            keeps.append(keep)
            to = o_ref.at[m, place(own["a"], own["b"])]
            seconds.append(
                [(k, copies.start(mine.at[m], to, grid.beside(own, "a", k))) for k in range(1, side_a)]
            )
            thirds += [copies.start(mine.at[m], to, grid.beside(own, "b", j)) for j in range(1, side_b)]
        for m in range(pairs):
            for k, copy in seconds[m]:
                copy.wait_recv()
                at = o_ref.at[m, place(own["a"] ^ k, own["b"])]
                thirds += [copies.start(at, at, grid.beside(own, "b", j)) for j in range(1, side_b)]
        for m in range(pairs):
            keeps[m].wait()
            for _, copy in seconds[m]:
                copy.wait_send()
        for copy in thirds:
            copy.wait()

    any_space = pl.BlockSpec(memory_space=pl.ANY)
    whole = pl.BlockSpec(memory_space=pltpu.VMEM)
    return pl.pallas_call(
        kernel,
        in_specs=[any_space, whole],
        out_specs=[any_space, whole],
        out_shape=[
            jax.ShapeDtypeStruct((pairs, side_b * part, cols), BF),
            jax.ShapeDtypeStruct(small.shape, F32),
        ],
        scratch_shapes=[
            pltpu.VMEM((pairs, piece, cols), BF),
            pltpu.VMEM((pairs, side_a - 1, piece, cols), BF),
            pltpu.VMEM((len(steps),) + small.shape, F32),
            pltpu.SemaphoreType.DMA((total,)),
            pltpu.SemaphoreType.DMA((total,)),
            pltpu.SemaphoreType.DMA((pairs,)),
        ],
        compiler_params=remote_params(3, 32),
        name="finish_gradients",
    )(partial, small)


def tile_total(grid, value, number):
    n_tile = grid.n_tile

    def kernel(v_ref, o_ref, got, send, recv):
        t, o = grid.at(grid.own())
        meet(grid.partners(("tile",)))
        copies = Copies(send, recv)
        got[t] = v_ref[...]
        sent = [copies.start(v_ref, got.at[t], (t ^ k, o)) for k in range(1, n_tile)]
        for copy in sent:
            copy.wait()
        total = got[0]
        for i in range(1, n_tile):
            total = total + got[i]
        o_ref[...] = total

    whole = pl.BlockSpec(memory_space=pltpu.VMEM)
    return pl.pallas_call(
        kernel,
        in_specs=[whole],
        out_specs=whole,
        out_shape=jax.ShapeDtypeStruct(value.shape, F32),
        scratch_shapes=[
            pltpu.VMEM((n_tile,) + value.shape, F32),
            pltpu.SemaphoreType.DMA((n_tile - 1,)),
            pltpu.SemaphoreType.DMA((n_tile - 1,)),
        ],
        compiler_params=remote_params(number, 16),
        name="tile_total",
    )(value)


def fill_halo(pad, halo, side):
    last = side + RIM
    up, down, left, right, corner = (halo(k) for k in range(5))
    for e in range(RIM):
        rows = slice(e * side, e * side + side)
        pad[pl.ds(e * PITCH + 8, side), :] = up[rows]
        pad[pl.ds((last + e) * PITCH + 8, side), :] = down[rows]
        pad[pl.ds(RIM * PITCH + 8 - RIM + e, side, stride=PITCH), :] = left[rows]
        pad[pl.ds(RIM * PITCH + 8 + side + e, side, stride=PITCH), :] = right[rows]
    places = ((0, 8 - RIM), (0, 8 + side), (last, 8 - RIM), (last, 8 + side))
    for k, (row, col) in enumerate(places):
        for e in range(RIM):
            at = 16 * k + RIM * e
            pad[pl.ds((row + e) * PITCH + col, RIM), :] = corner[at : at + RIM]


def conv_pass(pad, side, weight, emit):
    for block in range(side // 8):
        sums = [None] * side
        for b in range(7):
            taps = [weight(a, b) for a in range(7)]
            for r in range(side + 2 * RIM):
                cells = pad[pl.ds(r * PITCH + 8 - RIM + b + 8 * block, 8), :]
                for a in range(7):
                    i = r - a
                    if 0 <= i < side:
                        term = taps[a] * cells
                        sums[i] = term if sums[i] is None else sums[i] + term
        emit(block, sums)


def halo_block(halos):
    return pl.BlockSpec((1, 1) + halos.shape[2:], lambda c, s: (c, s, 0, 0, 0))


def conv_cost(n_chunk, slots, side, nbytes):
    return pl.CostEstimate(
        flops=n_chunk * slots * side * side * LANES * 98 * 100, bytes_accessed=nbytes, transcendentals=0
    )


def conv_forward(inputs, mask_lanes, halos, taps):
    slots, side, _, channels = inputs.shape
    n_chunk = halos.shape[0]

    def kernel(x_ref, m_ref, w_ref, h_ref, o_ref, s_ref, pad):
        for i in range(side):
            pad[pl.ds((i + RIM) * PITCH + 8, side), :] = (
                x_ref[0, i].astype(F32) * m_ref[0, pl.ds(i * side, side), :]
            )
        fill_halo(pad, lambda k: h_ref[0, 0, k].astype(F32), side)
        bias = w_ref[49]
        totals = [jnp.zeros((8, LANES), F32), jnp.zeros((8, LANES), F32)]

        def emit(block, sums):
            for i in range(side):
                value = sums[i] + bias
                rows = pl.ds(i * side + 8 * block, 8)
                o_ref[0, rows, :] = value
                weighted = m_ref[0, rows, :] * value
                totals[0] = totals[0] + weighted
                totals[1] = totals[1] + weighted * value

        conv_pass(pad, side, lambda a, b: w_ref[7 * a + b], emit)
        s_ref[0, 0], s_ref[0, 1] = totals

    cells = side * side
    return pl.pallas_call(
        kernel,
        grid=(n_chunk, slots),
        in_specs=[
            pl.BlockSpec((1, side, side, LANES), lambda c, s: (s, 0, 0, c)),
            pl.BlockSpec((1, cells, LANES), lambda c, s: (s, 0, 0)),
            pl.BlockSpec((50, 8, LANES), lambda c, s: (0, 0, c)),
            halo_block(halos),
        ],
        out_specs=[
            pl.BlockSpec((1, cells, LANES), lambda c, s: (s, 0, c)),
            pl.BlockSpec((1, 2, 8, LANES), lambda c, s: (s, 0, 0, c)),
        ],
        scratch_shapes=[pltpu.VMEM(((side + 2 * RIM) * PITCH, LANES), F32)],
        out_shape=[
            jax.ShapeDtypeStruct((slots, cells, channels), F32),
            jax.ShapeDtypeStruct((slots, 2, 8, channels), F32),
        ],
        cost_estimate=conv_cost(n_chunk, slots, side, 10 << 20),
        compiler_params=pltpu.CompilerParams(vmem_limit_bytes=32 << 20),
        name="conv_forward",
    )(inputs, mask_lanes, taps, halos)


def conv_gradient(d_shaped, conv_out, mask_lanes, coefs, side):
    slots, cells, channels = d_shaped.shape
    n_chunk = -(-channels // LANES)

    def kernel(d_ref, v_ref, m_ref, c_ref, o_ref, r_ref, held):
        one, two, three = c_ref[0, :1], c_ref[1, :1], c_ref[2, :1]
        for s in range(slots):
            value = d_ref[s] * one - m_ref[s] * (two + three * v_ref[s])
            o_ref[s] = value
            held[...] = value
            store_rims(held, r_ref, s, side)

    piece = (slots, 4, RIM * side, LANES)
    block = pl.BlockSpec((slots, cells, LANES), lambda c: (0, 0, c))
    return pl.pallas_call(
        kernel,
        grid=(n_chunk,),
        in_specs=[
            block,
            block,
            pl.BlockSpec((slots, cells, LANES), lambda c: (0, 0, 0)),
            pl.BlockSpec((3, 8, LANES), lambda c: (0, 0, c)),
        ],
        out_specs=[block, pl.BlockSpec((1,) + piece, lambda c: (c, 0, 0, 0, 0))],
        scratch_shapes=[pltpu.VMEM((cells, LANES), F32)],
        out_shape=[
            jax.ShapeDtypeStruct((slots, cells, channels), F32),
            jax.ShapeDtypeStruct((n_chunk,) + piece, BF),
        ],
        compiler_params=pltpu.CompilerParams(vmem_limit_bytes=32 << 20),
        name="conv_gradient",
    )(d_shaped, conv_out, mask_lanes, coefs)


def add_taps(x_ref, m_ref, d_ref, h_ref, o_ref, pad, sums, slots, side):
    slot = pl.program_id(1)
    for i in range(side):
        pad[pl.ds((i + RIM) * PITCH + 8, side), :] = x_ref[0, i].astype(F32) * m_ref[0, pl.ds(i * side, side), :]
    fill_halo(pad, lambda k: h_ref[0, 0, k].astype(F32), side)

    @pl.when(slot == 0)
    def _():
        sums[...] = jnp.zeros_like(sums)

    for block in range(side // 8):
        grads = [d_ref[0, pl.ds(i * side + 8 * block, 8), :] for i in range(side)]
        total = grads[0]
        for i in range(1, side):
            total = total + grads[i]
        sums[49] += total
        for b in range(7):
            taps = [None] * 7
            for r in range(side + 2 * RIM):
                window = pad[pl.ds(r * PITCH + 8 - RIM + b + 8 * block, 8), :]
                for a in range(7):
                    i = r - a
                    if 0 <= i < side:
                        term = window * grads[i]
                        taps[a] = term if taps[a] is None else taps[a] + term
            for a in range(7):
                sums[7 * a + b] += taps[a]

    @pl.when(slot == slots - 1)
    def _():
        o_ref[...] = jnp.sum(sums[...], axis=1)


def conv_backward(grid, d_conv, halos, cotangent, mask_lanes, taps, weight_lanes, change):
    slots, side, _, channels = cotangent.shape
    n_chunk = halos.shape[0]
    cells = side * side
    pairs, rows, cols = change.shape
    side_a, side_b = grid.size["a"], grid.size["b"]
    part = rows // side_b
    piece = part // side_a
    total = pairs * ((side_b - 1) + (side_a - 1))
    last = n_chunk * slots - 1

    def kernel(
        d_ref, g_ref, m_ref, w_ref, l_ref, h_ref, c_ref, o_ref, change_ref,
        pad, mine, from_b, from_a, send, recv, load_sems,
    ):
        own = grid.own()
        step = pl.program_id(0) * slots + pl.program_id(1)
        copies = Copies(send, recv)
        half = lambda b: pl.ds(pl.multiple_of(b * part, 16), part)
        rows_of = lambda a: pl.ds(pl.multiple_of(a * piece, 16), piece)
        firsts, seconds, loads = [], [], []
        for m in range(pairs):
            firsts.append(
                [
                    copies.make(c_ref.at[m, half(own["b"] ^ k)], from_b.at[k - 1, m], grid.beside(own, "b", k))
                    for k in range(1, side_b)
                ]
            )
            seconds.append(
                [
                    copies.make(mine.at[m, rows_of(own["a"] ^ k)], from_a.at[k - 1, m], grid.beside(own, "a", k))
                    for k in range(1, side_a)
                ]
            )
            loads.append(pltpu.make_async_copy(c_ref.at[m, half(own["b"])], mine.at[m], load_sems.at[m]))

        @pl.when(step == 0)
        def _():
            meet(grid.partners(("a", "b")))
            for m in range(pairs):
                for copy in firsts[m]:
                    copy.start()
                loads[m].start()

        for i in range(side):
            pad[pl.ds((i + RIM) * PITCH + 8, side), :] = d_ref[0, pl.ds(i * side, side), :]
        fill_halo(pad, lambda k: h_ref[0, 0, k].astype(F32), side)
        weight = l_ref[...]

        def emit(block, sums):
            for i in range(side):
                at = pl.ds(i * side + 8 * block, 8)
                scaled = weight * g_ref[0, i, pl.ds(8 * block, 8), :].astype(F32)
                o_ref[0, at, :] = m_ref[0, at, :] * (scaled + sums[i])

        conv_pass(pad, side, lambda a, b: w_ref[7 * (6 - a) + 6 - b], emit)

        for m in range(pairs):

            @pl.when(step == min(last, 9 + 4 * m))
            def _():
                loads[m].wait()
                for copy in firsts[m]:
                    copy.wait()
                add_rows(mine.at[m], [from_b.at[k, m] for k in range(side_b - 1)], part)
                for copy in seconds[m]:
                    copy.start()

        @pl.when(step == last)
        def _():
            for m in range(pairs):
                for copy in seconds[m]:
                    copy.wait()
                value = mine[m, rows_of(own["a"])].astype(F32)
                for k in range(side_a - 1):
                    value = value + from_a[k, m].astype(F32)
                change_ref[m] = value

    return pl.pallas_call(
        kernel,
        grid=(n_chunk, slots),
        in_specs=[
            pl.BlockSpec((1, cells, LANES), lambda c, s: (s, 0, c)),
            pl.BlockSpec((1, side, side, LANES), lambda c, s: (s, 0, 0, c)),
            pl.BlockSpec((1, cells, LANES), lambda c, s: (s, 0, 0)),
            pl.BlockSpec((50, 8, LANES), lambda c, s: (0, 0, c)),
            pl.BlockSpec((8, LANES), lambda c, s: (0, 0)),
            halo_block(halos),
            pl.BlockSpec(memory_space=pl.ANY),
        ],
        out_specs=[
            pl.BlockSpec((1, cells, LANES), lambda c, s: (s, 0, c)),
            pl.BlockSpec((pairs, piece, cols), lambda c, s: (0, 0, 0)),
        ],
        scratch_shapes=[
            pltpu.VMEM(((side + 2 * RIM) * PITCH, LANES), F32),
            pltpu.VMEM((pairs, part, cols), BF),
            pltpu.VMEM((side_b - 1, pairs, part, cols), BF),
            pltpu.VMEM((side_a - 1, pairs, piece, cols), BF),
            pltpu.SemaphoreType.DMA((total,)),
            pltpu.SemaphoreType.DMA((total,)),
            pltpu.SemaphoreType.DMA((pairs,)),
        ],
        out_shape=[
            jax.ShapeDtypeStruct((slots, cells, channels), F32),
            jax.ShapeDtypeStruct((pairs, piece, cols), F32),
        ],
        compiler_params=remote_params(4, 48),
        name="conv_backward",
    )(d_conv, cotangent, mask_lanes, taps, weight_lanes, halos, change)


def spread_lanes(value, parts, width):
    rows, channels = value.shape
    run = channels // parts
    if run == width:
        return value
    gap = jnp.zeros((rows, width - run), value.dtype)
    pieces = []
    for t in range(parts):
        pieces += [value[:, t * run : (t + 1) * run], gap]
    return jnp.concatenate(pieces, 1)


def close_lanes(value, parts, run):
    width = value.shape[1] // parts
    if run == width:
        return value
    return jnp.concatenate([value[:, t * width : t * width + run] for t in range(parts)], 1)


def arrange(body, args, specs, rows, channels, parts, width, name):
    step = 3 * LANES if rows % (3 * LANES) == 0 else LANES

    def kernel(*refs):
        given, (gap_ref, turned_ref, sum_ref) = refs[: len(args)], refs[len(args) :]
        low = body(*given).astype(BF)
        value = low.astype(F32)
        gap_ref[...] = spread_lanes(value, parts, width).astype(BF)
        turned_ref[...] = value.T.astype(BF)

        @pl.when(pl.program_id(0) == 0)
        def _():
            sum_ref[...] = jnp.zeros_like(sum_ref)

        sum_ref[...] += jnp.sum(value, axis=0, keepdims=True)

    return pl.pallas_call(
        kernel,
        grid=(rows // step,),
        in_specs=specs(step),
        out_specs=[
            pl.BlockSpec((step, parts * width), lambda i: (i, 0)),
            pl.BlockSpec((channels, step), lambda i: (0, i)),
            pl.BlockSpec((1, channels), lambda i: (0, 0)),
        ],
        out_shape=[
            jax.ShapeDtypeStruct((rows, parts * width), BF),
            jax.ShapeDtypeStruct((channels, rows), BF),
            jax.ShapeDtypeStruct((1, channels), F32),
        ],
        compiler_params=pltpu.CompilerParams(vmem_limit_bytes=48 << 20),
        name=name,
    )(*args)


def feed_forward(inverse, shaped, shaped_t, d_branch, d_branch_t, hidden_bias, weights, grad_rows):
    rows, depth = shaped.shape
    channels = shaped_t.shape[0]
    half, _, cols = hidden_bias.shape
    pairs, owners = weights.shape[:2]
    per_owner = 2 * pairs
    tile_rows = 3 * LANES if rows % (3 * LANES) == 0 else LANES

    def kernel(inv_ref, s_ref, st_ref, d_ref, dt_ref, hb_ref, w_ref, branch_ref, ds_ref, grad_ref, bias_ref, *scratch):
        packed, first, second, act, dpre, grads, sems, out_sem = scratch
        step = pl.program_id(0)

        def where(slot):
            owner, inside = slot // per_owner, slot % per_owner
            return owner, inside // 2, inside % 2

        def fetch(h, buffer):
            copies = []
            for which in range(2):
                owner, pair, _ = where(inv_ref[h + which * half])
                copies.append(
                    pltpu.make_async_copy(w_ref.at[pair, owner], packed.at[buffer, which], sems.at[buffer, which])
                )
            return copies

        @pl.when(step == 0)
        def _():
            for copy in fetch(0, 0):
                copy.start()
            if grad_rows > channels:
                rest = grad_rows - channels
                grads[:, :, pl.ds(channels, rest), :] = jnp.zeros(grads.shape[:2] + (rest, 2 * cols), BF)

        @pl.when(step + 1 < half)
        def _():
            for copy in fetch(step + 1, (step + 1) % 2):
                copy.start()

        now = step % 2
        slots = [where(inv_ref[step + which * half]) for which in range(2)]
        waits = fetch(step, now)
        for which, held in enumerate((first, second)):
            waits[which].wait()
            for parity in range(2):

                @pl.when(slots[which][2] == parity)
                def _():
                    held[...] = packed[now, which, :, parity * cols : (parity + 1) * cols]

        hidden = hb_ref[0]
        total = jnp.zeros((1, cols), F32)
        across = (((1,), (1,)), ((), ()))
        for i in range(rows // tile_rows):
            at = pl.ds(i * tile_rows, tile_rows)
            pre = jnp.dot(s_ref[at, :], first[...], preferred_element_type=F32) + hidden
            d_act = jnp.dot(d_ref[at, :], second[...], preferred_element_type=F32)
            square = pre * pre
            bend = jnp.tanh(ROOT * pre * (1.0 + CUBE * square))
            half_up = 0.5 * (1.0 + bend)
            low = (pre * half_up).astype(BF)
            slope = half_up + (0.5 * ROOT) * pre * (1.0 - bend * bend) * (1.0 + (3.0 * CUBE) * square)
            back = (d_act * slope).astype(BF)
            act[at, :] = low
            dpre[at, :] = back
            total = total + jnp.sum(back.astype(F32), axis=0, keepdims=True)
            out_add = lax.dot_general(low, second[...], across, preferred_element_type=F32)
            in_add = lax.dot_general(back, first[...], across, preferred_element_type=F32)

            @pl.when(step == 0)
            def _():
                branch_ref[at, :] = out_add
                ds_ref[at, :] = in_add

            @pl.when(step > 0)
            def _():
                branch_ref[at, :] += out_add
                ds_ref[at, :] += in_add

        bias_ref[0] = total
        for which, (left, right) in enumerate(((st_ref, dpre), (dt_ref, act))):
            owner, pair, half_of_pair = slots[which]
            value = jnp.dot(left[...], right[...], preferred_element_type=F32).astype(BF)
            for parity in range(2):

                @pl.when(half_of_pair == parity)
                def _():
                    at = (owner // 2) * pairs + pair
                    grads[owner % 2, at, pl.ds(0, channels), parity * cols : (parity + 1) * cols] = value

        @pl.when(step == half - 1)
        def _():
            out = pltpu.make_async_copy(grads, grad_ref, out_sem.at[0])
            out.start()
            out.wait()

    whole = lambda *shape: pl.BlockSpec(shape, lambda h, *_: (0,) * len(shape))
    line = pl.BlockSpec((1, 1, cols), lambda h, *_: (h, 0, 0))
    grad_shape = (2, owners // 2 * pairs, grad_rows, 2 * cols)
    return pl.pallas_call(
        kernel,
        grid_spec=pltpu.PrefetchScalarGridSpec(
            num_scalar_prefetch=1,
            grid=(half,),
            in_specs=[
                whole(rows, depth),
                whole(channels, rows),
                whole(rows, depth),
                whole(channels, rows),
                line,
                pl.BlockSpec(memory_space=pl.ANY),
            ],
            out_specs=[whole(rows, depth), whole(rows, depth), pl.BlockSpec(memory_space=pl.ANY), line],
            scratch_shapes=[
                pltpu.VMEM((2, 2, depth, 2 * cols), BF),
                pltpu.VMEM((depth, cols), BF),
                pltpu.VMEM((depth, cols), BF),
                pltpu.VMEM((rows, cols), BF),
                pltpu.VMEM((rows, cols), BF),
                pltpu.VMEM(grad_shape, BF),
                pltpu.SemaphoreType.DMA((2, 2)),
                pltpu.SemaphoreType.DMA((1,)),
            ],
        ),
        out_shape=[
            jax.ShapeDtypeStruct((rows, depth), F32),
            jax.ShapeDtypeStruct((rows, depth), F32),
            jax.ShapeDtypeStruct(grad_shape, BF),
            jax.ShapeDtypeStruct((half, 1, cols), F32),
        ],
        cost_estimate=pl.CostEstimate(
            flops=12 * rows * channels * half * cols, bytes_accessed=40 << 20, transcendentals=rows * half * cols
        ),
        compiler_params=pltpu.CompilerParams(vmem_limit_bytes=63 << 20),
        name="feed_forward",
    )(inverse, shaped, shaped_t, d_branch, d_branch_t, hidden_bias, weights)


def close_out(branch, d_shaped, inputs, conv_out, mask_lanes, out_bias, parts, run):
    rows, channels = inputs.shape
    depth = branch.shape[1]
    step = 3 * LANES if rows % (3 * LANES) == 0 else LANES

    def kernel(b_ref, d_ref, x_ref, v_ref, m_ref, o_ref, out_ref, ds_ref, sum_ref):
        branch_here = close_lanes(b_ref[...], parts, run) + o_ref[...]
        out_ref[...] = (m_ref[:, :1] * (x_ref[...].astype(F32) + branch_here)).astype(BF)
        grads = close_lanes(d_ref[...], parts, run)
        ds_ref[...] = grads

        @pl.when(pl.program_id(0) == 0)
        def _():
            sum_ref[...] = jnp.zeros_like(sum_ref)

        sum_ref[0] += jnp.sum(grads, axis=0, keepdims=True)
        sum_ref[1] += jnp.sum(grads * v_ref[...], axis=0, keepdims=True)

    line = lambda n: pl.BlockSpec((step, n), lambda i: (i, 0))
    return pl.pallas_call(
        kernel,
        grid=(rows // step,),
        in_specs=[
            line(depth),
            line(depth),
            line(channels),
            line(channels),
            line(LANES),
            pl.BlockSpec((1, channels), lambda i: (0, 0)),
        ],
        out_specs=[line(channels), line(channels), pl.BlockSpec((2, 1, channels), lambda i: (0, 0, 0))],
        out_shape=[
            jax.ShapeDtypeStruct((rows, channels), BF),
            jax.ShapeDtypeStruct((rows, channels), F32),
            jax.ShapeDtypeStruct((2, 1, channels), F32),
        ],
        compiler_params=pltpu.CompilerParams(vmem_limit_bytes=60 << 20),
        name="close_out",
    )(branch, d_shaped, inputs, conv_out, mask_lanes, out_bias)


def halves(value):
    high = value.astype(BF)
    return high, (value - high.astype(F32)).astype(BF)


def product(left, right, contract):
    dims = (contract, ((), ()))
    total = None
    for i, a in enumerate(left):
        for j, b in enumerate(right):
            if i + j < 2:
                term = lax.dot_general(a, b, dims, preferred_element_type=F32)
                total = term if total is None else total + term
    return total


def rotate(owned, left_basis, column_basis, moment_one, moment_two, correction, grid, width):
    slots, channels, run = left_basis.shape
    cols = column_basis.shape[1]
    pairs = slots // 2
    side_a, side_b = grid.size["a"], grid.size["b"]
    n_tile = grid.n_tile

    def kernel(f_ref, g_ref, l_ref, c_ref, one_ref, two_ref, first_ref, second_ref, o_ref):
        factor = f_ref[0]
        changes = []
        for p in range(2):
            grad = g_ref[0, pl.ds(0, channels), p * cols : (p + 1) * cols]
            left = halves(l_ref[p])
            column = halves(c_ref[p])
            rotated = product(left, (grad,), ((0,), (0,)))
            rotated = product(halves(rotated), column, ((1,), (0,)))
            first = decay_rate * one_ref[p] + (1.0 - decay_rate) * rotated
            second = decay_rate * two_ref[p] + (1.0 - decay_rate) * rotated * rotated
            first_ref[p] = first
            second_ref[p] = second
            direction = first * factor / (jnp.sqrt(second * factor) + adam_eps)
            turned = product(halves(direction), column, ((1,), (1,)))
            changes.append(product(left, halves(turned), ((1,), (0,))))
        change = jnp.concatenate(changes, 1)
        gap = jnp.zeros((width - run, 2 * cols), F32)
        for t in range(n_tile):
            piece = jnp.concatenate([change[t * run : (t + 1) * run], gap], 0)
            place = (t % side_b) * side_a + t // side_b
            o_ref[0, pl.ds(place * width, width), :] = piece.astype(BF)

    pair = lambda *shape: pl.BlockSpec(shape, lambda m: (m,) + (0,) * (len(shape) - 1))
    return pl.pallas_call(
        kernel,
        grid=(pairs,),
        in_specs=[
            pl.BlockSpec(memory_space=pltpu.SMEM),
            pair(1, owned.shape[1], 2 * cols),
            pair(2, channels, run),
            pair(2, cols, cols),
            pair(2, run, cols),
            pair(2, run, cols),
        ],
        out_specs=[pair(2, run, cols), pair(2, run, cols), pair(1, n_tile * width, 2 * cols)],
        out_shape=[
            jax.ShapeDtypeStruct(moment_one.shape, F32),
            jax.ShapeDtypeStruct(moment_one.shape, F32),
            jax.ShapeDtypeStruct((pairs, n_tile * width, 2 * cols), BF),
        ],
        compiler_params=pltpu.CompilerParams(vmem_limit_bytes=60 << 20),
        name="rotate",
    )(1.0 / correction.reshape(1), owned, left_basis, column_basis, moment_one, moment_two)


def up_to(value, unit):
    return -(-value // unit) * unit


def pack_pairs(value):
    slots, rows, cols = value.shape
    return value.reshape(slots // 2, 2, rows, cols).transpose(0, 2, 1, 3).reshape(slots // 2, rows, 2 * cols)


def unpack_pairs(value):
    pairs, rows, cols = value.shape
    return value.reshape(pairs, rows, 2, cols // 2).transpose(0, 2, 1, 3).reshape(2 * pairs, rows, cols // 2)


def per_device(
    grid,
    inputs,
    cotangent,
    master,
    moment_one,
    moment_two,
    left_basis,
    column_basis,
    small_params,
    small_first,
    small_second,
    land_mask,
    tile_count,
    neighbours,
    block_order,
    cell_weight,
    step_count,
):
    position = lax.axis_index("tile")
    sample = lax.axis_index("opt")
    inputs, cotangent = inputs[0], cotangent[0]
    slots, side, _, channels = inputs.shape
    cells = side * side
    rows = slots * cells
    n_tile = grid.n_tile
    n_chunk = -(-channels // LANES)
    per_group = channels // GROUPS
    per_owner, run, cols = master.shape
    pairs = per_owner // 2
    block_total = block_order.shape[0]
    half = block_total // 2
    width = up_to(run, 16)

    live = (jnp.arange(slots) < tile_count[position]).astype(F32)
    mask = (land_mask.astype(F32) * live[:, None, None]).reshape(slots, cells)
    mask_lanes = jnp.broadcast_to(mask[:, :, None], (slots, cells, LANES))
    flat_mask = mask_lanes.reshape(rows, LANES)
    taps = jnp.broadcast_to(small_params[:50, None, :], (50, 8, channels))

    low_master = jnp.pad(pack_pairs(master.astype(BF)), ((0, 0), (0, width - run), (0, 0)))
    rims = rims_of_input(inputs, mask_lanes)
    halos, weights, all_neighbours = exchange_forward(grid, rims, low_master, neighbours)

    weights_float = cell_weight.astype(F32)
    sample_weight = weights_float[sample] * weights_float.shape[0] / jnp.sum(weights_float)
    weight_lanes = jnp.broadcast_to(sample_weight, (8, LANES))
    weight_row = jnp.broadcast_to(sample_weight, (1, LANES))
    flat_cotangent = cotangent.reshape(rows, channels)

    def d_branch_body(g_ref, m_ref, w_ref):
        return m_ref[:, :1] * (w_ref[:, :1] * g_ref[...].astype(F32))

    d_branch, d_branch_t, d_out_bias = arrange(
        d_branch_body,
        (flat_cotangent, flat_mask, weight_row),
        lambda step: [
            pl.BlockSpec((step, channels), lambda i: (i, 0)),
            pl.BlockSpec((step, LANES), lambda i: (i, 0)),
            pl.BlockSpec((1, LANES), lambda i: (0, 0)),
        ],
        rows,
        channels,
        n_tile,
        width,
        "arrange_d_branch",
    )
    conv_out, sums = conv_forward(inputs, mask_lanes, halos, taps)
    sums = jnp.sum(sums, axis=(0, 2))
    occupied = jnp.broadcast_to(jnp.sum(mask), (1, channels))
    sums = tile_total(grid, jnp.concatenate([sums, occupied], 0), 5)
    counted = sums[2, 0] * per_group
    by_group = sums[:2].reshape(2, GROUPS, per_group).sum(2)
    group_mean = by_group[0] / counted
    variance = by_group[1] / counted - group_mean * group_mean
    inv_std = jnp.repeat(lax.rsqrt(variance + epsilon), per_group)
    mean = jnp.repeat(group_mean, per_group)
    gain, shift = small_params[50], small_params[51]
    norm_coefs = jnp.stack([inv_std, mean * inv_std, gain, shift])

    def shaped_body(v_ref, c_ref):
        normed = v_ref[...] * c_ref[0:1] - c_ref[1:2]
        return normed * c_ref[2:3] + c_ref[3:4]

    flat_conv = conv_out.reshape(rows, channels)
    shaped, shaped_t, _ = arrange(
        shaped_body,
        (flat_conv, norm_coefs),
        lambda step: [
            pl.BlockSpec((step, channels), lambda i: (i, 0)),
            pl.BlockSpec((4, channels), lambda i: (0, 0)),
        ],
        rows,
        channels,
        n_tile,
        width,
        "arrange_shaped",
    )

    block_ids = jnp.arange(block_total, dtype=jnp.int32)
    inverse = jnp.sum(
        jnp.where(block_order[None, :] == block_ids[:, None], block_ids[None, :], 0), axis=1
    ).astype(jnp.int32)
    hidden_bias = small_params[53:57].reshape(half, 1, cols)
    branch, d_shaped, grads, d_hidden = feed_forward(
        inverse, shaped, shaped_t, d_branch, d_branch_t, hidden_bias, weights, n_tile * width
    )
    block_output, d_shaped, d_sums = close_out(
        branch, d_shaped, inputs.reshape(rows, channels), flat_conv, flat_mask, small_params[52:53], n_tile, run
    )

    d_shift = d_sums[0, 0]
    d_gain = inv_std * (d_sums[1, 0] - mean * d_shift)
    parts = tile_total(grid, jnp.stack([gain * d_shift, gain * d_gain]), 6)
    parts = jnp.repeat(parts.reshape(2, GROUPS, per_group).sum(2) / counted, per_group, axis=1)
    grad_coefs = jnp.stack(
        [
            inv_std * gain,
            inv_std * (parts[0] - mean * inv_std * parts[1]),
            inv_std * inv_std * parts[1],
        ]
    )
    d_conv, grad_rims = conv_gradient(
        d_shaped.reshape(slots, cells, channels),
        conv_out,
        mask_lanes,
        jnp.broadcast_to(grad_coefs[:, None, :], (3, 8, channels)),
        side,
    )
    grad_halos, partial, d_taps = exchange_backward(
        grid, grad_rims, grads, all_neighbours, inputs, mask_lanes, d_conv, halos
    )

    correction = 1.0 - jnp.power(F32(decay_rate), step_count[0].astype(F32))
    d_small = jnp.concatenate(
        [d_taps, d_gain[None], d_shift[None], d_out_bias, d_hidden.reshape(4, channels)], 0
    )
    owned, d_small = finish_gradients(grid, partial, d_small)
    small_one = decay_rate * small_first + (1.0 - decay_rate) * d_small
    small_two = decay_rate * small_second + (1.0 - decay_rate) * d_small * d_small
    new_small = small_params - small_rate * (small_one / correction) / (
        jnp.sqrt(small_two / correction) + adam_eps
    )

    first_new, second_new, change = rotate(
        owned, left_basis, column_basis, moment_one, moment_two, correction, grid, width
    )
    input_grad, change = conv_backward(
        grid, d_conv, grad_halos, cotangent, mask_lanes, taps, weight_lanes, change
    )
    change = unpack_pairs(change[:, :run])
    new_master = master - 0.5 / math.sqrt(channels) * change
    return (
        block_output.reshape((1,) + inputs.shape),
        input_grad.reshape((1,) + inputs.shape),
        new_master,
        new_master.astype(BF),
        first_new,
        second_new,
        new_small,
        small_one,
        small_two,
    )


def solution(mesh):
    grid = Grid(mesh.shape["tile"], mesh.shape["opt"])

    def step(*args):
        return per_device(grid, *args)

    return jax.shard_map(
        step,
        mesh=mesh,
        in_specs=(
            P("opt", "tile", None, None, None),
            P("opt", "tile", None, None, None),
            P("opt", "tile", None),
            P("opt", "tile", None),
            P("opt", "tile", None),
            P("opt", None, "tile"),
            P("opt", None, None),
            P(),
            P(),
            P(),
            P("tile", None, None),
            P(),
            P("tile", None),
            P(),
            P(),
            P(),
        ),
        out_specs=(
            P("opt", "tile", None, None, None),
            P("opt", "tile", None, None, None),
            P("opt", "tile", None),
            P("opt", "tile", None),
            P("opt", "tile", None),
            P("opt", "tile", None),
            P(),
            P(),
            P(),
        ),
        check_vma=False,
    )
```

```python
import math

import jax
import jax.numpy as jnp
from jax import lax
from jax.experimental import pallas as pl
from jax.experimental.pallas import tpu as pltpu
from jax.sharding import PartitionSpec as P

GROUPS = 16
LANES = 128
RIM = 3
PITCH = 40
BF = jnp.bfloat16
F32 = jnp.float32

highest = lax.Precision.HIGHEST
epsilon = 1e-05
adam_eps = 1e-08
decay_rate = 0.5
small_rate = 0.05
ROOT = 0.7978845608028654
CUBE = 0.044715


class Grid:
    def __init__(self, n_tile, n_opt):
        b = 4 if n_tile % 16 == 0 else 2
        self.n_tile, self.n_opt = n_tile, n_opt
        self.size = {"a": n_tile // b, "b": b, "x": n_opt // 2, "c": 2}

    def own(self):
        t, o = lax.axis_index("tile"), lax.axis_index("opt")
        b = self.size["b"]
        return {"a": t // b, "b": t % b, "x": o // 2, "c": o % 2}

    def at(self, place):
        return place["a"] * self.size["b"] + place["b"], place["x"] * 2 + place["c"]

    def partners(self, dims):
        own = self.own()
        found = []
        for dim in dims:
            if dim == "tile":
                t, o = self.at(own)
                found += [(t ^ k, o) for k in range(1, self.n_tile)]
            else:
                found += [self.beside(own, dim, k) for k in range(1, self.size[dim])]
        return found

    def beside(self, own, dim, k):
        return self.at({**own, dim: own[dim] ^ k})


def meet(devices):
    barrier = pltpu.get_barrier_semaphore()
    for device in devices:
        pl.semaphore_signal(barrier, inc=1, device_id=device, device_id_type=pl.DeviceIdType.MESH)
    pl.semaphore_wait(barrier, len(devices))


class Copies:
    def __init__(self, send_sems, recv_sems):
        self.sems = send_sems, recv_sems
        self.used = 0

    def make(self, src, dst, device):
        i = self.used
        self.used += 1
        return pltpu.make_async_remote_copy(
            src_ref=src,
            dst_ref=dst,
            send_sem=self.sems[0].at[i],
            recv_sem=self.sems[1].at[i],
            device_id=device,
            device_id_type=pl.DeviceIdType.MESH,
        )

    def start(self, src, dst, device):
        copy = self.make(src, dst, device)
        copy.start()
        return copy


def remote_params(number, mib):
    return pltpu.CompilerParams(collective_id=number, has_side_effects=True, vmem_limit_bytes=mib << 20)


def add_rows(target, sources, rows, step=16):
    @pl.loop(0, rows // step)
    def _(i):
        at = pl.ds(pl.multiple_of(i * step, step), step)
        total = target[at, :].astype(F32)
        for source in sources:
            total = total + source[at, :].astype(F32)
        target[at, :] = total.astype(BF)


def store_rims(src, outs, slot, side):
    outs[0, slot, 0] = src[pl.ds(0, RIM * side), :].astype(BF)
    outs[0, slot, 1] = src[pl.ds((side - RIM) * side, RIM * side), :].astype(BF)
    for e in range(RIM):
        rows = pl.ds(e * side, side)
        outs[0, slot, 2, rows] = src[pl.ds(e, side, stride=side), :].astype(BF)
        outs[0, slot, 3, rows] = src[pl.ds(side - RIM + e, side, stride=side), :].astype(BF)


def rims_of_input(inputs, mask_lanes):
    slots, side, _, channels = inputs.shape
    n_chunk = -(-channels // LANES)

    def kernel(x_ref, m_ref, o_ref, cells):
        for s in range(slots):
            for i in range(side):
                cells[pl.ds(i * side, side), :] = (
                    x_ref[s, i].astype(F32) * m_ref[s, pl.ds(i * side, side), :]
                )
            store_rims(cells, o_ref, s, side)

    return pl.pallas_call(
        kernel,
        grid=(n_chunk,),
        in_specs=[
            pl.BlockSpec((slots, side, side, LANES), lambda c: (0, 0, 0, c)),
            pl.BlockSpec((slots, side * side, LANES), lambda c: (0, 0, 0)),
        ],
        out_specs=pl.BlockSpec((1, slots, 4, RIM * side, LANES), lambda c: (c, 0, 0, 0, 0)),
        out_shape=jax.ShapeDtypeStruct((n_chunk, slots, 4, RIM * side, LANES), BF),
        scratch_shapes=[pltpu.VMEM((side * side, LANES), F32)],
        compiler_params=pltpu.CompilerParams(vmem_limit_bytes=32 << 20),
        name="rims_of_input",
    )(inputs, mask_lanes)


class HaloExchange:
    def __init__(self, grid, n_chunk, slots, side):
        self.grid, self.n_chunk, self.slots, self.side = grid, n_chunk, slots, side
        self.count = 2 * (grid.n_tile - 1)

    def scratch(self):
        n, s, band = self.grid.n_tile, self.slots, RIM * self.side
        return [
            pltpu.VMEM((n, s, 4, band, LANES), BF),
            pltpu.VMEM((n, s, 5, band, LANES), BF),
            pltpu.SemaphoreType.DMA((2,)),
        ]

    def halo_shape(self):
        return jax.ShapeDtypeStruct((self.n_chunk, self.slots, 5, RIM * self.side, LANES), BF)

    def plan(self, copies, rims, arrived, picked, halos, local):
        t, o = self.grid.at(self.grid.own())
        self.t, self.arrived, self.picked = t, arrived, picked
        own_chunk = jnp.minimum(t, self.n_chunk - 1)
        self.first, self.second = [], []
        for k in range(1, self.grid.n_tile):
            to = t ^ k
            source = jnp.minimum(to, self.n_chunk - 1)
            self.first.append((to, copies.make(rims.at[source], arrived.at[t], (to, o))))
            self.second.append((to, copies.make(picked.at[to], halos.at[own_chunk], (to, o))))
        self.own_copy = pltpu.make_async_copy(rims.at[own_chunk], arrived.at[t], local.at[0])
        self.back_copy = pltpu.make_async_copy(picked.at[t], halos.at[own_chunk], local.at[1])

    def send_rims(self):
        for to, copy in self.first:

            @pl.when(to < self.n_chunk)
            def _():
                copy.start()

        self.own_copy.start()

    def pick_and_send(self, neighbours):
        grid, slots, side = self.grid, self.slots, self.side
        t, arrived, picked = self.t, self.arrived, self.picked
        self.own_copy.wait()
        for _, copy in self.first:

            @pl.when(t < self.n_chunk)
            def _():
                copy.wait_recv()

        @pl.when(t < self.n_chunk)
        def _():
            @pl.loop(0, grid.n_tile * slots)
            def _(d):
                def rim(direction, which):
                    slot = neighbours(d, direction)
                    at = jnp.maximum(slot, 0)
                    value = arrived[at // slots, at % slots, which].astype(F32)
                    return jnp.where(slot >= 0, value, 0.0)

                to_tile, to_slot = d // slots, d % slots
                for to, (direction, which) in enumerate(((1, 1), (6, 0), (3, 3), (4, 2))):
                    picked[to_tile, to_slot, to] = rim(direction, which).astype(BF)
                rows = []
                for direction, which, first in ((0, 1, side - RIM), (2, 1, 0), (5, 0, side - RIM), (7, 0, 0)):
                    value = rim(direction, which)
                    rows += [value[e * side + first : e * side + first + RIM] for e in range(RIM)]
                    rows.append(jnp.zeros((16 - RIM * RIM, LANES), F32))
                rows.append(jnp.zeros((RIM * side - 64, LANES), F32))
                picked[to_tile, to_slot, 4] = jnp.concatenate(rows, 0).astype(BF)

        for _, copy in self.second:

            @pl.when(t < self.n_chunk)
            def _():
                copy.start()

        @pl.when(t < self.n_chunk)
        def _():
            self.back_copy.start()

    def finish(self):
        t = self.t

        @pl.when(t < self.n_chunk)
        def _():
            self.back_copy.wait()

        for to, copy in self.first:

            @pl.when(to < self.n_chunk)
            def _():
                copy.wait_send()

        for to, copy in self.second:

            @pl.when(to < self.n_chunk)
            def _():
                copy.wait_recv()

            @pl.when(t < self.n_chunk)
            def _():
                copy.wait_send()


class WeightGather:
    def __init__(self, grid, pairs, width):
        self.grid, self.pairs, self.width = grid, pairs, width
        self.count = pairs * (grid.n_tile * grid.n_opt - 1)

    def plan(self, copies, packed, gathered, local):
        grid, width = self.grid, self.width
        own = grid.own()

        def place(m, rel):
            t, o = grid.at({d: own[d] ^ rel.get(d, 0) for d in own})
            return gathered.at[m, o, pl.ds(pl.multiple_of(t * width, width), width)]

        def onward(m, rel, dims):
            source = packed.at[m] if not rel else place(m, rel)
            return [
                ({**rel, dim: k}, copies.make(source, place(m, rel), grid.beside(own, dim, k)))
                for dim in dims
                for k in range(1, grid.size[dim])
            ]

        orders = [("a", "x", "b", "c") if m % 2 == 0 else ("a", "b", "x", "c") for m in range(self.pairs)]
        due = {}

        def note(m, fresh, after):
            for rel, copy in fresh:
                level = sum(1 for d in rel if d != "c")
                wave = max(rel.get("a", 0) + level - ("a" in rel), after)
                due.setdefault(wave, []).append((m, rel, copy))
            return [copy for _, copy in fresh]

        self.keeps = [pltpu.make_async_copy(packed.at[m], place(m, {}), local.at[m]) for m in range(self.pairs)]
        self.first = []
        for m in range(self.pairs):
            fresh = onward(m, {}, orders[m])
            self.first += note(m, fresh, 0)
        self.waves = []
        for wave in range(4 * sum(grid.size.values())):
            events = []
            for m, rel, copy in sorted(due.pop(wave, []), key=lambda e: "c" in e[1]):
                last = max(orders[m].index(d) for d in rel)
                events.append((copy, note(m, onward(m, rel, orders[m][last + 1 :]), wave + 1)))
            self.waves.append(events)
            if not due:
                break

    def start(self):
        for copy in self.keeps + self.first:
            copy.start()

    def run(self, waves):
        for events in waves:
            for copy, fresh in events:
                copy.wait_recv()
                for other in fresh:
                    other.start()

    def finish(self):
        for copy in self.keeps:
            copy.wait()
        for copy in self.first + [c for events in self.waves for _, fresh in events for c in fresh]:
            copy.wait_send()


def exchange_forward(grid, rims, packed, neighbours, inputs, mask_lanes, taps, cotangent, flat_mask, weight_row, width):
    n_chunk, slots, _, band, _ = rims.shape
    side, channels = inputs.shape[1], inputs.shape[3]
    cells = side * side
    pairs, _, cols = packed.shape
    n_tile = grid.n_tile
    rows = slots * cells
    block = row_block(rows)
    early = rows // block
    halo = HaloExchange(grid, n_chunk, slots, side)
    gather = WeightGather(grid, pairs, packed.shape[1])
    total = halo.count + gather.count + n_tile - 1
    last = early + n_chunk * slots

    def kernel(
        r_ref, p_ref, n_ref, x_ref, m_ref, t_ref, g_ref, f_ref, l_ref,
        halo_ref, w_ref, nbr_ref, conv_ref, sum_ref, gap_ref, turned_ref, bias_ref,
        arrived, picked, local, landed, table, pad, send, recv, locals_w, locals_n,
    ):
        step = pl.program_id(0)
        t, o = grid.at(grid.own())
        copies = Copies(send, recv)
        halo.plan(copies, r_ref, arrived, picked, landed, local)
        gather.plan(copies, p_ref, w_ref, locals_w)
        tables = [copies.make(n_ref, nbr_ref.at[t], (t ^ k, o)) for k in range(1, n_tile)]
        keep = pltpu.make_async_copy(n_ref, nbr_ref.at[t], locals_n.at[0])
        load = pltpu.make_async_copy(nbr_ref, table, locals_n.at[1])
        halo_out = pltpu.make_async_copy(landed, halo_ref, locals_n.at[0])
        head = len(gather.waves) // 2

        @pl.when(step == 0)
        def _():
            meet(grid.partners(("tile", "x", "c")))
            for copy in tables:
                copy.start()
            keep.start()
            halo.send_rims()
            gather.start()

        @pl.when((step > 0) & (step <= early))
        def _():
            value = f_ref[:, :1] * (l_ref[:, :1] * g_ref[...].astype(F32))
            arranged(value, gap_ref, turned_ref, bias_ref, step == 1, n_tile, width)

        @pl.when(step == early)
        def _():
            keep.wait()
            for copy in tables:
                copy.wait()
            load.start()
            load.wait()
            halo.pick_and_send(lambda d, k: table[d // slots, d % slots, k])
            gather.run(gather.waves[:head])
            halo.finish()
            halo_out.start()

        for i, events in enumerate(gather.waves[head:]):

            @pl.when(step == min(last, early + 4 + 3 * i))
            def _():
                gather.run([events])

        @pl.when(step > early)
        def _():
            at = step - early - 1
            conv_step(
                x_ref, m_ref, t_ref, lambda k: landed[at // slots, at % slots, k].astype(F32), conv_ref, sum_ref, pad, side
            )

        @pl.when(step == last)
        def _():
            gather.finish()
            halo_out.wait()

    conv_at = lambda i: jnp.maximum(i - early - 1, 0)
    row_at = lambda i: jnp.clip(i - 1, 0, early - 1)
    any_space = pl.BlockSpec(memory_space=pl.ANY)
    return pl.pallas_call(
        kernel,
        grid=(last + 1,),
        in_specs=[any_space] * 3
        + [
            pl.BlockSpec((1, side, side, LANES), lambda i: (conv_at(i) % slots, 0, 0, conv_at(i) // slots)),
            pl.BlockSpec((1, cells, LANES), lambda i: (conv_at(i) % slots, 0, 0)),
            pl.BlockSpec((50, 8, LANES), lambda i: (0, 0, conv_at(i) // slots)),
            pl.BlockSpec((block, channels), lambda i: (row_at(i), 0)),
            pl.BlockSpec((block, LANES), lambda i: (row_at(i), 0)),
            pl.BlockSpec((1, LANES), lambda i: (0, 0)),
        ],
        out_specs=[any_space] * 3
        + [
            pl.BlockSpec((1, cells, LANES), lambda i: (conv_at(i) % slots, 0, conv_at(i) // slots)),
            pl.BlockSpec((1, 2, 8, LANES), lambda i: (conv_at(i) % slots, 0, 0, conv_at(i) // slots)),
            pl.BlockSpec((block, n_tile * width), lambda i: (row_at(i), 0)),
            pl.BlockSpec((channels, block), lambda i: (0, row_at(i))),
            pl.BlockSpec((1, channels), lambda i: (0, 0)),
        ],
        out_shape=[
            halo.halo_shape(),
            jax.ShapeDtypeStruct((pairs, grid.n_opt, n_tile * packed.shape[1], cols), BF),
            jax.ShapeDtypeStruct((n_tile,) + neighbours.shape, jnp.int32),
            jax.ShapeDtypeStruct((slots, cells, channels), F32),
            jax.ShapeDtypeStruct((slots, 2, 8, channels), F32),
            jax.ShapeDtypeStruct((rows, n_tile * width), BF),
            jax.ShapeDtypeStruct((channels, rows), BF),
            jax.ShapeDtypeStruct((1, channels), F32),
        ],
        scratch_shapes=halo.scratch()
        + [
            pltpu.VMEM(halo.halo_shape().shape, BF),
            pltpu.SMEM((n_tile,) + neighbours.shape, jnp.int32),
            pltpu.VMEM(((side + 2 * RIM) * PITCH, LANES), F32),
            pltpu.SemaphoreType.DMA((total,)),
            pltpu.SemaphoreType.DMA((total,)),
            pltpu.SemaphoreType.DMA((pairs,)),
            pltpu.SemaphoreType.DMA((2,)),
        ],
        compiler_params=remote_params(1, 40),
        name="exchange_forward",
    )(rims, packed, neighbours, inputs, mask_lanes, taps, cotangent, flat_mask, weight_row)


def exchange_backward(grid, rims, grads, neighbours, inputs, mask_lanes, d_conv, halos):
    n_chunk, slots, _, band, _ = rims.shape
    side, channels = inputs.shape[1], inputs.shape[3]
    side_b, side_x = grid.size["b"], grid.size["x"]
    _, blocks, rows, cols = grads.shape
    pairs = blocks // side_x
    part = rows // side_b
    halo = HaloExchange(grid, n_chunk, slots, side)
    total = halo.count + blocks + pairs * side_x * (side_x - 1 + side_b - 1)
    last = n_chunk * slots - 1

    def kernel(
        r_ref, g_ref, n_ref, x_ref, m_ref, d_ref, h_ref, halo_ref, o_ref, tap_ref,
        arrived, picked, local, here, core, far, across, pad, sums, send, recv, load_sems,
    ):
        own = grid.own()
        own_x, own_b, own_c = own["x"], own["b"], own["c"]
        step = pl.program_id(0) * slots + pl.program_id(1)
        copies = Copies(send, recv)
        halo.plan(copies, r_ref, arrived, picked, halo_ref, local)
        order = [(k, m) for m in range(0, pairs, 2) for k in range(1, side_x)]
        order += [(k, m) for m in range(pairs) for k in range(side_x) if (k, m) not in order]
        index = lambda k, m: (own_x ^ k) * pairs + m
        rows_of = lambda b: pl.ds(pl.multiple_of(b * part, 16), part)
        cores, loads, to_x, to_b = [], [], {}, {}
        for i, (k, m) in enumerate(order):
            at = index(k, m)
            cores.append(copies.make(g_ref.at[1 - own_c, at], core.at[at], grid.beside(own, "c", 1)))
            loads.append(pltpu.make_async_copy(g_ref.at[own_c, at], here.at[at], load_sems.at[i]))
            if k > 0:
                to = grid.beside(own, "x", k)
                if m % 2 == 0:
                    to_x[k, m] = copies.make(here.at[at], far.at[k - 1, m], to)
                else:
                    to_x[k, m] = copies.make(here.at[at, rows_of(own_b)], far.at[k - 1, m, pl.ds(0, part)], to)
            if m % 2 == 1 or k == 0:
                to_b[k, m] = [
                    copies.make(here.at[at, rows_of(own_b ^ j)], across.at[j - 1, at], grid.beside(own, "b", j))
                    for j in range(1, side_b)
                ]

        def start(found):
            for copy in found:
                copy.start()

        def wait(found):
            for copy in found:
                copy.wait()

        @pl.when(step == 0)
        def _():
            meet(grid.partners(("tile", "x", "c")))
            halo.send_rims()
            start(cores)
            start(loads)

        add_taps(x_ref, m_ref, d_ref, h_ref, tap_ref, pad, sums, slots, side)

        for i, (k, m) in enumerate(order):

            @pl.when(step == min(last, 3 + 2 * i))
            def _():
                loads[i].wait()
                cores[i].wait()
                at = index(k, m)
                add_rows(here.at[at], [core.at[at]], rows)
                if m % 2 == 1:
                    start(to_b[k, m])
                elif k > 0:
                    to_x[k, m].start()

        @pl.when(step == last)
        def _():
            halo.pick_and_send(lambda d, k: n_ref[d // slots, d % slots, k])
            for m in range(pairs):
                others = range(1, side_x)
                if m % 2 == 1:
                    for k in [*others, 0]:
                        at = index(k, m)
                        wait(to_b[k, m])
                        add_rows(here.at[at, rows_of(own_b)], [across.at[j, at] for j in range(side_b - 1)], part)
                        if k > 0:
                            to_x[k, m].start()
                else:
                    wait(to_x[k, m] for k in others)
                    add_rows(here.at[index(0, m)], [far.at[k - 1, m] for k in others], rows)
                    start(to_b[0, m])
            outs = []
            for m in range(pairs):
                at = index(0, m)
                if m % 2 == 1:
                    wait(to_x[k, m] for k in range(1, side_x))
                    sources = [far.at[k - 1, m, pl.ds(0, part)] for k in range(1, side_x)]
                else:
                    wait(to_b[0, m])
                    sources = [across.at[j, at] for j in range(side_b - 1)]
                add_rows(here.at[at, rows_of(own_b)], sources, part)
                outs.append(pltpu.make_async_copy(here.at[at, rows_of(own_b)], o_ref.at[m], load_sems.at[m]))
                outs[-1].start()
            halo.finish()
            for out in outs:
                out.wait()

    any_space = pl.BlockSpec(memory_space=pl.ANY)
    cells = side * side
    return pl.pallas_call(
        kernel,
        grid=(n_chunk, slots),
        in_specs=[
            any_space,
            any_space,
            pl.BlockSpec(memory_space=pltpu.SMEM),
            pl.BlockSpec((1, side, side, LANES), lambda c, s: (s, 0, 0, c)),
            pl.BlockSpec((1, cells, LANES), lambda c, s: (s, 0, 0)),
            pl.BlockSpec((1, cells, LANES), lambda c, s: (s, 0, c)),
            halo_block(halos),
        ],
        out_specs=[any_space, any_space, pl.BlockSpec((50, LANES), lambda c, s: (0, c))],
        out_shape=[
            halo.halo_shape(),
            jax.ShapeDtypeStruct((pairs, part, cols), BF),
            jax.ShapeDtypeStruct((50, channels), F32),
        ],
        scratch_shapes=halo.scratch()
        + [
            pltpu.VMEM((blocks, rows, cols), BF),
            pltpu.VMEM((blocks, rows, cols), BF),
            pltpu.VMEM((side_x - 1, pairs, rows, cols), BF),
            pltpu.VMEM((side_b - 1, blocks, part, cols), BF),
            pltpu.VMEM(((side + 2 * RIM) * PITCH, LANES), F32),
            pltpu.VMEM((50, 8, LANES), F32),
            pltpu.SemaphoreType.DMA((total,)),
            pltpu.SemaphoreType.DMA((total,)),
            pltpu.SemaphoreType.DMA((blocks,)),
        ],
        compiler_params=remote_params(2, 60),
        name="exchange_backward",
    )(rims, grads, neighbours, inputs, mask_lanes, d_conv, halos)


def finish_gradients(grid, partial, small):
    pairs, part, cols = partial.shape
    side_a, side_b = grid.size["a"], grid.size["b"]
    piece = part // side_a
    steps = [(dim, 1 << i) for dim in ("c", "x", "b", "a") for i in range((grid.size[dim] - 1).bit_length())]
    total = pairs * 2 * (side_a - 1) + pairs * side_a * (side_b - 1) + len(steps)

    def kernel(p_ref, s_ref, o_ref, t_ref, mine, got, sums, send, recv, load_sems):
        own = grid.own()
        meet(grid.partners(("a", "b", "x", "c")))
        copies = Copies(send, recv)
        rows_of = lambda a: pl.ds(pl.multiple_of(a * piece, 16), piece)
        place = lambda a, b: pl.ds(pl.multiple_of((b * side_a + a) * piece, 16), piece)
        firsts, loads = [], []
        for m in range(pairs):
            firsts.append(
                [
                    copies.start(p_ref.at[m, rows_of(own["a"] ^ k)], got.at[m, k - 1], grid.beside(own, "a", k))
                    for k in range(1, side_a)
                ]
            )
            load = pltpu.make_async_copy(p_ref.at[m, rows_of(own["a"])], mine.at[m], load_sems.at[m])
            load.start()
            loads.append(load)
        t_ref[...] = s_ref[...]
        small_copies = []

        def small_step(i):
            dim, k = steps[i]
            copy = copies.start(t_ref, sums.at[i], grid.beside(own, dim, k))
            copy.wait()
            t_ref[...] = t_ref[...] + sums[i]

        for i in range(len(steps)):
            small_step(i)
        seconds, thirds, keeps = [], [], []
        for m in range(pairs):
            loads[m].wait()
            for copy in firsts[m]:
                copy.wait()
            add_rows(mine.at[m], [got.at[m, k] for k in range(side_a - 1)], piece)
            keep = pltpu.make_async_copy(mine.at[m], o_ref.at[m, place(own["a"], own["b"])], load_sems.at[m])
            keep.start()
            keeps.append(keep)
            to = o_ref.at[m, place(own["a"], own["b"])]
            seconds.append(
                [(k, copies.start(mine.at[m], to, grid.beside(own, "a", k))) for k in range(1, side_a)]
            )
            thirds += [copies.start(mine.at[m], to, grid.beside(own, "b", j)) for j in range(1, side_b)]
        for m in range(pairs):
            for k, copy in seconds[m]:
                copy.wait_recv()
                at = o_ref.at[m, place(own["a"] ^ k, own["b"])]
                thirds += [copies.start(at, at, grid.beside(own, "b", j)) for j in range(1, side_b)]
        for m in range(pairs):
            keeps[m].wait()
            for _, copy in seconds[m]:
                copy.wait_send()
        for copy in thirds:
            copy.wait()

    any_space = pl.BlockSpec(memory_space=pl.ANY)
    whole = pl.BlockSpec(memory_space=pltpu.VMEM)
    return pl.pallas_call(
        kernel,
        in_specs=[any_space, whole],
        out_specs=[any_space, whole],
        out_shape=[
            jax.ShapeDtypeStruct((pairs, side_b * part, cols), BF),
            jax.ShapeDtypeStruct(small.shape, F32),
        ],
        scratch_shapes=[
            pltpu.VMEM((pairs, piece, cols), BF),
            pltpu.VMEM((pairs, side_a - 1, piece, cols), BF),
            pltpu.VMEM((len(steps),) + small.shape, F32),
            pltpu.SemaphoreType.DMA((total,)),
            pltpu.SemaphoreType.DMA((total,)),
            pltpu.SemaphoreType.DMA((pairs,)),
        ],
        compiler_params=remote_params(3, 32),
        name="finish_gradients",
    )(partial, small)


def tile_total(grid, value, number):
    n_tile = grid.n_tile

    def kernel(v_ref, o_ref, got, send, recv):
        t, o = grid.at(grid.own())
        meet(grid.partners(("tile",)))
        copies = Copies(send, recv)
        got[t] = v_ref[...]
        sent = [copies.start(v_ref, got.at[t], (t ^ k, o)) for k in range(1, n_tile)]
        for copy in sent:
            copy.wait()
        total = got[0]
        for i in range(1, n_tile):
            total = total + got[i]
        o_ref[...] = total

    whole = pl.BlockSpec(memory_space=pltpu.VMEM)
    return pl.pallas_call(
        kernel,
        in_specs=[whole],
        out_specs=whole,
        out_shape=jax.ShapeDtypeStruct(value.shape, F32),
        scratch_shapes=[
            pltpu.VMEM((n_tile,) + value.shape, F32),
            pltpu.SemaphoreType.DMA((n_tile - 1,)),
            pltpu.SemaphoreType.DMA((n_tile - 1,)),
        ],
        compiler_params=remote_params(number, 16),
        name="tile_total",
    )(value)


def fill_halo(pad, halo, side):
    last = side + RIM
    up, down, left, right, corner = (halo(k) for k in range(5))
    for e in range(RIM):
        rows = slice(e * side, e * side + side)
        pad[pl.ds(e * PITCH + 8, side), :] = up[rows]
        pad[pl.ds((last + e) * PITCH + 8, side), :] = down[rows]
        pad[pl.ds(RIM * PITCH + 8 - RIM + e, side, stride=PITCH), :] = left[rows]
        pad[pl.ds(RIM * PITCH + 8 + side + e, side, stride=PITCH), :] = right[rows]
    places = ((0, 8 - RIM), (0, 8 + side), (last, 8 - RIM), (last, 8 + side))
    for k, (row, col) in enumerate(places):
        for e in range(RIM):
            at = 16 * k + RIM * e
            pad[pl.ds((row + e) * PITCH + col, RIM), :] = corner[at : at + RIM]


def conv_pass(pad, side, weight, emit):
    for block in range(side // 8):
        sums = [None] * side
        for b in range(7):
            taps = [weight(a, b) for a in range(7)]
            for r in range(side + 2 * RIM):
                cells = pad[pl.ds(r * PITCH + 8 - RIM + b + 8 * block, 8), :]
                for a in range(7):
                    i = r - a
                    if 0 <= i < side:
                        term = taps[a] * cells
                        sums[i] = term if sums[i] is None else sums[i] + term
        emit(block, sums)


def halo_block(halos):
    return pl.BlockSpec((1, 1) + halos.shape[2:], lambda c, s: (c, s, 0, 0, 0))


def conv_step(x_ref, m_ref, w_ref, halo, o_ref, s_ref, pad, side):
    for i in range(side):
        pad[pl.ds((i + RIM) * PITCH + 8, side), :] = x_ref[0, i].astype(F32) * m_ref[0, pl.ds(i * side, side), :]
    fill_halo(pad, halo, side)
    bias = w_ref[49]
    totals = [jnp.zeros((8, LANES), F32), jnp.zeros((8, LANES), F32)]

    def emit(block, sums):
        for i in range(side):
            value = sums[i] + bias
            rows = pl.ds(i * side + 8 * block, 8)
            o_ref[0, rows, :] = value
            weighted = m_ref[0, rows, :] * value
            totals[0] = totals[0] + weighted
            totals[1] = totals[1] + weighted * value

    conv_pass(pad, side, lambda a, b: w_ref[7 * a + b], emit)
    s_ref[0, 0], s_ref[0, 1] = totals


def conv_gradient(d_shaped, conv_out, mask_lanes, coefs, side):
    slots, cells, channels = d_shaped.shape
    n_chunk = -(-channels // LANES)

    def kernel(d_ref, v_ref, m_ref, c_ref, o_ref, r_ref, held):
        one, two, three = c_ref[0, :1], c_ref[1, :1], c_ref[2, :1]
        for s in range(slots):
            value = d_ref[s] * one - m_ref[s] * (two + three * v_ref[s])
            o_ref[s] = value
            held[...] = value
            store_rims(held, r_ref, s, side)

    piece = (slots, 4, RIM * side, LANES)
    block = pl.BlockSpec((slots, cells, LANES), lambda c: (0, 0, c))
    return pl.pallas_call(
        kernel,
        grid=(n_chunk,),
        in_specs=[
            block,
            block,
            pl.BlockSpec((slots, cells, LANES), lambda c: (0, 0, 0)),
            pl.BlockSpec((3, 8, LANES), lambda c: (0, 0, c)),
        ],
        out_specs=[block, pl.BlockSpec((1,) + piece, lambda c: (c, 0, 0, 0, 0))],
        scratch_shapes=[pltpu.VMEM((cells, LANES), F32)],
        out_shape=[
            jax.ShapeDtypeStruct((slots, cells, channels), F32),
            jax.ShapeDtypeStruct((n_chunk,) + piece, BF),
        ],
        compiler_params=pltpu.CompilerParams(vmem_limit_bytes=32 << 20),
        name="conv_gradient",
    )(d_shaped, conv_out, mask_lanes, coefs)


def add_taps(x_ref, m_ref, d_ref, h_ref, o_ref, pad, sums, slots, side):
    slot = pl.program_id(1)
    for i in range(side):
        pad[pl.ds((i + RIM) * PITCH + 8, side), :] = x_ref[0, i].astype(F32) * m_ref[0, pl.ds(i * side, side), :]
    fill_halo(pad, lambda k: h_ref[0, 0, k].astype(F32), side)

    @pl.when(slot == 0)
    def _():
        sums[...] = jnp.zeros_like(sums)

    for block in range(side // 8):
        grads = [d_ref[0, pl.ds(i * side + 8 * block, 8), :] for i in range(side)]
        total = grads[0]
        for i in range(1, side):
            total = total + grads[i]
        sums[49] += total
        for b in range(7):
            taps = [None] * 7
            for r in range(side + 2 * RIM):
                window = pad[pl.ds(r * PITCH + 8 - RIM + b + 8 * block, 8), :]
                for a in range(7):
                    i = r - a
                    if 0 <= i < side:
                        term = window * grads[i]
                        taps[a] = term if taps[a] is None else taps[a] + term
            for a in range(7):
                sums[7 * a + b] += taps[a]

    @pl.when(slot == slots - 1)
    def _():
        o_ref[...] = jnp.sum(sums[...], axis=1)


def conv_backward(grid, d_conv, halos, cotangent, mask_lanes, taps, weight_lanes, change):
    slots, side, _, channels = cotangent.shape
    n_chunk = halos.shape[0]
    cells = side * side
    pairs, rows, cols = change.shape
    side_a, side_b = grid.size["a"], grid.size["b"]
    part = rows // side_b
    piece = part // side_a
    total = pairs * ((side_b - 1) + (side_a - 1))
    last = n_chunk * slots - 1

    def kernel(
        d_ref, g_ref, m_ref, w_ref, l_ref, h_ref, c_ref, o_ref, change_ref,
        pad, mine, from_b, from_a, send, recv, load_sems,
    ):
        own = grid.own()
        step = pl.program_id(0) * slots + pl.program_id(1)
        copies = Copies(send, recv)
        half = lambda b: pl.ds(pl.multiple_of(b * part, 16), part)
        rows_of = lambda a: pl.ds(pl.multiple_of(a * piece, 16), piece)
        firsts, seconds, loads = [], [], []
        for m in range(pairs):
            firsts.append(
                [
                    copies.make(c_ref.at[m, half(own["b"] ^ k)], from_b.at[k - 1, m], grid.beside(own, "b", k))
                    for k in range(1, side_b)
                ]
            )
            seconds.append(
                [
                    copies.make(mine.at[m, rows_of(own["a"] ^ k)], from_a.at[k - 1, m], grid.beside(own, "a", k))
                    for k in range(1, side_a)
                ]
            )
            loads.append(pltpu.make_async_copy(c_ref.at[m, half(own["b"])], mine.at[m], load_sems.at[m]))

        @pl.when(step == 0)
        def _():
            meet(grid.partners(("a", "b")))
            for m in range(pairs):
                for copy in firsts[m]:
                    copy.start()
                loads[m].start()

        for i in range(side):
            pad[pl.ds((i + RIM) * PITCH + 8, side), :] = d_ref[0, pl.ds(i * side, side), :]
        fill_halo(pad, lambda k: h_ref[0, 0, k].astype(F32), side)
        weight = l_ref[...]

        def emit(block, sums):
            for i in range(side):
                at = pl.ds(i * side + 8 * block, 8)
                scaled = weight * g_ref[0, i, pl.ds(8 * block, 8), :].astype(F32)
                o_ref[0, at, :] = m_ref[0, at, :] * (scaled + sums[i])

        conv_pass(pad, side, lambda a, b: w_ref[7 * (6 - a) + 6 - b], emit)

        for m in range(pairs):

            @pl.when(step == min(last, 9 + 4 * m))
            def _():
                loads[m].wait()
                for copy in firsts[m]:
                    copy.wait()
                add_rows(mine.at[m], [from_b.at[k, m] for k in range(side_b - 1)], part)
                for copy in seconds[m]:
                    copy.start()

        @pl.when(step == last)
        def _():
            for m in range(pairs):
                for copy in seconds[m]:
                    copy.wait()
                value = mine[m, rows_of(own["a"])].astype(F32)
                for k in range(side_a - 1):
                    value = value + from_a[k, m].astype(F32)
                change_ref[m] = value

    return pl.pallas_call(
        kernel,
        grid=(n_chunk, slots),
        in_specs=[
            pl.BlockSpec((1, cells, LANES), lambda c, s: (s, 0, c)),
            pl.BlockSpec((1, side, side, LANES), lambda c, s: (s, 0, 0, c)),
            pl.BlockSpec((1, cells, LANES), lambda c, s: (s, 0, 0)),
            pl.BlockSpec((50, 8, LANES), lambda c, s: (0, 0, c)),
            pl.BlockSpec((8, LANES), lambda c, s: (0, 0)),
            halo_block(halos),
            pl.BlockSpec(memory_space=pl.ANY),
        ],
        out_specs=[
            pl.BlockSpec((1, cells, LANES), lambda c, s: (s, 0, c)),
            pl.BlockSpec((pairs, piece, cols), lambda c, s: (0, 0, 0)),
        ],
        scratch_shapes=[
            pltpu.VMEM(((side + 2 * RIM) * PITCH, LANES), F32),
            pltpu.VMEM((pairs, part, cols), BF),
            pltpu.VMEM((side_b - 1, pairs, part, cols), BF),
            pltpu.VMEM((side_a - 1, pairs, piece, cols), BF),
            pltpu.SemaphoreType.DMA((total,)),
            pltpu.SemaphoreType.DMA((total,)),
            pltpu.SemaphoreType.DMA((pairs,)),
        ],
        out_shape=[
            jax.ShapeDtypeStruct((slots, cells, channels), F32),
            jax.ShapeDtypeStruct((pairs, piece, cols), F32),
        ],
        compiler_params=remote_params(4, 48),
        name="conv_backward",
    )(d_conv, cotangent, mask_lanes, taps, weight_lanes, halos, change)


def spread_lanes(value, parts, width):
    rows, channels = value.shape
    run = channels // parts
    if run == width:
        return value
    gap = jnp.zeros((rows, width - run), value.dtype)
    pieces = []
    for t in range(parts):
        pieces += [value[:, t * run : (t + 1) * run], gap]
    return jnp.concatenate(pieces, 1)


def close_lanes(value, parts, run):
    width = value.shape[1] // parts
    if run == width:
        return value
    return jnp.concatenate([value[:, t * width : t * width + run] for t in range(parts)], 1)


def row_block(rows):
    return 3 * LANES if rows % (3 * LANES) == 0 else LANES


def arranged(value, gap_ref, turned_ref, sum_ref, first, parts, width):
    low = value.astype(BF).astype(F32)
    gap_ref[...] = spread_lanes(low, parts, width).astype(BF)
    turned_ref[...] = low.T.astype(BF)

    @pl.when(first)
    def _():
        sum_ref[...] = jnp.zeros_like(sum_ref)

    sum_ref[...] += jnp.sum(low, axis=0, keepdims=True)


def arrange(body, args, specs, rows, channels, parts, width, name):
    step = 3 * LANES if rows % (3 * LANES) == 0 else LANES

    def kernel(*refs):
        given, (gap_ref, turned_ref, sum_ref) = refs[: len(args)], refs[len(args) :]
        arranged(body(*given), gap_ref, turned_ref, sum_ref, pl.program_id(0) == 0, parts, width)

    return pl.pallas_call(
        kernel,
        grid=(rows // step,),
        in_specs=specs(step),
        out_specs=[
            pl.BlockSpec((step, parts * width), lambda i: (i, 0)),
            pl.BlockSpec((channels, step), lambda i: (0, i)),
            pl.BlockSpec((1, channels), lambda i: (0, 0)),
        ],
        out_shape=[
            jax.ShapeDtypeStruct((rows, parts * width), BF),
            jax.ShapeDtypeStruct((channels, rows), BF),
            jax.ShapeDtypeStruct((1, channels), F32),
        ],
        compiler_params=pltpu.CompilerParams(vmem_limit_bytes=48 << 20),
        name=name,
    )(*args)


def feed_forward(inverse, shaped, shaped_t, d_branch, d_branch_t, hidden_bias, weights, grad_rows):
    rows, depth = shaped.shape
    channels = shaped_t.shape[0]
    half, _, cols = hidden_bias.shape
    pairs, owners = weights.shape[:2]
    per_owner = 2 * pairs
    tile_rows = 3 * LANES if rows % (3 * LANES) == 0 else LANES

    def kernel(inv_ref, s_ref, st_ref, d_ref, dt_ref, hb_ref, w_ref, branch_ref, ds_ref, grad_ref, bias_ref, *scratch):
        packed, first, second, act, dpre, grads, sems, out_sem = scratch
        step = pl.program_id(0)

        def where(slot):
            owner, inside = slot // per_owner, slot % per_owner
            return owner, inside // 2, inside % 2

        def fetch(h, buffer):
            copies = []
            for which in range(2):
                owner, pair, _ = where(inv_ref[h + which * half])
                copies.append(
                    pltpu.make_async_copy(w_ref.at[pair, owner], packed.at[buffer, which], sems.at[buffer, which])
                )
            return copies

        @pl.when(step == 0)
        def _():
            for copy in fetch(0, 0):
                copy.start()
            if grad_rows > channels:
                rest = grad_rows - channels
                grads[:, :, pl.ds(channels, rest), :] = jnp.zeros(grads.shape[:2] + (rest, 2 * cols), BF)

        @pl.when(step + 1 < half)
        def _():
            for copy in fetch(step + 1, (step + 1) % 2):
                copy.start()

        now = step % 2
        slots = [where(inv_ref[step + which * half]) for which in range(2)]
        waits = fetch(step, now)
        for which, held in enumerate((first, second)):
            waits[which].wait()
            for parity in range(2):

                @pl.when(slots[which][2] == parity)
                def _():
                    held[...] = packed[now, which, :, parity * cols : (parity + 1) * cols]

        hidden = hb_ref[0]

        @pl.when(step == 0)
        def _():
            branch_ref[...] = jnp.zeros_like(branch_ref)
            ds_ref[...] = jnp.zeros_like(ds_ref)

        total = jnp.zeros((1, cols), F32)
        across = (((1,), (1,)), ((), ()))
        for i in range(rows // tile_rows):
            at = pl.ds(i * tile_rows, tile_rows)
            pre = jnp.dot(s_ref[at, :], first[...], preferred_element_type=F32) + hidden
            d_act = jnp.dot(d_ref[at, :], second[...], preferred_element_type=F32)
            square = pre * pre
            bend = jnp.tanh(ROOT * pre * (1.0 + CUBE * square))
            half_up = 0.5 * (1.0 + bend)
            low = (pre * half_up).astype(BF)
            slope = half_up + (0.5 * ROOT) * pre * (1.0 - bend * bend) * (1.0 + (3.0 * CUBE) * square)
            back = (d_act * slope).astype(BF)
            act[at, :] = low
            dpre[at, :] = back
            total = total + jnp.sum(back.astype(F32), axis=0, keepdims=True)
            out_add = lax.dot_general(low, second[...], across, preferred_element_type=F32)
            in_add = lax.dot_general(back, first[...], across, preferred_element_type=F32)

            branch_ref[at, :] += out_add
            ds_ref[at, :] += in_add

        bias_ref[0] = total
        for which, (left, right) in enumerate(((st_ref, dpre), (dt_ref, act))):
            owner, pair, half_of_pair = slots[which]
            value = jnp.dot(left[...], right[...], preferred_element_type=F32).astype(BF)
            for parity in range(2):

                @pl.when(half_of_pair == parity)
                def _():
                    at = (owner // 2) * pairs + pair
                    grads[owner % 2, at, pl.ds(0, channels), parity * cols : (parity + 1) * cols] = value

        @pl.when(step == half - 1)
        def _():
            out = pltpu.make_async_copy(grads, grad_ref, out_sem.at[0])
            out.start()
            out.wait()

    whole = lambda *shape: pl.BlockSpec(shape, lambda h, *_: (0,) * len(shape))
    line = pl.BlockSpec((1, 1, cols), lambda h, *_: (h, 0, 0))
    grad_shape = (2, owners // 2 * pairs, grad_rows, 2 * cols)
    return pl.pallas_call(
        kernel,
        grid_spec=pltpu.PrefetchScalarGridSpec(
            num_scalar_prefetch=1,
            grid=(half,),
            in_specs=[
                whole(rows, depth),
                whole(channels, rows),
                whole(rows, depth),
                whole(channels, rows),
                line,
                pl.BlockSpec(memory_space=pl.ANY),
            ],
            out_specs=[whole(rows, depth), whole(rows, depth), pl.BlockSpec(memory_space=pl.ANY), line],
            scratch_shapes=[
                pltpu.VMEM((2, 2, depth, 2 * cols), BF),
                pltpu.VMEM((depth, cols), BF),
                pltpu.VMEM((depth, cols), BF),
                pltpu.VMEM((rows, cols), BF),
                pltpu.VMEM((rows, cols), BF),
                pltpu.VMEM(grad_shape, BF),
                pltpu.SemaphoreType.DMA((2, 2)),
                pltpu.SemaphoreType.DMA((1,)),
            ],
        ),
        out_shape=[
            jax.ShapeDtypeStruct((rows, depth), F32),
            jax.ShapeDtypeStruct((rows, depth), F32),
            jax.ShapeDtypeStruct(grad_shape, BF),
            jax.ShapeDtypeStruct((half, 1, cols), F32),
        ],
        cost_estimate=pl.CostEstimate(
            flops=12 * rows * channels * half * cols, bytes_accessed=40 << 20, transcendentals=rows * half * cols
        ),
        compiler_params=pltpu.CompilerParams(vmem_limit_bytes=63 << 20),
        name="feed_forward",
    )(inverse, shaped, shaped_t, d_branch, d_branch_t, hidden_bias, weights)


def close_out(branch, d_shaped, inputs, conv_out, mask_lanes, out_bias, parts, run):
    rows, channels = inputs.shape
    depth = branch.shape[1]
    step = 3 * LANES if rows % (3 * LANES) == 0 else LANES

    def kernel(b_ref, d_ref, x_ref, v_ref, m_ref, o_ref, out_ref, ds_ref, sum_ref):
        branch_here = close_lanes(b_ref[...], parts, run) + o_ref[...]
        out_ref[...] = (m_ref[:, :1] * (x_ref[...].astype(F32) + branch_here)).astype(BF)
        grads = close_lanes(d_ref[...], parts, run)
        ds_ref[...] = grads

        @pl.when(pl.program_id(0) == 0)
        def _():
            sum_ref[...] = jnp.zeros_like(sum_ref)

        sum_ref[0] += jnp.sum(grads, axis=0, keepdims=True)
        sum_ref[1] += jnp.sum(grads * v_ref[...], axis=0, keepdims=True)

    line = lambda n: pl.BlockSpec((step, n), lambda i: (i, 0))
    return pl.pallas_call(
        kernel,
        grid=(rows // step,),
        in_specs=[
            line(depth),
            line(depth),
            line(channels),
            line(channels),
            line(LANES),
            pl.BlockSpec((1, channels), lambda i: (0, 0)),
        ],
        out_specs=[line(channels), line(channels), pl.BlockSpec((2, 1, channels), lambda i: (0, 0, 0))],
        out_shape=[
            jax.ShapeDtypeStruct((rows, channels), BF),
            jax.ShapeDtypeStruct((rows, channels), F32),
            jax.ShapeDtypeStruct((2, 1, channels), F32),
        ],
        compiler_params=pltpu.CompilerParams(vmem_limit_bytes=60 << 20),
        name="close_out",
    )(branch, d_shaped, inputs, conv_out, mask_lanes, out_bias)


def halves(value):
    high = value.astype(BF)
    return high, (value - high.astype(F32)).astype(BF)


def product(left, right, contract):
    dims = (contract, ((), ()))
    total = None
    for i, a in enumerate(left):
        for j, b in enumerate(right):
            if i + j < 2:
                term = lax.dot_general(a, b, dims, preferred_element_type=F32)
                total = term if total is None else total + term
    return total


def rotate(owned, left_basis, column_basis, moment_one, moment_two, correction, grid, width):
    slots, channels, run = left_basis.shape
    cols = column_basis.shape[1]
    pairs = slots // 2
    side_a, side_b = grid.size["a"], grid.size["b"]
    n_tile = grid.n_tile

    def kernel(f_ref, g_ref, l_ref, c_ref, one_ref, two_ref, first_ref, second_ref, o_ref):
        factor = f_ref[0]
        changes = []
        for p in range(2):
            grad = g_ref[0, pl.ds(0, channels), p * cols : (p + 1) * cols]
            left = halves(l_ref[p])
            column = halves(c_ref[p])
            rotated = product(left, (grad,), ((0,), (0,)))
            rotated = product(halves(rotated), column, ((1,), (0,)))
            first = decay_rate * one_ref[p] + (1.0 - decay_rate) * rotated
            second = decay_rate * two_ref[p] + (1.0 - decay_rate) * rotated * rotated
            first_ref[p] = first
            second_ref[p] = second
            direction = first * factor / (jnp.sqrt(second * factor) + adam_eps)
            turned = product(halves(direction), column, ((1,), (1,)))
            changes.append(product(left, halves(turned), ((1,), (0,))))
        change = jnp.concatenate(changes, 1)
        gap = jnp.zeros((width - run, 2 * cols), F32)
        for t in range(n_tile):
            piece = jnp.concatenate([change[t * run : (t + 1) * run], gap], 0)
            place = (t % side_b) * side_a + t // side_b
            o_ref[0, pl.ds(place * width, width), :] = piece.astype(BF)

    pair = lambda *shape: pl.BlockSpec(shape, lambda m: (m,) + (0,) * (len(shape) - 1))
    return pl.pallas_call(
        kernel,
        grid=(pairs,),
        in_specs=[
            pl.BlockSpec(memory_space=pltpu.SMEM),
            pair(1, owned.shape[1], 2 * cols),
            pair(2, channels, run),
            pair(2, cols, cols),
            pair(2, run, cols),
            pair(2, run, cols),
        ],
        out_specs=[pair(2, run, cols), pair(2, run, cols), pair(1, n_tile * width, 2 * cols)],
        out_shape=[
            jax.ShapeDtypeStruct(moment_one.shape, F32),
            jax.ShapeDtypeStruct(moment_one.shape, F32),
            jax.ShapeDtypeStruct((pairs, n_tile * width, 2 * cols), BF),
        ],
        compiler_params=pltpu.CompilerParams(vmem_limit_bytes=60 << 20),
        name="rotate",
    )(1.0 / correction.reshape(1), owned, left_basis, column_basis, moment_one, moment_two)


def up_to(value, unit):
    return -(-value // unit) * unit


def pack_pairs(value):
    slots, rows, cols = value.shape
    return value.reshape(slots // 2, 2, rows, cols).transpose(0, 2, 1, 3).reshape(slots // 2, rows, 2 * cols)


def unpack_pairs(value):
    pairs, rows, cols = value.shape
    return value.reshape(pairs, rows, 2, cols // 2).transpose(0, 2, 1, 3).reshape(2 * pairs, rows, cols // 2)


def per_device(
    grid,
    inputs,
    cotangent,
    master,
    moment_one,
    moment_two,
    left_basis,
    column_basis,
    small_params,
    small_first,
    small_second,
    land_mask,
    tile_count,
    neighbours,
    block_order,
    cell_weight,
    step_count,
):
    position = lax.axis_index("tile")
    sample = lax.axis_index("opt")
    inputs, cotangent = inputs[0], cotangent[0]
    slots, side, _, channels = inputs.shape
    cells = side * side
    rows = slots * cells
    n_tile = grid.n_tile
    n_chunk = -(-channels // LANES)
    per_group = channels // GROUPS
    per_owner, run, cols = master.shape
    pairs = per_owner // 2
    block_total = block_order.shape[0]
    half = block_total // 2
    width = up_to(run, 16)

    live = (jnp.arange(slots) < tile_count[position]).astype(F32)
    mask = (land_mask.astype(F32) * live[:, None, None]).reshape(slots, cells)
    mask_lanes = jnp.broadcast_to(mask[:, :, None], (slots, cells, LANES))
    flat_mask = mask_lanes.reshape(rows, LANES)
    taps = jnp.broadcast_to(small_params[:50, None, :], (50, 8, channels))

    weights_float = cell_weight.astype(F32)
    sample_weight = weights_float[sample] * weights_float.shape[0] / jnp.sum(weights_float)
    weight_lanes = jnp.broadcast_to(sample_weight, (8, LANES))
    weight_row = jnp.broadcast_to(sample_weight, (1, LANES))

    low_master = jnp.pad(pack_pairs(master.astype(BF)), ((0, 0), (0, width - run), (0, 0)))
    rims = rims_of_input(inputs, mask_lanes)
    halos, weights, all_neighbours, conv_out, sums, d_branch, d_branch_t, d_out_bias = exchange_forward(
        grid,
        rims,
        low_master,
        neighbours,
        inputs,
        mask_lanes,
        taps,
        cotangent.reshape(rows, channels),
        flat_mask,
        weight_row,
        width,
    )

    sums = jnp.sum(sums, axis=(0, 2))
    occupied = jnp.broadcast_to(jnp.sum(mask), (1, channels))
    sums = tile_total(grid, jnp.concatenate([sums, occupied], 0), 5)
    counted = sums[2, 0] * per_group
    by_group = sums[:2].reshape(2, GROUPS, per_group).sum(2)
    group_mean = by_group[0] / counted
    variance = by_group[1] / counted - group_mean * group_mean
    inv_std = jnp.repeat(lax.rsqrt(variance + epsilon), per_group)
    mean = jnp.repeat(group_mean, per_group)
    gain, shift = small_params[50], small_params[51]
    norm_coefs = jnp.stack([inv_std, mean * inv_std, gain, shift])

    def shaped_body(v_ref, c_ref):
        normed = v_ref[...] * c_ref[0:1] - c_ref[1:2]
        return normed * c_ref[2:3] + c_ref[3:4]

    flat_conv = conv_out.reshape(rows, channels)
    shaped, shaped_t, _ = arrange(
        shaped_body,
        (flat_conv, norm_coefs),
        lambda step: [
            pl.BlockSpec((step, channels), lambda i: (i, 0)),
            pl.BlockSpec((4, channels), lambda i: (0, 0)),
        ],
        rows,
        channels,
        n_tile,
        width,
        "arrange_shaped",
    )

    block_ids = jnp.arange(block_total, dtype=jnp.int32)
    inverse = jnp.sum(
        jnp.where(block_order[None, :] == block_ids[:, None], block_ids[None, :], 0), axis=1
    ).astype(jnp.int32)
    hidden_bias = small_params[53:57].reshape(half, 1, cols)
    branch, d_shaped, grads, d_hidden = feed_forward(
        inverse, shaped, shaped_t, d_branch, d_branch_t, hidden_bias, weights, n_tile * width
    )
    block_output, d_shaped, d_sums = close_out(
        branch, d_shaped, inputs.reshape(rows, channels), flat_conv, flat_mask, small_params[52:53], n_tile, run
    )

    d_shift = d_sums[0, 0]
    d_gain = inv_std * (d_sums[1, 0] - mean * d_shift)
    parts = tile_total(grid, jnp.stack([gain * d_shift, gain * d_gain]), 6)
    parts = jnp.repeat(parts.reshape(2, GROUPS, per_group).sum(2) / counted, per_group, axis=1)
    grad_coefs = jnp.stack(
        [
            inv_std * gain,
            inv_std * (parts[0] - mean * inv_std * parts[1]),
            inv_std * inv_std * parts[1],
        ]
    )
    d_conv, grad_rims = conv_gradient(
        d_shaped.reshape(slots, cells, channels),
        conv_out,
        mask_lanes,
        jnp.broadcast_to(grad_coefs[:, None, :], (3, 8, channels)),
        side,
    )
    grad_halos, partial, d_taps = exchange_backward(
        grid, grad_rims, grads, all_neighbours, inputs, mask_lanes, d_conv, halos
    )

    correction = 1.0 - jnp.power(F32(decay_rate), step_count[0].astype(F32))
    d_small = jnp.concatenate(
        [d_taps, d_gain[None], d_shift[None], d_out_bias, d_hidden.reshape(4, channels)], 0
    )
    owned, d_small = finish_gradients(grid, partial, d_small)
    small_one = decay_rate * small_first + (1.0 - decay_rate) * d_small
    small_two = decay_rate * small_second + (1.0 - decay_rate) * d_small * d_small
    new_small = small_params - small_rate * (small_one / correction) / (
        jnp.sqrt(small_two / correction) + adam_eps
    )

    first_new, second_new, change = rotate(
        owned, left_basis, column_basis, moment_one, moment_two, correction, grid, width
    )
    input_grad, change = conv_backward(
        grid, d_conv, grad_halos, cotangent, mask_lanes, taps, weight_lanes, change
    )
    change = unpack_pairs(change[:, :run])
    new_master = master - 0.5 / math.sqrt(channels) * change
    return (
        block_output.reshape((1,) + inputs.shape),
        input_grad.reshape((1,) + inputs.shape),
        new_master,
        new_master.astype(BF),
        first_new,
        second_new,
        new_small,
        small_one,
        small_two,
    )


def solution(mesh):
    grid = Grid(mesh.shape["tile"], mesh.shape["opt"])

    def step(*args):
        return per_device(grid, *args)

    return jax.shard_map(
        step,
        mesh=mesh,
        in_specs=(
            P("opt", "tile", None, None, None),
            P("opt", "tile", None, None, None),
            P("opt", "tile", None),
            P("opt", "tile", None),
            P("opt", "tile", None),
            P("opt", None, "tile"),
            P("opt", None, None),
            P(),
            P(),
            P(),
            P("tile", None, None),
            P(),
            P("tile", None),
            P(),
            P(),
            P(),
        ),
        out_specs=(
            P("opt", "tile", None, None, None),
            P("opt", "tile", None, None, None),
            P("opt", "tile", None),
            P("opt", "tile", None),
            P("opt", "tile", None),
            P("opt", "tile", None),
            P(),
            P(),
            P(),
        ),
        check_vma=False,
    )
```

```python
import math

import jax
import jax.numpy as jnp
from jax import lax
from jax.experimental import pallas as pl
from jax.experimental.pallas import tpu as pltpu
from jax.sharding import PartitionSpec as P

GROUPS = 16
LANES = 128
RIM = 3
PITCH = 40
BF = jnp.bfloat16
F32 = jnp.float32

highest = lax.Precision.HIGHEST
epsilon = 1e-05
adam_eps = 1e-08
decay_rate = 0.5
small_rate = 0.05
ROOT = 0.7978845608028654
CUBE = 0.044715


class Grid:
    def __init__(self, n_tile, n_opt):
        b = 4 if n_tile % 16 == 0 else 2
        self.n_tile, self.n_opt = n_tile, n_opt
        self.size = {"a": n_tile // b, "b": b, "x": n_opt // 2, "c": 2}

    def own(self):
        t, o = lax.axis_index("tile"), lax.axis_index("opt")
        b = self.size["b"]
        return {"a": t // b, "b": t % b, "x": o // 2, "c": o % 2}

    def at(self, place):
        return place["a"] * self.size["b"] + place["b"], place["x"] * 2 + place["c"]

    def partners(self, dims):
        own = self.own()
        found = []
        for dim in dims:
            if dim == "tile":
                t, o = self.at(own)
                found += [(t ^ k, o) for k in range(1, self.n_tile)]
            else:
                found += [self.beside(own, dim, k) for k in range(1, self.size[dim])]
        return found

    def beside(self, own, dim, k):
        return self.at({**own, dim: own[dim] ^ k})


def meet(devices):
    barrier = pltpu.get_barrier_semaphore()
    for device in devices:
        pl.semaphore_signal(barrier, inc=1, device_id=device, device_id_type=pl.DeviceIdType.MESH)
    pl.semaphore_wait(barrier, len(devices))


class Copies:
    def __init__(self, send_sems, recv_sems):
        self.sems = send_sems, recv_sems
        self.used = 0

    def make(self, src, dst, device):
        i = self.used
        self.used += 1
        return pltpu.make_async_remote_copy(
            src_ref=src,
            dst_ref=dst,
            send_sem=self.sems[0].at[i],
            recv_sem=self.sems[1].at[i],
            device_id=device,
            device_id_type=pl.DeviceIdType.MESH,
        )

    def start(self, src, dst, device):
        copy = self.make(src, dst, device)
        copy.start()
        return copy


def remote_params(number, mib):
    return pltpu.CompilerParams(collective_id=number, has_side_effects=True, vmem_limit_bytes=mib << 20)


def add_rows(target, sources, rows, step=16):
    @pl.loop(0, rows // step)
    def _(i):
        at = pl.ds(pl.multiple_of(i * step, step), step)
        total = target[at, :].astype(F32)
        for source in sources:
            total = total + source[at, :].astype(F32)
        target[at, :] = total.astype(BF)


def store_rims(src, outs, slot, side):
    outs[0, slot, 0] = src[pl.ds(0, RIM * side), :].astype(BF)
    outs[0, slot, 1] = src[pl.ds((side - RIM) * side, RIM * side), :].astype(BF)
    for e in range(RIM):
        rows = pl.ds(e * side, side)
        outs[0, slot, 2, rows] = src[pl.ds(e, side, stride=side), :].astype(BF)
        outs[0, slot, 3, rows] = src[pl.ds(side - RIM + e, side, stride=side), :].astype(BF)


def rims_of_input(inputs, mask_lanes):
    slots, side, _, channels = inputs.shape
    n_chunk = -(-channels // LANES)

    def kernel(x_ref, m_ref, o_ref, cells):
        for s in range(slots):
            for i in range(side):
                cells[pl.ds(i * side, side), :] = (
                    x_ref[s, i].astype(F32) * m_ref[s, pl.ds(i * side, side), :]
                )
            store_rims(cells, o_ref, s, side)

    return pl.pallas_call(
        kernel,
        grid=(n_chunk,),
        in_specs=[
            pl.BlockSpec((slots, side, side, LANES), lambda c: (0, 0, 0, c)),
            pl.BlockSpec((slots, side * side, LANES), lambda c: (0, 0, 0)),
        ],
        out_specs=pl.BlockSpec((1, slots, 4, RIM * side, LANES), lambda c: (c, 0, 0, 0, 0)),
        out_shape=jax.ShapeDtypeStruct((n_chunk, slots, 4, RIM * side, LANES), BF),
        scratch_shapes=[pltpu.VMEM((side * side, LANES), F32)],
        compiler_params=pltpu.CompilerParams(vmem_limit_bytes=32 << 20),
        name="rims_of_input",
    )(inputs, mask_lanes)


class HaloExchange:
    def __init__(self, grid, n_chunk, slots, side):
        self.grid, self.n_chunk, self.slots, self.side = grid, n_chunk, slots, side
        self.count = 2 * (grid.n_tile - 1)

    def scratch(self):
        n, s, band = self.grid.n_tile, self.slots, RIM * self.side
        return [
            pltpu.VMEM((n, s, 4, band, LANES), BF),
            pltpu.VMEM((n, s, 5, band, LANES), BF),
            pltpu.SemaphoreType.DMA((2,)),
        ]

    def halo_shape(self):
        return jax.ShapeDtypeStruct((self.n_chunk, self.slots, 5, RIM * self.side, LANES), BF)

    def plan(self, copies, rims, arrived, picked, halos, local):
        t, o = self.grid.at(self.grid.own())
        self.t, self.arrived, self.picked = t, arrived, picked
        own_chunk = jnp.minimum(t, self.n_chunk - 1)
        self.first, self.second = [], []
        for k in range(1, self.grid.n_tile):
            to = t ^ k
            source = jnp.minimum(to, self.n_chunk - 1)
            self.first.append((to, copies.make(rims.at[source], arrived.at[t], (to, o))))
            self.second.append((to, copies.make(picked.at[to], halos.at[own_chunk], (to, o))))
        self.own_copy = pltpu.make_async_copy(rims.at[own_chunk], arrived.at[t], local.at[0])
        self.back_copy = pltpu.make_async_copy(picked.at[t], halos.at[own_chunk], local.at[1])

    def send_rims(self):
        for to, copy in self.first:

            @pl.when(to < self.n_chunk)
            def _():
                copy.start()

        self.own_copy.start()

    def pick_and_send(self, neighbours):
        grid, slots, side = self.grid, self.slots, self.side
        t, arrived, picked = self.t, self.arrived, self.picked
        self.own_copy.wait()
        for _, copy in self.first:

            @pl.when(t < self.n_chunk)
            def _():
                copy.wait_recv()

        @pl.when(t < self.n_chunk)
        def _():
            @pl.loop(0, grid.n_tile * slots)
            def _(d):
                def rim(direction, which):
                    slot = neighbours(d, direction)
                    at = jnp.maximum(slot, 0)
                    value = arrived[at // slots, at % slots, which].astype(F32)
                    return jnp.where(slot >= 0, value, 0.0)

                to_tile, to_slot = d // slots, d % slots
                for to, (direction, which) in enumerate(((1, 1), (6, 0), (3, 3), (4, 2))):
                    picked[to_tile, to_slot, to] = rim(direction, which).astype(BF)
                rows = []
                for direction, which, first in ((0, 1, side - RIM), (2, 1, 0), (5, 0, side - RIM), (7, 0, 0)):
                    value = rim(direction, which)
                    rows += [value[e * side + first : e * side + first + RIM] for e in range(RIM)]
                    rows.append(jnp.zeros((16 - RIM * RIM, LANES), F32))
                rows.append(jnp.zeros((RIM * side - 64, LANES), F32))
                picked[to_tile, to_slot, 4] = jnp.concatenate(rows, 0).astype(BF)

        for _, copy in self.second:

            @pl.when(t < self.n_chunk)
            def _():
                copy.start()

        @pl.when(t < self.n_chunk)
        def _():
            self.back_copy.start()

    def finish(self):
        t = self.t

        @pl.when(t < self.n_chunk)
        def _():
            self.back_copy.wait()

        for to, copy in self.first:

            @pl.when(to < self.n_chunk)
            def _():
                copy.wait_send()

        for to, copy in self.second:

            @pl.when(to < self.n_chunk)
            def _():
                copy.wait_recv()

            @pl.when(t < self.n_chunk)
            def _():
                copy.wait_send()


class WeightGather:
    def __init__(self, grid, pairs, width):
        self.grid, self.pairs, self.width = grid, pairs, width
        self.count = pairs * (grid.n_tile * grid.n_opt - 1)

    def plan(self, copies, packed, gathered, local):
        grid, width = self.grid, self.width
        own = grid.own()

        def place(m, rel):
            t, o = grid.at({d: own[d] ^ rel.get(d, 0) for d in own})
            return gathered.at[m, o, pl.ds(pl.multiple_of(t * width, width), width)]

        def onward(m, rel, dims):
            source = packed.at[m] if not rel else place(m, rel)
            return [
                ({**rel, dim: k}, copies.make(source, place(m, rel), grid.beside(own, dim, k)))
                for dim in dims
                for k in range(1, grid.size[dim])
            ]

        orders = [("a", "x", "b", "c") if m % 2 == 0 else ("a", "b", "x", "c") for m in range(self.pairs)]
        due = {}

        def note(m, fresh, after):
            for rel, copy in fresh:
                level = sum(1 for d in rel if d != "c")
                wave = max(rel.get("a", 0) + level - ("a" in rel), after)
                due.setdefault(wave, []).append((m, rel, copy))
            return [copy for _, copy in fresh]

        self.keeps = [pltpu.make_async_copy(packed.at[m], place(m, {}), local.at[m]) for m in range(self.pairs)]
        self.first, self.later = [], []
        for m in range(self.pairs):
            fresh = onward(m, {}, orders[m])
            note(m, fresh, 0)
            for rel, copy in fresh:
                (self.later if rel.get("a", 0) > 1 else self.first).append(copy)
        self.waves = []
        for wave in range(4 * sum(grid.size.values())):
            events = []
            for m, rel, copy in sorted(due.pop(wave, []), key=lambda e: "c" in e[1]):
                last = max(orders[m].index(d) for d in rel)
                events.append((copy, note(m, onward(m, rel, orders[m][last + 1 :]), wave + 1)))
            self.waves.append(events)
            if not due:
                break

    def start(self):
        for copy in self.keeps + self.first:
            copy.start()

    def start_later(self):
        for copy in self.later:
            copy.start()

    def run(self, waves):
        for events in waves:
            for copy, fresh in events:
                copy.wait_recv()
                for other in fresh:
                    other.start()

    def finish(self):
        for copy in self.keeps:
            copy.wait()
        for copy in self.first + self.later + [c for events in self.waves for _, fresh in events for c in fresh]:
            copy.wait_send()


def exchange_forward(grid, rims, packed, neighbours, inputs, mask_lanes, taps, cotangent, flat_mask, weight_row, width):
    n_chunk, slots, _, band, _ = rims.shape
    side, channels = inputs.shape[1], inputs.shape[3]
    cells = side * side
    pairs, _, cols = packed.shape
    n_tile = grid.n_tile
    rows = slots * cells
    block = row_block(rows)
    early = rows // block
    halo = HaloExchange(grid, n_chunk, slots, side)
    gather = WeightGather(grid, pairs, packed.shape[1])
    total = halo.count + gather.count + n_tile - 1
    last = early + n_chunk * slots

    def kernel(
        r_ref, p_ref, n_ref, x_ref, m_ref, t_ref, g_ref, f_ref, l_ref,
        halo_ref, w_ref, nbr_ref, conv_ref, sum_ref, gap_ref, turned_ref, bias_ref,
        arrived, picked, local, landed, table, pad, send, recv, locals_w, locals_n,
    ):
        step = pl.program_id(0)
        t, o = grid.at(grid.own())
        copies = Copies(send, recv)
        halo.plan(copies, r_ref, arrived, picked, landed, local)
        gather.plan(copies, p_ref, w_ref, locals_w)
        tables = [copies.make(n_ref, nbr_ref.at[t], (t ^ k, o)) for k in range(1, n_tile)]
        keep = pltpu.make_async_copy(n_ref, nbr_ref.at[t], locals_n.at[0])
        load = pltpu.make_async_copy(nbr_ref, table, locals_n.at[1])
        halo_out = pltpu.make_async_copy(landed, halo_ref, locals_n.at[0])
        head = 2

        @pl.when(step == 0)
        def _():
            meet(grid.partners(("tile", "x", "c")))
            for copy in tables:
                copy.start()
            keep.start()
            halo.send_rims()
            gather.start()

        @pl.when((step > 0) & (step <= early))
        def _():
            value = f_ref[:, :1] * (l_ref[:, :1] * g_ref[...].astype(F32))
            arranged(value, gap_ref, turned_ref, bias_ref, step == 1, n_tile, width)

        @pl.when(step == early)
        def _():
            keep.wait()
            for copy in tables:
                copy.wait()
            load.start()
            load.wait()
            halo.pick_and_send(lambda d, k: table[d // slots, d % slots, k])
            gather.start_later()
            gather.run(gather.waves[:head])
            halo.finish()
            halo_out.start()

        for i, events in enumerate(gather.waves[head:]):

            @pl.when(step == min(last, early + 4 + 3 * i))
            def _():
                gather.run([events])

        @pl.when(step > early)
        def _():
            at = step - early - 1
            conv_step(
                x_ref, m_ref, t_ref, lambda k: landed[at // slots, at % slots, k].astype(F32), conv_ref, sum_ref, pad, side
            )

        @pl.when(step == last)
        def _():
            gather.finish()
            halo_out.wait()

    conv_at = lambda i: jnp.maximum(i - early - 1, 0)
    row_at = lambda i: jnp.clip(i - 1, 0, early - 1)
    any_space = pl.BlockSpec(memory_space=pl.ANY)
    return pl.pallas_call(
        kernel,
        grid=(last + 1,),
        in_specs=[any_space] * 3
        + [
            pl.BlockSpec((1, side, side, LANES), lambda i: (conv_at(i) % slots, 0, 0, conv_at(i) // slots)),
            pl.BlockSpec((1, cells, LANES), lambda i: (conv_at(i) % slots, 0, 0)),
            pl.BlockSpec((50, 8, LANES), lambda i: (0, 0, conv_at(i) // slots)),
            pl.BlockSpec((block, channels), lambda i: (row_at(i), 0)),
            pl.BlockSpec((block, LANES), lambda i: (row_at(i), 0)),
            pl.BlockSpec((1, LANES), lambda i: (0, 0)),
        ],
        out_specs=[any_space] * 3
        + [
            pl.BlockSpec((1, cells, LANES), lambda i: (conv_at(i) % slots, 0, conv_at(i) // slots)),
            pl.BlockSpec((1, 2, 8, LANES), lambda i: (conv_at(i) % slots, 0, 0, conv_at(i) // slots)),
            pl.BlockSpec((block, n_tile * width), lambda i: (row_at(i), 0)),
            pl.BlockSpec((channels, block), lambda i: (0, row_at(i))),
            pl.BlockSpec((1, channels), lambda i: (0, 0)),
        ],
        out_shape=[
            halo.halo_shape(),
            jax.ShapeDtypeStruct((pairs, grid.n_opt, n_tile * packed.shape[1], cols), BF),
            jax.ShapeDtypeStruct((n_tile,) + neighbours.shape, jnp.int32),
            jax.ShapeDtypeStruct((slots, cells, channels), F32),
            jax.ShapeDtypeStruct((slots, 2, 8, channels), F32),
            jax.ShapeDtypeStruct((rows, n_tile * width), BF),
            jax.ShapeDtypeStruct((channels, rows), BF),
            jax.ShapeDtypeStruct((1, channels), F32),
        ],
        scratch_shapes=halo.scratch()
        + [
            pltpu.VMEM(halo.halo_shape().shape, BF),
            pltpu.SMEM((n_tile,) + neighbours.shape, jnp.int32),
            pltpu.VMEM(((side + 2 * RIM) * PITCH, LANES), F32),
            pltpu.SemaphoreType.DMA((total,)),
            pltpu.SemaphoreType.DMA((total,)),
            pltpu.SemaphoreType.DMA((pairs,)),
            pltpu.SemaphoreType.DMA((2,)),
        ],
        compiler_params=remote_params(1, 63),
        name="exchange_forward",
    )(rims, packed, neighbours, inputs, mask_lanes, taps, cotangent, flat_mask, weight_row)


def exchange_backward(grid, rims, grads, neighbours, inputs, mask_lanes, d_conv, halos, small):
    n_chunk, slots, _, band, _ = rims.shape
    side, channels = inputs.shape[1], inputs.shape[3]
    side_b, side_x = grid.size["b"], grid.size["x"]
    _, blocks, rows, cols = grads.shape
    pairs = blocks // side_x
    part = rows // side_b
    side_a = grid.size["a"]
    piece = part // side_a
    halo = HaloExchange(grid, n_chunk, slots, side)
    steps = [(dim, 1 << i) for dim in ("c", "x", "b", "a") for i in range((grid.size[dim] - 1).bit_length())]
    total = halo.count + blocks + pairs * side_x * (side_x - 1 + side_b - 1)
    total += pairs * (2 * (side_a - 1) + side_a * (side_b - 1)) + len(steps)
    last = n_chunk * slots - 1
    small_rows = small.shape[0]
    small_shape = (up_to(50 + small_rows, 8), n_chunk * LANES)

    def kernel(
        r_ref, g_ref, n_ref, x_ref, m_ref, d_ref, h_ref, s_ref, halo_ref, o_ref, t_ref,
        arrived, picked, local, here, core, far, across, pad, sums, got, mine, heard, send, recv, load_sems,
    ):
        own = grid.own()
        own_x, own_b, own_c = own["x"], own["b"], own["c"]
        step = pl.program_id(0) * slots + pl.program_id(1)
        copies = Copies(send, recv)
        halo.plan(copies, r_ref, arrived, picked, halo_ref, local)
        order = [(k, m) for m in range(0, pairs, 2) for k in range(1, side_x)]
        order += [(k, m) for m in range(pairs) for k in range(side_x) if (k, m) not in order]
        index = lambda k, m: (own_x ^ k) * pairs + m
        rows_of = lambda b: pl.ds(pl.multiple_of(b * part, 16), part)
        cores, loads, to_x, to_b = [], [], {}, {}
        for i, (k, m) in enumerate(order):
            at = index(k, m)
            cores.append(copies.make(g_ref.at[1 - own_c, at], core.at[at], grid.beside(own, "c", 1)))
            loads.append(pltpu.make_async_copy(g_ref.at[own_c, at], here.at[at], load_sems.at[i]))
            if k > 0:
                to = grid.beside(own, "x", k)
                if m % 2 == 0:
                    to_x[k, m] = copies.make(here.at[at], far.at[k - 1, m], to)
                else:
                    to_x[k, m] = copies.make(here.at[at, rows_of(own_b)], far.at[k - 1, m, pl.ds(0, part)], to)
            if m % 2 == 1 or k == 0:
                to_b[k, m] = [
                    copies.make(here.at[at, rows_of(own_b ^ j)], across.at[j - 1, at], grid.beside(own, "b", j))
                    for j in range(1, side_b)
                ]

        own_a = own["a"]
        row_of = lambda a, b: pl.ds(pl.multiple_of((b * side_a + a) * piece, 16), piece)
        to_a, back_a, back_b, keeps = {}, {}, {}, []
        for m in range(pairs):
            at = index(0, m)
            done = here.at[at, row_of(own_a, own_b)]
            place = o_ref.at[m, row_of(own_a, own_b)]
            keeps.append(pltpu.make_async_copy(done, place, load_sems.at[m]))
            for k in range(1, side_a):
                to = grid.beside(own, "a", k)
                to_a[k, m] = copies.make(here.at[at, row_of(own_a ^ k, own_b)], got.at[m, k - 1], to)
                back_a[k, m] = copies.make(done, place, to)
            for k in range(side_a):
                for j in range(1, side_b):
                    came = o_ref.at[m, row_of(own_a ^ k, own_b)]
                    back_b[k, j, m] = copies.make(done if k == 0 else came, came, grid.beside(own, "b", j))
        small_copies = [
            copies.make(mine, heard.at[i], grid.beside(own, dim, k)) for i, (dim, k) in enumerate(steps)
        ]

        def start(found):
            for copy in found:
                copy.start()

        def wait(found):
            for copy in found:
                copy.wait()

        @pl.when(step == 0)
        def _():
            meet(grid.partners(("tile", "x", "c")))
            halo.send_rims()
            mine[...] = jnp.zeros_like(mine)
            start(cores)
            start(loads)

        add_taps(x_ref, m_ref, d_ref, h_ref, mine, pad, sums, slots, side)

        for i, (k, m) in enumerate(order):

            @pl.when(step == min(last, 3 + 2 * i))
            def _():
                loads[i].wait()
                cores[i].wait()
                at = index(k, m)
                add_rows(here.at[at], [core.at[at]], rows)
                if m % 2 == 1:
                    start(to_b[k, m])
                elif k > 0:
                    to_x[k, m].start()

        @pl.when(step == last)
        def _():
            halo.pick_and_send(lambda d, k: n_ref[d // slots, d % slots, k])
            for m in range(pairs):
                others = range(1, side_x)
                if m % 2 == 1:
                    for k in [*others, 0]:
                        at = index(k, m)
                        wait(to_b[k, m])
                        add_rows(here.at[at, rows_of(own_b)], [across.at[j, at] for j in range(side_b - 1)], part)
                        if k > 0:
                            to_x[k, m].start()
                else:
                    wait(to_x[k, m] for k in others)
                    add_rows(here.at[index(0, m)], [far.at[k - 1, m] for k in others], rows)
                    start(to_b[0, m])
            for m in range(pairs):
                at = index(0, m)
                if m % 2 == 1:
                    wait(to_x[k, m] for k in range(1, side_x))
                    sources = [far.at[k - 1, m, pl.ds(0, part)] for k in range(1, side_x)]
                else:
                    wait(to_b[0, m])
                    sources = [across.at[j, at] for j in range(side_b - 1)]
                add_rows(here.at[at, rows_of(own_b)], sources, part)
                start(to_a[k, m] for k in range(1, side_a))
            mine[pl.ds(50, small_rows), pl.ds(0, channels)] = s_ref[...]
            for i, copy in enumerate(small_copies):
                copy.start()
                copy.wait()
                mine[...] = mine[...] + heard[i]
            for m in range(pairs):
                wait(to_a[k, m] for k in range(1, side_a))
                done = here.at[index(0, m), row_of(own_a, own_b)]
                add_rows(done, [got.at[m, k] for k in range(side_a - 1)], piece)
                keeps[m].start()
                start(back_a[k, m] for k in range(1, side_a))
                start(back_b[0, j, m] for j in range(1, side_b))
            for k in range(1, side_a):
                for m in range(pairs):
                    back_a[k, m].wait_recv()
                    start(back_b[k, j, m] for j in range(1, side_b))
            halo.finish()
            t_ref[...] = mine[...]
            for m in range(pairs):
                keeps[m].wait()
                for k in range(1, side_a):
                    back_a[k, m].wait_send()
            wait(back_b.values())

    any_space = pl.BlockSpec(memory_space=pl.ANY)
    cells = side * side
    return pl.pallas_call(
        kernel,
        grid=(n_chunk, slots),
        in_specs=[
            any_space,
            any_space,
            pl.BlockSpec(memory_space=pltpu.SMEM),
            pl.BlockSpec((1, side, side, LANES), lambda c, s: (s, 0, 0, c)),
            pl.BlockSpec((1, cells, LANES), lambda c, s: (s, 0, 0)),
            pl.BlockSpec((1, cells, LANES), lambda c, s: (s, 0, c)),
            halo_block(halos),
            pl.BlockSpec(small.shape, lambda c, s: (0, 0)),
        ],
        out_specs=[any_space, any_space, pl.BlockSpec(small_shape, lambda c, s: (0, 0))],
        out_shape=[
            halo.halo_shape(),
            jax.ShapeDtypeStruct((pairs, rows, cols), BF),
            jax.ShapeDtypeStruct(small_shape, F32),
        ],
        scratch_shapes=halo.scratch()
        + [
            pltpu.VMEM((blocks, rows, cols), BF),
            pltpu.VMEM((blocks, rows, cols), BF),
            pltpu.VMEM((side_x - 1, pairs, rows, cols), BF),
            pltpu.VMEM((side_b - 1, blocks, part, cols), BF),
            pltpu.VMEM(((side + 2 * RIM) * PITCH, LANES), F32),
            pltpu.VMEM((50, 8, LANES), F32),
            pltpu.VMEM((pairs, side_a - 1, piece, cols), BF),
            pltpu.VMEM(small_shape, F32),
            pltpu.VMEM((len(steps),) + small_shape, F32),
            pltpu.SemaphoreType.DMA((total,)),
            pltpu.SemaphoreType.DMA((total,)),
            pltpu.SemaphoreType.DMA((blocks,)),
        ],
        compiler_params=remote_params(2, 60),
        name="exchange_backward",
    )(rims, grads, neighbours, inputs, mask_lanes, d_conv, halos, small)


def tile_total(grid, value, number):
    n_tile = grid.n_tile

    def kernel(v_ref, o_ref, got, send, recv):
        t, o = grid.at(grid.own())
        meet(grid.partners(("tile",)))
        copies = Copies(send, recv)
        got[t] = v_ref[...]
        sent = [copies.start(v_ref, got.at[t], (t ^ k, o)) for k in range(1, n_tile)]
        for copy in sent:
            copy.wait()
        total = got[0]
        for i in range(1, n_tile):
            total = total + got[i]
        o_ref[...] = total

    whole = pl.BlockSpec(memory_space=pltpu.VMEM)
    return pl.pallas_call(
        kernel,
        in_specs=[whole],
        out_specs=whole,
        out_shape=jax.ShapeDtypeStruct(value.shape, F32),
        scratch_shapes=[
            pltpu.VMEM((n_tile,) + value.shape, F32),
            pltpu.SemaphoreType.DMA((n_tile - 1,)),
            pltpu.SemaphoreType.DMA((n_tile - 1,)),
        ],
        compiler_params=remote_params(number, 16),
        name="tile_total",
    )(value)


def fill_halo(pad, halo, side):
    last = side + RIM
    up, down, left, right, corner = (halo(k) for k in range(5))
    for e in range(RIM):
        rows = slice(e * side, e * side + side)
        pad[pl.ds(e * PITCH + 8, side), :] = up[rows]
        pad[pl.ds((last + e) * PITCH + 8, side), :] = down[rows]
        pad[pl.ds(RIM * PITCH + 8 - RIM + e, side, stride=PITCH), :] = left[rows]
        pad[pl.ds(RIM * PITCH + 8 + side + e, side, stride=PITCH), :] = right[rows]
    places = ((0, 8 - RIM), (0, 8 + side), (last, 8 - RIM), (last, 8 + side))
    for k, (row, col) in enumerate(places):
        for e in range(RIM):
            at = 16 * k + RIM * e
            pad[pl.ds((row + e) * PITCH + col, RIM), :] = corner[at : at + RIM]


def conv_pass(pad, side, weight, emit):
    for block in range(side // 8):
        sums = [None] * side
        for b in range(7):
            taps = [weight(a, b) for a in range(7)]
            for r in range(side + 2 * RIM):
                cells = pad[pl.ds(r * PITCH + 8 - RIM + b + 8 * block, 8), :]
                for a in range(7):
                    i = r - a
                    if 0 <= i < side:
                        term = taps[a] * cells
                        sums[i] = term if sums[i] is None else sums[i] + term
        emit(block, sums)


def halo_block(halos):
    return pl.BlockSpec((1, 1) + halos.shape[2:], lambda c, s: (c, s, 0, 0, 0))


def conv_step(x_ref, m_ref, w_ref, halo, o_ref, s_ref, pad, side):
    for i in range(side):
        pad[pl.ds((i + RIM) * PITCH + 8, side), :] = x_ref[0, i].astype(F32) * m_ref[0, pl.ds(i * side, side), :]
    fill_halo(pad, halo, side)
    bias = w_ref[49]
    totals = [jnp.zeros((8, LANES), F32), jnp.zeros((8, LANES), F32)]

    def emit(block, sums):
        for i in range(side):
            value = sums[i] + bias
            rows = pl.ds(i * side + 8 * block, 8)
            o_ref[0, rows, :] = value
            weighted = m_ref[0, rows, :] * value
            totals[0] = totals[0] + weighted
            totals[1] = totals[1] + weighted * value

    conv_pass(pad, side, lambda a, b: w_ref[7 * a + b], emit)
    s_ref[0, 0], s_ref[0, 1] = totals


def conv_gradient(d_shaped, conv_out, mask_lanes, coefs, side):
    slots, cells, channels = d_shaped.shape
    n_chunk = -(-channels // LANES)

    def kernel(d_ref, v_ref, m_ref, c_ref, o_ref, r_ref, held):
        one, two, three = c_ref[0, :1], c_ref[1, :1], c_ref[2, :1]
        for s in range(slots):
            value = d_ref[s] * one - m_ref[s] * (two + three * v_ref[s])
            o_ref[s] = value
            held[...] = value
            store_rims(held, r_ref, s, side)

    piece = (slots, 4, RIM * side, LANES)
    block = pl.BlockSpec((slots, cells, LANES), lambda c: (0, 0, c))
    return pl.pallas_call(
        kernel,
        grid=(n_chunk,),
        in_specs=[
            block,
            block,
            pl.BlockSpec((slots, cells, LANES), lambda c: (0, 0, 0)),
            pl.BlockSpec((3, 8, LANES), lambda c: (0, 0, c)),
        ],
        out_specs=[block, pl.BlockSpec((1,) + piece, lambda c: (c, 0, 0, 0, 0))],
        scratch_shapes=[pltpu.VMEM((cells, LANES), F32)],
        out_shape=[
            jax.ShapeDtypeStruct((slots, cells, channels), F32),
            jax.ShapeDtypeStruct((n_chunk,) + piece, BF),
        ],
        compiler_params=pltpu.CompilerParams(vmem_limit_bytes=32 << 20),
        name="conv_gradient",
    )(d_shaped, conv_out, mask_lanes, coefs)


def add_taps(x_ref, m_ref, d_ref, h_ref, o_ref, pad, sums, slots, side):
    slot = pl.program_id(1)
    for i in range(side):
        pad[pl.ds((i + RIM) * PITCH + 8, side), :] = x_ref[0, i].astype(F32) * m_ref[0, pl.ds(i * side, side), :]
    fill_halo(pad, lambda k: h_ref[0, 0, k].astype(F32), side)

    @pl.when(slot == 0)
    def _():
        sums[...] = jnp.zeros_like(sums)

    for block in range(side // 8):
        grads = [d_ref[0, pl.ds(i * side + 8 * block, 8), :] for i in range(side)]
        total = grads[0]
        for i in range(1, side):
            total = total + grads[i]
        sums[49] += total
        for b in range(7):
            taps = [None] * 7
            for r in range(side + 2 * RIM):
                window = pad[pl.ds(r * PITCH + 8 - RIM + b + 8 * block, 8), :]
                for a in range(7):
                    i = r - a
                    if 0 <= i < side:
                        term = window * grads[i]
                        taps[a] = term if taps[a] is None else taps[a] + term
            for a in range(7):
                sums[7 * a + b] += taps[a]

    @pl.when(slot == slots - 1)
    def _():
        at = pl.multiple_of(pl.program_id(0) * LANES, LANES)
        o_ref[pl.ds(0, 50), pl.ds(at, LANES)] = jnp.sum(sums[...], axis=1)


def conv_backward(grid, d_conv, halos, cotangent, mask_lanes, taps, weight_lanes, change):
    slots, side, _, channels = cotangent.shape
    n_chunk = halos.shape[0]
    cells = side * side
    pairs, rows, cols = change.shape
    side_a, side_b = grid.size["a"], grid.size["b"]
    part = rows // side_b
    piece = part // side_a
    total = pairs * ((side_b - 1) + (side_a - 1))
    last = n_chunk * slots - 1

    def kernel(
        d_ref, g_ref, m_ref, w_ref, l_ref, h_ref, c_ref, o_ref, change_ref,
        pad, mine, from_b, from_a, send, recv, load_sems,
    ):
        own = grid.own()
        step = pl.program_id(0) * slots + pl.program_id(1)
        copies = Copies(send, recv)
        half = lambda b: pl.ds(pl.multiple_of(b * part, 16), part)
        rows_of = lambda a: pl.ds(pl.multiple_of(a * piece, 16), piece)
        firsts, seconds, loads = [], [], []
        for m in range(pairs):
            firsts.append(
                [
                    copies.make(c_ref.at[m, half(own["b"] ^ k)], from_b.at[k - 1, m], grid.beside(own, "b", k))
                    for k in range(1, side_b)
                ]
            )
            seconds.append(
                [
                    copies.make(mine.at[m, rows_of(own["a"] ^ k)], from_a.at[k - 1, m], grid.beside(own, "a", k))
                    for k in range(1, side_a)
                ]
            )
            loads.append(pltpu.make_async_copy(c_ref.at[m, half(own["b"])], mine.at[m], load_sems.at[m]))

        @pl.when(step == 0)
        def _():
            meet(grid.partners(("a", "b")))
            for m in range(pairs):
                for copy in firsts[m]:
                    copy.start()
                loads[m].start()

        for i in range(side):
            pad[pl.ds((i + RIM) * PITCH + 8, side), :] = d_ref[0, pl.ds(i * side, side), :]
        fill_halo(pad, lambda k: h_ref[0, 0, k].astype(F32), side)
        weight = l_ref[...]

        def emit(block, sums):
            for i in range(side):
                at = pl.ds(i * side + 8 * block, 8)
                scaled = weight * g_ref[0, i, pl.ds(8 * block, 8), :].astype(F32)
                o_ref[0, at, :] = m_ref[0, at, :] * (scaled + sums[i])

        conv_pass(pad, side, lambda a, b: w_ref[7 * (6 - a) + 6 - b], emit)

        for m in range(pairs):

            @pl.when(step == min(last, 9 + 4 * m))
            def _():
                loads[m].wait()
                for copy in firsts[m]:
                    copy.wait()
                add_rows(mine.at[m], [from_b.at[k, m] for k in range(side_b - 1)], part)
                for copy in seconds[m]:
                    copy.start()

        @pl.when(step == last)
        def _():
            for m in range(pairs):
                for copy in seconds[m]:
                    copy.wait()
                value = mine[m, rows_of(own["a"])].astype(F32)
                for k in range(side_a - 1):
                    value = value + from_a[k, m].astype(F32)
                change_ref[m] = value

    return pl.pallas_call(
        kernel,
        grid=(n_chunk, slots),
        in_specs=[
            pl.BlockSpec((1, cells, LANES), lambda c, s: (s, 0, c)),
            pl.BlockSpec((1, side, side, LANES), lambda c, s: (s, 0, 0, c)),
            pl.BlockSpec((1, cells, LANES), lambda c, s: (s, 0, 0)),
            pl.BlockSpec((50, 8, LANES), lambda c, s: (0, 0, c)),
            pl.BlockSpec((8, LANES), lambda c, s: (0, 0)),
            halo_block(halos),
            pl.BlockSpec(memory_space=pl.ANY),
        ],
        out_specs=[
            pl.BlockSpec((1, cells, LANES), lambda c, s: (s, 0, c)),
            pl.BlockSpec((pairs, piece, cols), lambda c, s: (0, 0, 0)),
        ],
        scratch_shapes=[
            pltpu.VMEM(((side + 2 * RIM) * PITCH, LANES), F32),
            pltpu.VMEM((pairs, part, cols), BF),
            pltpu.VMEM((side_b - 1, pairs, part, cols), BF),
            pltpu.VMEM((side_a - 1, pairs, piece, cols), BF),
            pltpu.SemaphoreType.DMA((total,)),
            pltpu.SemaphoreType.DMA((total,)),
            pltpu.SemaphoreType.DMA((pairs,)),
        ],
        out_shape=[
            jax.ShapeDtypeStruct((slots, cells, channels), F32),
            jax.ShapeDtypeStruct((pairs, piece, cols), F32),
        ],
        compiler_params=remote_params(4, 48),
        name="conv_backward",
    )(d_conv, cotangent, mask_lanes, taps, weight_lanes, halos, change)


def spread_lanes(value, parts, width):
    rows, channels = value.shape
    run = channels // parts
    if run == width:
        return value
    gap = jnp.zeros((rows, width - run), value.dtype)
    pieces = []
    for t in range(parts):
        pieces += [value[:, t * run : (t + 1) * run], gap]
    return jnp.concatenate(pieces, 1)


def close_lanes(value, parts, run):
    width = value.shape[1] // parts
    if run == width:
        return value
    return jnp.concatenate([value[:, t * width : t * width + run] for t in range(parts)], 1)


def row_block(rows):
    return 3 * LANES if rows % (3 * LANES) == 0 else LANES


def arranged(value, gap_ref, turned_ref, sum_ref, first, parts, width):
    low = value.astype(BF).astype(F32)
    gap_ref[...] = spread_lanes(low, parts, width).astype(BF)
    turned_ref[...] = low.T.astype(BF)

    @pl.when(first)
    def _():
        sum_ref[...] = jnp.zeros_like(sum_ref)

    sum_ref[...] += jnp.sum(low, axis=0, keepdims=True)


def arrange(body, args, specs, rows, channels, parts, width, name):
    step = 3 * LANES if rows % (3 * LANES) == 0 else LANES

    def kernel(*refs):
        given, (gap_ref, turned_ref, sum_ref) = refs[: len(args)], refs[len(args) :]
        arranged(body(*given), gap_ref, turned_ref, sum_ref, pl.program_id(0) == 0, parts, width)

    return pl.pallas_call(
        kernel,
        grid=(rows // step,),
        in_specs=specs(step),
        out_specs=[
            pl.BlockSpec((step, parts * width), lambda i: (i, 0)),
            pl.BlockSpec((channels, step), lambda i: (0, i)),
            pl.BlockSpec((1, channels), lambda i: (0, 0)),
        ],
        out_shape=[
            jax.ShapeDtypeStruct((rows, parts * width), BF),
            jax.ShapeDtypeStruct((channels, rows), BF),
            jax.ShapeDtypeStruct((1, channels), F32),
        ],
        compiler_params=pltpu.CompilerParams(vmem_limit_bytes=48 << 20),
        name=name,
    )(*args)


def feed_forward(inverse, shaped, shaped_t, d_branch, d_branch_t, hidden_bias, weights, grad_rows):
    rows, depth = shaped.shape
    channels = shaped_t.shape[0]
    half, _, cols = hidden_bias.shape
    pairs, owners = weights.shape[:2]
    per_owner = 2 * pairs
    tile_rows = 3 * LANES if rows % (3 * LANES) == 0 else LANES

    def kernel(inv_ref, s_ref, st_ref, d_ref, dt_ref, hb_ref, w_ref, branch_ref, ds_ref, grad_ref, bias_ref, *scratch):
        packed, first, second, act, dpre, grads, sems, out_sem = scratch
        step = pl.program_id(0)

        def where(slot):
            owner, inside = slot // per_owner, slot % per_owner
            return owner, inside // 2, inside % 2

        def fetch(h, buffer):
            copies = []
            for which in range(2):
                owner, pair, _ = where(inv_ref[h + which * half])
                copies.append(
                    pltpu.make_async_copy(w_ref.at[pair, owner], packed.at[buffer, which], sems.at[buffer, which])
                )
            return copies

        @pl.when(step == 0)
        def _():
            for copy in fetch(0, 0):
                copy.start()
            if grad_rows > channels:
                rest = grad_rows - channels
                grads[:, :, pl.ds(channels, rest), :] = jnp.zeros(grads.shape[:2] + (rest, 2 * cols), BF)

        @pl.when(step + 1 < half)
        def _():
            for copy in fetch(step + 1, (step + 1) % 2):
                copy.start()

        now = step % 2
        slots = [where(inv_ref[step + which * half]) for which in range(2)]
        waits = fetch(step, now)
        for which, held in enumerate((first, second)):
            waits[which].wait()
            for parity in range(2):

                @pl.when(slots[which][2] == parity)
                def _():
                    held[...] = packed[now, which, :, parity * cols : (parity + 1) * cols]

        hidden = hb_ref[0]

        @pl.when(step == 0)
        def _():
            branch_ref[...] = jnp.zeros_like(branch_ref)
            ds_ref[...] = jnp.zeros_like(ds_ref)

        total = jnp.zeros((1, cols), F32)
        across = (((1,), (1,)), ((), ()))
        for i in range(rows // tile_rows):
            at = pl.ds(i * tile_rows, tile_rows)
            pre = jnp.dot(s_ref[at, :], first[...], preferred_element_type=F32) + hidden
            d_act = jnp.dot(d_ref[at, :], second[...], preferred_element_type=F32)
            square = pre * pre
            bend = jnp.tanh(ROOT * pre * (1.0 + CUBE * square))
            half_up = 0.5 * (1.0 + bend)
            low = (pre * half_up).astype(BF)
            slope = half_up + (0.5 * ROOT) * pre * (1.0 - bend * bend) * (1.0 + (3.0 * CUBE) * square)
            back = (d_act * slope).astype(BF)
            act[at, :] = low
            dpre[at, :] = back
            total = total + jnp.sum(back.astype(F32), axis=0, keepdims=True)
            out_add = lax.dot_general(low, second[...], across, preferred_element_type=F32)
            in_add = lax.dot_general(back, first[...], across, preferred_element_type=F32)

            branch_ref[at, :] += out_add
            ds_ref[at, :] += in_add

        bias_ref[0] = total
        for which, (left, right) in enumerate(((st_ref, dpre), (dt_ref, act))):
            owner, pair, half_of_pair = slots[which]
            value = jnp.dot(left[...], right[...], preferred_element_type=F32).astype(BF)
            for parity in range(2):

                @pl.when(half_of_pair == parity)
                def _():
                    at = (owner // 2) * pairs + pair
                    grads[owner % 2, at, pl.ds(0, channels), parity * cols : (parity + 1) * cols] = value

        @pl.when(step == half - 1)
        def _():
            out = pltpu.make_async_copy(grads, grad_ref, out_sem.at[0])
            out.start()
            out.wait()

    whole = lambda *shape: pl.BlockSpec(shape, lambda h, *_: (0,) * len(shape))
    line = pl.BlockSpec((1, 1, cols), lambda h, *_: (h, 0, 0))
    grad_shape = (2, owners // 2 * pairs, grad_rows, 2 * cols)
    return pl.pallas_call(
        kernel,
        grid_spec=pltpu.PrefetchScalarGridSpec(
            num_scalar_prefetch=1,
            grid=(half,),
            in_specs=[
                whole(rows, depth),
                whole(channels, rows),
                whole(rows, depth),
                whole(channels, rows),
                line,
                pl.BlockSpec(memory_space=pl.ANY),
            ],
            out_specs=[whole(rows, depth), whole(rows, depth), pl.BlockSpec(memory_space=pl.ANY), line],
            scratch_shapes=[
                pltpu.VMEM((2, 2, depth, 2 * cols), BF),
                pltpu.VMEM((depth, cols), BF),
                pltpu.VMEM((depth, cols), BF),
                pltpu.VMEM((rows, cols), BF),
                pltpu.VMEM((rows, cols), BF),
                pltpu.VMEM(grad_shape, BF),
                pltpu.SemaphoreType.DMA((2, 2)),
                pltpu.SemaphoreType.DMA((1,)),
            ],
        ),
        out_shape=[
            jax.ShapeDtypeStruct((rows, depth), F32),
            jax.ShapeDtypeStruct((rows, depth), F32),
            jax.ShapeDtypeStruct(grad_shape, BF),
            jax.ShapeDtypeStruct((half, 1, cols), F32),
        ],
        cost_estimate=pl.CostEstimate(
            flops=12 * rows * channels * half * cols, bytes_accessed=40 << 20, transcendentals=rows * half * cols
        ),
        compiler_params=pltpu.CompilerParams(vmem_limit_bytes=63 << 20),
        name="feed_forward",
    )(inverse, shaped, shaped_t, d_branch, d_branch_t, hidden_bias, weights)


def close_out(branch, d_shaped, inputs, conv_out, mask_lanes, out_bias, parts, run):
    rows, channels = inputs.shape
    depth = branch.shape[1]
    step = 3 * LANES if rows % (3 * LANES) == 0 else LANES

    def kernel(b_ref, d_ref, x_ref, v_ref, m_ref, o_ref, out_ref, ds_ref, sum_ref):
        branch_here = close_lanes(b_ref[...], parts, run) + o_ref[...]
        out_ref[...] = (m_ref[:, :1] * (x_ref[...].astype(F32) + branch_here)).astype(BF)
        grads = close_lanes(d_ref[...], parts, run)
        ds_ref[...] = grads

        @pl.when(pl.program_id(0) == 0)
        def _():
            sum_ref[...] = jnp.zeros_like(sum_ref)

        sum_ref[0] += jnp.sum(grads, axis=0, keepdims=True)
        sum_ref[1] += jnp.sum(grads * v_ref[...], axis=0, keepdims=True)

    line = lambda n: pl.BlockSpec((step, n), lambda i: (i, 0))
    return pl.pallas_call(
        kernel,
        grid=(rows // step,),
        in_specs=[
            line(depth),
            line(depth),
            line(channels),
            line(channels),
            line(LANES),
            pl.BlockSpec((1, channels), lambda i: (0, 0)),
        ],
        out_specs=[line(channels), line(channels), pl.BlockSpec((2, 1, channels), lambda i: (0, 0, 0))],
        out_shape=[
            jax.ShapeDtypeStruct((rows, channels), BF),
            jax.ShapeDtypeStruct((rows, channels), F32),
            jax.ShapeDtypeStruct((2, 1, channels), F32),
        ],
        compiler_params=pltpu.CompilerParams(vmem_limit_bytes=60 << 20),
        name="close_out",
    )(branch, d_shaped, inputs, conv_out, mask_lanes, out_bias)


def halves(value):
    high = value.astype(BF)
    return high, (value - high.astype(F32)).astype(BF)


def product(left, right, contract):
    dims = (contract, ((), ()))
    total = None
    for i, a in enumerate(left):
        for j, b in enumerate(right):
            if i + j < 2:
                term = lax.dot_general(a, b, dims, preferred_element_type=F32)
                total = term if total is None else total + term
    return total


def rotate(owned, left_basis, column_basis, moment_one, moment_two, correction, grid, width):
    slots, channels, run = left_basis.shape
    cols = column_basis.shape[1]
    pairs = slots // 2
    side_a, side_b = grid.size["a"], grid.size["b"]
    n_tile = grid.n_tile

    def kernel(f_ref, g_ref, l_ref, c_ref, one_ref, two_ref, first_ref, second_ref, o_ref):
        factor = f_ref[0]
        changes = []
        for p in range(2):
            grad = g_ref[0, pl.ds(0, channels), p * cols : (p + 1) * cols]
            left = halves(l_ref[p])
            column = halves(c_ref[p])
            rotated = product(left, (grad,), ((0,), (0,)))
            rotated = product(halves(rotated), column, ((1,), (0,)))
            first = decay_rate * one_ref[p] + (1.0 - decay_rate) * rotated
            second = decay_rate * two_ref[p] + (1.0 - decay_rate) * rotated * rotated
            first_ref[p] = first
            second_ref[p] = second
            direction = first * factor / (jnp.sqrt(second * factor) + adam_eps)
            turned = product(halves(direction), column, ((1,), (1,)))
            changes.append(product(left, halves(turned), ((1,), (0,))))
        change = jnp.concatenate(changes, 1)
        gap = jnp.zeros((width - run, 2 * cols), F32)
        for t in range(n_tile):
            piece = jnp.concatenate([change[t * run : (t + 1) * run], gap], 0)
            place = (t % side_b) * side_a + t // side_b
            o_ref[0, pl.ds(place * width, width), :] = piece.astype(BF)

    pair = lambda *shape: pl.BlockSpec(shape, lambda m: (m,) + (0,) * (len(shape) - 1))
    return pl.pallas_call(
        kernel,
        grid=(pairs,),
        in_specs=[
            pl.BlockSpec(memory_space=pltpu.SMEM),
            pair(1, owned.shape[1], 2 * cols),
            pair(2, channels, run),
            pair(2, cols, cols),
            pair(2, run, cols),
            pair(2, run, cols),
        ],
        out_specs=[pair(2, run, cols), pair(2, run, cols), pair(1, n_tile * width, 2 * cols)],
        out_shape=[
            jax.ShapeDtypeStruct(moment_one.shape, F32),
            jax.ShapeDtypeStruct(moment_one.shape, F32),
            jax.ShapeDtypeStruct((pairs, n_tile * width, 2 * cols), BF),
        ],
        compiler_params=pltpu.CompilerParams(vmem_limit_bytes=60 << 20),
        name="rotate",
    )(1.0 / correction.reshape(1), owned, left_basis, column_basis, moment_one, moment_two)


def up_to(value, unit):
    return -(-value // unit) * unit


def pack_pairs(value):
    slots, rows, cols = value.shape
    return value.reshape(slots // 2, 2, rows, cols).transpose(0, 2, 1, 3).reshape(slots // 2, rows, 2 * cols)


def unpack_pairs(value):
    pairs, rows, cols = value.shape
    return value.reshape(pairs, rows, 2, cols // 2).transpose(0, 2, 1, 3).reshape(2 * pairs, rows, cols // 2)


def per_device(
    grid,
    inputs,
    cotangent,
    master,
    moment_one,
    moment_two,
    left_basis,
    column_basis,
    small_params,
    small_first,
    small_second,
    land_mask,
    tile_count,
    neighbours,
    block_order,
    cell_weight,
    step_count,
):
    position = lax.axis_index("tile")
    sample = lax.axis_index("opt")
    inputs, cotangent = inputs[0], cotangent[0]
    slots, side, _, channels = inputs.shape
    cells = side * side
    rows = slots * cells
    n_tile = grid.n_tile
    n_chunk = -(-channels // LANES)
    per_group = channels // GROUPS
    per_owner, run, cols = master.shape
    pairs = per_owner // 2
    block_total = block_order.shape[0]
    half = block_total // 2
    width = up_to(run, 16)

    live = (jnp.arange(slots) < tile_count[position]).astype(F32)
    mask = (land_mask.astype(F32) * live[:, None, None]).reshape(slots, cells)
    mask_lanes = jnp.broadcast_to(mask[:, :, None], (slots, cells, LANES))
    flat_mask = mask_lanes.reshape(rows, LANES)
    taps = jnp.broadcast_to(small_params[:50, None, :], (50, 8, channels))

    weights_float = cell_weight.astype(F32)
    sample_weight = weights_float[sample] * weights_float.shape[0] / jnp.sum(weights_float)
    weight_lanes = jnp.broadcast_to(sample_weight, (8, LANES))
    weight_row = jnp.broadcast_to(sample_weight, (1, LANES))

    low_master = jnp.pad(pack_pairs(master.astype(BF)), ((0, 0), (0, width - run), (0, 0)))
    rims = rims_of_input(inputs, mask_lanes)
    halos, weights, all_neighbours, conv_out, sums, d_branch, d_branch_t, d_out_bias = exchange_forward(
        grid,
        rims,
        low_master,
        neighbours,
        inputs,
        mask_lanes,
        taps,
        cotangent.reshape(rows, channels),
        flat_mask,
        weight_row,
        width,
    )

    sums = jnp.sum(sums, axis=(0, 2))
    occupied = jnp.broadcast_to(jnp.sum(mask), (1, channels))
    sums = tile_total(grid, jnp.concatenate([sums, occupied], 0), 5)
    counted = sums[2, 0] * per_group
    by_group = sums[:2].reshape(2, GROUPS, per_group).sum(2)
    group_mean = by_group[0] / counted
    variance = by_group[1] / counted - group_mean * group_mean
    inv_std = jnp.repeat(lax.rsqrt(variance + epsilon), per_group)
    mean = jnp.repeat(group_mean, per_group)
    gain, shift = small_params[50], small_params[51]
    norm_coefs = jnp.stack([inv_std, mean * inv_std, gain, shift])

    def shaped_body(v_ref, c_ref):
        normed = v_ref[...] * c_ref[0:1] - c_ref[1:2]
        return normed * c_ref[2:3] + c_ref[3:4]

    flat_conv = conv_out.reshape(rows, channels)
    shaped, shaped_t, _ = arrange(
        shaped_body,
        (flat_conv, norm_coefs),
        lambda step: [
            pl.BlockSpec((step, channels), lambda i: (i, 0)),
            pl.BlockSpec((4, channels), lambda i: (0, 0)),
        ],
        rows,
        channels,
        n_tile,
        width,
        "arrange_shaped",
    )

    block_ids = jnp.arange(block_total, dtype=jnp.int32)
    inverse = jnp.sum(
        jnp.where(block_order[None, :] == block_ids[:, None], block_ids[None, :], 0), axis=1
    ).astype(jnp.int32)
    hidden_bias = small_params[53:57].reshape(half, 1, cols)
    branch, d_shaped, grads, d_hidden = feed_forward(
        inverse, shaped, shaped_t, d_branch, d_branch_t, hidden_bias, weights, n_tile * width
    )
    block_output, d_shaped, d_sums = close_out(
        branch, d_shaped, inputs.reshape(rows, channels), flat_conv, flat_mask, small_params[52:53], n_tile, run
    )

    d_shift = d_sums[0, 0]
    d_gain = inv_std * (d_sums[1, 0] - mean * d_shift)
    parts = tile_total(grid, jnp.stack([gain * d_shift, gain * d_gain]), 6)
    parts = jnp.repeat(parts.reshape(2, GROUPS, per_group).sum(2) / counted, per_group, axis=1)
    grad_coefs = jnp.stack(
        [
            inv_std * gain,
            inv_std * (parts[0] - mean * inv_std * parts[1]),
            inv_std * inv_std * parts[1],
        ]
    )
    d_conv, grad_rims = conv_gradient(
        d_shaped.reshape(slots, cells, channels),
        conv_out,
        mask_lanes,
        jnp.broadcast_to(grad_coefs[:, None, :], (3, 8, channels)),
        side,
    )
    small = jnp.concatenate([d_gain[None], d_shift[None], d_out_bias, d_hidden.reshape(4, channels)], 0)
    grad_halos, owned, d_small = exchange_backward(
        grid, grad_rims, grads, all_neighbours, inputs, mask_lanes, d_conv, halos, small
    )

    correction = 1.0 - jnp.power(F32(decay_rate), step_count[0].astype(F32))
    d_small = d_small[: small_params.shape[0], :channels]
    small_one = decay_rate * small_first + (1.0 - decay_rate) * d_small
    small_two = decay_rate * small_second + (1.0 - decay_rate) * d_small * d_small
    new_small = small_params - small_rate * (small_one / correction) / (
        jnp.sqrt(small_two / correction) + adam_eps
    )

    first_new, second_new, change = rotate(
        owned, left_basis, column_basis, moment_one, moment_two, correction, grid, width
    )
    input_grad, change = conv_backward(
        grid, d_conv, grad_halos, cotangent, mask_lanes, taps, weight_lanes, change
    )
    change = unpack_pairs(change[:, :run])
    new_master = master - 0.5 / math.sqrt(channels) * change
    return (
        block_output.reshape((1,) + inputs.shape),
        input_grad.reshape((1,) + inputs.shape),
        new_master,
        new_master.astype(BF),
        first_new,
        second_new,
        new_small,
        small_one,
        small_two,
    )


def solution(mesh):
    grid = Grid(mesh.shape["tile"], mesh.shape["opt"])

    def step(*args):
        return per_device(grid, *args)

    return jax.shard_map(
        step,
        mesh=mesh,
        in_specs=(
            P("opt", "tile", None, None, None),
            P("opt", "tile", None, None, None),
            P("opt", "tile", None),
            P("opt", "tile", None),
            P("opt", "tile", None),
            P("opt", None, "tile"),
            P("opt", None, None),
            P(),
            P(),
            P(),
            P("tile", None, None),
            P(),
            P("tile", None),
            P(),
            P(),
            P(),
        ),
        out_specs=(
            P("opt", "tile", None, None, None),
            P("opt", "tile", None, None, None),
            P("opt", "tile", None),
            P("opt", "tile", None),
            P("opt", "tile", None),
            P("opt", "tile", None),
            P(),
            P(),
            P(),
        ),
        check_vma=False,
    )
```

```python
import math

import jax
import jax.numpy as jnp
from jax import lax
from jax.experimental import pallas as pl
from jax.experimental.pallas import tpu as pltpu
from jax.sharding import PartitionSpec as P

GROUPS = 16
LANES = 128
RIM = 3
PITCH = 40
BF = jnp.bfloat16
F32 = jnp.float32

highest = lax.Precision.HIGHEST
epsilon = 1e-05
adam_eps = 1e-08
decay_rate = 0.5
small_rate = 0.05
ROOT = 0.7978845608028654
CUBE = 0.044715


class Grid:
    def __init__(self, n_tile, n_opt):
        b = 4 if n_tile % 16 == 0 else 2
        self.n_tile, self.n_opt = n_tile, n_opt
        self.size = {"a": n_tile // b, "b": b, "x": n_opt // 2, "c": 2}

    def own(self):
        t, o = lax.axis_index("tile"), lax.axis_index("opt")
        b = self.size["b"]
        return {"a": t // b, "b": t % b, "x": o // 2, "c": o % 2}

    def at(self, place):
        return place["a"] * self.size["b"] + place["b"], place["x"] * 2 + place["c"]

    def partners(self, dims):
        own = self.own()
        found = []
        for dim in dims:
            if dim == "tile":
                t, o = self.at(own)
                found += [(t ^ k, o) for k in range(1, self.n_tile)]
            else:
                found += [self.beside(own, dim, k) for k in range(1, self.size[dim])]
        return found

    def beside(self, own, dim, k):
        return self.at({**own, dim: own[dim] ^ k})


def meet(devices):
    barrier = pltpu.get_barrier_semaphore()
    for device in devices:
        pl.semaphore_signal(barrier, inc=1, device_id=device, device_id_type=pl.DeviceIdType.MESH)
    pl.semaphore_wait(barrier, len(devices))


class Copies:
    def __init__(self, send_sems, recv_sems):
        self.sems = send_sems, recv_sems
        self.used = 0

    def make(self, src, dst, device):
        i = self.used
        self.used += 1
        return pltpu.make_async_remote_copy(
            src_ref=src,
            dst_ref=dst,
            send_sem=self.sems[0].at[i],
            recv_sem=self.sems[1].at[i],
            device_id=device,
            device_id_type=pl.DeviceIdType.MESH,
        )

    def start(self, src, dst, device):
        copy = self.make(src, dst, device)
        copy.start()
        return copy


def remote_params(number, mib):
    return pltpu.CompilerParams(collective_id=number, has_side_effects=True, vmem_limit_bytes=mib << 20)


def add_rows(target, sources, rows, step=16):
    @pl.loop(0, rows // step)
    def _(i):
        at = pl.ds(pl.multiple_of(i * step, step), step)
        total = target[at, :].astype(F32)
        for source in sources:
            total = total + source[at, :].astype(F32)
        target[at, :] = total.astype(BF)


def store_rims(src, outs, slot, side):
    outs[0, slot, 0] = src[pl.ds(0, RIM * side), :].astype(BF)
    outs[0, slot, 1] = src[pl.ds((side - RIM) * side, RIM * side), :].astype(BF)
    for e in range(RIM):
        rows = pl.ds(e * side, side)
        outs[0, slot, 2, rows] = src[pl.ds(e, side, stride=side), :].astype(BF)
        outs[0, slot, 3, rows] = src[pl.ds(side - RIM + e, side, stride=side), :].astype(BF)


def rims_of_input(inputs, mask_lanes):
    slots, side, _, channels = inputs.shape
    n_chunk = -(-channels // LANES)

    def kernel(x_ref, m_ref, o_ref, cells):
        for s in range(slots):
            for i in range(side):
                cells[pl.ds(i * side, side), :] = (
                    x_ref[s, i].astype(F32) * m_ref[s, pl.ds(i * side, side), :]
                )
            store_rims(cells, o_ref, s, side)

    return pl.pallas_call(
        kernel,
        grid=(n_chunk,),
        in_specs=[
            pl.BlockSpec((slots, side, side, LANES), lambda c: (0, 0, 0, c)),
            pl.BlockSpec((slots, side * side, LANES), lambda c: (0, 0, 0)),
        ],
        out_specs=pl.BlockSpec((1, slots, 4, RIM * side, LANES), lambda c: (c, 0, 0, 0, 0)),
        out_shape=jax.ShapeDtypeStruct((n_chunk, slots, 4, RIM * side, LANES), BF),
        scratch_shapes=[pltpu.VMEM((side * side, LANES), F32)],
        compiler_params=pltpu.CompilerParams(vmem_limit_bytes=32 << 20),
        name="rims_of_input",
    )(inputs, mask_lanes)


class HaloExchange:
    def __init__(self, grid, n_chunk, slots, side):
        self.grid, self.n_chunk, self.slots, self.side = grid, n_chunk, slots, side
        self.count = 2 * (grid.n_tile - 1)

    def scratch(self):
        n, s, band = self.grid.n_tile, self.slots, RIM * self.side
        return [
            pltpu.VMEM((n, s, 4, band, LANES), BF),
            pltpu.VMEM((n, s, 5, band, LANES), BF),
            pltpu.SemaphoreType.DMA((2,)),
        ]

    def halo_shape(self):
        return jax.ShapeDtypeStruct((self.n_chunk, self.slots, 5, RIM * self.side, LANES), BF)

    def plan(self, copies, rims, arrived, picked, halos, local):
        t, o = self.grid.at(self.grid.own())
        self.t, self.arrived, self.picked = t, arrived, picked
        own_chunk = jnp.minimum(t, self.n_chunk - 1)
        self.first, self.second = [], []
        for k in range(1, self.grid.n_tile):
            to = t ^ k
            source = jnp.minimum(to, self.n_chunk - 1)
            self.first.append((to, copies.make(rims.at[source], arrived.at[t], (to, o))))
            self.second.append((to, copies.make(picked.at[to], halos.at[own_chunk], (to, o))))
        self.own_copy = pltpu.make_async_copy(rims.at[own_chunk], arrived.at[t], local.at[0])
        self.back_copy = pltpu.make_async_copy(picked.at[t], halos.at[own_chunk], local.at[1])

    def send_rims(self):
        for to, copy in self.first:

            @pl.when(to < self.n_chunk)
            def _():
                copy.start()

        self.own_copy.start()

    def pick_and_send(self, neighbours):
        grid, slots, side = self.grid, self.slots, self.side
        t, arrived, picked = self.t, self.arrived, self.picked
        self.own_copy.wait()
        for _, copy in self.first:

            @pl.when(t < self.n_chunk)
            def _():
                copy.wait_recv()

        @pl.when(t < self.n_chunk)
        def _():
            @pl.loop(0, grid.n_tile * slots)
            def _(d):
                def rim(direction, which):
                    slot = neighbours(d, direction)
                    at = jnp.maximum(slot, 0)
                    value = arrived[at // slots, at % slots, which].astype(F32)
                    return jnp.where(slot >= 0, value, 0.0)

                to_tile, to_slot = d // slots, d % slots
                for to, (direction, which) in enumerate(((1, 1), (6, 0), (3, 3), (4, 2))):
                    picked[to_tile, to_slot, to] = rim(direction, which).astype(BF)
                rows = []
                for direction, which, first in ((0, 1, side - RIM), (2, 1, 0), (5, 0, side - RIM), (7, 0, 0)):
                    value = rim(direction, which)
                    rows += [value[e * side + first : e * side + first + RIM] for e in range(RIM)]
                    rows.append(jnp.zeros((16 - RIM * RIM, LANES), F32))
                rows.append(jnp.zeros((RIM * side - 64, LANES), F32))
                picked[to_tile, to_slot, 4] = jnp.concatenate(rows, 0).astype(BF)

        for _, copy in self.second:

            @pl.when(t < self.n_chunk)
            def _():
                copy.start()

        @pl.when(t < self.n_chunk)
        def _():
            self.back_copy.start()

    def finish(self):
        t = self.t

        @pl.when(t < self.n_chunk)
        def _():
            self.back_copy.wait()

        for to, copy in self.first:

            @pl.when(to < self.n_chunk)
            def _():
                copy.wait_send()

        for to, copy in self.second:

            @pl.when(to < self.n_chunk)
            def _():
                copy.wait_recv()

            @pl.when(t < self.n_chunk)
            def _():
                copy.wait_send()


class WeightGather:
    def __init__(self, grid, pairs, width):
        self.grid, self.pairs, self.width = grid, pairs, width
        self.count = pairs * (grid.n_tile * grid.n_opt - 1)

    def plan(self, copies, packed, gathered, local):
        grid, width = self.grid, self.width
        own = grid.own()

        def place(m, rel):
            t, o = grid.at({d: own[d] ^ rel.get(d, 0) for d in own})
            return gathered.at[m, o, pl.ds(pl.multiple_of(t * width, width), width)]

        def onward(m, rel, dims):
            source = packed.at[m] if not rel else place(m, rel)
            return [
                ({**rel, dim: k}, copies.make(source, place(m, rel), grid.beside(own, dim, k)))
                for dim in dims
                for k in range(1, grid.size[dim])
            ]

        orders = [("a", "x", "b", "c") if m % 2 == 0 else ("a", "b", "x", "c") for m in range(self.pairs)]
        due = {}

        def note(m, fresh, after):
            for rel, copy in fresh:
                level = sum(1 for d in rel if d != "c")
                wave = max(rel.get("a", 0) + level - ("a" in rel), after)
                due.setdefault(wave, []).append((m, rel, copy))
            return [copy for _, copy in fresh]

        self.keeps = [pltpu.make_async_copy(packed.at[m], place(m, {}), local.at[m]) for m in range(self.pairs)]
        self.first, self.later = [], []
        for m in range(self.pairs):
            fresh = onward(m, {}, orders[m])
            note(m, fresh, 0)
            for rel, copy in fresh:
                (self.later if rel.get("a", 0) > 1 else self.first).append(copy)
        self.waves = []
        for wave in range(4 * sum(grid.size.values())):
            events = []
            for m, rel, copy in sorted(due.pop(wave, []), key=lambda e: "c" in e[1]):
                last = max(orders[m].index(d) for d in rel)
                events.append((copy, note(m, onward(m, rel, orders[m][last + 1 :]), wave + 1)))
            self.waves.append(events)
            if not due:
                break

    def start(self):
        for copy in self.keeps + self.first:
            copy.start()

    def start_later(self):
        for copy in self.later:
            copy.start()

    def run(self, waves):
        for events in waves:
            for copy, fresh in events:
                copy.wait_recv()
                for other in fresh:
                    other.start()

    def finish(self):
        for copy in self.keeps:
            copy.wait()
        for copy in self.first + self.later + [c for events in self.waves for _, fresh in events for c in fresh]:
            copy.wait_send()


def exchange_forward(grid, rims, packed, neighbours, inputs, mask_lanes, taps, cotangent, flat_mask, weight_row, width):
    n_chunk, slots, _, band, _ = rims.shape
    side, channels = inputs.shape[1], inputs.shape[3]
    cells = side * side
    pairs, _, cols = packed.shape
    n_tile = grid.n_tile
    rows = slots * cells
    block = row_block(rows)
    early = rows // block
    halo = HaloExchange(grid, n_chunk, slots, side)
    gather = WeightGather(grid, pairs, packed.shape[1])
    total = halo.count + gather.count + n_tile - 1
    last = early + n_chunk * slots

    def kernel(
        r_ref, p_ref, n_ref, x_ref, m_ref, t_ref, g_ref, f_ref, l_ref,
        halo_ref, w_ref, nbr_ref, conv_ref, sum_ref, gap_ref, turned_ref, bias_ref,
        arrived, picked, local, landed, table, pad, send, recv, locals_w, locals_n,
    ):
        step = pl.program_id(0)
        t, o = grid.at(grid.own())
        copies = Copies(send, recv)
        halo.plan(copies, r_ref, arrived, picked, landed, local)
        gather.plan(copies, p_ref, w_ref, locals_w)
        tables = [copies.make(n_ref, nbr_ref.at[t], (t ^ k, o)) for k in range(1, n_tile)]
        keep = pltpu.make_async_copy(n_ref, nbr_ref.at[t], locals_n.at[0])
        load = pltpu.make_async_copy(nbr_ref, table, locals_n.at[1])
        halo_out = pltpu.make_async_copy(landed, halo_ref, locals_n.at[0])
        head = 2

        @pl.when(step == 0)
        def _():
            meet(grid.partners(("tile", "x", "c")))
            for copy in tables:
                copy.start()
            keep.start()
            halo.send_rims()
            gather.start()

        @pl.when((step > 0) & (step <= early))
        def _():
            value = f_ref[:, :1] * (l_ref[:, :1] * g_ref[...].astype(F32))
            arranged(value, gap_ref, turned_ref, bias_ref, step == 1, n_tile, width)

        @pl.when(step == early)
        def _():
            keep.wait()
            for copy in tables:
                copy.wait()
            load.start()
            load.wait()
            halo.pick_and_send(lambda d, k: table[d // slots, d % slots, k])
            gather.start_later()
            gather.run(gather.waves[:head])
            halo.finish()
            halo_out.start()

        for i, events in enumerate(gather.waves[head:]):

            @pl.when(step == min(last, early + 4 + 3 * i))
            def _():
                gather.run([events])

        @pl.when(step > early)
        def _():
            at = step - early - 1
            conv_step(
                x_ref, m_ref, t_ref, lambda k: landed[at // slots, at % slots, k].astype(F32), conv_ref, sum_ref, pad, side
            )

        @pl.when(step == last)
        def _():
            gather.finish()
            halo_out.wait()

    conv_at = lambda i: jnp.maximum(i - early - 1, 0)
    row_at = lambda i: jnp.clip(i - 1, 0, early - 1)
    any_space = pl.BlockSpec(memory_space=pl.ANY)
    return pl.pallas_call(
        kernel,
        grid=(last + 1,),
        in_specs=[any_space] * 3
        + [
            pl.BlockSpec((1, side, side, LANES), lambda i: (conv_at(i) % slots, 0, 0, conv_at(i) // slots)),
            pl.BlockSpec((1, cells, LANES), lambda i: (conv_at(i) % slots, 0, 0)),
            pl.BlockSpec((50, 8, LANES), lambda i: (0, 0, conv_at(i) // slots)),
            pl.BlockSpec((block, channels), lambda i: (row_at(i), 0)),
            pl.BlockSpec((block, LANES), lambda i: (row_at(i), 0)),
            pl.BlockSpec((1, LANES), lambda i: (0, 0)),
        ],
        out_specs=[any_space] * 3
        + [
            pl.BlockSpec((1, cells, LANES), lambda i: (conv_at(i) % slots, 0, conv_at(i) // slots)),
            pl.BlockSpec((1, 2, 8, LANES), lambda i: (conv_at(i) % slots, 0, 0, conv_at(i) // slots)),
            pl.BlockSpec((block, n_tile * width), lambda i: (row_at(i), 0)),
            pl.BlockSpec((channels, block), lambda i: (0, row_at(i))),
            pl.BlockSpec((1, channels), lambda i: (0, 0)),
        ],
        out_shape=[
            halo.halo_shape(),
            jax.ShapeDtypeStruct((pairs, grid.n_opt, n_tile * packed.shape[1], cols), BF),
            jax.ShapeDtypeStruct((n_tile,) + neighbours.shape, jnp.int32),
            jax.ShapeDtypeStruct((slots, cells, channels), F32),
            jax.ShapeDtypeStruct((slots, 2, 8, channels), F32),
            jax.ShapeDtypeStruct((rows, n_tile * width), BF),
            jax.ShapeDtypeStruct((channels, rows), BF),
            jax.ShapeDtypeStruct((1, channels), F32),
        ],
        scratch_shapes=halo.scratch()
        + [
            pltpu.VMEM(halo.halo_shape().shape, BF),
            pltpu.SMEM((n_tile,) + neighbours.shape, jnp.int32),
            pltpu.VMEM(((side + 2 * RIM) * PITCH, LANES), F32),
            pltpu.SemaphoreType.DMA((total,)),
            pltpu.SemaphoreType.DMA((total,)),
            pltpu.SemaphoreType.DMA((pairs,)),
            pltpu.SemaphoreType.DMA((2,)),
        ],
        compiler_params=remote_params(1, 63),
        name="exchange_forward",
    )(rims, packed, neighbours, inputs, mask_lanes, taps, cotangent, flat_mask, weight_row)


def exchange_backward(grid, rims, grads, neighbours, inputs, mask_lanes, d_conv, halos, small):
    n_chunk, slots, _, band, _ = rims.shape
    side, channels = inputs.shape[1], inputs.shape[3]
    side_b, side_x = grid.size["b"], grid.size["x"]
    _, blocks, rows, cols = grads.shape
    pairs = blocks // side_x
    part = rows // side_b
    side_a = grid.size["a"]
    piece = part // side_a
    halo = HaloExchange(grid, n_chunk, slots, side)
    steps = [(dim, 1 << i) for dim in ("c", "x", "b", "a") for i in range((grid.size[dim] - 1).bit_length())]
    total = halo.count + blocks + side_a * pairs * side_x * side_b * 2
    total += pairs * (2 * (side_a - 1) + side_a * (side_b - 1)) + len(steps)
    last = n_chunk * slots - 1
    small_rows = small.shape[0]
    small_shape = (up_to(50 + small_rows, 8), n_chunk * LANES)

    def kernel(
        r_ref, g_ref, n_ref, x_ref, m_ref, d_ref, h_ref, s_ref, halo_ref, o_ref, t_ref,
        arrived, picked, local, here, core, far, across, pad, sums, got, mine, heard, send, recv, load_sems,
    ):
        own = grid.own()
        own_x, own_b, own_c = own["x"], own["b"], own["c"]
        step = pl.program_id(0) * slots + pl.program_id(1)
        copies = Copies(send, recv)
        halo.plan(copies, r_ref, arrived, picked, halo_ref, local)
        order = [(k, m) for m in range(pairs) for k in range(1, side_x)]
        order += [(0, m) for m in range(pairs - 1, -1, -1)]
        index = lambda k, m: (own_x ^ k) * pairs + m
        own_a = own["a"]
        row_of = lambda a, b: pl.ds(pl.multiple_of((b * side_a + a) * piece, 16), piece)
        part_row = lambda a: pl.ds(pl.multiple_of(a * piece, 16), piece)
        turns = [*range(1, side_a), 0]
        cores, loads = [], []
        for i, (k, m) in enumerate(order):
            at = index(k, m)
            cores.append(copies.make(g_ref.at[1 - own_c, at], core.at[at], grid.beside(own, "c", 1)))
            loads.append(pltpu.make_async_copy(g_ref.at[own_c, at], here.at[at], load_sems.at[i]))
        one, two, one_adds, two_adds = {}, {}, {}, {}
        for m in range(pairs):
            for k in turns:
                a = own_a ^ k
                mine_at = here.at[index(0, m), row_of(a, own_b)]
                across_x = lambda q, b: (
                    copies.make(
                        here.at[index(q, m), row_of(a, b)], far.at[q - 1, m, row_of(a, b)], grid.beside(own, "x", q)
                    )
                )
                across_b = lambda q, j: (
                    copies.make(
                        here.at[index(q, m), row_of(a, own_b ^ j)],
                        across.at[j - 1, index(q, m), part_row(a)],
                        grid.beside(own, "b", j),
                    )
                )
                from_x = lambda b: [far.at[q - 1, m, row_of(a, b)] for q in range(1, side_x)]
                from_b = lambda q: [across.at[j - 1, index(q, m), part_row(a)] for j in range(1, side_b)]
                if m % 2 == 0:
                    one[k, m] = [across_x(q, b) for q in range(1, side_x) for b in range(side_b)]
                    one_adds[k, m] = [(here.at[index(0, m), row_of(a, b)], from_x(b)) for b in range(side_b)]
                    two[k, m] = [across_b(0, j) for j in range(1, side_b)]
                    two_adds[k, m] = [(mine_at, from_b(0))]
                else:
                    one[k, m] = [across_b(q, j) for q in range(side_x) for j in range(1, side_b)]
                    one_adds[k, m] = [(here.at[index(q, m), row_of(a, own_b)], from_b(q)) for q in range(side_x)]
                    two[k, m] = [across_x(q, own_b) for q in range(1, side_x)]
                    two_adds[k, m] = [(mine_at, from_x(own_b))]

        to_a, back_a, back_b, keeps = {}, {}, {}, []
        for m in range(pairs):
            at = index(0, m)
            done = here.at[at, row_of(own_a, own_b)]
            place = o_ref.at[m, row_of(own_a, own_b)]
            keeps.append(pltpu.make_async_copy(done, place, load_sems.at[m]))
            for k in range(1, side_a):
                to = grid.beside(own, "a", k)
                to_a[k, m] = copies.make(here.at[at, row_of(own_a ^ k, own_b)], got.at[m, k - 1], to)
                back_a[k, m] = copies.make(done, place, to)
            for k in range(side_a):
                for j in range(1, side_b):
                    came = o_ref.at[m, row_of(own_a ^ k, own_b)]
                    back_b[k, j, m] = copies.make(done if k == 0 else came, came, grid.beside(own, "b", j))
        small_copies = [
            copies.make(mine, heard.at[i], grid.beside(own, dim, k)) for i, (dim, k) in enumerate(steps)
        ]

        def start(found):
            for copy in found:
                copy.start()

        def wait(found):
            for copy in found:
                copy.wait()

        @pl.when(step == 0)
        def _():
            meet(grid.partners(("tile", "x", "c")))
            halo.send_rims()
            mine[...] = jnp.zeros_like(mine)
            start(cores)
            start(loads)

        add_taps(x_ref, m_ref, d_ref, h_ref, mine, pad, sums, slots, side)

        ready = {}
        for i, (k, m) in enumerate(order):
            ready[m] = max(ready.get(m, 0), i) if m % 2 == 1 or k > 0 else ready.get(m, 0)
        for i, (k, m) in enumerate(order):

            @pl.when(step == min(last, 3 + 2 * i))
            def _():
                loads[i].wait()
                cores[i].wait()
                at = index(k, m)
                add_rows(here.at[at], [core.at[at]], rows)
                for n in range(pairs):
                    if ready[n] == i:
                        start(one[turns[0], n])
                        start(one[turns[1], n])

        @pl.when(step == last)
        def _():
            halo.pick_and_send(lambda d, k: n_ref[d // slots, d % slots, k])
            for i in range(side_a + 1):
                for m in range(pairs):
                    if i < side_a:
                        k = turns[i]
                        wait(one[k, m])
                        if i + 2 < side_a:
                            start(one[turns[i + 2], m])
                        for target, sources in one_adds[k, m]:
                            add_rows(target, sources, piece)
                        start(two[k, m])
                for m in range(pairs):
                    if i > 0:
                        k = turns[i - 1]
                        wait(two[k, m])
                        for target, sources in two_adds[k, m]:
                            add_rows(target, sources, piece)
                        if k > 0:
                            to_a[k, m].start()
            mine[pl.ds(50, small_rows), pl.ds(0, channels)] = s_ref[...]
            for m in range(pairs):
                wait(to_a[k, m] for k in range(1, side_a))
                done = here.at[index(0, m), row_of(own_a, own_b)]
                add_rows(done, [got.at[m, k] for k in range(side_a - 1)], piece)
                keeps[m].start()
                start(back_a[k, m] for k in range(1, side_a))
                start(back_b[0, j, m] for j in range(1, side_b))
            for k in range(1, side_a):
                last_turn = k == side_a - 1
                for copy, i in [(c, i) for i, c in enumerate(small_copies) if last_turn or i // 2 == k - 1]:
                    if i // 2 >= k - 1:
                        copy.start()
                        copy.wait()
                        mine[...] = mine[...] + heard[i]
                for m in range(pairs):
                    back_a[k, m].wait_recv()
                    start(back_b[k, j, m] for j in range(1, side_b))
            halo.finish()
            t_ref[...] = mine[...]
            for m in range(pairs):
                keeps[m].wait()
                for k in range(1, side_a):
                    back_a[k, m].wait_send()
            wait(back_b.values())

    any_space = pl.BlockSpec(memory_space=pl.ANY)
    cells = side * side
    return pl.pallas_call(
        kernel,
        grid=(n_chunk, slots),
        in_specs=[
            any_space,
            any_space,
            pl.BlockSpec(memory_space=pltpu.SMEM),
            pl.BlockSpec((1, side, side, LANES), lambda c, s: (s, 0, 0, c)),
            pl.BlockSpec((1, cells, LANES), lambda c, s: (s, 0, 0)),
            pl.BlockSpec((1, cells, LANES), lambda c, s: (s, 0, c)),
            halo_block(halos),
            pl.BlockSpec(small.shape, lambda c, s: (0, 0)),
        ],
        out_specs=[any_space, any_space, pl.BlockSpec(small_shape, lambda c, s: (0, 0))],
        out_shape=[
            halo.halo_shape(),
            jax.ShapeDtypeStruct((pairs, rows, cols), BF),
            jax.ShapeDtypeStruct(small_shape, F32),
        ],
        scratch_shapes=halo.scratch()
        + [
            pltpu.VMEM((blocks, rows, cols), BF),
            pltpu.VMEM((blocks, rows, cols), BF),
            pltpu.VMEM((side_x - 1, pairs, rows, cols), BF),
            pltpu.VMEM((side_b - 1, blocks, part, cols), BF),
            pltpu.VMEM(((side + 2 * RIM) * PITCH, LANES), F32),
            pltpu.VMEM((50, 8, LANES), F32),
            pltpu.VMEM((pairs, side_a - 1, piece, cols), BF),
            pltpu.VMEM(small_shape, F32),
            pltpu.VMEM((len(steps),) + small_shape, F32),
            pltpu.SemaphoreType.DMA((total,)),
            pltpu.SemaphoreType.DMA((total,)),
            pltpu.SemaphoreType.DMA((blocks,)),
        ],
        compiler_params=remote_params(2, 60),
        name="exchange_backward",
    )(rims, grads, neighbours, inputs, mask_lanes, d_conv, halos, small)


def tile_total(grid, value, number):
    n_tile = grid.n_tile

    def kernel(v_ref, o_ref, got, send, recv):
        t, o = grid.at(grid.own())
        meet(grid.partners(("tile",)))
        copies = Copies(send, recv)
        got[t] = v_ref[...]
        sent = [copies.start(v_ref, got.at[t], (t ^ k, o)) for k in range(1, n_tile)]
        for copy in sent:
            copy.wait()
        total = got[0]
        for i in range(1, n_tile):
            total = total + got[i]
        o_ref[...] = total

    whole = pl.BlockSpec(memory_space=pltpu.VMEM)
    return pl.pallas_call(
        kernel,
        in_specs=[whole],
        out_specs=whole,
        out_shape=jax.ShapeDtypeStruct(value.shape, F32),
        scratch_shapes=[
            pltpu.VMEM((n_tile,) + value.shape, F32),
            pltpu.SemaphoreType.DMA((n_tile - 1,)),
            pltpu.SemaphoreType.DMA((n_tile - 1,)),
        ],
        compiler_params=remote_params(number, 16),
        name="tile_total",
    )(value)


def fill_halo(pad, halo, side):
    last = side + RIM
    up, down, left, right, corner = (halo(k) for k in range(5))
    for e in range(RIM):
        rows = slice(e * side, e * side + side)
        pad[pl.ds(e * PITCH + 8, side), :] = up[rows]
        pad[pl.ds((last + e) * PITCH + 8, side), :] = down[rows]
        pad[pl.ds(RIM * PITCH + 8 - RIM + e, side, stride=PITCH), :] = left[rows]
        pad[pl.ds(RIM * PITCH + 8 + side + e, side, stride=PITCH), :] = right[rows]
    places = ((0, 8 - RIM), (0, 8 + side), (last, 8 - RIM), (last, 8 + side))
    for k, (row, col) in enumerate(places):
        for e in range(RIM):
            at = 16 * k + RIM * e
            pad[pl.ds((row + e) * PITCH + col, RIM), :] = corner[at : at + RIM]


def conv_pass(pad, side, weight, emit):
    for block in range(side // 8):
        sums = [None] * side
        for b in range(7):
            taps = [weight(a, b) for a in range(7)]
            for r in range(side + 2 * RIM):
                cells = pad[pl.ds(r * PITCH + 8 - RIM + b + 8 * block, 8), :]
                for a in range(7):
                    i = r - a
                    if 0 <= i < side:
                        term = taps[a] * cells
                        sums[i] = term if sums[i] is None else sums[i] + term
        emit(block, sums)


def halo_block(halos):
    return pl.BlockSpec((1, 1) + halos.shape[2:], lambda c, s: (c, s, 0, 0, 0))


def conv_step(x_ref, m_ref, w_ref, halo, o_ref, s_ref, pad, side):
    for i in range(side):
        pad[pl.ds((i + RIM) * PITCH + 8, side), :] = x_ref[0, i].astype(F32) * m_ref[0, pl.ds(i * side, side), :]
    fill_halo(pad, halo, side)
    bias = w_ref[49]
    totals = [jnp.zeros((8, LANES), F32), jnp.zeros((8, LANES), F32)]

    def emit(block, sums):
        for i in range(side):
            value = sums[i] + bias
            rows = pl.ds(i * side + 8 * block, 8)
            o_ref[0, rows, :] = value
            weighted = m_ref[0, rows, :] * value
            totals[0] = totals[0] + weighted
            totals[1] = totals[1] + weighted * value

    conv_pass(pad, side, lambda a, b: w_ref[7 * a + b], emit)
    s_ref[0, 0], s_ref[0, 1] = totals


def conv_gradient(d_shaped, conv_out, mask_lanes, coefs, side):
    slots, cells, channels = d_shaped.shape
    n_chunk = -(-channels // LANES)

    def kernel(d_ref, v_ref, m_ref, c_ref, o_ref, r_ref, held):
        one, two, three = c_ref[0, :1], c_ref[1, :1], c_ref[2, :1]
        for s in range(slots):
            value = d_ref[s] * one - m_ref[s] * (two + three * v_ref[s])
            o_ref[s] = value
            held[...] = value
            store_rims(held, r_ref, s, side)

    piece = (slots, 4, RIM * side, LANES)
    block = pl.BlockSpec((slots, cells, LANES), lambda c: (0, 0, c))
    return pl.pallas_call(
        kernel,
        grid=(n_chunk,),
        in_specs=[
            block,
            block,
            pl.BlockSpec((slots, cells, LANES), lambda c: (0, 0, 0)),
            pl.BlockSpec((3, 8, LANES), lambda c: (0, 0, c)),
        ],
        out_specs=[block, pl.BlockSpec((1,) + piece, lambda c: (c, 0, 0, 0, 0))],
        scratch_shapes=[pltpu.VMEM((cells, LANES), F32)],
        out_shape=[
            jax.ShapeDtypeStruct((slots, cells, channels), F32),
            jax.ShapeDtypeStruct((n_chunk,) + piece, BF),
        ],
        compiler_params=pltpu.CompilerParams(vmem_limit_bytes=32 << 20),
        name="conv_gradient",
    )(d_shaped, conv_out, mask_lanes, coefs)


def add_taps(x_ref, m_ref, d_ref, h_ref, o_ref, pad, sums, slots, side):
    slot = pl.program_id(1)
    for i in range(side):
        pad[pl.ds((i + RIM) * PITCH + 8, side), :] = x_ref[0, i].astype(F32) * m_ref[0, pl.ds(i * side, side), :]
    fill_halo(pad, lambda k: h_ref[0, 0, k].astype(F32), side)

    @pl.when(slot == 0)
    def _():
        sums[...] = jnp.zeros_like(sums)

    for block in range(side // 8):
        grads = [d_ref[0, pl.ds(i * side + 8 * block, 8), :] for i in range(side)]
        total = grads[0]
        for i in range(1, side):
            total = total + grads[i]
        sums[49] += total
        for b in range(7):
            taps = [None] * 7
            for r in range(side + 2 * RIM):
                window = pad[pl.ds(r * PITCH + 8 - RIM + b + 8 * block, 8), :]
                for a in range(7):
                    i = r - a
                    if 0 <= i < side:
                        term = window * grads[i]
                        taps[a] = term if taps[a] is None else taps[a] + term
            for a in range(7):
                sums[7 * a + b] += taps[a]

    @pl.when(slot == slots - 1)
    def _():
        at = pl.multiple_of(pl.program_id(0) * LANES, LANES)
        o_ref[pl.ds(0, 50), pl.ds(at, LANES)] = jnp.sum(sums[...], axis=1)


def conv_backward(grid, d_conv, halos, cotangent, mask_lanes, taps, weight_lanes, change):
    slots, side, _, channels = cotangent.shape
    n_chunk = halos.shape[0]
    cells = side * side
    pairs, rows, cols = change.shape
    side_a, side_b = grid.size["a"], grid.size["b"]
    part = rows // side_b
    piece = part // side_a
    total = pairs * (side_a * (side_b - 1) + (side_a - 1))
    last = n_chunk * slots - 1

    def kernel(
        d_ref, g_ref, m_ref, w_ref, l_ref, h_ref, c_ref, o_ref, change_ref,
        pad, mine, from_b, from_a, send, recv, load_sems,
    ):
        own = grid.own()
        step = pl.program_id(0) * slots + pl.program_id(1)
        copies = Copies(send, recv)
        own_a, own_b = own["a"], own["b"]
        half = lambda b: pl.ds(pl.multiple_of(b * part, 16), part)
        row_of = lambda a, b: pl.ds(pl.multiple_of((b * side_a + a) * piece, 16), piece)
        part_row = lambda a: pl.ds(pl.multiple_of(a * piece, 16), piece)
        turns = [*range(1, side_a), 0]
        firsts, seconds, loads = {}, {}, []
        for m in range(pairs):
            for k in turns:
                a = own_a ^ k
                firsts[k, m] = [
                    copies.make(
                        c_ref.at[m, row_of(a, own_b ^ j)], from_b.at[j - 1, m, part_row(a)], grid.beside(own, "b", j)
                    )
                    for j in range(1, side_b)
                ]
                if k > 0:
                    seconds[k, m] = copies.make(
                        mine.at[m, part_row(a)], from_a.at[k - 1, m], grid.beside(own, "a", k)
                    )
            loads.append(pltpu.make_async_copy(c_ref.at[m, half(own_b)], mine.at[m], load_sems.at[m]))

        @pl.when(step == 0)
        def _():
            meet(grid.partners(("a", "b")))
            for load in loads:
                load.start()
            for k in turns:
                for m in range(pairs):
                    for copy in firsts[k, m]:
                        copy.start()

        for i in range(side):
            pad[pl.ds((i + RIM) * PITCH + 8, side), :] = d_ref[0, pl.ds(i * side, side), :]
        fill_halo(pad, lambda k: h_ref[0, 0, k].astype(F32), side)
        weight = l_ref[...]

        def emit(block, sums):
            for i in range(side):
                at = pl.ds(i * side + 8 * block, 8)
                scaled = weight * g_ref[0, i, pl.ds(8 * block, 8), :].astype(F32)
                o_ref[0, at, :] = m_ref[0, at, :] * (scaled + sums[i])

        conv_pass(pad, side, lambda a, b: w_ref[7 * (6 - a) + 6 - b], emit)

        for i, k in enumerate(turns):

            @pl.when(step == min(last, 5 + 4 * i))
            def _():
                for m in range(pairs):
                    if i == 0:
                        loads[m].wait()
                    for copy in firsts[k, m]:
                        copy.wait()
                    rows_here = part_row(own_a ^ k)
                    sources = [from_b.at[j, m, rows_here] for j in range(side_b - 1)]
                    add_rows(mine.at[m, rows_here], sources, piece)
                    if k > 0:
                        seconds[k, m].start()

        @pl.when(step == last)
        def _():
            for m in range(pairs):
                for k in range(1, side_a):
                    seconds[k, m].wait()
                value = mine[m, part_row(own_a)].astype(F32)
                for k in range(side_a - 1):
                    value = value + from_a[k, m].astype(F32)
                change_ref[m] = value

    return pl.pallas_call(
        kernel,
        grid=(n_chunk, slots),
        in_specs=[
            pl.BlockSpec((1, cells, LANES), lambda c, s: (s, 0, c)),
            pl.BlockSpec((1, side, side, LANES), lambda c, s: (s, 0, 0, c)),
            pl.BlockSpec((1, cells, LANES), lambda c, s: (s, 0, 0)),
            pl.BlockSpec((50, 8, LANES), lambda c, s: (0, 0, c)),
            pl.BlockSpec((8, LANES), lambda c, s: (0, 0)),
            halo_block(halos),
            pl.BlockSpec(memory_space=pl.ANY),
        ],
        out_specs=[
            pl.BlockSpec((1, cells, LANES), lambda c, s: (s, 0, c)),
            pl.BlockSpec((pairs, piece, cols), lambda c, s: (0, 0, 0)),
        ],
        scratch_shapes=[
            pltpu.VMEM(((side + 2 * RIM) * PITCH, LANES), F32),
            pltpu.VMEM((pairs, part, cols), BF),
            pltpu.VMEM((side_b - 1, pairs, part, cols), BF),
            pltpu.VMEM((side_a - 1, pairs, piece, cols), BF),
            pltpu.SemaphoreType.DMA((total,)),
            pltpu.SemaphoreType.DMA((total,)),
            pltpu.SemaphoreType.DMA((pairs,)),
        ],
        out_shape=[
            jax.ShapeDtypeStruct((slots, cells, channels), F32),
            jax.ShapeDtypeStruct((pairs, piece, cols), F32),
        ],
        compiler_params=remote_params(4, 48),
        name="conv_backward",
    )(d_conv, cotangent, mask_lanes, taps, weight_lanes, halos, change)


def spread_lanes(value, parts, width):
    rows, channels = value.shape
    run = channels // parts
    if run == width:
        return value
    gap = jnp.zeros((rows, width - run), value.dtype)
    pieces = []
    for t in range(parts):
        pieces += [value[:, t * run : (t + 1) * run], gap]
    return jnp.concatenate(pieces, 1)


def close_lanes(value, parts, run):
    width = value.shape[1] // parts
    if run == width:
        return value
    return jnp.concatenate([value[:, t * width : t * width + run] for t in range(parts)], 1)


def row_block(rows):
    return 3 * LANES if rows % (3 * LANES) == 0 else LANES


def arranged(value, gap_ref, turned_ref, sum_ref, first, parts, width):
    low = value.astype(BF).astype(F32)
    gap_ref[...] = spread_lanes(low, parts, width).astype(BF)
    turned_ref[...] = low.T.astype(BF)

    @pl.when(first)
    def _():
        sum_ref[...] = jnp.zeros_like(sum_ref)

    sum_ref[...] += jnp.sum(low, axis=0, keepdims=True)


def arrange(body, args, specs, rows, channels, parts, width, name):
    step = 3 * LANES if rows % (3 * LANES) == 0 else LANES

    def kernel(*refs):
        given, (gap_ref, turned_ref, sum_ref) = refs[: len(args)], refs[len(args) :]
        arranged(body(*given), gap_ref, turned_ref, sum_ref, pl.program_id(0) == 0, parts, width)

    return pl.pallas_call(
        kernel,
        grid=(rows // step,),
        in_specs=specs(step),
        out_specs=[
            pl.BlockSpec((step, parts * width), lambda i: (i, 0)),
            pl.BlockSpec((channels, step), lambda i: (0, i)),
            pl.BlockSpec((1, channels), lambda i: (0, 0)),
        ],
        out_shape=[
            jax.ShapeDtypeStruct((rows, parts * width), BF),
            jax.ShapeDtypeStruct((channels, rows), BF),
            jax.ShapeDtypeStruct((1, channels), F32),
        ],
        compiler_params=pltpu.CompilerParams(vmem_limit_bytes=48 << 20),
        name=name,
    )(*args)


def feed_forward(inverse, shaped, shaped_t, d_branch, d_branch_t, hidden_bias, weights, grad_rows):
    rows, depth = shaped.shape
    channels = shaped_t.shape[0]
    half, _, cols = hidden_bias.shape
    pairs, owners = weights.shape[:2]
    per_owner = 2 * pairs
    tile_rows = 3 * LANES if rows % (3 * LANES) == 0 else LANES

    def kernel(inv_ref, s_ref, st_ref, d_ref, dt_ref, hb_ref, w_ref, branch_ref, ds_ref, grad_ref, bias_ref, *scratch):
        packed, first, second, act, dpre, grads, sems, out_sem = scratch
        step = pl.program_id(0)

        def where(slot):
            owner, inside = slot // per_owner, slot % per_owner
            return owner, inside // 2, inside % 2

        def fetch(h, buffer):
            copies = []
            for which in range(2):
                owner, pair, _ = where(inv_ref[h + which * half])
                copies.append(
                    pltpu.make_async_copy(w_ref.at[pair, owner], packed.at[buffer, which], sems.at[buffer, which])
                )
            return copies

        @pl.when(step == 0)
        def _():
            for copy in fetch(0, 0):
                copy.start()
            if grad_rows > channels:
                rest = grad_rows - channels
                grads[:, :, pl.ds(channels, rest), :] = jnp.zeros(grads.shape[:2] + (rest, 2 * cols), BF)

        @pl.when(step + 1 < half)
        def _():
            for copy in fetch(step + 1, (step + 1) % 2):
                copy.start()

        now = step % 2
        slots = [where(inv_ref[step + which * half]) for which in range(2)]
        waits = fetch(step, now)
        for which, held in enumerate((first, second)):
            waits[which].wait()
            for parity in range(2):

                @pl.when(slots[which][2] == parity)
                def _():
                    held[...] = packed[now, which, :, parity * cols : (parity + 1) * cols]

        hidden = hb_ref[0]

        @pl.when(step == 0)
        def _():
            branch_ref[...] = jnp.zeros_like(branch_ref)
            ds_ref[...] = jnp.zeros_like(ds_ref)

        total = jnp.zeros((1, cols), F32)
        across = (((1,), (1,)), ((), ()))
        for i in range(rows // tile_rows):
            at = pl.ds(i * tile_rows, tile_rows)
            pre = jnp.dot(s_ref[at, :], first[...], preferred_element_type=F32) + hidden
            d_act = jnp.dot(d_ref[at, :], second[...], preferred_element_type=F32)
            square = pre * pre
            bend = jnp.tanh(ROOT * pre * (1.0 + CUBE * square))
            half_up = 0.5 * (1.0 + bend)
            low = (pre * half_up).astype(BF)
            slope = half_up + (0.5 * ROOT) * pre * (1.0 - bend * bend) * (1.0 + (3.0 * CUBE) * square)
            back = (d_act * slope).astype(BF)
            act[at, :] = low
            dpre[at, :] = back
            total = total + jnp.sum(back.astype(F32), axis=0, keepdims=True)
            out_add = lax.dot_general(low, second[...], across, preferred_element_type=F32)
            in_add = lax.dot_general(back, first[...], across, preferred_element_type=F32)

            branch_ref[at, :] += out_add
            ds_ref[at, :] += in_add

        bias_ref[0] = total
        for which, (left, right) in enumerate(((st_ref, dpre), (dt_ref, act))):
            owner, pair, half_of_pair = slots[which]
            value = jnp.dot(left[...], right[...], preferred_element_type=F32).astype(BF)
            for parity in range(2):

                @pl.when(half_of_pair == parity)
                def _():
                    at = (owner // 2) * pairs + pair
                    grads[owner % 2, at, pl.ds(0, channels), parity * cols : (parity + 1) * cols] = value

        @pl.when(step == half - 1)
        def _():
            out = pltpu.make_async_copy(grads, grad_ref, out_sem.at[0])
            out.start()
            out.wait()

    whole = lambda *shape: pl.BlockSpec(shape, lambda h, *_: (0,) * len(shape))
    line = pl.BlockSpec((1, 1, cols), lambda h, *_: (h, 0, 0))
    grad_shape = (2, owners // 2 * pairs, grad_rows, 2 * cols)
    return pl.pallas_call(
        kernel,
        grid_spec=pltpu.PrefetchScalarGridSpec(
            num_scalar_prefetch=1,
            grid=(half,),
            in_specs=[
                whole(rows, depth),
                whole(channels, rows),
                whole(rows, depth),
                whole(channels, rows),
                line,
                pl.BlockSpec(memory_space=pl.ANY),
            ],
            out_specs=[whole(rows, depth), whole(rows, depth), pl.BlockSpec(memory_space=pl.ANY), line],
            scratch_shapes=[
                pltpu.VMEM((2, 2, depth, 2 * cols), BF),
                pltpu.VMEM((depth, cols), BF),
                pltpu.VMEM((depth, cols), BF),
                pltpu.VMEM((rows, cols), BF),
                pltpu.VMEM((rows, cols), BF),
                pltpu.VMEM(grad_shape, BF),
                pltpu.SemaphoreType.DMA((2, 2)),
                pltpu.SemaphoreType.DMA((1,)),
            ],
        ),
        out_shape=[
            jax.ShapeDtypeStruct((rows, depth), F32),
            jax.ShapeDtypeStruct((rows, depth), F32),
            jax.ShapeDtypeStruct(grad_shape, BF),
            jax.ShapeDtypeStruct((half, 1, cols), F32),
        ],
        cost_estimate=pl.CostEstimate(
            flops=12 * rows * channels * half * cols, bytes_accessed=40 << 20, transcendentals=rows * half * cols
        ),
        compiler_params=pltpu.CompilerParams(vmem_limit_bytes=63 << 20),
        name="feed_forward",
    )(inverse, shaped, shaped_t, d_branch, d_branch_t, hidden_bias, weights)


def close_out(branch, d_shaped, inputs, conv_out, mask_lanes, out_bias, parts, run):
    rows, channels = inputs.shape
    depth = branch.shape[1]
    step = 3 * LANES if rows % (3 * LANES) == 0 else LANES

    def kernel(b_ref, d_ref, x_ref, v_ref, m_ref, o_ref, out_ref, ds_ref, sum_ref):
        branch_here = close_lanes(b_ref[...], parts, run) + o_ref[...]
        out_ref[...] = (m_ref[:, :1] * (x_ref[...].astype(F32) + branch_here)).astype(BF)
        grads = close_lanes(d_ref[...], parts, run)
        ds_ref[...] = grads

        @pl.when(pl.program_id(0) == 0)
        def _():
            sum_ref[...] = jnp.zeros_like(sum_ref)

        sum_ref[0] += jnp.sum(grads, axis=0, keepdims=True)
        sum_ref[1] += jnp.sum(grads * v_ref[...], axis=0, keepdims=True)

    line = lambda n: pl.BlockSpec((step, n), lambda i: (i, 0))
    return pl.pallas_call(
        kernel,
        grid=(rows // step,),
        in_specs=[
            line(depth),
            line(depth),
            line(channels),
            line(channels),
            line(LANES),
            pl.BlockSpec((1, channels), lambda i: (0, 0)),
        ],
        out_specs=[line(channels), line(channels), pl.BlockSpec((2, 1, channels), lambda i: (0, 0, 0))],
        out_shape=[
            jax.ShapeDtypeStruct((rows, channels), BF),
            jax.ShapeDtypeStruct((rows, channels), F32),
            jax.ShapeDtypeStruct((2, 1, channels), F32),
        ],
        compiler_params=pltpu.CompilerParams(vmem_limit_bytes=60 << 20),
        name="close_out",
    )(branch, d_shaped, inputs, conv_out, mask_lanes, out_bias)


def halves(value):
    high = value.astype(BF)
    return high, (value - high.astype(F32)).astype(BF)


def product(left, right, contract):
    dims = (contract, ((), ()))
    total = None
    for i, a in enumerate(left):
        for j, b in enumerate(right):
            if i + j < 2:
                term = lax.dot_general(a, b, dims, preferred_element_type=F32)
                total = term if total is None else total + term
    return total


def rotate(owned, left_basis, column_basis, moment_one, moment_two, correction, grid, width):
    slots, channels, run = left_basis.shape
    cols = column_basis.shape[1]
    pairs = slots // 2
    side_a, side_b = grid.size["a"], grid.size["b"]
    n_tile = grid.n_tile

    def kernel(f_ref, g_ref, l_ref, c_ref, one_ref, two_ref, first_ref, second_ref, o_ref):
        factor = f_ref[0]
        changes = []
        for p in range(2):
            grad = g_ref[0, pl.ds(0, channels), p * cols : (p + 1) * cols]
            left = halves(l_ref[p])
            column = halves(c_ref[p])
            rotated = product(left, (grad,), ((0,), (0,)))
            rotated = product(halves(rotated), column, ((1,), (0,)))
            first = decay_rate * one_ref[p] + (1.0 - decay_rate) * rotated
            second = decay_rate * two_ref[p] + (1.0 - decay_rate) * rotated * rotated
            first_ref[p] = first
            second_ref[p] = second
            direction = first * factor / (jnp.sqrt(second * factor) + adam_eps)
            turned = product(halves(direction), column, ((1,), (1,)))
            changes.append(product(left, halves(turned), ((1,), (0,))))
        change = jnp.concatenate(changes, 1)
        gap = jnp.zeros((width - run, 2 * cols), F32)
        for t in range(n_tile):
            piece = jnp.concatenate([change[t * run : (t + 1) * run], gap], 0)
            place = (t % side_b) * side_a + t // side_b
            o_ref[0, pl.ds(place * width, width), :] = piece.astype(BF)

    pair = lambda *shape: pl.BlockSpec(shape, lambda m: (m,) + (0,) * (len(shape) - 1))
    return pl.pallas_call(
        kernel,
        grid=(pairs,),
        in_specs=[
            pl.BlockSpec(memory_space=pltpu.SMEM),
            pair(1, owned.shape[1], 2 * cols),
            pair(2, channels, run),
            pair(2, cols, cols),
            pair(2, run, cols),
            pair(2, run, cols),
        ],
        out_specs=[pair(2, run, cols), pair(2, run, cols), pair(1, n_tile * width, 2 * cols)],
        out_shape=[
            jax.ShapeDtypeStruct(moment_one.shape, F32),
            jax.ShapeDtypeStruct(moment_one.shape, F32),
            jax.ShapeDtypeStruct((pairs, n_tile * width, 2 * cols), BF),
        ],
        compiler_params=pltpu.CompilerParams(vmem_limit_bytes=60 << 20),
        name="rotate",
    )(1.0 / correction.reshape(1), owned, left_basis, column_basis, moment_one, moment_two)


def up_to(value, unit):
    return -(-value // unit) * unit


def pack_pairs(value):
    slots, rows, cols = value.shape
    return value.reshape(slots // 2, 2, rows, cols).transpose(0, 2, 1, 3).reshape(slots // 2, rows, 2 * cols)


def unpack_pairs(value):
    pairs, rows, cols = value.shape
    return value.reshape(pairs, rows, 2, cols // 2).transpose(0, 2, 1, 3).reshape(2 * pairs, rows, cols // 2)


def per_device(
    grid,
    inputs,
    cotangent,
    master,
    moment_one,
    moment_two,
    left_basis,
    column_basis,
    small_params,
    small_first,
    small_second,
    land_mask,
    tile_count,
    neighbours,
    block_order,
    cell_weight,
    step_count,
):
    position = lax.axis_index("tile")
    sample = lax.axis_index("opt")
    inputs, cotangent = inputs[0], cotangent[0]
    slots, side, _, channels = inputs.shape
    cells = side * side
    rows = slots * cells
    n_tile = grid.n_tile
    n_chunk = -(-channels // LANES)
    per_group = channels // GROUPS
    per_owner, run, cols = master.shape
    pairs = per_owner // 2
    block_total = block_order.shape[0]
    half = block_total // 2
    width = up_to(run, 16)

    live = (jnp.arange(slots) < tile_count[position]).astype(F32)
    mask = (land_mask.astype(F32) * live[:, None, None]).reshape(slots, cells)
    mask_lanes = jnp.broadcast_to(mask[:, :, None], (slots, cells, LANES))
    flat_mask = mask_lanes.reshape(rows, LANES)
    taps = jnp.broadcast_to(small_params[:50, None, :], (50, 8, channels))

    weights_float = cell_weight.astype(F32)
    sample_weight = weights_float[sample] * weights_float.shape[0] / jnp.sum(weights_float)
    weight_lanes = jnp.broadcast_to(sample_weight, (8, LANES))
    weight_row = jnp.broadcast_to(sample_weight, (1, LANES))

    low_master = jnp.pad(pack_pairs(master.astype(BF)), ((0, 0), (0, width - run), (0, 0)))
    rims = rims_of_input(inputs, mask_lanes)
    halos, weights, all_neighbours, conv_out, sums, d_branch, d_branch_t, d_out_bias = exchange_forward(
        grid,
        rims,
        low_master,
        neighbours,
        inputs,
        mask_lanes,
        taps,
        cotangent.reshape(rows, channels),
        flat_mask,
        weight_row,
        width,
    )

    sums = jnp.sum(sums, axis=(0, 2))
    occupied = jnp.broadcast_to(jnp.sum(mask), (1, channels))
    sums = tile_total(grid, jnp.concatenate([sums, occupied], 0), 5)
    counted = sums[2, 0] * per_group
    by_group = sums[:2].reshape(2, GROUPS, per_group).sum(2)
    group_mean = by_group[0] / counted
    variance = by_group[1] / counted - group_mean * group_mean
    inv_std = jnp.repeat(lax.rsqrt(variance + epsilon), per_group)
    mean = jnp.repeat(group_mean, per_group)
    gain, shift = small_params[50], small_params[51]
    norm_coefs = jnp.stack([inv_std, mean * inv_std, gain, shift])

    def shaped_body(v_ref, c_ref):
        normed = v_ref[...] * c_ref[0:1] - c_ref[1:2]
        return normed * c_ref[2:3] + c_ref[3:4]

    flat_conv = conv_out.reshape(rows, channels)
    shaped, shaped_t, _ = arrange(
        shaped_body,
        (flat_conv, norm_coefs),
        lambda step: [
            pl.BlockSpec((step, channels), lambda i: (i, 0)),
            pl.BlockSpec((4, channels), lambda i: (0, 0)),
        ],
        rows,
        channels,
        n_tile,
        width,
        "arrange_shaped",
    )

    block_ids = jnp.arange(block_total, dtype=jnp.int32)
    inverse = jnp.sum(
        jnp.where(block_order[None, :] == block_ids[:, None], block_ids[None, :], 0), axis=1
    ).astype(jnp.int32)
    hidden_bias = small_params[53:57].reshape(half, 1, cols)
    branch, d_shaped, grads, d_hidden = feed_forward(
        inverse, shaped, shaped_t, d_branch, d_branch_t, hidden_bias, weights, n_tile * width
    )
    block_output, d_shaped, d_sums = close_out(
        branch, d_shaped, inputs.reshape(rows, channels), flat_conv, flat_mask, small_params[52:53], n_tile, run
    )

    d_shift = d_sums[0, 0]
    d_gain = inv_std * (d_sums[1, 0] - mean * d_shift)
    parts = tile_total(grid, jnp.stack([gain * d_shift, gain * d_gain]), 6)
    parts = jnp.repeat(parts.reshape(2, GROUPS, per_group).sum(2) / counted, per_group, axis=1)
    grad_coefs = jnp.stack(
        [
            inv_std * gain,
            inv_std * (parts[0] - mean * inv_std * parts[1]),
            inv_std * inv_std * parts[1],
        ]
    )
    d_conv, grad_rims = conv_gradient(
        d_shaped.reshape(slots, cells, channels),
        conv_out,
        mask_lanes,
        jnp.broadcast_to(grad_coefs[:, None, :], (3, 8, channels)),
        side,
    )
    small = jnp.concatenate([d_gain[None], d_shift[None], d_out_bias, d_hidden.reshape(4, channels)], 0)
    grad_halos, owned, d_small = exchange_backward(
        grid, grad_rims, grads, all_neighbours, inputs, mask_lanes, d_conv, halos, small
    )

    correction = 1.0 - jnp.power(F32(decay_rate), step_count[0].astype(F32))
    d_small = d_small[: small_params.shape[0], :channels]
    small_one = decay_rate * small_first + (1.0 - decay_rate) * d_small
    small_two = decay_rate * small_second + (1.0 - decay_rate) * d_small * d_small
    new_small = small_params - small_rate * (small_one / correction) / (
        jnp.sqrt(small_two / correction) + adam_eps
    )

    first_new, second_new, change = rotate(
        owned, left_basis, column_basis, moment_one, moment_two, correction, grid, width
    )
    input_grad, change = conv_backward(
        grid, d_conv, grad_halos, cotangent, mask_lanes, taps, weight_lanes, change
    )
    change = unpack_pairs(change[:, :run])
    new_master = master - 0.5 / math.sqrt(channels) * change
    return (
        block_output.reshape((1,) + inputs.shape),
        input_grad.reshape((1,) + inputs.shape),
        new_master,
        new_master.astype(BF),
        first_new,
        second_new,
        new_small,
        small_one,
        small_two,
    )


def solution(mesh):
    grid = Grid(mesh.shape["tile"], mesh.shape["opt"])

    def step(*args):
        return per_device(grid, *args)

    return jax.shard_map(
        step,
        mesh=mesh,
        in_specs=(
            P("opt", "tile", None, None, None),
            P("opt", "tile", None, None, None),
            P("opt", "tile", None),
            P("opt", "tile", None),
            P("opt", "tile", None),
            P("opt", None, "tile"),
            P("opt", None, None),
            P(),
            P(),
            P(),
            P("tile", None, None),
            P(),
            P("tile", None),
            P(),
            P(),
            P(),
        ),
        out_specs=(
            P("opt", "tile", None, None, None),
            P("opt", "tile", None, None, None),
            P("opt", "tile", None),
            P("opt", "tile", None),
            P("opt", "tile", None),
            P("opt", "tile", None),
            P(),
            P(),
            P(),
        ),
        check_vma=False,
    )
```

```python
import math

import jax
import jax.numpy as jnp
from jax import lax
from jax.experimental import pallas as pl
from jax.experimental.pallas import tpu as pltpu
from jax.sharding import PartitionSpec as P

GROUPS = 16
LANES = 128
RIM = 3
PITCH = 40
BF = jnp.bfloat16
F32 = jnp.float32

highest = lax.Precision.HIGHEST
epsilon = 1e-05
adam_eps = 1e-08
decay_rate = 0.5
small_rate = 0.05
ROOT = 0.7978845608028654
CUBE = 0.044715


class Grid:
    def __init__(self, n_tile, n_opt):
        b = n_tile // 4
        self.n_tile, self.n_opt = n_tile, n_opt
        self.size = {"a": 4, "b": b, "x": n_opt // 2, "c": 2}

    def own(self):
        t, o = lax.axis_index("tile"), lax.axis_index("opt")
        b = self.size["b"]
        return {"a": t // b, "b": t % b, "x": o // 2, "c": o % 2}

    def at(self, place):
        return place["a"] * self.size["b"] + place["b"], place["x"] * 2 + place["c"]

    def partners(self, dims):
        own = self.own()
        found = []
        for dim in dims:
            if dim == "tile":
                t, o = self.at(own)
                found += [(t ^ k, o) for k in range(1, self.n_tile)]
            else:
                found += [self.beside(own, dim, k) for k in range(1, self.size[dim])]
        return found

    def beside(self, own, dim, k):
        return self.at({**own, dim: own[dim] ^ k})


def meet(devices):
    barrier = pltpu.get_barrier_semaphore()
    for device in devices:
        pl.semaphore_signal(barrier, inc=1, device_id=device, device_id_type=pl.DeviceIdType.MESH)
    pl.semaphore_wait(barrier, len(devices))


class Copies:
    def __init__(self, send_sems, recv_sems):
        self.sems = send_sems, recv_sems
        self.used = 0

    def make(self, src, dst, device):
        i = self.used
        self.used += 1
        return pltpu.make_async_remote_copy(
            src_ref=src,
            dst_ref=dst,
            send_sem=self.sems[0].at[i],
            recv_sem=self.sems[1].at[i],
            device_id=device,
            device_id_type=pl.DeviceIdType.MESH,
        )

    def start(self, src, dst, device):
        copy = self.make(src, dst, device)
        copy.start()
        return copy


def remote_params(number, mib):
    return pltpu.CompilerParams(collective_id=number, has_side_effects=True, vmem_limit_bytes=mib << 20)


def add_rows(target, sources, rows, step=16):
    @pl.loop(0, rows // step)
    def _(i):
        at = pl.ds(pl.multiple_of(i * step, step), step)
        total = target[at, :].astype(F32)
        for source in sources:
            total = total + source[at, :].astype(F32)
        target[at, :] = total.astype(BF)


def store_rims(src, outs, slot, side):
    outs[0, slot, 0] = src[pl.ds(0, RIM * side), :].astype(BF)
    outs[0, slot, 1] = src[pl.ds((side - RIM) * side, RIM * side), :].astype(BF)
    for e in range(RIM):
        rows = pl.ds(e * side, side)
        outs[0, slot, 2, rows] = src[pl.ds(e, side, stride=side), :].astype(BF)
        outs[0, slot, 3, rows] = src[pl.ds(side - RIM + e, side, stride=side), :].astype(BF)


def rims_of_input(inputs, mask_lanes):
    slots, side, _, channels = inputs.shape
    n_chunk = -(-channels // LANES)

    def kernel(x_ref, m_ref, o_ref, cells):
        for s in range(slots):
            for i in range(side):
                cells[pl.ds(i * side, side), :] = (
                    x_ref[s, i].astype(F32) * m_ref[s, pl.ds(i * side, side), :]
                )
            store_rims(cells, o_ref, s, side)

    return pl.pallas_call(
        kernel,
        grid=(n_chunk,),
        in_specs=[
            pl.BlockSpec((slots, side, side, LANES), lambda c: (0, 0, 0, c)),
            pl.BlockSpec((slots, side * side, LANES), lambda c: (0, 0, 0)),
        ],
        out_specs=pl.BlockSpec((1, slots, 4, RIM * side, LANES), lambda c: (c, 0, 0, 0, 0)),
        out_shape=jax.ShapeDtypeStruct((n_chunk, slots, 4, RIM * side, LANES), BF),
        scratch_shapes=[pltpu.VMEM((side * side, LANES), F32)],
        compiler_params=pltpu.CompilerParams(vmem_limit_bytes=32 << 20),
        name="rims_of_input",
    )(inputs, mask_lanes)


class HaloExchange:
    def __init__(self, grid, n_chunk, slots, side):
        self.grid, self.n_chunk, self.slots, self.side = grid, n_chunk, slots, side
        self.count = 2 * (grid.n_tile - 1)

    def scratch(self):
        n, s, band = self.grid.n_tile, self.slots, RIM * self.side
        return [
            pltpu.VMEM((n, s, 4, band, LANES), BF),
            pltpu.VMEM((n, s, 5, band, LANES), BF),
            pltpu.SemaphoreType.DMA((2,)),
        ]

    def halo_shape(self):
        return jax.ShapeDtypeStruct((self.n_chunk, self.slots, 5, RIM * self.side, LANES), BF)

    def plan(self, copies, rims, arrived, picked, halos, local):
        t, o = self.grid.at(self.grid.own())
        self.t, self.arrived, self.picked = t, arrived, picked
        own_chunk = jnp.minimum(t, self.n_chunk - 1)
        self.first, self.second = [], []
        for k in range(1, self.grid.n_tile):
            to = t ^ k
            source = jnp.minimum(to, self.n_chunk - 1)
            self.first.append((to, copies.make(rims.at[source], arrived.at[t], (to, o))))
            self.second.append((to, copies.make(picked.at[to], halos.at[own_chunk], (to, o))))
        self.own_copy = pltpu.make_async_copy(rims.at[own_chunk], arrived.at[t], local.at[0])
        self.back_copy = pltpu.make_async_copy(picked.at[t], halos.at[own_chunk], local.at[1])

    def send_rims(self):
        for to, copy in self.first:

            @pl.when(to < self.n_chunk)
            def _():
                copy.start()

        self.own_copy.start()

    def pick_and_send(self, neighbours):
        grid, slots, side = self.grid, self.slots, self.side
        t, arrived, picked = self.t, self.arrived, self.picked
        self.own_copy.wait()
        for _, copy in self.first:

            @pl.when(t < self.n_chunk)
            def _():
                copy.wait_recv()

        @pl.when(t < self.n_chunk)
        def _():
            @pl.loop(0, grid.n_tile * slots)
            def _(d):
                def rim(direction, which):
                    slot = neighbours(d, direction)
                    at = jnp.maximum(slot, 0)
                    value = arrived[at // slots, at % slots, which].astype(F32)
                    return jnp.where(slot >= 0, value, 0.0)

                to_tile, to_slot = d // slots, d % slots
                for to, (direction, which) in enumerate(((1, 1), (6, 0), (3, 3), (4, 2))):
                    picked[to_tile, to_slot, to] = rim(direction, which).astype(BF)
                rows = []
                for direction, which, first in ((0, 1, side - RIM), (2, 1, 0), (5, 0, side - RIM), (7, 0, 0)):
                    value = rim(direction, which)
                    rows += [value[e * side + first : e * side + first + RIM] for e in range(RIM)]
                    rows.append(jnp.zeros((16 - RIM * RIM, LANES), F32))
                rows.append(jnp.zeros((RIM * side - 64, LANES), F32))
                picked[to_tile, to_slot, 4] = jnp.concatenate(rows, 0).astype(BF)

        for _, copy in self.second:

            @pl.when(t < self.n_chunk)
            def _():
                copy.start()

        @pl.when(t < self.n_chunk)
        def _():
            self.back_copy.start()

    def finish(self):
        t = self.t

        @pl.when(t < self.n_chunk)
        def _():
            self.back_copy.wait()

        for to, copy in self.first:

            @pl.when(to < self.n_chunk)
            def _():
                copy.wait_send()

        for to, copy in self.second:

            @pl.when(to < self.n_chunk)
            def _():
                copy.wait_recv()

            @pl.when(t < self.n_chunk)
            def _():
                copy.wait_send()


class WeightGather:
    def __init__(self, grid, pairs, width):
        self.grid, self.pairs, self.width = grid, pairs, width
        self.count = pairs * (grid.n_tile * grid.n_opt - 1)

    def plan(self, copies, packed, gathered, local):
        grid, width = self.grid, self.width
        own = grid.own()

        def place(m, rel):
            t, o = grid.at({d: own[d] ^ rel.get(d, 0) for d in own})
            return gathered.at[m, o, pl.ds(pl.multiple_of(t * width, width), width)]

        def onward(m, rel, dims):
            source = packed.at[m] if not rel else place(m, rel)
            return [
                ({**rel, dim: k}, copies.make(source, place(m, rel), grid.beside(own, dim, k)))
                for dim in dims
                for k in range(1, grid.size[dim])
            ]

        orders = [("a", "x", "b", "c") if m % 2 == 0 else ("a", "b", "x", "c") for m in range(self.pairs)]
        due = {}

        def note(m, fresh, after):
            for rel, copy in fresh:
                level = sum(1 for d in rel if d != "c")
                wave = max(rel.get("a", 0) + level - ("a" in rel), after)
                due.setdefault(wave, []).append((m, rel, copy))
            return [copy for _, copy in fresh]

        self.keeps = [pltpu.make_async_copy(packed.at[m], place(m, {}), local.at[m]) for m in range(self.pairs)]
        self.first, self.later = [], []
        for m in range(self.pairs):
            fresh = onward(m, {}, orders[m])
            note(m, fresh, 0)
            for rel, copy in fresh:
                (self.later if rel.get("a", 0) > 1 else self.first).append(copy)
        self.waves = []
        for wave in range(4 * sum(grid.size.values())):
            events = []
            for m, rel, copy in sorted(due.pop(wave, []), key=lambda e: "c" in e[1]):
                last = max(orders[m].index(d) for d in rel)
                events.append((copy, note(m, onward(m, rel, orders[m][last + 1 :]), wave + 1)))
            self.waves.append(events)
            if not due:
                break

    def start(self):
        for copy in self.keeps + self.first:
            copy.start()

    def start_later(self):
        for copy in self.later:
            copy.start()

    def run(self, waves):
        for events in waves:
            for copy, fresh in events:
                copy.wait_recv()
                for other in fresh:
                    other.start()

    def finish(self):
        for copy in self.keeps:
            copy.wait()
        for copy in self.first + self.later + [c for events in self.waves for _, fresh in events for c in fresh]:
            copy.wait_send()


def exchange_forward(grid, rims, packed, neighbours, inputs, mask_lanes, taps, cotangent, flat_mask, weight_row, width):
    n_chunk, slots, _, band, _ = rims.shape
    side, channels = inputs.shape[1], inputs.shape[3]
    cells = side * side
    pairs, _, cols = packed.shape
    n_tile = grid.n_tile
    rows = slots * cells
    block = row_block(rows)
    early = rows // block
    halo = HaloExchange(grid, n_chunk, slots, side)
    gather = WeightGather(grid, pairs, packed.shape[1])
    total = halo.count + gather.count + n_tile - 1
    last = early + n_chunk * slots

    def kernel(
        r_ref, p_ref, n_ref, x_ref, m_ref, t_ref, g_ref, f_ref, l_ref,
        halo_ref, w_ref, nbr_ref, conv_ref, sum_ref, gap_ref, turned_ref, bias_ref,
        arrived, picked, local, landed, table, pad, send, recv, locals_w, locals_n,
    ):
        step = pl.program_id(0)
        t, o = grid.at(grid.own())
        copies = Copies(send, recv)
        halo.plan(copies, r_ref, arrived, picked, landed, local)
        gather.plan(copies, p_ref, w_ref, locals_w)
        tables = [copies.make(n_ref, nbr_ref.at[t], (t ^ k, o)) for k in range(1, n_tile)]
        keep = pltpu.make_async_copy(n_ref, nbr_ref.at[t], locals_n.at[0])
        load = pltpu.make_async_copy(nbr_ref, table, locals_n.at[1])
        halo_out = pltpu.make_async_copy(landed, halo_ref, locals_n.at[0])
        head = 2

        @pl.when(step == 0)
        def _():
            meet(grid.partners(("tile", "x", "c")))
            for copy in tables:
                copy.start()
            keep.start()
            halo.send_rims()
            gather.start()

        @pl.when((step > 0) & (step <= early))
        def _():
            value = f_ref[:, :1] * (l_ref[:, :1] * g_ref[...].astype(F32))
            arranged(value, gap_ref, turned_ref, bias_ref, step == 1, n_tile, width)

        @pl.when(step == early)
        def _():
            keep.wait()
            for copy in tables:
                copy.wait()
            load.start()
            load.wait()
            halo.pick_and_send(lambda d, k: table[d // slots, d % slots, k])
            gather.start_later()
            gather.run(gather.waves[:head])
            halo.finish()
            halo_out.start()

        for i, events in enumerate(gather.waves[head:]):

            @pl.when(step == min(last, early + 4 + 3 * i))
            def _():
                gather.run([events])

        @pl.when(step > early)
        def _():
            at = step - early - 1
            conv_step(
                x_ref, m_ref, t_ref, lambda k: landed[at // slots, at % slots, k].astype(F32), conv_ref, sum_ref, pad, side
            )

        @pl.when(step == last)
        def _():
            gather.finish()
            halo_out.wait()

    conv_at = lambda i: jnp.maximum(i - early - 1, 0)
    row_at = lambda i: jnp.clip(i - 1, 0, early - 1)
    any_space = pl.BlockSpec(memory_space=pl.ANY)
    return pl.pallas_call(
        kernel,
        grid=(last + 1,),
        in_specs=[any_space] * 3
        + [
            pl.BlockSpec((1, side, side, LANES), lambda i: (conv_at(i) % slots, 0, 0, conv_at(i) // slots)),
            pl.BlockSpec((1, cells, LANES), lambda i: (conv_at(i) % slots, 0, 0)),
            pl.BlockSpec((50, 8, LANES), lambda i: (0, 0, conv_at(i) // slots)),
            pl.BlockSpec((block, channels), lambda i: (row_at(i), 0)),
            pl.BlockSpec((block, LANES), lambda i: (row_at(i), 0)),
            pl.BlockSpec((1, LANES), lambda i: (0, 0)),
        ],
        out_specs=[any_space] * 3
        + [
            pl.BlockSpec((1, cells, LANES), lambda i: (conv_at(i) % slots, 0, conv_at(i) // slots)),
            pl.BlockSpec((1, 2, 8, LANES), lambda i: (conv_at(i) % slots, 0, 0, conv_at(i) // slots)),
            pl.BlockSpec((block, n_tile * width), lambda i: (row_at(i), 0)),
            pl.BlockSpec((channels, block), lambda i: (0, row_at(i))),
            pl.BlockSpec((1, channels), lambda i: (0, 0)),
        ],
        out_shape=[
            halo.halo_shape(),
            jax.ShapeDtypeStruct((pairs, grid.n_opt, n_tile * packed.shape[1], cols), BF),
            jax.ShapeDtypeStruct((n_tile,) + neighbours.shape, jnp.int32),
            jax.ShapeDtypeStruct((slots, cells, channels), F32),
            jax.ShapeDtypeStruct((slots, 2, 8, channels), F32),
            jax.ShapeDtypeStruct((rows, n_tile * width), BF),
            jax.ShapeDtypeStruct((channels, rows), BF),
            jax.ShapeDtypeStruct((1, channels), F32),
        ],
        scratch_shapes=halo.scratch()
        + [
            pltpu.VMEM(halo.halo_shape().shape, BF),
            pltpu.SMEM((n_tile,) + neighbours.shape, jnp.int32),
            pltpu.VMEM(((side + 2 * RIM) * PITCH, LANES), F32),
            pltpu.SemaphoreType.DMA((total,)),
            pltpu.SemaphoreType.DMA((total,)),
            pltpu.SemaphoreType.DMA((pairs,)),
            pltpu.SemaphoreType.DMA((2,)),
        ],
        compiler_params=remote_params(1, 63),
        name="exchange_forward",
    )(rims, packed, neighbours, inputs, mask_lanes, taps, cotangent, flat_mask, weight_row)


def exchange_backward(grid, rims, grads, neighbours, inputs, mask_lanes, d_conv, halos, small):
    n_chunk, slots, _, band, _ = rims.shape
    side, channels = inputs.shape[1], inputs.shape[3]
    side_b, side_x = grid.size["b"], grid.size["x"]
    _, blocks, rows, cols = grads.shape
    pairs = blocks // side_x
    part = rows // side_b
    side_a = grid.size["a"]
    piece = part // side_a
    halo = HaloExchange(grid, n_chunk, slots, side)
    total = halo.count + blocks + side_a * pairs * side_x * side_b * 2
    total += pairs * (side_a - 1 + 5 + side_a * (side_b - 1))
    last = n_chunk * slots - 1
    small_rows = small.shape[0]
    small_shape = (up_to(50 + small_rows, 8), n_chunk * LANES)

    def kernel(
        r_ref, g_ref, n_ref, x_ref, m_ref, d_ref, h_ref, s_ref, halo_ref, o_ref, t_ref,
        arrived, picked, local, here, core, far, across, pad, sums, got, mine, send, recv, load_sems,
    ):
        own = grid.own()
        own_x, own_b, own_c = own["x"], own["b"], own["c"]
        step = pl.program_id(0) * slots + pl.program_id(1)
        copies = Copies(send, recv)
        halo.plan(copies, r_ref, arrived, picked, halo_ref, local)
        order = [(k, m) for m in range(pairs) for k in range(1, side_x)]
        order += [(0, m) for m in range(pairs - 1, -1, -1)]
        index = lambda k, m: (own_x ^ k) * pairs + m
        own_a = own["a"]
        row_of = lambda a, b: pl.ds(pl.multiple_of((b * side_a + a) * piece, 16), piece)
        part_row = lambda a: pl.ds(pl.multiple_of(a * piece, 16), piece)
        turns = [*range(1, side_a), 0]
        cores, loads = [], []
        for i, (k, m) in enumerate(order):
            at = index(k, m)
            cores.append(copies.make(g_ref.at[1 - own_c, at], core.at[at], grid.beside(own, "c", 1)))
            loads.append(pltpu.make_async_copy(g_ref.at[own_c, at], here.at[at], load_sems.at[i]))
        one, two, one_adds, two_adds = {}, {}, {}, {}
        for m in range(pairs):
            for k in turns:
                a = own_a ^ k
                mine_at = here.at[index(0, m), row_of(a, own_b)]
                across_x = lambda q, b: (
                    copies.make(
                        here.at[index(q, m), row_of(a, b)], far.at[q - 1, m, row_of(a, b)], grid.beside(own, "x", q)
                    )
                )
                across_b = lambda q, j: (
                    copies.make(
                        here.at[index(q, m), row_of(a, own_b ^ j)],
                        across.at[j - 1, index(q, m), part_row(a)],
                        grid.beside(own, "b", j),
                    )
                )
                from_x = lambda b: [far.at[q - 1, m, row_of(a, b)] for q in range(1, side_x)]
                from_b = lambda q: [across.at[j - 1, index(q, m), part_row(a)] for j in range(1, side_b)]
                if m % 2 == 0:
                    one[k, m] = [across_x(q, b) for q in range(1, side_x) for b in range(side_b)]
                    one_adds[k, m] = [(here.at[index(0, m), row_of(a, b)], from_x(b)) for b in range(side_b)]
                    two[k, m] = [across_b(0, j) for j in range(1, side_b)]
                    two_adds[k, m] = [(mine_at, from_b(0))]
                else:
                    one[k, m] = [across_b(q, j) for q in range(side_x) for j in range(1, side_b)]
                    one_adds[k, m] = [(here.at[index(q, m), row_of(a, own_b)], from_b(q)) for q in range(side_x)]
                    two[k, m] = [across_x(q, own_b) for q in range(1, side_x)]
                    two_adds[k, m] = [(mine_at, from_x(own_b))]

        to_a, back_a, back_b, keeps = {}, {}, {}, []
        for m in range(pairs):
            at = index(0, m)
            done = here.at[at, row_of(own_a, own_b)]
            place = o_ref.at[m, row_of(own_a, own_b)]
            keeps.append(pltpu.make_async_copy(done, place, load_sems.at[m]))
            for k in range(1, side_a):
                to = grid.beside(own, "a", k)
                to_a[k, m] = copies.make(here.at[at, row_of(own_a ^ k, own_b)], got.at[m, k - 1], to)
            got_at = lambda k: o_ref.at[m, row_of(own_a ^ k, own_b)]
            beside_a = lambda k: grid.beside(own, "a", k)
            back_a["near", m] = copies.make(done, place, beside_a(1))
            back_a["over", m] = copies.make(done, place, beside_a(3))
            back_a["over2", m] = copies.make(got_at(1), got_at(1), beside_a(3))
            back_a["out", m] = copies.make(got_at(3), got_at(3), beside_a(1))
            back_a["out2", m] = copies.make(got_at(2), got_at(2), beside_a(1))
            for k in range(side_a):
                for j in range(1, side_b):
                    came = o_ref.at[m, row_of(own_a ^ k, own_b)]
                    back_b[k, j, m] = copies.make(done if k == 0 else came, came, grid.beside(own, "b", j))
        middle = (own_a == 1) | (own_a == 2)

        def start(found):
            for copy in found:
                copy.start()

        def wait(found):
            for copy in found:
                copy.wait()

        @pl.when(step == 0)
        def _():
            meet(grid.partners(("tile", "x", "c")))
            halo.send_rims()
            mine[...] = jnp.zeros_like(mine)
            start(cores)
            start(loads)

        add_taps(x_ref, m_ref, d_ref, h_ref, mine, pad, sums, slots, side)

        ready = {}
        for i, (k, m) in enumerate(order):
            ready[m] = max(ready.get(m, 0), i) if m % 2 == 1 or k > 0 else ready.get(m, 0)
        for i, (k, m) in enumerate(order):

            @pl.when(step == min(last, 3 + 2 * i))
            def _():
                loads[i].wait()
                cores[i].wait()
                at = index(k, m)
                add_rows(here.at[at], [core.at[at]], rows)
                for n in range(pairs):
                    if ready[n] == i:
                        start(one[turns[0], n])
                        start(one[turns[1], n])

        @pl.when(step == last)
        def _():
            halo.pick_and_send(lambda d, k: n_ref[d // slots, d % slots, k])
            for i in range(side_a + 1):
                for m in range(pairs):
                    if i < side_a:
                        k = turns[i]
                        wait(one[k, m])
                        if i + 2 < side_a:
                            start(one[turns[i + 2], m])
                        for target, sources in one_adds[k, m]:
                            add_rows(target, sources, piece)
                        start(two[k, m])
                for m in range(pairs):
                    if i > 0:
                        k = turns[i - 1]
                        wait(two[k, m])
                        for target, sources in two_adds[k, m]:
                            add_rows(target, sources, piece)
                        if k > 0:
                            to_a[k, m].start()
            mine[pl.ds(50, small_rows), pl.ds(0, channels)] = s_ref[...]
            for m in range(pairs):
                wait(to_a[k, m] for k in range(1, side_a))
                done = here.at[index(0, m), row_of(own_a, own_b)]
                add_rows(done, [got.at[m, k] for k in range(side_a - 1)], piece)
                keeps[m].start()
                back_a["near", m].start()

                @pl.when(middle)
                def _():
                    back_a["over", m].start()

                start(back_b[0, j, m] for j in range(1, side_b))

            def arrive(came, k, onward):
                for m in range(pairs):
                    back_a[came, m].wait_recv()
                    if onward is not None:
                        back_a[onward, m].start()
                    start(back_b[k, j, m] for j in range(1, side_b))

            for m in range(pairs):
                back_a["near", m].wait_recv()

                @pl.when(middle)
                def _():
                    back_a["over2", m].start()

                start(back_b[1, j, m] for j in range(1, side_b))

            @pl.when(middle)
            def _():
                arrive("over", 3, "out")
                arrive("over2", 2, "out2")

            @pl.when(~middle)
            def _():
                arrive("out", 2, None)
                arrive("out2", 3, None)

            halo.finish()
            t_ref[...] = mine[...]
            for m in range(pairs):
                keeps[m].wait()
                back_a["near", m].wait_send()

                @pl.when(middle)
                def _():
                    for name in ("over", "over2", "out", "out2"):
                        back_a[name, m].wait_send()

            wait(back_b.values())

    any_space = pl.BlockSpec(memory_space=pl.ANY)
    cells = side * side
    return pl.pallas_call(
        kernel,
        grid=(n_chunk, slots),
        in_specs=[
            any_space,
            any_space,
            pl.BlockSpec(memory_space=pltpu.SMEM),
            pl.BlockSpec((1, side, side, LANES), lambda c, s: (s, 0, 0, c)),
            pl.BlockSpec((1, cells, LANES), lambda c, s: (s, 0, 0)),
            pl.BlockSpec((1, cells, LANES), lambda c, s: (s, 0, c)),
            halo_block(halos),
            pl.BlockSpec(small.shape, lambda c, s: (0, 0)),
        ],
        out_specs=[any_space, any_space, pl.BlockSpec(small_shape, lambda c, s: (0, 0))],
        out_shape=[
            halo.halo_shape(),
            jax.ShapeDtypeStruct((pairs, rows, cols), BF),
            jax.ShapeDtypeStruct(small_shape, F32),
        ],
        scratch_shapes=halo.scratch()
        + [
            pltpu.VMEM((blocks, rows, cols), BF),
            pltpu.VMEM((blocks, rows, cols), BF),
            pltpu.VMEM((side_x - 1, pairs, rows, cols), BF),
            pltpu.VMEM((side_b - 1, blocks, part, cols), BF),
            pltpu.VMEM(((side + 2 * RIM) * PITCH, LANES), F32),
            pltpu.VMEM((50, 8, LANES), F32),
            pltpu.VMEM((pairs, side_a - 1, piece, cols), BF),
            pltpu.VMEM(small_shape, F32),
            pltpu.SemaphoreType.DMA((total,)),
            pltpu.SemaphoreType.DMA((total,)),
            pltpu.SemaphoreType.DMA((blocks,)),
        ],
        compiler_params=remote_params(2, 60),
        name="exchange_backward",
    )(rims, grads, neighbours, inputs, mask_lanes, d_conv, halos, small)


def tile_total(grid, value, number):
    n_tile = grid.n_tile

    def kernel(v_ref, o_ref, got, send, recv):
        t, o = grid.at(grid.own())
        meet(grid.partners(("tile",)))
        copies = Copies(send, recv)
        got[t] = v_ref[...]
        sent = [copies.start(v_ref, got.at[t], (t ^ k, o)) for k in range(1, n_tile)]
        for copy in sent:
            copy.wait()
        total = got[0]
        for i in range(1, n_tile):
            total = total + got[i]
        o_ref[...] = total

    whole = pl.BlockSpec(memory_space=pltpu.VMEM)
    return pl.pallas_call(
        kernel,
        in_specs=[whole],
        out_specs=whole,
        out_shape=jax.ShapeDtypeStruct(value.shape, F32),
        scratch_shapes=[
            pltpu.VMEM((n_tile,) + value.shape, F32),
            pltpu.SemaphoreType.DMA((n_tile - 1,)),
            pltpu.SemaphoreType.DMA((n_tile - 1,)),
        ],
        compiler_params=remote_params(number, 16),
        name="tile_total",
    )(value)


def fill_halo(pad, halo, side):
    last = side + RIM
    up, down, left, right, corner = (halo(k) for k in range(5))
    for e in range(RIM):
        rows = slice(e * side, e * side + side)
        pad[pl.ds(e * PITCH + 8, side), :] = up[rows]
        pad[pl.ds((last + e) * PITCH + 8, side), :] = down[rows]
        pad[pl.ds(RIM * PITCH + 8 - RIM + e, side, stride=PITCH), :] = left[rows]
        pad[pl.ds(RIM * PITCH + 8 + side + e, side, stride=PITCH), :] = right[rows]
    places = ((0, 8 - RIM), (0, 8 + side), (last, 8 - RIM), (last, 8 + side))
    for k, (row, col) in enumerate(places):
        for e in range(RIM):
            at = 16 * k + RIM * e
            pad[pl.ds((row + e) * PITCH + col, RIM), :] = corner[at : at + RIM]


def conv_pass(pad, side, weight, emit):
    for block in range(side // 8):
        sums = [None] * side
        for b in range(7):
            taps = [weight(a, b) for a in range(7)]
            for r in range(side + 2 * RIM):
                cells = pad[pl.ds(r * PITCH + 8 - RIM + b + 8 * block, 8), :]
                for a in range(7):
                    i = r - a
                    if 0 <= i < side:
                        term = taps[a] * cells
                        sums[i] = term if sums[i] is None else sums[i] + term
        emit(block, sums)


def halo_block(halos):
    return pl.BlockSpec((1, 1) + halos.shape[2:], lambda c, s: (c, s, 0, 0, 0))


def conv_step(x_ref, m_ref, w_ref, halo, o_ref, s_ref, pad, side):
    for i in range(side):
        pad[pl.ds((i + RIM) * PITCH + 8, side), :] = x_ref[0, i].astype(F32) * m_ref[0, pl.ds(i * side, side), :]
    fill_halo(pad, halo, side)
    bias = w_ref[49]
    totals = [jnp.zeros((8, LANES), F32), jnp.zeros((8, LANES), F32)]

    def emit(block, sums):
        for i in range(side):
            value = sums[i] + bias
            rows = pl.ds(i * side + 8 * block, 8)
            o_ref[0, rows, :] = value
            weighted = m_ref[0, rows, :] * value
            totals[0] = totals[0] + weighted
            totals[1] = totals[1] + weighted * value

    conv_pass(pad, side, lambda a, b: w_ref[7 * a + b], emit)
    s_ref[0, 0], s_ref[0, 1] = totals


def conv_gradient(d_shaped, conv_out, mask_lanes, coefs, side):
    slots, cells, channels = d_shaped.shape
    n_chunk = -(-channels // LANES)

    def kernel(d_ref, v_ref, m_ref, c_ref, o_ref, r_ref, held):
        one, two, three = c_ref[0, :1], c_ref[1, :1], c_ref[2, :1]
        for s in range(slots):
            value = d_ref[s] * one - m_ref[s] * (two + three * v_ref[s])
            o_ref[s] = value
            held[...] = value
            store_rims(held, r_ref, s, side)

    piece = (slots, 4, RIM * side, LANES)
    block = pl.BlockSpec((slots, cells, LANES), lambda c: (0, 0, c))
    return pl.pallas_call(
        kernel,
        grid=(n_chunk,),
        in_specs=[
            block,
            block,
            pl.BlockSpec((slots, cells, LANES), lambda c: (0, 0, 0)),
            pl.BlockSpec((3, 8, LANES), lambda c: (0, 0, c)),
        ],
        out_specs=[block, pl.BlockSpec((1,) + piece, lambda c: (c, 0, 0, 0, 0))],
        scratch_shapes=[pltpu.VMEM((cells, LANES), F32)],
        out_shape=[
            jax.ShapeDtypeStruct((slots, cells, channels), F32),
            jax.ShapeDtypeStruct((n_chunk,) + piece, BF),
        ],
        compiler_params=pltpu.CompilerParams(vmem_limit_bytes=32 << 20),
        name="conv_gradient",
    )(d_shaped, conv_out, mask_lanes, coefs)


def add_taps(x_ref, m_ref, d_ref, h_ref, o_ref, pad, sums, slots, side):
    slot = pl.program_id(1)
    for i in range(side):
        pad[pl.ds((i + RIM) * PITCH + 8, side), :] = x_ref[0, i].astype(F32) * m_ref[0, pl.ds(i * side, side), :]
    fill_halo(pad, lambda k: h_ref[0, 0, k].astype(F32), side)

    @pl.when(slot == 0)
    def _():
        sums[...] = jnp.zeros_like(sums)

    for block in range(side // 8):
        grads = [d_ref[0, pl.ds(i * side + 8 * block, 8), :] for i in range(side)]
        total = grads[0]
        for i in range(1, side):
            total = total + grads[i]
        sums[49] += total
        for b in range(7):
            taps = [None] * 7
            for r in range(side + 2 * RIM):
                window = pad[pl.ds(r * PITCH + 8 - RIM + b + 8 * block, 8), :]
                for a in range(7):
                    i = r - a
                    if 0 <= i < side:
                        term = window * grads[i]
                        taps[a] = term if taps[a] is None else taps[a] + term
            for a in range(7):
                sums[7 * a + b] += taps[a]

    @pl.when(slot == slots - 1)
    def _():
        at = pl.multiple_of(pl.program_id(0) * LANES, LANES)
        o_ref[pl.ds(0, 50), pl.ds(at, LANES)] = jnp.sum(sums[...], axis=1)


def conv_backward(grid, d_conv, halos, cotangent, mask_lanes, taps, weight_lanes, change, small):
    slots, side, _, channels = cotangent.shape
    n_chunk = halos.shape[0]
    cells = side * side
    pairs, rows, cols = change.shape
    side_a, side_b = grid.size["a"], grid.size["b"]
    part = rows // side_b
    piece = part // side_a
    hops = [(dim, 1 << i) for dim in ("c", "x", "b", "a") for i in range((grid.size[dim] - 1).bit_length())]
    total = pairs * (side_a * (side_b - 1) + (side_a - 1)) + len(hops)
    last = n_chunk * slots - 1

    def kernel(
        d_ref, g_ref, m_ref, w_ref, l_ref, h_ref, c_ref, s_ref, o_ref, change_ref, small_ref,
        pad, mine, from_b, from_a, heard, send, recv, load_sems,
    ):
        own = grid.own()
        step = pl.program_id(0) * slots + pl.program_id(1)
        copies = Copies(send, recv)
        own_a, own_b = own["a"], own["b"]
        half = lambda b: pl.ds(pl.multiple_of(b * part, 16), part)
        row_of = lambda a, b: pl.ds(pl.multiple_of((b * side_a + a) * piece, 16), piece)
        part_row = lambda a: pl.ds(pl.multiple_of(a * piece, 16), piece)
        turns = [*range(1, side_a), 0]
        firsts, seconds, loads = {}, {}, []
        for m in range(pairs):
            for k in turns:
                a = own_a ^ k
                firsts[k, m] = [
                    copies.make(
                        c_ref.at[m, row_of(a, own_b ^ j)], from_b.at[j - 1, m, part_row(a)], grid.beside(own, "b", j)
                    )
                    for j in range(1, side_b)
                ]
                if k > 0:
                    seconds[k, m] = copies.make(
                        mine.at[m, part_row(a)], from_a.at[k - 1, m], grid.beside(own, "a", k)
                    )
            loads.append(pltpu.make_async_copy(c_ref.at[m, half(own_b)], mine.at[m], load_sems.at[m]))

        hop_copies = [
            copies.make(small_ref, heard.at[i], grid.beside(own, dim, k)) for i, (dim, k) in enumerate(hops)
        ]

        def start_turn(i):
            for m in range(pairs):
                for copy in firsts[turns[i], m]:
                    copy.start()

        @pl.when(step == 0)
        def _():
            meet(grid.partners(("a", "b", "x", "c")))
            for load in loads:
                load.start()
            start_turn(0)
            small_ref[...] = s_ref[...]
            hop_copies[0].start()

        for i in range(side):
            pad[pl.ds((i + RIM) * PITCH + 8, side), :] = d_ref[0, pl.ds(i * side, side), :]
        fill_halo(pad, lambda k: h_ref[0, 0, k].astype(F32), side)
        weight = l_ref[...]

        def emit(block, sums):
            for i in range(side):
                at = pl.ds(i * side + 8 * block, 8)
                scaled = weight * g_ref[0, i, pl.ds(8 * block, 8), :].astype(F32)
                o_ref[0, at, :] = m_ref[0, at, :] * (scaled + sums[i])

        conv_pass(pad, side, lambda a, b: w_ref[7 * (6 - a) + 6 - b], emit)

        for i, k in enumerate(turns):

            @pl.when(step == min(last, 7 + 6 * i))
            def _():
                for m in range(pairs):
                    if i == 0:
                        loads[m].wait()
                    for copy in firsts[k, m]:
                        copy.wait()
                if i + 1 < side_a:
                    start_turn(i + 1)
                for m in range(pairs):
                    rows_here = part_row(own_a ^ k)
                    sources = [from_b.at[j, m, rows_here] for j in range(side_b - 1)]
                    add_rows(mine.at[m, rows_here], sources, piece)
                    if k > 0:
                        seconds[k, m].start()

        for i, copy in enumerate(hop_copies):

            @pl.when(step == min(last, 2 + 3 * i))
            def _():
                copy.wait()
                small_ref[...] = small_ref[...] + heard[i]
                if i + 1 < len(hops):
                    hop_copies[i + 1].start()

        @pl.when(step == last)
        def _():
            for m in range(pairs):
                for k in range(1, side_a):
                    seconds[k, m].wait()
                value = mine[m, part_row(own_a)].astype(F32)
                for k in range(side_a - 1):
                    value = value + from_a[k, m].astype(F32)
                change_ref[m] = value

    return pl.pallas_call(
        kernel,
        grid=(n_chunk, slots),
        in_specs=[
            pl.BlockSpec((1, cells, LANES), lambda c, s: (s, 0, c)),
            pl.BlockSpec((1, side, side, LANES), lambda c, s: (s, 0, 0, c)),
            pl.BlockSpec((1, cells, LANES), lambda c, s: (s, 0, 0)),
            pl.BlockSpec((50, 8, LANES), lambda c, s: (0, 0, c)),
            pl.BlockSpec((8, LANES), lambda c, s: (0, 0)),
            halo_block(halos),
            pl.BlockSpec(memory_space=pl.ANY),
            pl.BlockSpec(small.shape, lambda c, s: (0, 0)),
        ],
        out_specs=[
            pl.BlockSpec((1, cells, LANES), lambda c, s: (s, 0, c)),
            pl.BlockSpec((pairs, piece, cols), lambda c, s: (0, 0, 0)),
            pl.BlockSpec(small.shape, lambda c, s: (0, 0)),
        ],
        scratch_shapes=[
            pltpu.VMEM(((side + 2 * RIM) * PITCH, LANES), F32),
            pltpu.VMEM((pairs, part, cols), BF),
            pltpu.VMEM((side_b - 1, pairs, part, cols), BF),
            pltpu.VMEM((side_a - 1, pairs, piece, cols), BF),
            pltpu.VMEM((len(hops),) + small.shape, F32),
            pltpu.SemaphoreType.DMA((total,)),
            pltpu.SemaphoreType.DMA((total,)),
            pltpu.SemaphoreType.DMA((pairs,)),
        ],
        out_shape=[
            jax.ShapeDtypeStruct((slots, cells, channels), F32),
            jax.ShapeDtypeStruct((pairs, piece, cols), F32),
            jax.ShapeDtypeStruct(small.shape, F32),
        ],
        compiler_params=remote_params(4, 48),
        name="conv_backward",
    )(d_conv, cotangent, mask_lanes, taps, weight_lanes, halos, change, small)


def spread_lanes(value, parts, width):
    rows, channels = value.shape
    run = channels // parts
    if run == width:
        return value
    gap = jnp.zeros((rows, width - run), value.dtype)
    pieces = []
    for t in range(parts):
        pieces += [value[:, t * run : (t + 1) * run], gap]
    return jnp.concatenate(pieces, 1)


def close_lanes(value, parts, run):
    width = value.shape[1] // parts
    if run == width:
        return value
    return jnp.concatenate([value[:, t * width : t * width + run] for t in range(parts)], 1)


def row_block(rows):
    return 3 * LANES if rows % (3 * LANES) == 0 else LANES


def arranged(value, gap_ref, turned_ref, sum_ref, first, parts, width):
    low = value.astype(BF).astype(F32)
    gap_ref[...] = spread_lanes(low, parts, width).astype(BF)
    turned_ref[...] = low.T.astype(BF)

    @pl.when(first)
    def _():
        sum_ref[...] = jnp.zeros_like(sum_ref)

    sum_ref[...] += jnp.sum(low, axis=0, keepdims=True)


def arrange(body, args, specs, rows, channels, parts, width, name):
    step = 3 * LANES if rows % (3 * LANES) == 0 else LANES

    def kernel(*refs):
        given, (gap_ref, turned_ref, sum_ref) = refs[: len(args)], refs[len(args) :]
        arranged(body(*given), gap_ref, turned_ref, sum_ref, pl.program_id(0) == 0, parts, width)

    return pl.pallas_call(
        kernel,
        grid=(rows // step,),
        in_specs=specs(step),
        out_specs=[
            pl.BlockSpec((step, parts * width), lambda i: (i, 0)),
            pl.BlockSpec((channels, step), lambda i: (0, i)),
            pl.BlockSpec((1, channels), lambda i: (0, 0)),
        ],
        out_shape=[
            jax.ShapeDtypeStruct((rows, parts * width), BF),
            jax.ShapeDtypeStruct((channels, rows), BF),
            jax.ShapeDtypeStruct((1, channels), F32),
        ],
        compiler_params=pltpu.CompilerParams(vmem_limit_bytes=48 << 20),
        name=name,
    )(*args)


def feed_forward(inverse, shaped, shaped_t, d_branch, d_branch_t, hidden_bias, weights, grad_rows):
    rows, depth = shaped.shape
    channels = shaped_t.shape[0]
    half, _, cols = hidden_bias.shape
    pairs, owners = weights.shape[:2]
    per_owner = 2 * pairs
    tile_rows = 3 * LANES if rows % (3 * LANES) == 0 else LANES

    def kernel(inv_ref, s_ref, st_ref, d_ref, dt_ref, hb_ref, w_ref, branch_ref, ds_ref, grad_ref, bias_ref, *scratch):
        packed, first, second, act, dpre, grads, sems, out_sem = scratch
        step = pl.program_id(0)

        def where(slot):
            owner, inside = slot // per_owner, slot % per_owner
            return owner, inside // 2, inside % 2

        def fetch(h, buffer):
            copies = []
            for which in range(2):
                owner, pair, _ = where(inv_ref[h + which * half])
                copies.append(
                    pltpu.make_async_copy(w_ref.at[pair, owner], packed.at[buffer, which], sems.at[buffer, which])
                )
            return copies

        @pl.when(step == 0)
        def _():
            for copy in fetch(0, 0):
                copy.start()
            if grad_rows > channels:
                rest = grad_rows - channels
                grads[:, :, pl.ds(channels, rest), :] = jnp.zeros(grads.shape[:2] + (rest, 2 * cols), BF)

        @pl.when(step + 1 < half)
        def _():
            for copy in fetch(step + 1, (step + 1) % 2):
                copy.start()

        now = step % 2
        slots = [where(inv_ref[step + which * half]) for which in range(2)]
        waits = fetch(step, now)
        for which, held in enumerate((first, second)):
            waits[which].wait()
            for parity in range(2):

                @pl.when(slots[which][2] == parity)
                def _():
                    held[...] = packed[now, which, :, parity * cols : (parity + 1) * cols]

        hidden = hb_ref[0]

        @pl.when(step == 0)
        def _():
            branch_ref[...] = jnp.zeros_like(branch_ref)
            ds_ref[...] = jnp.zeros_like(ds_ref)

        total = jnp.zeros((1, cols), F32)
        across = (((1,), (1,)), ((), ()))
        for i in range(rows // tile_rows):
            at = pl.ds(i * tile_rows, tile_rows)
            pre = jnp.dot(s_ref[at, :], first[...], preferred_element_type=F32) + hidden
            d_act = jnp.dot(d_ref[at, :], second[...], preferred_element_type=F32)
            square = pre * pre
            bend = jnp.tanh(ROOT * pre * (1.0 + CUBE * square))
            half_up = 0.5 * (1.0 + bend)
            low = (pre * half_up).astype(BF)
            slope = half_up + (0.5 * ROOT) * pre * (1.0 - bend * bend) * (1.0 + (3.0 * CUBE) * square)
            back = (d_act * slope).astype(BF)
            act[at, :] = low
            dpre[at, :] = back
            total = total + jnp.sum(back.astype(F32), axis=0, keepdims=True)
            out_add = lax.dot_general(low, second[...], across, preferred_element_type=F32)
            in_add = lax.dot_general(back, first[...], across, preferred_element_type=F32)

            branch_ref[at, :] += out_add
            ds_ref[at, :] += in_add

        bias_ref[0] = total
        for which, (left, right) in enumerate(((st_ref, dpre), (dt_ref, act))):
            owner, pair, half_of_pair = slots[which]
            value = jnp.dot(left[...], right[...], preferred_element_type=F32).astype(BF)
            for parity in range(2):

                @pl.when(half_of_pair == parity)
                def _():
                    at = (owner // 2) * pairs + pair
                    grads[owner % 2, at, pl.ds(0, channels), parity * cols : (parity + 1) * cols] = value

        @pl.when(step == half - 1)
        def _():
            out = pltpu.make_async_copy(grads, grad_ref, out_sem.at[0])
            out.start()
            out.wait()

    whole = lambda *shape: pl.BlockSpec(shape, lambda h, *_: (0,) * len(shape))
    line = pl.BlockSpec((1, 1, cols), lambda h, *_: (h, 0, 0))
    grad_shape = (2, owners // 2 * pairs, grad_rows, 2 * cols)
    return pl.pallas_call(
        kernel,
        grid_spec=pltpu.PrefetchScalarGridSpec(
            num_scalar_prefetch=1,
            grid=(half,),
            in_specs=[
                whole(rows, depth),
                whole(channels, rows),
                whole(rows, depth),
                whole(channels, rows),
                line,
                pl.BlockSpec(memory_space=pl.ANY),
            ],
            out_specs=[whole(rows, depth), whole(rows, depth), pl.BlockSpec(memory_space=pl.ANY), line],
            scratch_shapes=[
                pltpu.VMEM((2, 2, depth, 2 * cols), BF),
                pltpu.VMEM((depth, cols), BF),
                pltpu.VMEM((depth, cols), BF),
                pltpu.VMEM((rows, cols), BF),
                pltpu.VMEM((rows, cols), BF),
                pltpu.VMEM(grad_shape, BF),
                pltpu.SemaphoreType.DMA((2, 2)),
                pltpu.SemaphoreType.DMA((1,)),
            ],
        ),
        out_shape=[
            jax.ShapeDtypeStruct((rows, depth), F32),
            jax.ShapeDtypeStruct((rows, depth), F32),
            jax.ShapeDtypeStruct(grad_shape, BF),
            jax.ShapeDtypeStruct((half, 1, cols), F32),
        ],
        cost_estimate=pl.CostEstimate(
            flops=12 * rows * channels * half * cols, bytes_accessed=40 << 20, transcendentals=rows * half * cols
        ),
        compiler_params=pltpu.CompilerParams(vmem_limit_bytes=63 << 20),
        name="feed_forward",
    )(inverse, shaped, shaped_t, d_branch, d_branch_t, hidden_bias, weights)


def close_out(branch, d_shaped, inputs, conv_out, mask_lanes, out_bias, parts, run):
    rows, channels = inputs.shape
    depth = branch.shape[1]
    step = 3 * LANES if rows % (3 * LANES) == 0 else LANES

    def kernel(b_ref, d_ref, x_ref, v_ref, m_ref, o_ref, out_ref, ds_ref, sum_ref):
        branch_here = close_lanes(b_ref[...], parts, run) + o_ref[...]
        out_ref[...] = (m_ref[:, :1] * (x_ref[...].astype(F32) + branch_here)).astype(BF)
        grads = close_lanes(d_ref[...], parts, run)
        ds_ref[...] = grads

        @pl.when(pl.program_id(0) == 0)
        def _():
            sum_ref[...] = jnp.zeros_like(sum_ref)

        sum_ref[0] += jnp.sum(grads, axis=0, keepdims=True)
        sum_ref[1] += jnp.sum(grads * v_ref[...], axis=0, keepdims=True)

    line = lambda n: pl.BlockSpec((step, n), lambda i: (i, 0))
    return pl.pallas_call(
        kernel,
        grid=(rows // step,),
        in_specs=[
            line(depth),
            line(depth),
            line(channels),
            line(channels),
            line(LANES),
            pl.BlockSpec((1, channels), lambda i: (0, 0)),
        ],
        out_specs=[line(channels), line(channels), pl.BlockSpec((2, 1, channels), lambda i: (0, 0, 0))],
        out_shape=[
            jax.ShapeDtypeStruct((rows, channels), BF),
            jax.ShapeDtypeStruct((rows, channels), F32),
            jax.ShapeDtypeStruct((2, 1, channels), F32),
        ],
        compiler_params=pltpu.CompilerParams(vmem_limit_bytes=60 << 20),
        name="close_out",
    )(branch, d_shaped, inputs, conv_out, mask_lanes, out_bias)


def halves(value):
    high = value.astype(BF)
    return high, (value - high.astype(F32)).astype(BF)


def product(left, right, contract):
    dims = (contract, ((), ()))
    total = None
    for i, a in enumerate(left):
        for j, b in enumerate(right):
            if i + j < 2:
                term = lax.dot_general(a, b, dims, preferred_element_type=F32)
                total = term if total is None else total + term
    return total


def rotate(owned, left_basis, column_basis, moment_one, moment_two, correction, grid, width):
    slots, channels, run = left_basis.shape
    cols = column_basis.shape[1]
    pairs = slots // 2
    side_a, side_b = grid.size["a"], grid.size["b"]
    n_tile = grid.n_tile

    def kernel(f_ref, g_ref, l_ref, c_ref, one_ref, two_ref, first_ref, second_ref, o_ref):
        factor = f_ref[0]
        changes = []
        for p in range(2):
            grad = g_ref[0, pl.ds(0, channels), p * cols : (p + 1) * cols]
            left = halves(l_ref[p])
            column = halves(c_ref[p])
            rotated = product(left, (grad,), ((0,), (0,)))
            rotated = product(halves(rotated), column, ((1,), (0,)))
            first = decay_rate * one_ref[p] + (1.0 - decay_rate) * rotated
            second = decay_rate * two_ref[p] + (1.0 - decay_rate) * rotated * rotated
            first_ref[p] = first
            second_ref[p] = second
            direction = first * factor / (jnp.sqrt(second * factor) + adam_eps)
            turned = product(halves(direction), column, ((1,), (1,)))
            changes.append(product(left, halves(turned), ((1,), (0,))))
        change = jnp.concatenate(changes, 1)
        gap = jnp.zeros((width - run, 2 * cols), F32)
        for t in range(n_tile):
            piece = jnp.concatenate([change[t * run : (t + 1) * run], gap], 0)
            place = (t % side_b) * side_a + t // side_b
            o_ref[0, pl.ds(place * width, width), :] = piece.astype(BF)

    pair = lambda *shape: pl.BlockSpec(shape, lambda m: (m,) + (0,) * (len(shape) - 1))
    return pl.pallas_call(
        kernel,
        grid=(pairs,),
        in_specs=[
            pl.BlockSpec(memory_space=pltpu.SMEM),
            pair(1, owned.shape[1], 2 * cols),
            pair(2, channels, run),
            pair(2, cols, cols),
            pair(2, run, cols),
            pair(2, run, cols),
        ],
        out_specs=[pair(2, run, cols), pair(2, run, cols), pair(1, n_tile * width, 2 * cols)],
        out_shape=[
            jax.ShapeDtypeStruct(moment_one.shape, F32),
            jax.ShapeDtypeStruct(moment_one.shape, F32),
            jax.ShapeDtypeStruct((pairs, n_tile * width, 2 * cols), BF),
        ],
        compiler_params=pltpu.CompilerParams(vmem_limit_bytes=60 << 20),
        name="rotate",
    )(1.0 / correction.reshape(1), owned, left_basis, column_basis, moment_one, moment_two)


def up_to(value, unit):
    return -(-value // unit) * unit


def pack_pairs(value):
    slots, rows, cols = value.shape
    return value.reshape(slots // 2, 2, rows, cols).transpose(0, 2, 1, 3).reshape(slots // 2, rows, 2 * cols)


def unpack_pairs(value):
    pairs, rows, cols = value.shape
    return value.reshape(pairs, rows, 2, cols // 2).transpose(0, 2, 1, 3).reshape(2 * pairs, rows, cols // 2)


def per_device(
    grid,
    inputs,
    cotangent,
    master,
    moment_one,
    moment_two,
    left_basis,
    column_basis,
    small_params,
    small_first,
    small_second,
    land_mask,
    tile_count,
    neighbours,
    block_order,
    cell_weight,
    step_count,
):
    position = lax.axis_index("tile")
    sample = lax.axis_index("opt")
    inputs, cotangent = inputs[0], cotangent[0]
    slots, side, _, channels = inputs.shape
    cells = side * side
    rows = slots * cells
    n_tile = grid.n_tile
    n_chunk = -(-channels // LANES)
    per_group = channels // GROUPS
    per_owner, run, cols = master.shape
    pairs = per_owner // 2
    block_total = block_order.shape[0]
    half = block_total // 2
    width = up_to(run, 16)

    live = (jnp.arange(slots) < tile_count[position]).astype(F32)
    mask = (land_mask.astype(F32) * live[:, None, None]).reshape(slots, cells)
    mask_lanes = jnp.broadcast_to(mask[:, :, None], (slots, cells, LANES))
    flat_mask = mask_lanes.reshape(rows, LANES)
    taps = jnp.broadcast_to(small_params[:50, None, :], (50, 8, channels))

    weights_float = cell_weight.astype(F32)
    sample_weight = weights_float[sample] * weights_float.shape[0] / jnp.sum(weights_float)
    weight_lanes = jnp.broadcast_to(sample_weight, (8, LANES))
    weight_row = jnp.broadcast_to(sample_weight, (1, LANES))

    low_master = jnp.pad(pack_pairs(master.astype(BF)), ((0, 0), (0, width - run), (0, 0)))
    rims = rims_of_input(inputs, mask_lanes)
    halos, weights, all_neighbours, conv_out, sums, d_branch, d_branch_t, d_out_bias = exchange_forward(
        grid,
        rims,
        low_master,
        neighbours,
        inputs,
        mask_lanes,
        taps,
        cotangent.reshape(rows, channels),
        flat_mask,
        weight_row,
        width,
    )

    sums = jnp.sum(sums, axis=(0, 2))
    occupied = jnp.broadcast_to(jnp.sum(mask), (1, channels))
    sums = tile_total(grid, jnp.concatenate([sums, occupied], 0), 5)
    counted = sums[2, 0] * per_group
    by_group = sums[:2].reshape(2, GROUPS, per_group).sum(2)
    group_mean = by_group[0] / counted
    variance = by_group[1] / counted - group_mean * group_mean
    inv_std = jnp.repeat(lax.rsqrt(variance + epsilon), per_group)
    mean = jnp.repeat(group_mean, per_group)
    gain, shift = small_params[50], small_params[51]
    norm_coefs = jnp.stack([inv_std, mean * inv_std, gain, shift])

    def shaped_body(v_ref, c_ref):
        normed = v_ref[...] * c_ref[0:1] - c_ref[1:2]
        return normed * c_ref[2:3] + c_ref[3:4]

    flat_conv = conv_out.reshape(rows, channels)
    shaped, shaped_t, _ = arrange(
        shaped_body,
        (flat_conv, norm_coefs),
        lambda step: [
            pl.BlockSpec((step, channels), lambda i: (i, 0)),
            pl.BlockSpec((4, channels), lambda i: (0, 0)),
        ],
        rows,
        channels,
        n_tile,
        width,
        "arrange_shaped",
    )

    block_ids = jnp.arange(block_total, dtype=jnp.int32)
    inverse = jnp.sum(
        jnp.where(block_order[None, :] == block_ids[:, None], block_ids[None, :], 0), axis=1
    ).astype(jnp.int32)
    hidden_bias = small_params[53:57].reshape(half, 1, cols)
    branch, d_shaped, grads, d_hidden = feed_forward(
        inverse, shaped, shaped_t, d_branch, d_branch_t, hidden_bias, weights, n_tile * width
    )
    block_output, d_shaped, d_sums = close_out(
        branch, d_shaped, inputs.reshape(rows, channels), flat_conv, flat_mask, small_params[52:53], n_tile, run
    )

    d_shift = d_sums[0, 0]
    d_gain = inv_std * (d_sums[1, 0] - mean * d_shift)
    parts = tile_total(grid, jnp.stack([gain * d_shift, gain * d_gain]), 6)
    parts = jnp.repeat(parts.reshape(2, GROUPS, per_group).sum(2) / counted, per_group, axis=1)
    grad_coefs = jnp.stack(
        [
            inv_std * gain,
            inv_std * (parts[0] - mean * inv_std * parts[1]),
            inv_std * inv_std * parts[1],
        ]
    )
    d_conv, grad_rims = conv_gradient(
        d_shaped.reshape(slots, cells, channels),
        conv_out,
        mask_lanes,
        jnp.broadcast_to(grad_coefs[:, None, :], (3, 8, channels)),
        side,
    )
    small = jnp.concatenate([d_gain[None], d_shift[None], d_out_bias, d_hidden.reshape(4, channels)], 0)
    grad_halos, owned, d_small = exchange_backward(
        grid, grad_rims, grads, all_neighbours, inputs, mask_lanes, d_conv, halos, small
    )

    correction = 1.0 - jnp.power(F32(decay_rate), step_count[0].astype(F32))

    first_new, second_new, change = rotate(
        owned, left_basis, column_basis, moment_one, moment_two, correction, grid, width
    )
    input_grad, change, d_small = conv_backward(
        grid, d_conv, grad_halos, cotangent, mask_lanes, taps, weight_lanes, change, d_small
    )
    change = unpack_pairs(change[:, :run])
    d_small = d_small[: small_params.shape[0], :channels]
    small_one = decay_rate * small_first + (1.0 - decay_rate) * d_small
    small_two = decay_rate * small_second + (1.0 - decay_rate) * d_small * d_small
    new_small = small_params - small_rate * (small_one / correction) / (
        jnp.sqrt(small_two / correction) + adam_eps
    )
    new_master = master - 0.5 / math.sqrt(channels) * change
    return (
        block_output.reshape((1,) + inputs.shape),
        input_grad.reshape((1,) + inputs.shape),
        new_master,
        new_master.astype(BF),
        first_new,
        second_new,
        new_small,
        small_one,
        small_two,
    )


def solution(mesh):
    grid = Grid(mesh.shape["tile"], mesh.shape["opt"])

    def step(*args):
        return per_device(grid, *args)

    return jax.shard_map(
        step,
        mesh=mesh,
        in_specs=(
            P("opt", "tile", None, None, None),
            P("opt", "tile", None, None, None),
            P("opt", "tile", None),
            P("opt", "tile", None),
            P("opt", "tile", None),
            P("opt", None, "tile"),
            P("opt", None, None),
            P(),
            P(),
            P(),
            P("tile", None, None),
            P(),
            P("tile", None),
            P(),
            P(),
            P(),
        ),
        out_specs=(
            P("opt", "tile", None, None, None),
            P("opt", "tile", None, None, None),
            P("opt", "tile", None),
            P("opt", "tile", None),
            P("opt", "tile", None),
            P("opt", "tile", None),
            P(),
            P(),
            P(),
        ),
        check_vma=False,
    )
```

```python
import math

import jax
import jax.numpy as jnp
from jax import lax
from jax.experimental import pallas as pl
from jax.experimental.pallas import tpu as pltpu
from jax.sharding import PartitionSpec as P

GROUPS = 16
LANES = 128
RIM = 3
PITCH = 40
BF = jnp.bfloat16
F32 = jnp.float32

highest = lax.Precision.HIGHEST
epsilon = 1e-05
adam_eps = 1e-08
decay_rate = 0.5
small_rate = 0.05
ROOT = 0.7978845608028654
CUBE = 0.044715


class Grid:
    def __init__(self, n_tile, n_opt):
        b = n_tile // 4
        self.n_tile, self.n_opt = n_tile, n_opt
        self.size = {"a": 4, "b": b, "x": n_opt // 2, "c": 2}

    def own(self):
        t, o = lax.axis_index("tile"), lax.axis_index("opt")
        b = self.size["b"]
        return {"a": t // b, "b": t % b, "x": o // 2, "c": o % 2}

    def at(self, place):
        return place["a"] * self.size["b"] + place["b"], place["x"] * 2 + place["c"]

    def partners(self, dims):
        own = self.own()
        found = []
        for dim in dims:
            if dim == "tile":
                t, o = self.at(own)
                found += [(t ^ k, o) for k in range(1, self.n_tile)]
            else:
                found += [self.beside(own, dim, k) for k in range(1, self.size[dim])]
        return found

    def beside(self, own, dim, k):
        return self.at({**own, dim: own[dim] ^ k})


def meet(devices):
    barrier = pltpu.get_barrier_semaphore()
    for device in devices:
        pl.semaphore_signal(barrier, inc=1, device_id=device, device_id_type=pl.DeviceIdType.MESH)
    pl.semaphore_wait(barrier, len(devices))


class Copies:
    def __init__(self, send_sems, recv_sems):
        self.sems = send_sems, recv_sems
        self.used = 0

    def make(self, src, dst, device):
        i = self.used
        self.used += 1
        return pltpu.make_async_remote_copy(
            src_ref=src,
            dst_ref=dst,
            send_sem=self.sems[0].at[i],
            recv_sem=self.sems[1].at[i],
            device_id=device,
            device_id_type=pl.DeviceIdType.MESH,
        )

    def start(self, src, dst, device):
        copy = self.make(src, dst, device)
        copy.start()
        return copy


def remote_params(number, mib):
    return pltpu.CompilerParams(collective_id=number, has_side_effects=True, vmem_limit_bytes=mib << 20)


def add_rows(target, sources, rows, step=16):
    @pl.loop(0, rows // step)
    def _(i):
        at = pl.ds(pl.multiple_of(i * step, step), step)
        total = target[at, :].astype(F32)
        for source in sources:
            total = total + source[at, :].astype(F32)
        target[at, :] = total.astype(BF)


def store_rims(src, outs, slot, side):
    outs[0, slot, 0] = src[pl.ds(0, RIM * side), :].astype(BF)
    outs[0, slot, 1] = src[pl.ds((side - RIM) * side, RIM * side), :].astype(BF)
    for e in range(RIM):
        rows = pl.ds(e * side, side)
        outs[0, slot, 2, rows] = src[pl.ds(e, side, stride=side), :].astype(BF)
        outs[0, slot, 3, rows] = src[pl.ds(side - RIM + e, side, stride=side), :].astype(BF)


def rims_of_input(inputs, mask_lanes):
    slots, side, _, channels = inputs.shape
    n_chunk = -(-channels // LANES)

    def kernel(x_ref, m_ref, o_ref, cells):
        for s in range(slots):
            for i in range(side):
                cells[pl.ds(i * side, side), :] = (
                    x_ref[s, i].astype(F32) * m_ref[s, pl.ds(i * side, side), :]
                )
            store_rims(cells, o_ref, s, side)

    return pl.pallas_call(
        kernel,
        grid=(n_chunk,),
        in_specs=[
            pl.BlockSpec((slots, side, side, LANES), lambda c: (0, 0, 0, c)),
            pl.BlockSpec((slots, side * side, LANES), lambda c: (0, 0, 0)),
        ],
        out_specs=pl.BlockSpec((1, slots, 4, RIM * side, LANES), lambda c: (c, 0, 0, 0, 0)),
        out_shape=jax.ShapeDtypeStruct((n_chunk, slots, 4, RIM * side, LANES), BF),
        scratch_shapes=[pltpu.VMEM((side * side, LANES), F32)],
        compiler_params=pltpu.CompilerParams(vmem_limit_bytes=32 << 20),
        name="rims_of_input",
    )(inputs, mask_lanes)


class HaloExchange:
    def __init__(self, grid, n_chunk, slots, side):
        self.grid, self.n_chunk, self.slots, self.side = grid, n_chunk, slots, side
        self.count = 2 * (grid.n_tile - 1)

    def scratch(self):
        n, s, band = self.grid.n_tile, self.slots, RIM * self.side
        return [
            pltpu.VMEM((n, s, 4, band, LANES), BF),
            pltpu.VMEM((n, s, 5, band, LANES), BF),
            pltpu.SemaphoreType.DMA((2,)),
        ]

    def halo_shape(self):
        return jax.ShapeDtypeStruct((self.n_chunk, self.slots, 5, RIM * self.side, LANES), BF)

    def plan(self, copies, rims, arrived, picked, halos, local):
        t, o = self.grid.at(self.grid.own())
        self.t, self.arrived, self.picked = t, arrived, picked
        own_chunk = jnp.minimum(t, self.n_chunk - 1)
        self.first, self.second = [], []
        for k in range(1, self.grid.n_tile):
            to = t ^ k
            source = jnp.minimum(to, self.n_chunk - 1)
            self.first.append((to, copies.make(rims.at[source], arrived.at[t], (to, o))))
            self.second.append((to, copies.make(picked.at[to], halos.at[own_chunk], (to, o))))
        self.own_copy = pltpu.make_async_copy(rims.at[own_chunk], arrived.at[t], local.at[0])
        self.back_copy = pltpu.make_async_copy(picked.at[t], halos.at[own_chunk], local.at[1])

    def send_rims(self):
        for to, copy in self.first:

            @pl.when(to < self.n_chunk)
            def _():
                copy.start()

        self.own_copy.start()

    def pick_and_send(self, neighbours):
        grid, slots, side = self.grid, self.slots, self.side
        t, arrived, picked = self.t, self.arrived, self.picked
        self.own_copy.wait()
        for _, copy in self.first:

            @pl.when(t < self.n_chunk)
            def _():
                copy.wait_recv()

        @pl.when(t < self.n_chunk)
        def _():
            @pl.loop(0, grid.n_tile * slots)
            def _(d):
                def rim(direction, which):
                    slot = neighbours(d, direction)
                    at = jnp.maximum(slot, 0)
                    value = arrived[at // slots, at % slots, which].astype(F32)
                    return jnp.where(slot >= 0, value, 0.0)

                to_tile, to_slot = d // slots, d % slots
                for to, (direction, which) in enumerate(((1, 1), (6, 0), (3, 3), (4, 2))):
                    picked[to_tile, to_slot, to] = rim(direction, which).astype(BF)
                rows = []
                for direction, which, first in ((0, 1, side - RIM), (2, 1, 0), (5, 0, side - RIM), (7, 0, 0)):
                    value = rim(direction, which)
                    rows += [value[e * side + first : e * side + first + RIM] for e in range(RIM)]
                    rows.append(jnp.zeros((16 - RIM * RIM, LANES), F32))
                rows.append(jnp.zeros((RIM * side - 64, LANES), F32))
                picked[to_tile, to_slot, 4] = jnp.concatenate(rows, 0).astype(BF)

        for _, copy in self.second:

            @pl.when(t < self.n_chunk)
            def _():
                copy.start()

        @pl.when(t < self.n_chunk)
        def _():
            self.back_copy.start()

    def finish(self):
        t = self.t

        @pl.when(t < self.n_chunk)
        def _():
            self.back_copy.wait()

        for to, copy in self.first:

            @pl.when(to < self.n_chunk)
            def _():
                copy.wait_send()

        for to, copy in self.second:

            @pl.when(to < self.n_chunk)
            def _():
                copy.wait_recv()

            @pl.when(t < self.n_chunk)
            def _():
                copy.wait_send()


class WeightGather:
    def __init__(self, grid, pairs, width):
        self.grid, self.pairs, self.width = grid, pairs, width
        self.count = pairs * (grid.n_tile * grid.n_opt + 2)

    def plan(self, copies, packed, gathered, local):
        grid, width = self.grid, self.width
        own = grid.own()
        self.middle = (own["a"] == 1) | (own["a"] == 2)

        def place(m, rel):
            t, o = grid.at({d: own[d] ^ rel.get(d, 0) for d in own})
            return gathered.at[m, o, pl.ds(pl.multiple_of(t * width, width), width)]

        def send(m, rel, dim, k):
            source = packed.at[m] if not rel else place(m, rel)
            return copies.make(source, place(m, rel), grid.beside(own, dim, k))

        self.keeps = [pltpu.make_async_copy(packed.at[m], place(m, {}), local.at[m]) for m in range(self.pairs)]
        self.first, self.chain, self.onward, arrivals = [], {}, {}, []
        for m in range(self.pairs):
            self.chain["near", m] = send(m, {}, "a", 1)
            self.chain["over", m] = send(m, {}, "a", 3)
            self.chain["over2", m] = send(m, {"a": 1}, "a", 3)
            self.chain["out", m] = send(m, {"a": 3}, "a", 1)
            self.chain["out2", m] = send(m, {"a": 2}, "a", 1)
            order = ("x", "b", "c") if m % 2 == 0 else ("b", "x", "c")

            def spread(rel, left):
                self.onward[m, tuple(rel.items())] = sends = []
                for i, dim in enumerate(left):
                    for k in range(1, grid.size[dim]):
                        copy = send(m, rel, dim, k)
                        sends.append(copy)
                        child = {**rel, dim: k}
                        arrivals.append((m, child, copy))
                        spread(child, left[i + 1 :])

            for k in range(4):
                spread({"a": k} if k else {}, order)

        def waves(turn):
            found = [[] for _ in range(6)]
            for m, rel, copy in arrivals:
                found[turn[rel.get("a", 0)] + ("x" in rel) + ("b" in rel)].append((m, rel, copy))
            return [sorted(wave, key=lambda e: "c" in e[1]) for wave in found]

        self.sides = {True: waves({0: 0, 1: 1, 3: 2, 2: 3}), False: waves({0: 0, 1: 1, 2: 2, 3: 3})}

    def start(self):
        for copy in self.keeps:
            copy.start()
        for m in range(self.pairs):
            self.chain["near", m].start()

            @pl.when(self.middle)
            def _():
                self.chain["over", m].start()

            self.pass_on(m, {})

    def pass_on(self, m, rel):
        for copy in self.onward[m, tuple(rel.items())]:
            copy.start()

    def run(self, wave):
        along = {True: {1: ("near", 1, "over2"), 2: ("over", 3, "out"), 3: ("over2", 2, "out2")}}
        along[False] = {1: ("near", 1, None), 2: ("out", 2, None), 3: ("out2", 3, None)}
        for side in (True, False):

            @pl.when(self.middle == side)
            def _():
                if wave in along[side]:
                    came, k, goes = along[side][wave]
                    for m in range(self.pairs):
                        self.chain[came, m].wait_recv()
                        if goes is not None:
                            self.chain[goes, m].start()
                        self.pass_on(m, {"a": k})
                for m, rel, copy in self.sides[side][wave]:
                    copy.wait_recv()
                    self.pass_on(m, rel)

    def finish(self):
        for copy in self.keeps:
            copy.wait()
        for m in range(self.pairs):
            self.chain["near", m].wait_send()

            @pl.when(self.middle)
            def _():
                for name in ("over", "over2", "out", "out2"):
                    self.chain[name, m].wait_send()

        for sends in self.onward.values():
            for copy in sends:
                copy.wait_send()


def exchange_forward(grid, rims, packed, neighbours, inputs, mask_lanes, taps, cotangent, flat_mask, weight_row, width):
    n_chunk, slots, _, band, _ = rims.shape
    side, channels = inputs.shape[1], inputs.shape[3]
    cells = side * side
    pairs, _, cols = packed.shape
    n_tile = grid.n_tile
    rows = slots * cells
    block = row_block(rows)
    early = rows // block
    halo = HaloExchange(grid, n_chunk, slots, side)
    gather = WeightGather(grid, pairs, packed.shape[1])
    total = halo.count + gather.count + n_tile - 1
    last = early + n_chunk * slots

    def kernel(
        r_ref, p_ref, n_ref, x_ref, m_ref, t_ref, g_ref, f_ref, l_ref,
        halo_ref, w_ref, nbr_ref, conv_ref, sum_ref, gap_ref, turned_ref, bias_ref,
        arrived, picked, local, landed, table, pad, send, recv, locals_w, locals_n,
    ):
        step = pl.program_id(0)
        t, o = grid.at(grid.own())
        copies = Copies(send, recv)
        halo.plan(copies, r_ref, arrived, picked, landed, local)
        gather.plan(copies, p_ref, w_ref, locals_w)
        tables = [copies.make(n_ref, nbr_ref.at[t], (t ^ k, o)) for k in range(1, n_tile)]
        keep = pltpu.make_async_copy(n_ref, nbr_ref.at[t], locals_n.at[0])
        load = pltpu.make_async_copy(nbr_ref, table, locals_n.at[1])
        halo_out = pltpu.make_async_copy(landed, halo_ref, locals_n.at[0])

        @pl.when(step == 0)
        def _():
            meet(grid.partners(("tile", "x", "c")))
            for copy in tables:
                copy.start()
            keep.start()
            halo.send_rims()
            gather.start()

        @pl.when((step > 0) & (step <= early))
        def _():
            value = f_ref[:, :1] * (l_ref[:, :1] * g_ref[...].astype(F32))
            arranged(value, gap_ref, turned_ref, bias_ref, step == 1, n_tile, width)

        @pl.when(step == early)
        def _():
            keep.wait()
            for copy in tables:
                copy.wait()
            load.start()
            load.wait()
            gather.run(0)
            halo.pick_and_send(lambda d, k: table[d // slots, d % slots, k])
            gather.run(1)
            gather.run(2)
            halo.finish()
            halo_out.start()

        for i in range(3):

            @pl.when(step == min(last, early + 3 + 4 * i))
            def _():
                gather.run(3 + i)

        @pl.when(step > early)
        def _():
            at = step - early - 1
            conv_step(
                x_ref, m_ref, t_ref, lambda k: landed[at // slots, at % slots, k].astype(F32), conv_ref, sum_ref, pad, side
            )

        @pl.when(step == last)
        def _():
            gather.finish()
            halo_out.wait()

    conv_at = lambda i: jnp.maximum(i - early - 1, 0)
    row_at = lambda i: jnp.clip(i - 1, 0, early - 1)
    any_space = pl.BlockSpec(memory_space=pl.ANY)
    return pl.pallas_call(
        kernel,
        grid=(last + 1,),
        in_specs=[any_space] * 3
        + [
            pl.BlockSpec((1, side, side, LANES), lambda i: (conv_at(i) % slots, 0, 0, conv_at(i) // slots)),
            pl.BlockSpec((1, cells, LANES), lambda i: (conv_at(i) % slots, 0, 0)),
            pl.BlockSpec((50, 8, LANES), lambda i: (0, 0, conv_at(i) // slots)),
            pl.BlockSpec((block, channels), lambda i: (row_at(i), 0)),
            pl.BlockSpec((block, LANES), lambda i: (row_at(i), 0)),
            pl.BlockSpec((1, LANES), lambda i: (0, 0)),
        ],
        out_specs=[any_space] * 3
        + [
            pl.BlockSpec((1, cells, LANES), lambda i: (conv_at(i) % slots, 0, conv_at(i) // slots)),
            pl.BlockSpec((1, 2, 8, LANES), lambda i: (conv_at(i) % slots, 0, 0, conv_at(i) // slots)),
            pl.BlockSpec((block, n_tile * width), lambda i: (row_at(i), 0)),
            pl.BlockSpec((channels, block), lambda i: (0, row_at(i))),
            pl.BlockSpec((1, channels), lambda i: (0, 0)),
        ],
        out_shape=[
            halo.halo_shape(),
            jax.ShapeDtypeStruct((pairs, grid.n_opt, n_tile * packed.shape[1], cols), BF),
            jax.ShapeDtypeStruct((n_tile,) + neighbours.shape, jnp.int32),
            jax.ShapeDtypeStruct((slots, cells, channels), F32),
            jax.ShapeDtypeStruct((slots, 2, 8, channels), F32),
            jax.ShapeDtypeStruct((rows, n_tile * width), BF),
            jax.ShapeDtypeStruct((channels, rows), BF),
            jax.ShapeDtypeStruct((1, channels), F32),
        ],
        scratch_shapes=halo.scratch()
        + [
            pltpu.VMEM(halo.halo_shape().shape, BF),
            pltpu.SMEM((n_tile,) + neighbours.shape, jnp.int32),
            pltpu.VMEM(((side + 2 * RIM) * PITCH, LANES), F32),
            pltpu.SemaphoreType.DMA((total,)),
            pltpu.SemaphoreType.DMA((total,)),
            pltpu.SemaphoreType.DMA((pairs,)),
            pltpu.SemaphoreType.DMA((2,)),
        ],
        compiler_params=remote_params(1, 63),
        name="exchange_forward",
    )(rims, packed, neighbours, inputs, mask_lanes, taps, cotangent, flat_mask, weight_row)


def exchange_backward(grid, rims, grads, neighbours, inputs, mask_lanes, d_conv, halos, small):
    n_chunk, slots, _, band, _ = rims.shape
    side, channels = inputs.shape[1], inputs.shape[3]
    side_b, side_x = grid.size["b"], grid.size["x"]
    _, blocks, rows, cols = grads.shape
    pairs = blocks // side_x
    part = rows // side_b
    side_a = grid.size["a"]
    piece = part // side_a
    halo = HaloExchange(grid, n_chunk, slots, side)
    hops = [(dim, 1 << i) for dim in ("c", "x", "b", "a") for i in range((grid.size[dim] - 1).bit_length())]
    total = len(hops) + halo.count + blocks + side_a * pairs * side_x * side_b * 2
    total += pairs * (side_a - 1 + 5 + side_a * (side_b - 1))
    last = n_chunk * slots - 1
    small_rows = small.shape[0]
    small_shape = (up_to(50 + small_rows, 8), n_chunk * LANES)

    def kernel(
        r_ref, g_ref, n_ref, x_ref, m_ref, d_ref, h_ref, s_ref, halo_ref, o_ref, t_ref,
        arrived, picked, local, here, core, far, across, pad, sums, got, mine, heard, send, recv, load_sems,
    ):
        own = grid.own()
        own_x, own_b, own_c = own["x"], own["b"], own["c"]
        step = pl.program_id(0) * slots + pl.program_id(1)
        copies = Copies(send, recv)
        halo.plan(copies, r_ref, arrived, picked, halo_ref, local)
        order = [(k, m) for m in range(pairs) for k in range(1, side_x)]
        order += [(0, m) for m in range(pairs - 1, -1, -1)]
        index = lambda k, m: (own_x ^ k) * pairs + m
        own_a = own["a"]
        row_of = lambda a, b: pl.ds(pl.multiple_of((b * side_a + a) * piece, 16), piece)
        part_row = lambda a: pl.ds(pl.multiple_of(a * piece, 16), piece)
        turns = [*range(1, side_a), 0]
        cores, loads = [], []
        for i, (k, m) in enumerate(order):
            at = index(k, m)
            cores.append(copies.make(g_ref.at[1 - own_c, at], core.at[at], grid.beside(own, "c", 1)))
            loads.append(pltpu.make_async_copy(g_ref.at[own_c, at], here.at[at], load_sems.at[i]))
        one, two, one_adds, two_adds = {}, {}, {}, {}
        for m in range(pairs):
            for k in turns:
                a = own_a ^ k
                mine_at = here.at[index(0, m), row_of(a, own_b)]
                across_x = lambda q, b: (
                    copies.make(
                        here.at[index(q, m), row_of(a, b)], far.at[q - 1, m, row_of(a, b)], grid.beside(own, "x", q)
                    )
                )
                across_b = lambda q, j: (
                    copies.make(
                        here.at[index(q, m), row_of(a, own_b ^ j)],
                        across.at[j - 1, index(q, m), part_row(a)],
                        grid.beside(own, "b", j),
                    )
                )
                from_x = lambda b: [far.at[q - 1, m, row_of(a, b)] for q in range(1, side_x)]
                from_b = lambda q: [across.at[j - 1, index(q, m), part_row(a)] for j in range(1, side_b)]
                if m % 2 == 0:
                    one[k, m] = [across_x(q, b) for q in range(1, side_x) for b in range(side_b)]
                    one_adds[k, m] = [(here.at[index(0, m), row_of(a, b)], from_x(b)) for b in range(side_b)]
                    two[k, m] = [across_b(0, j) for j in range(1, side_b)]
                    two_adds[k, m] = [(mine_at, from_b(0))]
                else:
                    one[k, m] = [across_b(q, j) for q in range(side_x) for j in range(1, side_b)]
                    one_adds[k, m] = [(here.at[index(q, m), row_of(a, own_b)], from_b(q)) for q in range(side_x)]
                    two[k, m] = [across_x(q, own_b) for q in range(1, side_x)]
                    two_adds[k, m] = [(mine_at, from_x(own_b))]

        to_a, back_a, back_b, keeps = {}, {}, {}, []
        for m in range(pairs):
            at = index(0, m)
            done = here.at[at, row_of(own_a, own_b)]
            place = o_ref.at[m, row_of(own_a, own_b)]
            keeps.append(pltpu.make_async_copy(done, place, load_sems.at[m]))
            for k in range(1, side_a):
                to = grid.beside(own, "a", k)
                to_a[k, m] = copies.make(here.at[at, row_of(own_a ^ k, own_b)], got.at[m, k - 1], to)
            got_at = lambda k: o_ref.at[m, row_of(own_a ^ k, own_b)]
            beside_a = lambda k: grid.beside(own, "a", k)
            back_a["near", m] = copies.make(done, place, beside_a(1))
            back_a["over", m] = copies.make(done, place, beside_a(3))
            back_a["over2", m] = copies.make(got_at(1), got_at(1), beside_a(3))
            back_a["out", m] = copies.make(got_at(3), got_at(3), beside_a(1))
            back_a["out2", m] = copies.make(got_at(2), got_at(2), beside_a(1))
            for k in range(side_a):
                for j in range(1, side_b):
                    came = o_ref.at[m, row_of(own_a ^ k, own_b)]
                    back_b[k, j, m] = copies.make(done if k == 0 else came, came, grid.beside(own, "b", j))
        middle = (own_a == 1) | (own_a == 2)
        hop_copies = [copies.make(mine, heard.at[i], grid.beside(own, dim, k)) for i, (dim, k) in enumerate(hops)]

        def hop(i):
            if 0 < i <= len(hops):
                hop_copies[i - 1].wait()
                mine[...] = mine[...] + heard[i - 1]
            if i < len(hops):
                hop_copies[i].start()

        def start(found):
            for copy in found:
                copy.start()

        def wait(found):
            for copy in found:
                copy.wait()

        @pl.when(step == 0)
        def _():
            meet(grid.partners(("tile", "x", "c")))
            halo.send_rims()
            mine[...] = jnp.zeros_like(mine)
            start(cores)
            start(loads)

        add_taps(x_ref, m_ref, d_ref, h_ref, mine, pad, sums, slots, side)

        ready = {}
        for i, (k, m) in enumerate(order):
            ready[m] = max(ready.get(m, 0), i) if m % 2 == 1 or k > 0 else ready.get(m, 0)
        for i, (k, m) in enumerate(order):

            @pl.when(step == min(last, 3 + 2 * i))
            def _():
                loads[i].wait()
                cores[i].wait()
                at = index(k, m)
                add_rows(here.at[at], [core.at[at]], rows)
                for n in range(pairs):
                    if ready[n] == i:
                        start(one[turns[0], n])
                        start(one[turns[1], n])

        @pl.when(step == last)
        def _():
            halo.pick_and_send(lambda d, k: n_ref[d // slots, d % slots, k])
            mine[pl.ds(50, small_rows), pl.ds(0, channels)] = s_ref[...]
            for i in range(side_a + 1):
                hop(i)
                for m in range(pairs):
                    if i < side_a:
                        k = turns[i]
                        wait(one[k, m])
                        if i + 2 < side_a:
                            start(one[turns[i + 2], m])
                        for target, sources in one_adds[k, m]:
                            add_rows(target, sources, piece)
                        start(two[k, m])
                for m in range(pairs):
                    if i > 0:
                        k = turns[i - 1]
                        wait(two[k, m])
                        for target, sources in two_adds[k, m]:
                            add_rows(target, sources, piece)
                        if k > 0:
                            to_a[k, m].start()
            for m in range(pairs):
                wait(to_a[k, m] for k in range(1, side_a))
                done = here.at[index(0, m), row_of(own_a, own_b)]
                add_rows(done, [got.at[m, k] for k in range(side_a - 1)], piece)
                keeps[m].start()
                back_a["near", m].start()

                @pl.when(middle)
                def _():
                    back_a["over", m].start()

                start(back_b[0, j, m] for j in range(1, side_b))

            def arrive(came, k, onward):
                for m in range(pairs):
                    back_a[came, m].wait_recv()
                    if onward is not None:
                        back_a[onward, m].start()
                    start(back_b[k, j, m] for j in range(1, side_b))

            for m in range(pairs):
                back_a["near", m].wait_recv()

                @pl.when(middle)
                def _():
                    back_a["over2", m].start()

                start(back_b[1, j, m] for j in range(1, side_b))

            @pl.when(middle)
            def _():
                arrive("over", 3, "out")
                arrive("over2", 2, "out2")

            @pl.when(~middle)
            def _():
                arrive("out", 2, None)
                arrive("out2", 3, None)

            for i in range(side_a + 1, len(hops) + 1):
                hop(i)
            halo.finish()
            t_ref[...] = mine[...]
            for m in range(pairs):
                keeps[m].wait()
                back_a["near", m].wait_send()

                @pl.when(middle)
                def _():
                    for name in ("over", "over2", "out", "out2"):
                        back_a[name, m].wait_send()

            wait(back_b.values())

    any_space = pl.BlockSpec(memory_space=pl.ANY)
    cells = side * side
    return pl.pallas_call(
        kernel,
        grid=(n_chunk, slots),
        in_specs=[
            any_space,
            any_space,
            pl.BlockSpec(memory_space=pltpu.SMEM),
            pl.BlockSpec((1, side, side, LANES), lambda c, s: (s, 0, 0, c)),
            pl.BlockSpec((1, cells, LANES), lambda c, s: (s, 0, 0)),
            pl.BlockSpec((1, cells, LANES), lambda c, s: (s, 0, c)),
            halo_block(halos),
            pl.BlockSpec(small.shape, lambda c, s: (0, 0)),
        ],
        out_specs=[any_space, any_space, pl.BlockSpec(small_shape, lambda c, s: (0, 0))],
        out_shape=[
            halo.halo_shape(),
            jax.ShapeDtypeStruct((pairs, rows, cols), BF),
            jax.ShapeDtypeStruct(small_shape, F32),
        ],
        scratch_shapes=halo.scratch()
        + [
            pltpu.VMEM((blocks, rows, cols), BF),
            pltpu.VMEM((blocks, rows, cols), BF),
            pltpu.VMEM((side_x - 1, pairs, rows, cols), BF),
            pltpu.VMEM((side_b - 1, blocks, part, cols), BF),
            pltpu.VMEM(((side + 2 * RIM) * PITCH, LANES), F32),
            pltpu.VMEM((50, 8, LANES), F32),
            pltpu.VMEM((pairs, side_a - 1, piece, cols), BF),
            pltpu.VMEM(small_shape, F32),
            pltpu.VMEM((len(hops),) + small_shape, F32),
            pltpu.SemaphoreType.DMA((total,)),
            pltpu.SemaphoreType.DMA((total,)),
            pltpu.SemaphoreType.DMA((blocks,)),
        ],
        compiler_params=remote_params(2, 60),
        name="exchange_backward",
    )(rims, grads, neighbours, inputs, mask_lanes, d_conv, halos, small)


def tile_total(grid, value, number):
    n_tile = grid.n_tile

    def kernel(v_ref, o_ref, got, send, recv):
        t, o = grid.at(grid.own())
        meet(grid.partners(("tile",)))
        copies = Copies(send, recv)
        got[t] = v_ref[...]
        sent = [copies.start(v_ref, got.at[t], (t ^ k, o)) for k in range(1, n_tile)]
        for copy in sent:
            copy.wait()
        total = got[0]
        for i in range(1, n_tile):
            total = total + got[i]
        o_ref[...] = total

    whole = pl.BlockSpec(memory_space=pltpu.VMEM)
    return pl.pallas_call(
        kernel,
        in_specs=[whole],
        out_specs=whole,
        out_shape=jax.ShapeDtypeStruct(value.shape, F32),
        scratch_shapes=[
            pltpu.VMEM((n_tile,) + value.shape, F32),
            pltpu.SemaphoreType.DMA((n_tile - 1,)),
            pltpu.SemaphoreType.DMA((n_tile - 1,)),
        ],
        compiler_params=remote_params(number, 16),
        name="tile_total",
    )(value)


def fill_halo(pad, halo, side):
    last = side + RIM
    up, down, left, right, corner = (halo(k) for k in range(5))
    for e in range(RIM):
        rows = slice(e * side, e * side + side)
        pad[pl.ds(e * PITCH + 8, side), :] = up[rows]
        pad[pl.ds((last + e) * PITCH + 8, side), :] = down[rows]
        pad[pl.ds(RIM * PITCH + 8 - RIM + e, side, stride=PITCH), :] = left[rows]
        pad[pl.ds(RIM * PITCH + 8 + side + e, side, stride=PITCH), :] = right[rows]
    places = ((0, 8 - RIM), (0, 8 + side), (last, 8 - RIM), (last, 8 + side))
    for k, (row, col) in enumerate(places):
        for e in range(RIM):
            at = 16 * k + RIM * e
            pad[pl.ds((row + e) * PITCH + col, RIM), :] = corner[at : at + RIM]


def conv_pass(pad, side, weight, emit):
    for block in range(side // 8):
        sums = [None] * side
        for b in range(7):
            taps = [weight(a, b) for a in range(7)]
            for r in range(side + 2 * RIM):
                cells = pad[pl.ds(r * PITCH + 8 - RIM + b + 8 * block, 8), :]
                for a in range(7):
                    i = r - a
                    if 0 <= i < side:
                        term = taps[a] * cells
                        sums[i] = term if sums[i] is None else sums[i] + term
        emit(block, sums)


def halo_block(halos):
    return pl.BlockSpec((1, 1) + halos.shape[2:], lambda c, s: (c, s, 0, 0, 0))


def conv_step(x_ref, m_ref, w_ref, halo, o_ref, s_ref, pad, side):
    for i in range(side):
        pad[pl.ds((i + RIM) * PITCH + 8, side), :] = x_ref[0, i].astype(F32) * m_ref[0, pl.ds(i * side, side), :]
    fill_halo(pad, halo, side)
    bias = w_ref[49]
    totals = [jnp.zeros((8, LANES), F32), jnp.zeros((8, LANES), F32)]

    def emit(block, sums):
        for i in range(side):
            value = sums[i] + bias
            rows = pl.ds(i * side + 8 * block, 8)
            o_ref[0, rows, :] = value
            weighted = m_ref[0, rows, :] * value
            totals[0] = totals[0] + weighted
            totals[1] = totals[1] + weighted * value

    conv_pass(pad, side, lambda a, b: w_ref[7 * a + b], emit)
    s_ref[0, 0], s_ref[0, 1] = totals


def conv_gradient(d_shaped, conv_out, mask_lanes, coefs, side):
    slots, cells, channels = d_shaped.shape
    n_chunk = -(-channels // LANES)

    def kernel(d_ref, v_ref, m_ref, c_ref, o_ref, r_ref, held):
        one, two, three = c_ref[0, :1], c_ref[1, :1], c_ref[2, :1]
        for s in range(slots):
            value = d_ref[s] * one - m_ref[s] * (two + three * v_ref[s])
            o_ref[s] = value
            held[...] = value
            store_rims(held, r_ref, s, side)

    piece = (slots, 4, RIM * side, LANES)
    block = pl.BlockSpec((slots, cells, LANES), lambda c: (0, 0, c))
    return pl.pallas_call(
        kernel,
        grid=(n_chunk,),
        in_specs=[
            block,
            block,
            pl.BlockSpec((slots, cells, LANES), lambda c: (0, 0, 0)),
            pl.BlockSpec((3, 8, LANES), lambda c: (0, 0, c)),
        ],
        out_specs=[block, pl.BlockSpec((1,) + piece, lambda c: (c, 0, 0, 0, 0))],
        scratch_shapes=[pltpu.VMEM((cells, LANES), F32)],
        out_shape=[
            jax.ShapeDtypeStruct((slots, cells, channels), F32),
            jax.ShapeDtypeStruct((n_chunk,) + piece, BF),
        ],
        compiler_params=pltpu.CompilerParams(vmem_limit_bytes=32 << 20),
        name="conv_gradient",
    )(d_shaped, conv_out, mask_lanes, coefs)


def add_taps(x_ref, m_ref, d_ref, h_ref, o_ref, pad, sums, slots, side):
    slot = pl.program_id(1)
    for i in range(side):
        pad[pl.ds((i + RIM) * PITCH + 8, side), :] = x_ref[0, i].astype(F32) * m_ref[0, pl.ds(i * side, side), :]
    fill_halo(pad, lambda k: h_ref[0, 0, k].astype(F32), side)

    @pl.when(slot == 0)
    def _():
        sums[...] = jnp.zeros_like(sums)

    for block in range(side // 8):
        grads = [d_ref[0, pl.ds(i * side + 8 * block, 8), :] for i in range(side)]
        total = grads[0]
        for i in range(1, side):
            total = total + grads[i]
        sums[49] += total
        for b in range(7):
            taps = [None] * 7
            for r in range(side + 2 * RIM):
                window = pad[pl.ds(r * PITCH + 8 - RIM + b + 8 * block, 8), :]
                for a in range(7):
                    i = r - a
                    if 0 <= i < side:
                        term = window * grads[i]
                        taps[a] = term if taps[a] is None else taps[a] + term
            for a in range(7):
                sums[7 * a + b] += taps[a]

    @pl.when(slot == slots - 1)
    def _():
        at = pl.multiple_of(pl.program_id(0) * LANES, LANES)
        o_ref[pl.ds(0, 50), pl.ds(at, LANES)] = jnp.sum(sums[...], axis=1)


def conv_backward(grid, d_conv, halos, cotangent, mask_lanes, taps, weight_lanes, change):
    slots, side, _, channels = cotangent.shape
    n_chunk = halos.shape[0]
    cells = side * side
    pairs, rows, cols = change.shape
    side_a, side_b = grid.size["a"], grid.size["b"]
    part = rows // side_b
    piece = part // side_a
    total = pairs * (side_a * (side_b - 1) + (side_a - 1))
    last = n_chunk * slots - 1

    def kernel(
        d_ref, g_ref, m_ref, w_ref, l_ref, h_ref, c_ref, o_ref, change_ref,
        pad, mine, from_b, from_a, send, recv, load_sems,
    ):
        own = grid.own()
        step = pl.program_id(0) * slots + pl.program_id(1)
        copies = Copies(send, recv)
        own_a, own_b = own["a"], own["b"]
        half = lambda b: pl.ds(pl.multiple_of(b * part, 16), part)
        row_of = lambda a, b: pl.ds(pl.multiple_of((b * side_a + a) * piece, 16), piece)
        part_row = lambda a: pl.ds(pl.multiple_of(a * piece, 16), piece)
        turns = [*range(1, side_a), 0]
        firsts, seconds, loads = {}, {}, []
        for m in range(pairs):
            for k in turns:
                a = own_a ^ k
                firsts[k, m] = [
                    copies.make(
                        c_ref.at[m, row_of(a, own_b ^ j)], from_b.at[j - 1, m, part_row(a)], grid.beside(own, "b", j)
                    )
                    for j in range(1, side_b)
                ]
                if k > 0:
                    seconds[k, m] = copies.make(
                        mine.at[m, part_row(a)], from_a.at[k - 1, m], grid.beside(own, "a", k)
                    )
            loads.append(pltpu.make_async_copy(c_ref.at[m, half(own_b)], mine.at[m], load_sems.at[m]))

        @pl.when(step == 0)
        def _():
            meet(grid.partners(("a", "b")))
            for load in loads:
                load.start()
            for k in turns:
                for m in range(pairs):
                    for copy in firsts[k, m]:
                        copy.start()

        for i in range(side):
            pad[pl.ds((i + RIM) * PITCH + 8, side), :] = d_ref[0, pl.ds(i * side, side), :]
        fill_halo(pad, lambda k: h_ref[0, 0, k].astype(F32), side)
        weight = l_ref[...]

        def emit(block, sums):
            for i in range(side):
                at = pl.ds(i * side + 8 * block, 8)
                scaled = weight * g_ref[0, i, pl.ds(8 * block, 8), :].astype(F32)
                o_ref[0, at, :] = m_ref[0, at, :] * (scaled + sums[i])

        conv_pass(pad, side, lambda a, b: w_ref[7 * (6 - a) + 6 - b], emit)

        for i, k in enumerate(turns):

            @pl.when(step == min(last, 5 + 4 * i))
            def _():
                for m in range(pairs):
                    if i == 0:
                        loads[m].wait()
                    for copy in firsts[k, m]:
                        copy.wait()
                    rows_here = part_row(own_a ^ k)
                    sources = [from_b.at[j, m, rows_here] for j in range(side_b - 1)]
                    add_rows(mine.at[m, rows_here], sources, piece)
                    if k > 0:
                        seconds[k, m].start()

        @pl.when(step == last)
        def _():
            for m in range(pairs):
                for k in range(1, side_a):
                    seconds[k, m].wait()
                value = mine[m, part_row(own_a)].astype(F32)
                for k in range(side_a - 1):
                    value = value + from_a[k, m].astype(F32)
                change_ref[m] = value

    return pl.pallas_call(
        kernel,
        grid=(n_chunk, slots),
        in_specs=[
            pl.BlockSpec((1, cells, LANES), lambda c, s: (s, 0, c)),
            pl.BlockSpec((1, side, side, LANES), lambda c, s: (s, 0, 0, c)),
            pl.BlockSpec((1, cells, LANES), lambda c, s: (s, 0, 0)),
            pl.BlockSpec((50, 8, LANES), lambda c, s: (0, 0, c)),
            pl.BlockSpec((8, LANES), lambda c, s: (0, 0)),
            halo_block(halos),
            pl.BlockSpec(memory_space=pl.ANY),
        ],
        out_specs=[
            pl.BlockSpec((1, cells, LANES), lambda c, s: (s, 0, c)),
            pl.BlockSpec((pairs, piece, cols), lambda c, s: (0, 0, 0)),
        ],
        scratch_shapes=[
            pltpu.VMEM(((side + 2 * RIM) * PITCH, LANES), F32),
            pltpu.VMEM((pairs, part, cols), BF),
            pltpu.VMEM((side_b - 1, pairs, part, cols), BF),
            pltpu.VMEM((side_a - 1, pairs, piece, cols), BF),
            pltpu.SemaphoreType.DMA((total,)),
            pltpu.SemaphoreType.DMA((total,)),
            pltpu.SemaphoreType.DMA((pairs,)),
        ],
        out_shape=[
            jax.ShapeDtypeStruct((slots, cells, channels), F32),
            jax.ShapeDtypeStruct((pairs, piece, cols), F32),
        ],
        compiler_params=remote_params(4, 48),
        name="conv_backward",
    )(d_conv, cotangent, mask_lanes, taps, weight_lanes, halos, change)


def spread_lanes(value, parts, width):
    rows, channels = value.shape
    run = channels // parts
    if run == width:
        return value
    gap = jnp.zeros((rows, width - run), value.dtype)
    pieces = []
    for t in range(parts):
        pieces += [value[:, t * run : (t + 1) * run], gap]
    return jnp.concatenate(pieces, 1)


def close_lanes(value, parts, run):
    width = value.shape[1] // parts
    if run == width:
        return value
    return jnp.concatenate([value[:, t * width : t * width + run] for t in range(parts)], 1)


def row_block(rows):
    return LANES


def arranged(value, gap_ref, turned_ref, sum_ref, first, parts, width):
    low = value.astype(BF).astype(F32)
    gap_ref[...] = spread_lanes(low, parts, width).astype(BF)
    turned_ref[...] = low.T.astype(BF)

    @pl.when(first)
    def _():
        sum_ref[...] = jnp.zeros_like(sum_ref)

    sum_ref[...] += jnp.sum(low, axis=0, keepdims=True)


def arrange(body, args, specs, rows, channels, parts, width, name):
    step = row_block(rows)

    def kernel(*refs):
        given, (gap_ref, turned_ref, sum_ref) = refs[: len(args)], refs[len(args) :]
        arranged(body(*given), gap_ref, turned_ref, sum_ref, pl.program_id(0) == 0, parts, width)

    return pl.pallas_call(
        kernel,
        grid=(rows // step,),
        in_specs=specs(step),
        out_specs=[
            pl.BlockSpec((step, parts * width), lambda i: (i, 0)),
            pl.BlockSpec((channels, step), lambda i: (0, i)),
            pl.BlockSpec((1, channels), lambda i: (0, 0)),
        ],
        out_shape=[
            jax.ShapeDtypeStruct((rows, parts * width), BF),
            jax.ShapeDtypeStruct((channels, rows), BF),
            jax.ShapeDtypeStruct((1, channels), F32),
        ],
        compiler_params=pltpu.CompilerParams(vmem_limit_bytes=48 << 20),
        name=name,
    )(*args)


def feed_forward(inverse, shaped, shaped_t, d_branch, d_branch_t, hidden_bias, weights, grad_rows):
    rows, depth = shaped.shape
    channels = shaped_t.shape[0]
    half, _, cols = hidden_bias.shape
    pairs, owners = weights.shape[:2]
    per_owner = 2 * pairs
    tile_rows = 3 * LANES if rows % (3 * LANES) == 0 else LANES

    def kernel(inv_ref, s_ref, st_ref, d_ref, dt_ref, hb_ref, w_ref, branch_ref, ds_ref, grad_ref, bias_ref, *scratch):
        packed, first, second, act, dpre, grads, sems, out_sem = scratch
        step = pl.program_id(0)

        def where(slot):
            owner, inside = slot // per_owner, slot % per_owner
            return owner, inside // 2, inside % 2

        def fetch(h, buffer):
            copies = []
            for which in range(2):
                owner, pair, _ = where(inv_ref[h + which * half])
                copies.append(
                    pltpu.make_async_copy(w_ref.at[pair, owner], packed.at[buffer, which], sems.at[buffer, which])
                )
            return copies

        @pl.when(step == 0)
        def _():
            for copy in fetch(0, 0):
                copy.start()
            if grad_rows > channels:
                rest = grad_rows - channels
                grads[:, :, pl.ds(channels, rest), :] = jnp.zeros(grads.shape[:2] + (rest, 2 * cols), BF)

        @pl.when(step + 1 < half)
        def _():
            for copy in fetch(step + 1, (step + 1) % 2):
                copy.start()

        now = step % 2
        slots = [where(inv_ref[step + which * half]) for which in range(2)]
        waits = fetch(step, now)
        for which, held in enumerate((first, second)):
            waits[which].wait()
            for parity in range(2):

                @pl.when(slots[which][2] == parity)
                def _():
                    held[...] = packed[now, which, :, parity * cols : (parity + 1) * cols]

        hidden = hb_ref[0]

        @pl.when(step == 0)
        def _():
            branch_ref[...] = jnp.zeros_like(branch_ref)
            ds_ref[...] = jnp.zeros_like(ds_ref)

        total = jnp.zeros((1, cols), F32)
        across = (((1,), (1,)), ((), ()))
        for i in range(rows // tile_rows):
            at = pl.ds(i * tile_rows, tile_rows)
            pre = jnp.dot(s_ref[at, :], first[...], preferred_element_type=F32) + hidden
            d_act = jnp.dot(d_ref[at, :], second[...], preferred_element_type=F32)
            square = pre * pre
            bend = jnp.tanh(ROOT * pre * (1.0 + CUBE * square))
            half_up = 0.5 * (1.0 + bend)
            low = (pre * half_up).astype(BF)
            slope = half_up + (0.5 * ROOT) * pre * (1.0 - bend * bend) * (1.0 + (3.0 * CUBE) * square)
            back = (d_act * slope).astype(BF)
            act[at, :] = low
            dpre[at, :] = back
            total = total + jnp.sum(back.astype(F32), axis=0, keepdims=True)
            out_add = lax.dot_general(low, second[...], across, preferred_element_type=F32)
            in_add = lax.dot_general(back, first[...], across, preferred_element_type=F32)

            branch_ref[at, :] += out_add
            ds_ref[at, :] += in_add

        bias_ref[0] = total
        for which, (left, right) in enumerate(((st_ref, dpre), (dt_ref, act))):
            owner, pair, half_of_pair = slots[which]
            value = jnp.dot(left[...], right[...], preferred_element_type=F32).astype(BF)
            for parity in range(2):

                @pl.when(half_of_pair == parity)
                def _():
                    at = (owner // 2) * pairs + pair
                    grads[owner % 2, at, pl.ds(0, channels), parity * cols : (parity + 1) * cols] = value

        @pl.when(step == half - 1)
        def _():
            out = pltpu.make_async_copy(grads, grad_ref, out_sem.at[0])
            out.start()
            out.wait()

    whole = lambda *shape: pl.BlockSpec(shape, lambda h, *_: (0,) * len(shape))
    line = pl.BlockSpec((1, 1, cols), lambda h, *_: (h, 0, 0))
    grad_shape = (2, owners // 2 * pairs, grad_rows, 2 * cols)
    return pl.pallas_call(
        kernel,
        grid_spec=pltpu.PrefetchScalarGridSpec(
            num_scalar_prefetch=1,
            grid=(half,),
            in_specs=[
                whole(rows, depth),
                whole(channels, rows),
                whole(rows, depth),
                whole(channels, rows),
                line,
                pl.BlockSpec(memory_space=pl.ANY),
            ],
            out_specs=[whole(rows, depth), whole(rows, depth), pl.BlockSpec(memory_space=pl.ANY), line],
            scratch_shapes=[
                pltpu.VMEM((2, 2, depth, 2 * cols), BF),
                pltpu.VMEM((depth, cols), BF),
                pltpu.VMEM((depth, cols), BF),
                pltpu.VMEM((rows, cols), BF),
                pltpu.VMEM((rows, cols), BF),
                pltpu.VMEM(grad_shape, BF),
                pltpu.SemaphoreType.DMA((2, 2)),
                pltpu.SemaphoreType.DMA((1,)),
            ],
        ),
        out_shape=[
            jax.ShapeDtypeStruct((rows, depth), F32),
            jax.ShapeDtypeStruct((rows, depth), F32),
            jax.ShapeDtypeStruct(grad_shape, BF),
            jax.ShapeDtypeStruct((half, 1, cols), F32),
        ],
        cost_estimate=pl.CostEstimate(
            flops=12 * rows * channels * half * cols, bytes_accessed=40 << 20, transcendentals=rows * half * cols
        ),
        compiler_params=pltpu.CompilerParams(vmem_limit_bytes=63 << 20),
        name="feed_forward",
    )(inverse, shaped, shaped_t, d_branch, d_branch_t, hidden_bias, weights)


def close_out(branch, d_shaped, inputs, conv_out, mask_lanes, out_bias, parts, run):
    rows, channels = inputs.shape
    depth = branch.shape[1]
    step = row_block(rows)

    def kernel(b_ref, d_ref, x_ref, v_ref, m_ref, o_ref, out_ref, ds_ref, sum_ref):
        branch_here = close_lanes(b_ref[...], parts, run) + o_ref[...]
        out_ref[...] = (m_ref[:, :1] * (x_ref[...].astype(F32) + branch_here)).astype(BF)
        grads = close_lanes(d_ref[...], parts, run)
        ds_ref[...] = grads

        @pl.when(pl.program_id(0) == 0)
        def _():
            sum_ref[...] = jnp.zeros_like(sum_ref)

        sum_ref[0] += jnp.sum(grads, axis=0, keepdims=True)
        sum_ref[1] += jnp.sum(grads * v_ref[...], axis=0, keepdims=True)

    line = lambda n: pl.BlockSpec((step, n), lambda i: (i, 0))
    return pl.pallas_call(
        kernel,
        grid=(rows // step,),
        in_specs=[
            line(depth),
            line(depth),
            line(channels),
            line(channels),
            line(LANES),
            pl.BlockSpec((1, channels), lambda i: (0, 0)),
        ],
        out_specs=[line(channels), line(channels), pl.BlockSpec((2, 1, channels), lambda i: (0, 0, 0))],
        out_shape=[
            jax.ShapeDtypeStruct((rows, channels), BF),
            jax.ShapeDtypeStruct((rows, channels), F32),
            jax.ShapeDtypeStruct((2, 1, channels), F32),
        ],
        compiler_params=pltpu.CompilerParams(vmem_limit_bytes=60 << 20),
        name="close_out",
    )(branch, d_shaped, inputs, conv_out, mask_lanes, out_bias)


def halves(value):
    high = value.astype(BF)
    return high, (value - high.astype(F32)).astype(BF)


def product(left, right, contract):
    dims = (contract, ((), ()))
    total = None
    for i, a in enumerate(left):
        for j, b in enumerate(right):
            if i + j < 2:
                term = lax.dot_general(a, b, dims, preferred_element_type=F32)
                total = term if total is None else total + term
    return total


def rotate(owned, left_basis, column_basis, moment_one, moment_two, correction, grid, width):
    slots, channels, run = left_basis.shape
    cols = column_basis.shape[1]
    pairs = slots // 2
    side_a, side_b = grid.size["a"], grid.size["b"]
    n_tile = grid.n_tile

    def kernel(f_ref, g_ref, l_ref, c_ref, one_ref, two_ref, first_ref, second_ref, o_ref):
        factor = f_ref[0]
        changes = []
        for p in range(2):
            grad = g_ref[0, pl.ds(0, channels), p * cols : (p + 1) * cols]
            left = halves(l_ref[p])
            column = halves(c_ref[p])
            rotated = product(left, (grad,), ((0,), (0,)))
            rotated = product(halves(rotated), column, ((1,), (0,)))
            first = decay_rate * one_ref[p] + (1.0 - decay_rate) * rotated
            second = decay_rate * two_ref[p] + (1.0 - decay_rate) * rotated * rotated
            first_ref[p] = first
            second_ref[p] = second
            direction = first * factor / (jnp.sqrt(second * factor) + adam_eps)
            turned = product(halves(direction), column, ((1,), (1,)))
            changes.append(product(left, halves(turned), ((1,), (0,))))
        change = jnp.concatenate(changes, 1)
        gap = jnp.zeros((width - run, 2 * cols), F32)
        for t in range(n_tile):
            piece = jnp.concatenate([change[t * run : (t + 1) * run], gap], 0)
            place = (t % side_b) * side_a + t // side_b
            o_ref[0, pl.ds(place * width, width), :] = piece.astype(BF)

    pair = lambda *shape: pl.BlockSpec(shape, lambda m: (m,) + (0,) * (len(shape) - 1))
    return pl.pallas_call(
        kernel,
        grid=(pairs,),
        in_specs=[
            pl.BlockSpec(memory_space=pltpu.SMEM),
            pair(1, owned.shape[1], 2 * cols),
            pair(2, channels, run),
            pair(2, cols, cols),
            pair(2, run, cols),
            pair(2, run, cols),
        ],
        out_specs=[pair(2, run, cols), pair(2, run, cols), pair(1, n_tile * width, 2 * cols)],
        out_shape=[
            jax.ShapeDtypeStruct(moment_one.shape, F32),
            jax.ShapeDtypeStruct(moment_one.shape, F32),
            jax.ShapeDtypeStruct((pairs, n_tile * width, 2 * cols), BF),
        ],
        compiler_params=pltpu.CompilerParams(vmem_limit_bytes=60 << 20),
        name="rotate",
    )(1.0 / correction.reshape(1), owned, left_basis, column_basis, moment_one, moment_two)


def up_to(value, unit):
    return -(-value // unit) * unit


def pack_pairs(value):
    slots, rows, cols = value.shape
    return value.reshape(slots // 2, 2, rows, cols).transpose(0, 2, 1, 3).reshape(slots // 2, rows, 2 * cols)


def unpack_pairs(value):
    pairs, rows, cols = value.shape
    return value.reshape(pairs, rows, 2, cols // 2).transpose(0, 2, 1, 3).reshape(2 * pairs, rows, cols // 2)


def per_device(
    grid,
    inputs,
    cotangent,
    master,
    moment_one,
    moment_two,
    left_basis,
    column_basis,
    small_params,
    small_first,
    small_second,
    land_mask,
    tile_count,
    neighbours,
    block_order,
    cell_weight,
    step_count,
):
    position = lax.axis_index("tile")
    sample = lax.axis_index("opt")
    inputs, cotangent = inputs[0], cotangent[0]
    slots, side, _, channels = inputs.shape
    cells = side * side
    rows = slots * cells
    n_tile = grid.n_tile
    n_chunk = -(-channels // LANES)
    per_group = channels // GROUPS
    per_owner, run, cols = master.shape
    pairs = per_owner // 2
    block_total = block_order.shape[0]
    half = block_total // 2
    width = up_to(run, 16)

    live = (jnp.arange(slots) < tile_count[position]).astype(F32)
    mask = (land_mask.astype(F32) * live[:, None, None]).reshape(slots, cells)
    mask_lanes = jnp.broadcast_to(mask[:, :, None], (slots, cells, LANES))
    flat_mask = mask_lanes.reshape(rows, LANES)
    taps = jnp.broadcast_to(small_params[:50, None, :], (50, 8, channels))

    weights_float = cell_weight.astype(F32)
    sample_weight = weights_float[sample] * weights_float.shape[0] / jnp.sum(weights_float)
    weight_lanes = jnp.broadcast_to(sample_weight, (8, LANES))
    weight_row = jnp.broadcast_to(sample_weight, (1, LANES))

    low_master = jnp.pad(pack_pairs(master.astype(BF)), ((0, 0), (0, width - run), (0, 0)))
    rims = rims_of_input(inputs, mask_lanes)
    halos, weights, all_neighbours, conv_out, sums, d_branch, d_branch_t, d_out_bias = exchange_forward(
        grid,
        rims,
        low_master,
        neighbours,
        inputs,
        mask_lanes,
        taps,
        cotangent.reshape(rows, channels),
        flat_mask,
        weight_row,
        width,
    )

    sums = jnp.sum(sums, axis=(0, 2))
    occupied = jnp.broadcast_to(jnp.sum(mask), (1, channels))
    sums = tile_total(grid, jnp.concatenate([sums, occupied], 0), 5)
    counted = sums[2, 0] * per_group
    by_group = sums[:2].reshape(2, GROUPS, per_group).sum(2)
    group_mean = by_group[0] / counted
    variance = by_group[1] / counted - group_mean * group_mean
    inv_std = jnp.repeat(lax.rsqrt(variance + epsilon), per_group)
    mean = jnp.repeat(group_mean, per_group)
    gain, shift = small_params[50], small_params[51]
    norm_coefs = jnp.stack([inv_std, mean * inv_std, gain, shift])

    def shaped_body(v_ref, c_ref):
        normed = v_ref[...] * c_ref[0:1] - c_ref[1:2]
        return normed * c_ref[2:3] + c_ref[3:4]

    flat_conv = conv_out.reshape(rows, channels)
    shaped, shaped_t, _ = arrange(
        shaped_body,
        (flat_conv, norm_coefs),
        lambda step: [
            pl.BlockSpec((step, channels), lambda i: (i, 0)),
            pl.BlockSpec((4, channels), lambda i: (0, 0)),
        ],
        rows,
        channels,
        n_tile,
        width,
        "arrange_shaped",
    )

    block_ids = jnp.arange(block_total, dtype=jnp.int32)
    inverse = jnp.sum(
        jnp.where(block_order[None, :] == block_ids[:, None], block_ids[None, :], 0), axis=1
    ).astype(jnp.int32)
    hidden_bias = small_params[53:57].reshape(half, 1, cols)
    branch, d_shaped, grads, d_hidden = feed_forward(
        inverse, shaped, shaped_t, d_branch, d_branch_t, hidden_bias, weights, n_tile * width
    )
    block_output, d_shaped, d_sums = close_out(
        branch, d_shaped, inputs.reshape(rows, channels), flat_conv, flat_mask, small_params[52:53], n_tile, run
    )

    d_shift = d_sums[0, 0]
    d_gain = inv_std * (d_sums[1, 0] - mean * d_shift)
    parts = tile_total(grid, jnp.stack([gain * d_shift, gain * d_gain]), 6)
    parts = jnp.repeat(parts.reshape(2, GROUPS, per_group).sum(2) / counted, per_group, axis=1)
    grad_coefs = jnp.stack(
        [
            inv_std * gain,
            inv_std * (parts[0] - mean * inv_std * parts[1]),
            inv_std * inv_std * parts[1],
        ]
    )
    d_conv, grad_rims = conv_gradient(
        d_shaped.reshape(slots, cells, channels),
        conv_out,
        mask_lanes,
        jnp.broadcast_to(grad_coefs[:, None, :], (3, 8, channels)),
        side,
    )
    small = jnp.concatenate([d_gain[None], d_shift[None], d_out_bias, d_hidden.reshape(4, channels)], 0)
    grad_halos, owned, d_small = exchange_backward(
        grid, grad_rims, grads, all_neighbours, inputs, mask_lanes, d_conv, halos, small
    )

    correction = 1.0 - jnp.power(F32(decay_rate), step_count[0].astype(F32))

    first_new, second_new, change = rotate(
        owned, left_basis, column_basis, moment_one, moment_two, correction, grid, width
    )
    input_grad, change = conv_backward(
        grid, d_conv, grad_halos, cotangent, mask_lanes, taps, weight_lanes, change
    )
    change = unpack_pairs(change[:, :run])
    d_small = d_small[: small_params.shape[0], :channels]
    small_one = decay_rate * small_first + (1.0 - decay_rate) * d_small
    small_two = decay_rate * small_second + (1.0 - decay_rate) * d_small * d_small
    new_small = small_params - small_rate * (small_one / correction) / (
        jnp.sqrt(small_two / correction) + adam_eps
    )
    new_master = master - 0.5 / math.sqrt(channels) * change
    return (
        block_output.reshape((1,) + inputs.shape),
        input_grad.reshape((1,) + inputs.shape),
        new_master,
        new_master.astype(BF),
        first_new,
        second_new,
        new_small,
        small_one,
        small_two,
    )


def solution(mesh):
    grid = Grid(mesh.shape["tile"], mesh.shape["opt"])

    def step(*args):
        return per_device(grid, *args)

    return jax.shard_map(
        step,
        mesh=mesh,
        in_specs=(
            P("opt", "tile", None, None, None),
            P("opt", "tile", None, None, None),
            P("opt", "tile", None),
            P("opt", "tile", None),
            P("opt", "tile", None),
            P("opt", None, "tile"),
            P("opt", None, None),
            P(),
            P(),
            P(),
            P("tile", None, None),
            P(),
            P("tile", None),
            P(),
            P(),
            P(),
        ),
        out_specs=(
            P("opt", "tile", None, None, None),
            P("opt", "tile", None, None, None),
            P("opt", "tile", None),
            P("opt", "tile", None),
            P("opt", "tile", None),
            P("opt", "tile", None),
            P(),
            P(),
            P(),
        ),
        check_vma=False,
    )
```

```python
import math

import jax
import jax.numpy as jnp
from jax import lax
from jax.experimental import pallas as pl
from jax.experimental.pallas import tpu as pltpu
from jax.sharding import PartitionSpec as P

GROUPS = 16
LANES = 128
RIM = 3
PITCH = 40
BF = jnp.bfloat16
F32 = jnp.float32

highest = lax.Precision.HIGHEST
epsilon = 1e-05
adam_eps = 1e-08
decay_rate = 0.5
small_rate = 0.05
ROOT = 0.7978845608028654
CUBE = 0.044715


class Grid:
    def __init__(self, n_tile, n_opt):
        b = n_tile // 4
        self.n_tile, self.n_opt = n_tile, n_opt
        self.size = {"a": 4, "b": b, "x": n_opt // 2, "c": 2}

    def own(self):
        t, o = lax.axis_index("tile"), lax.axis_index("opt")
        b = self.size["b"]
        return {"a": t // b, "b": t % b, "x": o // 2, "c": o % 2}

    def at(self, place):
        return place["a"] * self.size["b"] + place["b"], place["x"] * 2 + place["c"]

    def partners(self, dims):
        own = self.own()
        found = []
        for dim in dims:
            if dim == "tile":
                t, o = self.at(own)
                found += [(t ^ k, o) for k in range(1, self.n_tile)]
            else:
                found += [self.beside(own, dim, k) for k in range(1, self.size[dim])]
        return found

    def beside(self, own, dim, k):
        return self.at({**own, dim: own[dim] ^ k})


def meet(devices):
    barrier = pltpu.get_barrier_semaphore()
    for device in devices:
        pl.semaphore_signal(barrier, inc=1, device_id=device, device_id_type=pl.DeviceIdType.MESH)
    pl.semaphore_wait(barrier, len(devices))


class Copies:
    def __init__(self, send_sems, recv_sems):
        self.sems = send_sems, recv_sems
        self.used = 0

    def make(self, src, dst, device):
        i = self.used
        self.used += 1
        return pltpu.make_async_remote_copy(
            src_ref=src,
            dst_ref=dst,
            send_sem=self.sems[0].at[i],
            recv_sem=self.sems[1].at[i],
            device_id=device,
            device_id_type=pl.DeviceIdType.MESH,
        )

    def start(self, src, dst, device):
        copy = self.make(src, dst, device)
        copy.start()
        return copy


def remote_params(number, mib):
    return pltpu.CompilerParams(collective_id=number, has_side_effects=True, vmem_limit_bytes=mib << 20)


def add_rows(target, sources, rows, step=16):
    @pl.loop(0, rows // step)
    def _(i):
        at = pl.ds(pl.multiple_of(i * step, step), step)
        total = target[at, :].astype(F32)
        for source in sources:
            total = total + source[at, :].astype(F32)
        target[at, :] = total.astype(BF)


def store_rims(src, outs, slot, side):
    outs[0, slot, 0] = src[pl.ds(0, RIM * side), :].astype(BF)
    outs[0, slot, 1] = src[pl.ds((side - RIM) * side, RIM * side), :].astype(BF)
    for e in range(RIM):
        rows = pl.ds(e * side, side)
        outs[0, slot, 2, rows] = src[pl.ds(e, side, stride=side), :].astype(BF)
        outs[0, slot, 3, rows] = src[pl.ds(side - RIM + e, side, stride=side), :].astype(BF)


def rims_of_input(inputs, mask_lanes):
    slots, side, _, channels = inputs.shape
    n_chunk = -(-channels // LANES)

    def kernel(x_ref, m_ref, o_ref, cells):
        for s in range(slots):
            for i in range(side):
                cells[pl.ds(i * side, side), :] = (
                    x_ref[s, i].astype(F32) * m_ref[s, pl.ds(i * side, side), :]
                )
            store_rims(cells, o_ref, s, side)

    return pl.pallas_call(
        kernel,
        grid=(n_chunk,),
        in_specs=[
            pl.BlockSpec((slots, side, side, LANES), lambda c: (0, 0, 0, c)),
            pl.BlockSpec((slots, side * side, LANES), lambda c: (0, 0, 0)),
        ],
        out_specs=pl.BlockSpec((1, slots, 4, RIM * side, LANES), lambda c: (c, 0, 0, 0, 0)),
        out_shape=jax.ShapeDtypeStruct((n_chunk, slots, 4, RIM * side, LANES), BF),
        scratch_shapes=[pltpu.VMEM((side * side, LANES), F32)],
        compiler_params=pltpu.CompilerParams(vmem_limit_bytes=32 << 20),
        name="rims_of_input",
    )(inputs, mask_lanes)


class HaloExchange:
    def __init__(self, grid, n_chunk, slots, side):
        self.grid, self.n_chunk, self.slots, self.side = grid, n_chunk, slots, side
        self.count = 2 * (grid.n_tile - 1)

    def scratch(self):
        n, s, band = self.grid.n_tile, self.slots, RIM * self.side
        return [
            pltpu.VMEM((n, s, 4, band, LANES), BF),
            pltpu.VMEM((n, s, 5, band, LANES), BF),
            pltpu.SemaphoreType.DMA((2,)),
        ]

    def halo_shape(self):
        return jax.ShapeDtypeStruct((self.n_chunk, self.slots, 5, RIM * self.side, LANES), BF)

    def plan(self, copies, rims, arrived, picked, halos, local):
        t, o = self.grid.at(self.grid.own())
        self.t, self.arrived, self.picked = t, arrived, picked
        own_chunk = jnp.minimum(t, self.n_chunk - 1)
        self.first, self.second = [], []
        for k in range(1, self.grid.n_tile):
            to = t ^ k
            source = jnp.minimum(to, self.n_chunk - 1)
            self.first.append((to, copies.make(rims.at[source], arrived.at[t], (to, o))))
            self.second.append((to, copies.make(picked.at[to], halos.at[own_chunk], (to, o))))
        self.own_copy = pltpu.make_async_copy(rims.at[own_chunk], arrived.at[t], local.at[0])
        self.back_copy = pltpu.make_async_copy(picked.at[t], halos.at[own_chunk], local.at[1])

    def send_rims(self):
        for to, copy in self.first:

            @pl.when(to < self.n_chunk)
            def _():
                copy.start()

        self.own_copy.start()

    def pick_and_send(self, neighbours):
        grid, slots, side = self.grid, self.slots, self.side
        t, arrived, picked = self.t, self.arrived, self.picked
        self.own_copy.wait()
        for _, copy in self.first:

            @pl.when(t < self.n_chunk)
            def _():
                copy.wait_recv()

        @pl.when(t < self.n_chunk)
        def _():
            @pl.loop(0, grid.n_tile * slots)
            def _(d):
                def rim(direction, which):
                    slot = neighbours(d, direction)
                    at = jnp.maximum(slot, 0)
                    value = arrived[at // slots, at % slots, which].astype(F32)
                    return jnp.where(slot >= 0, value, 0.0)

                to_tile, to_slot = d // slots, d % slots
                for to, (direction, which) in enumerate(((1, 1), (6, 0), (3, 3), (4, 2))):
                    picked[to_tile, to_slot, to] = rim(direction, which).astype(BF)
                rows = []
                for direction, which, first in ((0, 1, side - RIM), (2, 1, 0), (5, 0, side - RIM), (7, 0, 0)):
                    value = rim(direction, which)
                    rows += [value[e * side + first : e * side + first + RIM] for e in range(RIM)]
                    rows.append(jnp.zeros((16 - RIM * RIM, LANES), F32))
                rows.append(jnp.zeros((RIM * side - 64, LANES), F32))
                picked[to_tile, to_slot, 4] = jnp.concatenate(rows, 0).astype(BF)

        for _, copy in self.second:

            @pl.when(t < self.n_chunk)
            def _():
                copy.start()

        @pl.when(t < self.n_chunk)
        def _():
            self.back_copy.start()

    def finish(self):
        t = self.t

        @pl.when(t < self.n_chunk)
        def _():
            self.back_copy.wait()

        for to, copy in self.first:

            @pl.when(to < self.n_chunk)
            def _():
                copy.wait_send()

        for to, copy in self.second:

            @pl.when(to < self.n_chunk)
            def _():
                copy.wait_recv()

            @pl.when(t < self.n_chunk)
            def _():
                copy.wait_send()


class WeightGather:
    def __init__(self, grid, pairs, width):
        self.grid, self.pairs, self.width = grid, pairs, width
        self.count = pairs * (grid.n_tile * grid.n_opt + 2)

    def plan(self, copies, packed, gathered, local):
        grid, width = self.grid, self.width
        own = grid.own()
        self.middle = (own["a"] == 1) | (own["a"] == 2)

        def place(m, rel):
            t, o = grid.at({d: own[d] ^ rel.get(d, 0) for d in own})
            return gathered.at[m, o, pl.ds(pl.multiple_of(t * width, width), width)]

        def send(m, rel, dim, k):
            source = packed.at[m] if not rel else place(m, rel)
            return copies.make(source, place(m, rel), grid.beside(own, dim, k))

        self.keeps = [pltpu.make_async_copy(packed.at[m], place(m, {}), local.at[m]) for m in range(self.pairs)]
        self.first, self.chain, self.onward, arrivals = [], {}, {}, []
        for m in range(self.pairs):
            self.chain["near", m] = send(m, {}, "a", 1)
            self.chain["over", m] = send(m, {}, "a", 3)
            self.chain["over2", m] = send(m, {"a": 1}, "a", 3)
            self.chain["out", m] = send(m, {"a": 3}, "a", 1)
            self.chain["out2", m] = send(m, {"a": 2}, "a", 1)
            order = ("x", "b", "c") if m % 2 == 0 else ("b", "x", "c")

            def spread(rel, left):
                self.onward[m, tuple(rel.items())] = sends = []
                for i, dim in enumerate(left):
                    for k in range(1, grid.size[dim]):
                        copy = send(m, rel, dim, k)
                        sends.append(copy)
                        child = {**rel, dim: k}
                        arrivals.append((m, child, copy))
                        spread(child, left[i + 1 :])

            for k in range(4):
                spread({"a": k} if k else {}, order)

        def waves(turn):
            found = [[] for _ in range(6)]
            for m, rel, copy in arrivals:
                found[turn[rel.get("a", 0)] + ("x" in rel) + ("b" in rel)].append((m, rel, copy))
            return [sorted(wave, key=lambda e: "c" in e[1]) for wave in found]

        self.sides = {True: waves({0: 0, 1: 1, 3: 2, 2: 3}), False: waves({0: 0, 1: 1, 2: 2, 3: 3})}

    def start(self):
        for copy in self.keeps:
            copy.start()
        for m in range(self.pairs):
            self.chain["near", m].start()

            @pl.when(self.middle)
            def _():
                self.chain["over", m].start()

            self.pass_on(m, {})

    def pass_on(self, m, rel):
        for copy in self.onward[m, tuple(rel.items())]:
            copy.start()

    def run(self, wave):
        along = {True: {1: ("near", 1, "over2"), 2: ("over", 3, "out"), 3: ("over2", 2, "out2")}}
        along[False] = {1: ("near", 1, None), 2: ("out", 2, None), 3: ("out2", 3, None)}
        for side in (True, False):

            @pl.when(self.middle == side)
            def _():
                if wave in along[side]:
                    came, k, goes = along[side][wave]
                    for m in range(self.pairs):
                        self.chain[came, m].wait_recv()
                        if goes is not None:
                            self.chain[goes, m].start()
                        self.pass_on(m, {"a": k})
                for m, rel, copy in self.sides[side][wave]:
                    copy.wait_recv()
                    self.pass_on(m, rel)

    def finish(self):
        for copy in self.keeps:
            copy.wait()
        for m in range(self.pairs):
            self.chain["near", m].wait_send()

            @pl.when(self.middle)
            def _():
                for name in ("over", "over2", "out", "out2"):
                    self.chain[name, m].wait_send()

        for sends in self.onward.values():
            for copy in sends:
                copy.wait_send()


def exchange_forward(grid, rims, packed, neighbours, inputs, mask_lanes, taps, cotangent, flat_mask, weight_row, width):
    n_chunk, slots, _, band, _ = rims.shape
    side, channels = inputs.shape[1], inputs.shape[3]
    cells = side * side
    pairs, _, cols = packed.shape
    n_tile = grid.n_tile
    rows = slots * cells
    block = row_block(rows)
    early = rows // block
    halo = HaloExchange(grid, n_chunk, slots, side)
    gather = WeightGather(grid, pairs, packed.shape[1])
    total = halo.count + gather.count + n_tile - 1
    last = early + n_chunk * slots

    def kernel(
        r_ref, p_ref, n_ref, x_ref, m_ref, t_ref, g_ref, f_ref, l_ref,
        halo_ref, w_ref, nbr_ref, conv_ref, sum_ref, gap_ref, turned_ref, bias_ref,
        arrived, picked, local, landed, table, pad, send, recv, locals_w, locals_n,
    ):
        step = pl.program_id(0)
        t, o = grid.at(grid.own())
        copies = Copies(send, recv)
        halo.plan(copies, r_ref, arrived, picked, landed, local)
        gather.plan(copies, p_ref, w_ref, locals_w)
        tables = [copies.make(n_ref, nbr_ref.at[t], (t ^ k, o)) for k in range(1, n_tile)]
        keep = pltpu.make_async_copy(n_ref, nbr_ref.at[t], locals_n.at[0])
        load = pltpu.make_async_copy(nbr_ref, table, locals_n.at[1])
        halo_out = pltpu.make_async_copy(landed, halo_ref, locals_n.at[0])

        @pl.when(step == 0)
        def _():
            meet(grid.partners(("tile", "x", "c")))
            for copy in tables:
                copy.start()
            keep.start()
            halo.send_rims()
            gather.start()

        @pl.when((step > 0) & (step <= early))
        def _():
            value = f_ref[:, :1] * (l_ref[:, :1] * g_ref[...].astype(F32))
            arranged(value, gap_ref, turned_ref, bias_ref, step == 1, n_tile, width)

        @pl.when(step == early)
        def _():
            keep.wait()
            for copy in tables:
                copy.wait()
            load.start()
            load.wait()
            gather.run(0)
            halo.pick_and_send(lambda d, k: table[d // slots, d % slots, k])
            gather.run(1)
            gather.run(2)
            halo.finish()
            halo_out.start()

        for i in range(3):

            @pl.when(step == min(last, early + 3 + 4 * i))
            def _():
                gather.run(3 + i)

        @pl.when(step > early)
        def _():
            at = step - early - 1
            conv_step(
                x_ref, m_ref, t_ref, lambda k: landed[at // slots, at % slots, k].astype(F32), conv_ref, sum_ref, pad, side
            )

        @pl.when(step == last)
        def _():
            gather.finish()
            halo_out.wait()

    conv_at = lambda i: jnp.maximum(i - early - 1, 0)
    row_at = lambda i: jnp.clip(i - 1, 0, early - 1)
    any_space = pl.BlockSpec(memory_space=pl.ANY)
    return pl.pallas_call(
        kernel,
        grid=(last + 1,),
        in_specs=[any_space] * 3
        + [
            pl.BlockSpec((1, side, side, LANES), lambda i: (conv_at(i) % slots, 0, 0, conv_at(i) // slots)),
            pl.BlockSpec((1, cells, LANES), lambda i: (conv_at(i) % slots, 0, 0)),
            pl.BlockSpec((50, 8, LANES), lambda i: (0, 0, conv_at(i) // slots)),
            pl.BlockSpec((block, channels), lambda i: (row_at(i), 0)),
            pl.BlockSpec((block, LANES), lambda i: (row_at(i), 0)),
            pl.BlockSpec((1, LANES), lambda i: (0, 0)),
        ],
        out_specs=[any_space] * 3
        + [
            pl.BlockSpec((1, cells, LANES), lambda i: (conv_at(i) % slots, 0, conv_at(i) // slots)),
            pl.BlockSpec((1, 2, 8, LANES), lambda i: (conv_at(i) % slots, 0, 0, conv_at(i) // slots)),
            pl.BlockSpec((block, n_tile * width), lambda i: (row_at(i), 0)),
            pl.BlockSpec((channels, block), lambda i: (0, row_at(i))),
            pl.BlockSpec((1, channels), lambda i: (0, 0)),
        ],
        out_shape=[
            halo.halo_shape(),
            jax.ShapeDtypeStruct((pairs, grid.n_opt, n_tile * packed.shape[1], cols), BF),
            jax.ShapeDtypeStruct((n_tile,) + neighbours.shape, jnp.int32),
            jax.ShapeDtypeStruct((slots, cells, channels), F32),
            jax.ShapeDtypeStruct((slots, 2, 8, channels), F32),
            jax.ShapeDtypeStruct((rows, n_tile * width), BF),
            jax.ShapeDtypeStruct((channels, rows), BF),
            jax.ShapeDtypeStruct((1, channels), F32),
        ],
        scratch_shapes=halo.scratch()
        + [
            pltpu.VMEM(halo.halo_shape().shape, BF),
            pltpu.SMEM((n_tile,) + neighbours.shape, jnp.int32),
            pltpu.VMEM(((side + 2 * RIM) * PITCH, LANES), F32),
            pltpu.SemaphoreType.DMA((total,)),
            pltpu.SemaphoreType.DMA((total,)),
            pltpu.SemaphoreType.DMA((pairs,)),
            pltpu.SemaphoreType.DMA((2,)),
        ],
        compiler_params=remote_params(1, 63),
        name="exchange_forward",
    )(rims, packed, neighbours, inputs, mask_lanes, taps, cotangent, flat_mask, weight_row)


def exchange_backward(grid, rims, grads, neighbours, inputs, mask_lanes, d_conv, halos, small):
    n_chunk, slots, _, band, _ = rims.shape
    side, channels = inputs.shape[1], inputs.shape[3]
    side_b, side_x = grid.size["b"], grid.size["x"]
    _, blocks, rows, cols = grads.shape
    pairs = blocks // side_x
    part = rows // side_b
    side_a = grid.size["a"]
    piece = part // side_a
    halo = HaloExchange(grid, n_chunk, slots, side)
    hops = [(dim, 1 << i) for dim in ("c", "x", "b", "a") for i in range((grid.size[dim] - 1).bit_length())]
    total = len(hops) + 1 + halo.count + blocks + side_a * pairs * side_x * side_b * 2
    total += pairs * (side_a - 1 + 5 + side_a * (side_b - 1))
    last = n_chunk * slots - 1
    small_rows = small.shape[0]
    small_shape = (up_to(50 + small_rows, 16), n_chunk * LANES)

    def kernel(
        r_ref, g_ref, n_ref, x_ref, m_ref, d_ref, h_ref, s_ref, halo_ref, o_ref, t_ref,
        arrived, picked, local, here, core, far, across, pad, sums, got, mine, heard, send, recv, load_sems,
    ):
        own = grid.own()
        own_x, own_b, own_c = own["x"], own["b"], own["c"]
        step = pl.program_id(0) * slots + pl.program_id(1)
        copies = Copies(send, recv)
        halo.plan(copies, r_ref, arrived, picked, halo_ref, local)
        order = [(k, m) for m in range(pairs) for k in range(1, side_x)]
        order += [(0, m) for m in range(pairs - 1, -1, -1)]
        index = lambda k, m: (own_x ^ k) * pairs + m
        own_a = own["a"]
        row_of = lambda a, b: pl.ds(pl.multiple_of((b * side_a + a) * piece, 16), piece)
        part_row = lambda a: pl.ds(pl.multiple_of(a * piece, 16), piece)
        turns = [*range(1, side_a), 0]
        cores, loads = [], []
        for i, (k, m) in enumerate(order):
            at = index(k, m)
            cores.append(copies.make(g_ref.at[1 - own_c, at], core.at[at], grid.beside(own, "c", 1)))
            loads.append(pltpu.make_async_copy(g_ref.at[own_c, at], here.at[at], load_sems.at[i]))
        one, two, one_adds, two_adds = {}, {}, {}, {}
        for m in range(pairs):
            for k in turns:
                a = own_a ^ k
                mine_at = here.at[index(0, m), row_of(a, own_b)]
                across_x = lambda q, b: (
                    copies.make(
                        here.at[index(q, m), row_of(a, b)], far.at[q - 1, m, row_of(a, b)], grid.beside(own, "x", q)
                    )
                )
                across_b = lambda q, j: (
                    copies.make(
                        here.at[index(q, m), row_of(a, own_b ^ j)],
                        across.at[j - 1, index(q, m), part_row(a)],
                        grid.beside(own, "b", j),
                    )
                )
                from_x = lambda b: [far.at[q - 1, m, row_of(a, b)] for q in range(1, side_x)]
                from_b = lambda q: [across.at[j - 1, index(q, m), part_row(a)] for j in range(1, side_b)]
                if m % 2 == 0:
                    one[k, m] = [across_x(q, b) for q in range(1, side_x) for b in range(side_b)]
                    one_adds[k, m] = [(here.at[index(0, m), row_of(a, b)], from_x(b)) for b in range(side_b)]
                    two[k, m] = [across_b(0, j) for j in range(1, side_b)]
                    two_adds[k, m] = [(mine_at, from_b(0))]
                else:
                    one[k, m] = [across_b(q, j) for q in range(side_x) for j in range(1, side_b)]
                    one_adds[k, m] = [(here.at[index(q, m), row_of(a, own_b)], from_b(q)) for q in range(side_x)]
                    two[k, m] = [across_x(q, own_b) for q in range(1, side_x)]
                    two_adds[k, m] = [(mine_at, from_x(own_b))]

        to_a, back_a, back_b, keeps = {}, {}, {}, []
        for m in range(pairs):
            at = index(0, m)
            done = here.at[at, row_of(own_a, own_b)]
            place = o_ref.at[m, row_of(own_a, own_b)]
            keeps.append(pltpu.make_async_copy(done, place, load_sems.at[m]))
            for k in range(1, side_a):
                to = grid.beside(own, "a", k)
                to_a[k, m] = copies.make(here.at[at, row_of(own_a ^ k, own_b)], got.at[m, k - 1], to)
            got_at = lambda k: o_ref.at[m, row_of(own_a ^ k, own_b)]
            beside_a = lambda k: grid.beside(own, "a", k)
            back_a["near", m] = copies.make(done, place, beside_a(1))
            back_a["over", m] = copies.make(done, place, beside_a(3))
            back_a["over2", m] = copies.make(got_at(1), got_at(1), beside_a(3))
            back_a["out", m] = copies.make(got_at(3), got_at(3), beside_a(1))
            back_a["out2", m] = copies.make(got_at(2), got_at(2), beside_a(1))
            for k in range(side_a):
                for j in range(1, side_b):
                    came = o_ref.at[m, row_of(own_a ^ k, own_b)]
                    back_b[k, j, m] = copies.make(done if k == 0 else came, came, grid.beside(own, "b", j))
        middle = (own_a == 1) | (own_a == 2)
        lines = small_shape[0] // 2
        own_half = pl.ds(pl.multiple_of(own_c * lines, 8), lines)
        other_half = pl.ds(pl.multiple_of((1 - own_c) * lines, 8), lines)
        hop_copies = [copies.make(mine.at[other_half], heard.at[0], grid.beside(own, "c", 1))]
        hop_copies += [
            copies.make(mine.at[own_half], heard.at[i], grid.beside(own, dim, k))
            for i, (dim, k) in enumerate(hops)
            if i > 0
        ]
        hop_copies.append(copies.make(mine.at[own_half], heard.at[len(hops)], grid.beside(own, "c", 1)))

        def hop(i):
            if 0 < i <= len(hops):
                hop_copies[i - 1].wait()
                mine[own_half, :] = mine[own_half, :] + heard[i - 1]
            if i <= len(hops):
                hop_copies[i].start()
            else:
                hop_copies[i - 1].wait()

        def start(found):
            for copy in found:
                copy.start()

        def wait(found):
            for copy in found:
                copy.wait()

        @pl.when(step == 0)
        def _():
            meet(grid.partners(("tile", "x", "c")))
            halo.send_rims()
            mine[...] = jnp.zeros_like(mine)
            start(cores)
            start(loads)

        add_taps(x_ref, m_ref, d_ref, h_ref, mine, pad, sums, slots, side)

        ready = {}
        for i, (k, m) in enumerate(order):
            ready[m] = max(ready.get(m, 0), i) if m % 2 == 1 or k > 0 else ready.get(m, 0)
        for i, (k, m) in enumerate(order):

            @pl.when(step == min(last, 3 + 2 * i))
            def _():
                loads[i].wait()
                cores[i].wait()
                at = index(k, m)
                add_rows(here.at[at], [core.at[at]], rows)
                for n in range(pairs):
                    if ready[n] == i:
                        start(one[turns[0], n])
                        start(one[turns[1], n])

        @pl.when(step == last)
        def _():
            halo.pick_and_send(lambda d, k: n_ref[d // slots, d % slots, k])
            mine[pl.ds(50, small_rows), pl.ds(0, channels)] = s_ref[...]
            for i in range(side_a + 1):
                hop(i)
                for m in range(pairs):
                    if i < side_a:
                        k = turns[i]
                        wait(one[k, m])
                        if i + 2 < side_a:
                            start(one[turns[i + 2], m])
                        for target, sources in one_adds[k, m]:
                            add_rows(target, sources, piece)
                        start(two[k, m])
                for m in range(pairs):
                    if i > 0:
                        k = turns[i - 1]
                        wait(two[k, m])
                        for target, sources in two_adds[k, m]:
                            add_rows(target, sources, piece)
                        if k > 0:
                            to_a[k, m].start()
            for m in range(pairs):
                wait(to_a[k, m] for k in range(1, side_a))
                done = here.at[index(0, m), row_of(own_a, own_b)]
                add_rows(done, [got.at[m, k] for k in range(side_a - 1)], piece)
                keeps[m].start()
                back_a["near", m].start()

                @pl.when(middle)
                def _():
                    back_a["over", m].start()

                start(back_b[0, j, m] for j in range(1, side_b))

            def arrive(came, k, onward):
                for m in range(pairs):
                    back_a[came, m].wait_recv()
                    if onward is not None:
                        back_a[onward, m].start()
                    start(back_b[k, j, m] for j in range(1, side_b))

            for m in range(pairs):
                back_a["near", m].wait_recv()

                @pl.when(middle)
                def _():
                    back_a["over2", m].start()

                start(back_b[1, j, m] for j in range(1, side_b))

            @pl.when(middle)
            def _():
                arrive("over", 3, "out")
                arrive("over2", 2, "out2")

            @pl.when(~middle)
            def _():
                arrive("out", 2, None)
                arrive("out2", 3, None)

            for i in range(side_a + 1, len(hops) + 2):
                hop(i)
            halo.finish()
            t_ref[own_half, :] = mine[own_half, :]
            t_ref[other_half, :] = heard[len(hops)]
            for m in range(pairs):
                keeps[m].wait()
                back_a["near", m].wait_send()

                @pl.when(middle)
                def _():
                    for name in ("over", "over2", "out", "out2"):
                        back_a[name, m].wait_send()

            wait(back_b.values())

    any_space = pl.BlockSpec(memory_space=pl.ANY)
    cells = side * side
    return pl.pallas_call(
        kernel,
        grid=(n_chunk, slots),
        in_specs=[
            any_space,
            any_space,
            pl.BlockSpec(memory_space=pltpu.SMEM),
            pl.BlockSpec((1, side, side, LANES), lambda c, s: (s, 0, 0, c)),
            pl.BlockSpec((1, cells, LANES), lambda c, s: (s, 0, 0)),
            pl.BlockSpec((1, cells, LANES), lambda c, s: (s, 0, c)),
            halo_block(halos),
            pl.BlockSpec(small.shape, lambda c, s: (0, 0)),
        ],
        out_specs=[any_space, any_space, pl.BlockSpec(small_shape, lambda c, s: (0, 0))],
        out_shape=[
            halo.halo_shape(),
            jax.ShapeDtypeStruct((pairs, rows, cols), BF),
            jax.ShapeDtypeStruct(small_shape, F32),
        ],
        scratch_shapes=halo.scratch()
        + [
            pltpu.VMEM((blocks, rows, cols), BF),
            pltpu.VMEM((blocks, rows, cols), BF),
            pltpu.VMEM((side_x - 1, pairs, rows, cols), BF),
            pltpu.VMEM((side_b - 1, blocks, part, cols), BF),
            pltpu.VMEM(((side + 2 * RIM) * PITCH, LANES), F32),
            pltpu.VMEM((50, 8, LANES), F32),
            pltpu.VMEM((pairs, side_a - 1, piece, cols), BF),
            pltpu.VMEM(small_shape, F32),
            pltpu.VMEM((len(hops) + 1, small_shape[0] // 2, small_shape[1]), F32),
            pltpu.SemaphoreType.DMA((total,)),
            pltpu.SemaphoreType.DMA((total,)),
            pltpu.SemaphoreType.DMA((blocks,)),
        ],
        compiler_params=remote_params(2, 60),
        name="exchange_backward",
    )(rims, grads, neighbours, inputs, mask_lanes, d_conv, halos, small)


def tile_total(grid, value, number):
    n_tile = grid.n_tile

    def kernel(v_ref, o_ref, got, send, recv):
        t, o = grid.at(grid.own())
        meet(grid.partners(("tile",)))
        copies = Copies(send, recv)
        got[t] = v_ref[...]
        sent = [copies.start(v_ref, got.at[t], (t ^ k, o)) for k in range(1, n_tile)]
        for copy in sent:
            copy.wait()
        total = got[0]
        for i in range(1, n_tile):
            total = total + got[i]
        o_ref[...] = total

    whole = pl.BlockSpec(memory_space=pltpu.VMEM)
    return pl.pallas_call(
        kernel,
        in_specs=[whole],
        out_specs=whole,
        out_shape=jax.ShapeDtypeStruct(value.shape, F32),
        scratch_shapes=[
            pltpu.VMEM((n_tile,) + value.shape, F32),
            pltpu.SemaphoreType.DMA((n_tile - 1,)),
            pltpu.SemaphoreType.DMA((n_tile - 1,)),
        ],
        compiler_params=remote_params(number, 16),
        name="tile_total",
    )(value)


def fill_halo(pad, halo, side):
    last = side + RIM
    up, down, left, right, corner = (halo(k) for k in range(5))
    for e in range(RIM):
        rows = slice(e * side, e * side + side)
        pad[pl.ds(e * PITCH + 8, side), :] = up[rows]
        pad[pl.ds((last + e) * PITCH + 8, side), :] = down[rows]
        pad[pl.ds(RIM * PITCH + 8 - RIM + e, side, stride=PITCH), :] = left[rows]
        pad[pl.ds(RIM * PITCH + 8 + side + e, side, stride=PITCH), :] = right[rows]
    places = ((0, 8 - RIM), (0, 8 + side), (last, 8 - RIM), (last, 8 + side))
    for k, (row, col) in enumerate(places):
        for e in range(RIM):
            at = 16 * k + RIM * e
            pad[pl.ds((row + e) * PITCH + col, RIM), :] = corner[at : at + RIM]


def conv_pass(pad, side, weight, emit):
    for block in range(side // 8):
        sums = [None] * side
        for b in range(7):
            taps = [weight(a, b) for a in range(7)]
            for r in range(side + 2 * RIM):
                cells = pad[pl.ds(r * PITCH + 8 - RIM + b + 8 * block, 8), :]
                for a in range(7):
                    i = r - a
                    if 0 <= i < side:
                        term = taps[a] * cells
                        sums[i] = term if sums[i] is None else sums[i] + term
        emit(block, sums)


def halo_block(halos):
    return pl.BlockSpec((1, 1) + halos.shape[2:], lambda c, s: (c, s, 0, 0, 0))


def conv_step(x_ref, m_ref, w_ref, halo, o_ref, s_ref, pad, side):
    for i in range(side):
        pad[pl.ds((i + RIM) * PITCH + 8, side), :] = x_ref[0, i].astype(F32) * m_ref[0, pl.ds(i * side, side), :]
    fill_halo(pad, halo, side)
    bias = w_ref[49]
    totals = [jnp.zeros((8, LANES), F32), jnp.zeros((8, LANES), F32)]

    def emit(block, sums):
        for i in range(side):
            value = sums[i] + bias
            rows = pl.ds(i * side + 8 * block, 8)
            o_ref[0, rows, :] = value
            weighted = m_ref[0, rows, :] * value
            totals[0] = totals[0] + weighted
            totals[1] = totals[1] + weighted * value

    conv_pass(pad, side, lambda a, b: w_ref[7 * a + b], emit)
    s_ref[0, 0], s_ref[0, 1] = totals


def conv_gradient(d_shaped, conv_out, mask_lanes, coefs, side):
    slots, cells, channels = d_shaped.shape
    n_chunk = -(-channels // LANES)

    def kernel(d_ref, v_ref, m_ref, c_ref, o_ref, r_ref, held):
        one, two, three = c_ref[0, :1], c_ref[1, :1], c_ref[2, :1]
        for s in range(slots):
            value = d_ref[s] * one - m_ref[s] * (two + three * v_ref[s])
            o_ref[s] = value
            held[...] = value
            store_rims(held, r_ref, s, side)

    piece = (slots, 4, RIM * side, LANES)
    block = pl.BlockSpec((slots, cells, LANES), lambda c: (0, 0, c))
    return pl.pallas_call(
        kernel,
        grid=(n_chunk,),
        in_specs=[
            block,
            block,
            pl.BlockSpec((slots, cells, LANES), lambda c: (0, 0, 0)),
            pl.BlockSpec((3, 8, LANES), lambda c: (0, 0, c)),
        ],
        out_specs=[block, pl.BlockSpec((1,) + piece, lambda c: (c, 0, 0, 0, 0))],
        scratch_shapes=[pltpu.VMEM((cells, LANES), F32)],
        out_shape=[
            jax.ShapeDtypeStruct((slots, cells, channels), F32),
            jax.ShapeDtypeStruct((n_chunk,) + piece, BF),
        ],
        compiler_params=pltpu.CompilerParams(vmem_limit_bytes=32 << 20),
        name="conv_gradient",
    )(d_shaped, conv_out, mask_lanes, coefs)


def add_taps(x_ref, m_ref, d_ref, h_ref, o_ref, pad, sums, slots, side):
    slot = pl.program_id(1)
    for i in range(side):
        pad[pl.ds((i + RIM) * PITCH + 8, side), :] = x_ref[0, i].astype(F32) * m_ref[0, pl.ds(i * side, side), :]
    fill_halo(pad, lambda k: h_ref[0, 0, k].astype(F32), side)

    @pl.when(slot == 0)
    def _():
        sums[...] = jnp.zeros_like(sums)

    for block in range(side // 8):
        grads = [d_ref[0, pl.ds(i * side + 8 * block, 8), :] for i in range(side)]
        total = grads[0]
        for i in range(1, side):
            total = total + grads[i]
        sums[49] += total
        for b in range(7):
            taps = [None] * 7
            for r in range(side + 2 * RIM):
                window = pad[pl.ds(r * PITCH + 8 - RIM + b + 8 * block, 8), :]
                for a in range(7):
                    i = r - a
                    if 0 <= i < side:
                        term = window * grads[i]
                        taps[a] = term if taps[a] is None else taps[a] + term
            for a in range(7):
                sums[7 * a + b] += taps[a]

    @pl.when(slot == slots - 1)
    def _():
        at = pl.multiple_of(pl.program_id(0) * LANES, LANES)
        o_ref[pl.ds(0, 50), pl.ds(at, LANES)] = jnp.sum(sums[...], axis=1)


def conv_backward(grid, d_conv, halos, cotangent, mask_lanes, taps, weight_lanes, change):
    slots, side, _, channels = cotangent.shape
    n_chunk = halos.shape[0]
    cells = side * side
    pairs, rows, cols = change.shape
    side_a, side_b = grid.size["a"], grid.size["b"]
    part = rows // side_b
    piece = part // side_a
    total = pairs * (side_a * (side_b - 1) + (side_a - 1))
    last = n_chunk * slots - 1

    def kernel(
        d_ref, g_ref, m_ref, w_ref, l_ref, h_ref, c_ref, o_ref, change_ref,
        pad, mine, from_b, from_a, send, recv, load_sems,
    ):
        own = grid.own()
        step = pl.program_id(0) * slots + pl.program_id(1)
        copies = Copies(send, recv)
        own_a, own_b = own["a"], own["b"]
        half = lambda b: pl.ds(pl.multiple_of(b * part, 16), part)
        row_of = lambda a, b: pl.ds(pl.multiple_of((b * side_a + a) * piece, 16), piece)
        part_row = lambda a: pl.ds(pl.multiple_of(a * piece, 16), piece)
        turns = [*range(1, side_a), 0]
        firsts, seconds, loads = {}, {}, []
        for m in range(pairs):
            for k in turns:
                a = own_a ^ k
                firsts[k, m] = [
                    copies.make(
                        c_ref.at[m, row_of(a, own_b ^ j)], from_b.at[j - 1, m, part_row(a)], grid.beside(own, "b", j)
                    )
                    for j in range(1, side_b)
                ]
                if k > 0:
                    seconds[k, m] = copies.make(
                        mine.at[m, part_row(a)], from_a.at[k - 1, m], grid.beside(own, "a", k)
                    )
            loads.append(pltpu.make_async_copy(c_ref.at[m, half(own_b)], mine.at[m], load_sems.at[m]))

        @pl.when(step == 0)
        def _():
            meet(grid.partners(("a", "b")))
            for load in loads:
                load.start()
            for k in turns:
                for m in range(pairs):
                    for copy in firsts[k, m]:
                        copy.start()

        for i in range(side):
            pad[pl.ds((i + RIM) * PITCH + 8, side), :] = d_ref[0, pl.ds(i * side, side), :]
        fill_halo(pad, lambda k: h_ref[0, 0, k].astype(F32), side)
        weight = l_ref[...]

        def emit(block, sums):
            for i in range(side):
                at = pl.ds(i * side + 8 * block, 8)
                scaled = weight * g_ref[0, i, pl.ds(8 * block, 8), :].astype(F32)
                o_ref[0, at, :] = m_ref[0, at, :] * (scaled + sums[i])

        conv_pass(pad, side, lambda a, b: w_ref[7 * (6 - a) + 6 - b], emit)

        for i, k in enumerate(turns):

            @pl.when(step == min(last, 5 + 4 * i))
            def _():
                for m in range(pairs):
                    if i == 0:
                        loads[m].wait()
                    for copy in firsts[k, m]:
                        copy.wait()
                    rows_here = part_row(own_a ^ k)
                    sources = [from_b.at[j, m, rows_here] for j in range(side_b - 1)]
                    add_rows(mine.at[m, rows_here], sources, piece)
                    if k > 0:
                        seconds[k, m].start()

        @pl.when(step == last)
        def _():
            for m in range(pairs):
                for k in range(1, side_a):
                    seconds[k, m].wait()
                value = mine[m, part_row(own_a)].astype(F32)
                for k in range(side_a - 1):
                    value = value + from_a[k, m].astype(F32)
                change_ref[m] = value

    return pl.pallas_call(
        kernel,
        grid=(n_chunk, slots),
        in_specs=[
            pl.BlockSpec((1, cells, LANES), lambda c, s: (s, 0, c)),
            pl.BlockSpec((1, side, side, LANES), lambda c, s: (s, 0, 0, c)),
            pl.BlockSpec((1, cells, LANES), lambda c, s: (s, 0, 0)),
            pl.BlockSpec((50, 8, LANES), lambda c, s: (0, 0, c)),
            pl.BlockSpec((8, LANES), lambda c, s: (0, 0)),
            halo_block(halos),
            pl.BlockSpec(memory_space=pl.ANY),
        ],
        out_specs=[
            pl.BlockSpec((1, cells, LANES), lambda c, s: (s, 0, c)),
            pl.BlockSpec((pairs, piece, cols), lambda c, s: (0, 0, 0)),
        ],
        scratch_shapes=[
            pltpu.VMEM(((side + 2 * RIM) * PITCH, LANES), F32),
            pltpu.VMEM((pairs, part, cols), BF),
            pltpu.VMEM((side_b - 1, pairs, part, cols), BF),
            pltpu.VMEM((side_a - 1, pairs, piece, cols), BF),
            pltpu.SemaphoreType.DMA((total,)),
            pltpu.SemaphoreType.DMA((total,)),
            pltpu.SemaphoreType.DMA((pairs,)),
        ],
        out_shape=[
            jax.ShapeDtypeStruct((slots, cells, channels), F32),
            jax.ShapeDtypeStruct((pairs, piece, cols), F32),
        ],
        compiler_params=remote_params(4, 48),
        name="conv_backward",
    )(d_conv, cotangent, mask_lanes, taps, weight_lanes, halos, change)


def spread_lanes(value, parts, width):
    rows, channels = value.shape
    run = channels // parts
    if run == width:
        return value
    gap = jnp.zeros((rows, width - run), value.dtype)
    pieces = []
    for t in range(parts):
        pieces += [value[:, t * run : (t + 1) * run], gap]
    return jnp.concatenate(pieces, 1)


def close_lanes(value, parts, run):
    width = value.shape[1] // parts
    if run == width:
        return value
    return jnp.concatenate([value[:, t * width : t * width + run] for t in range(parts)], 1)


def row_block(rows):
    return 3 * LANES if rows % (3 * LANES) == 0 else LANES


def arranged(value, gap_ref, turned_ref, sum_ref, first, parts, width):
    low = value.astype(BF).astype(F32)
    gap_ref[...] = spread_lanes(low, parts, width).astype(BF)
    turned_ref[...] = low.T.astype(BF)

    @pl.when(first)
    def _():
        sum_ref[...] = jnp.zeros_like(sum_ref)

    sum_ref[...] += jnp.sum(low, axis=0, keepdims=True)


def arrange(body, args, specs, rows, channels, parts, width, name):
    step = row_block(rows)

    def kernel(*refs):
        given, (gap_ref, turned_ref, sum_ref) = refs[: len(args)], refs[len(args) :]
        arranged(body(*given), gap_ref, turned_ref, sum_ref, pl.program_id(0) == 0, parts, width)

    return pl.pallas_call(
        kernel,
        grid=(rows // step,),
        in_specs=specs(step),
        out_specs=[
            pl.BlockSpec((step, parts * width), lambda i: (i, 0)),
            pl.BlockSpec((channels, step), lambda i: (0, i)),
            pl.BlockSpec((1, channels), lambda i: (0, 0)),
        ],
        out_shape=[
            jax.ShapeDtypeStruct((rows, parts * width), BF),
            jax.ShapeDtypeStruct((channels, rows), BF),
            jax.ShapeDtypeStruct((1, channels), F32),
        ],
        compiler_params=pltpu.CompilerParams(vmem_limit_bytes=48 << 20),
        name=name,
    )(*args)


def feed_forward(inverse, shaped, shaped_t, d_branch, d_branch_t, hidden_bias, weights, grad_rows):
    rows, depth = shaped.shape
    channels = shaped_t.shape[0]
    half, _, cols = hidden_bias.shape
    pairs, owners = weights.shape[:2]
    per_owner = 2 * pairs
    tile_rows = 3 * LANES if rows % (3 * LANES) == 0 else LANES

    def kernel(inv_ref, s_ref, st_ref, d_ref, dt_ref, hb_ref, w_ref, branch_ref, ds_ref, grad_ref, bias_ref, *scratch):
        packed, first, second, act, dpre, grads, sems, out_sem = scratch
        step = pl.program_id(0)

        def where(slot):
            owner, inside = slot // per_owner, slot % per_owner
            return owner, inside // 2, inside % 2

        def fetch(h, buffer):
            copies = []
            for which in range(2):
                owner, pair, _ = where(inv_ref[h + which * half])
                copies.append(
                    pltpu.make_async_copy(w_ref.at[pair, owner], packed.at[buffer, which], sems.at[buffer, which])
                )
            return copies

        @pl.when(step == 0)
        def _():
            for copy in fetch(0, 0):
                copy.start()
            if grad_rows > channels:
                rest = grad_rows - channels
                grads[:, :, pl.ds(channels, rest), :] = jnp.zeros(grads.shape[:2] + (rest, 2 * cols), BF)

        @pl.when(step + 1 < half)
        def _():
            for copy in fetch(step + 1, (step + 1) % 2):
                copy.start()

        now = step % 2
        slots = [where(inv_ref[step + which * half]) for which in range(2)]
        waits = fetch(step, now)
        for which, held in enumerate((first, second)):
            waits[which].wait()
            for parity in range(2):

                @pl.when(slots[which][2] == parity)
                def _():
                    held[...] = packed[now, which, :, parity * cols : (parity + 1) * cols]

        hidden = hb_ref[0]

        @pl.when(step == 0)
        def _():
            branch_ref[...] = jnp.zeros_like(branch_ref)
            ds_ref[...] = jnp.zeros_like(ds_ref)

        total = jnp.zeros((1, cols), F32)
        across = (((1,), (1,)), ((), ()))
        for i in range(rows // tile_rows):
            at = pl.ds(i * tile_rows, tile_rows)
            pre = jnp.dot(s_ref[at, :], first[...], preferred_element_type=F32) + hidden
            d_act = jnp.dot(d_ref[at, :], second[...], preferred_element_type=F32)
            square = pre * pre
            bend = jnp.tanh(ROOT * pre * (1.0 + CUBE * square))
            half_up = 0.5 * (1.0 + bend)
            low = (pre * half_up).astype(BF)
            slope = half_up + (0.5 * ROOT) * pre * (1.0 - bend * bend) * (1.0 + (3.0 * CUBE) * square)
            back = (d_act * slope).astype(BF)
            act[at, :] = low
            dpre[at, :] = back
            total = total + jnp.sum(back.astype(F32), axis=0, keepdims=True)
            out_add = lax.dot_general(low, second[...], across, preferred_element_type=F32)
            in_add = lax.dot_general(back, first[...], across, preferred_element_type=F32)

            branch_ref[at, :] += out_add
            ds_ref[at, :] += in_add

        bias_ref[0] = total
        for which, (left, right) in enumerate(((st_ref, dpre), (dt_ref, act))):
            owner, pair, half_of_pair = slots[which]
            value = jnp.dot(left[...], right[...], preferred_element_type=F32).astype(BF)
            for parity in range(2):

                @pl.when(half_of_pair == parity)
                def _():
                    at = (owner // 2) * pairs + pair
                    grads[owner % 2, at, pl.ds(0, channels), parity * cols : (parity + 1) * cols] = value

        @pl.when(step == half - 1)
        def _():
            out = pltpu.make_async_copy(grads, grad_ref, out_sem.at[0])
            out.start()
            out.wait()

    whole = lambda *shape: pl.BlockSpec(shape, lambda h, *_: (0,) * len(shape))
    line = pl.BlockSpec((1, 1, cols), lambda h, *_: (h, 0, 0))
    grad_shape = (2, owners // 2 * pairs, grad_rows, 2 * cols)
    return pl.pallas_call(
        kernel,
        grid_spec=pltpu.PrefetchScalarGridSpec(
            num_scalar_prefetch=1,
            grid=(half,),
            in_specs=[
                whole(rows, depth),
                whole(channels, rows),
                whole(rows, depth),
                whole(channels, rows),
                line,
                pl.BlockSpec(memory_space=pl.ANY),
            ],
            out_specs=[whole(rows, depth), whole(rows, depth), pl.BlockSpec(memory_space=pl.ANY), line],
            scratch_shapes=[
                pltpu.VMEM((2, 2, depth, 2 * cols), BF),
                pltpu.VMEM((depth, cols), BF),
                pltpu.VMEM((depth, cols), BF),
                pltpu.VMEM((rows, cols), BF),
                pltpu.VMEM((rows, cols), BF),
                pltpu.VMEM(grad_shape, BF),
                pltpu.SemaphoreType.DMA((2, 2)),
                pltpu.SemaphoreType.DMA((1,)),
            ],
        ),
        out_shape=[
            jax.ShapeDtypeStruct((rows, depth), F32),
            jax.ShapeDtypeStruct((rows, depth), F32),
            jax.ShapeDtypeStruct(grad_shape, BF),
            jax.ShapeDtypeStruct((half, 1, cols), F32),
        ],
        cost_estimate=pl.CostEstimate(
            flops=12 * rows * channels * half * cols, bytes_accessed=40 << 20, transcendentals=rows * half * cols
        ),
        compiler_params=pltpu.CompilerParams(vmem_limit_bytes=63 << 20),
        name="feed_forward",
    )(inverse, shaped, shaped_t, d_branch, d_branch_t, hidden_bias, weights)


def close_out(branch, d_shaped, inputs, conv_out, mask_lanes, out_bias, parts, run):
    rows, channels = inputs.shape
    depth = branch.shape[1]
    step = row_block(rows)

    def kernel(b_ref, d_ref, x_ref, v_ref, m_ref, o_ref, out_ref, ds_ref, sum_ref):
        branch_here = close_lanes(b_ref[...], parts, run) + o_ref[...]
        out_ref[...] = (m_ref[:, :1] * (x_ref[...].astype(F32) + branch_here)).astype(BF)
        grads = close_lanes(d_ref[...], parts, run)
        ds_ref[...] = grads

        @pl.when(pl.program_id(0) == 0)
        def _():
            sum_ref[...] = jnp.zeros_like(sum_ref)

        sum_ref[0] += jnp.sum(grads, axis=0, keepdims=True)
        sum_ref[1] += jnp.sum(grads * v_ref[...], axis=0, keepdims=True)

    line = lambda n: pl.BlockSpec((step, n), lambda i: (i, 0))
    return pl.pallas_call(
        kernel,
        grid=(rows // step,),
        in_specs=[
            line(depth),
            line(depth),
            line(channels),
            line(channels),
            line(LANES),
            pl.BlockSpec((1, channels), lambda i: (0, 0)),
        ],
        out_specs=[line(channels), line(channels), pl.BlockSpec((2, 1, channels), lambda i: (0, 0, 0))],
        out_shape=[
            jax.ShapeDtypeStruct((rows, channels), BF),
            jax.ShapeDtypeStruct((rows, channels), F32),
            jax.ShapeDtypeStruct((2, 1, channels), F32),
        ],
        compiler_params=pltpu.CompilerParams(vmem_limit_bytes=60 << 20),
        name="close_out",
    )(branch, d_shaped, inputs, conv_out, mask_lanes, out_bias)


def halves(value):
    high = value.astype(BF)
    return high, (value - high.astype(F32)).astype(BF)


def product(left, right, contract):
    dims = (contract, ((), ()))
    total = None
    for i, a in enumerate(left):
        for j, b in enumerate(right):
            if i + j < 2:
                term = lax.dot_general(a, b, dims, preferred_element_type=F32)
                total = term if total is None else total + term
    return total


def rotate(owned, left_basis, column_basis, moment_one, moment_two, correction, grid, width):
    slots, channels, run = left_basis.shape
    cols = column_basis.shape[1]
    pairs = slots // 2
    side_a, side_b = grid.size["a"], grid.size["b"]
    n_tile = grid.n_tile

    def kernel(f_ref, g_ref, l_ref, c_ref, one_ref, two_ref, first_ref, second_ref, o_ref):
        factor = f_ref[0]
        changes = []
        for p in range(2):
            grad = g_ref[0, pl.ds(0, channels), p * cols : (p + 1) * cols]
            left = halves(l_ref[p])
            column = halves(c_ref[p])
            rotated = product(left, (grad,), ((0,), (0,)))
            rotated = product(halves(rotated), column, ((1,), (0,)))
            first = decay_rate * one_ref[p] + (1.0 - decay_rate) * rotated
            second = decay_rate * two_ref[p] + (1.0 - decay_rate) * rotated * rotated
            first_ref[p] = first
            second_ref[p] = second
            direction = first * factor / (jnp.sqrt(second * factor) + adam_eps)
            turned = product(halves(direction), column, ((1,), (1,)))
            changes.append(product(left, halves(turned), ((1,), (0,))))
        change = jnp.concatenate(changes, 1)
        gap = jnp.zeros((width - run, 2 * cols), F32)
        for t in range(n_tile):
            piece = jnp.concatenate([change[t * run : (t + 1) * run], gap], 0)
            place = (t % side_b) * side_a + t // side_b
            o_ref[0, pl.ds(place * width, width), :] = piece.astype(BF)

    pair = lambda *shape: pl.BlockSpec(shape, lambda m: (m,) + (0,) * (len(shape) - 1))
    return pl.pallas_call(
        kernel,
        grid=(pairs,),
        in_specs=[
            pl.BlockSpec(memory_space=pltpu.SMEM),
            pair(1, owned.shape[1], 2 * cols),
            pair(2, channels, run),
            pair(2, cols, cols),
            pair(2, run, cols),
            pair(2, run, cols),
        ],
        out_specs=[pair(2, run, cols), pair(2, run, cols), pair(1, n_tile * width, 2 * cols)],
        out_shape=[
            jax.ShapeDtypeStruct(moment_one.shape, F32),
            jax.ShapeDtypeStruct(moment_one.shape, F32),
            jax.ShapeDtypeStruct((pairs, n_tile * width, 2 * cols), BF),
        ],
        compiler_params=pltpu.CompilerParams(vmem_limit_bytes=60 << 20),
        name="rotate",
    )(1.0 / correction.reshape(1), owned, left_basis, column_basis, moment_one, moment_two)


def up_to(value, unit):
    return -(-value // unit) * unit


def pack_pairs(value):
    slots, rows, cols = value.shape
    return value.reshape(slots // 2, 2, rows, cols).transpose(0, 2, 1, 3).reshape(slots // 2, rows, 2 * cols)


def unpack_pairs(value):
    pairs, rows, cols = value.shape
    return value.reshape(pairs, rows, 2, cols // 2).transpose(0, 2, 1, 3).reshape(2 * pairs, rows, cols // 2)


def per_device(
    grid,
    inputs,
    cotangent,
    master,
    moment_one,
    moment_two,
    left_basis,
    column_basis,
    small_params,
    small_first,
    small_second,
    land_mask,
    tile_count,
    neighbours,
    block_order,
    cell_weight,
    step_count,
):
    position = lax.axis_index("tile")
    sample = lax.axis_index("opt")
    inputs, cotangent = inputs[0], cotangent[0]
    slots, side, _, channels = inputs.shape
    cells = side * side
    rows = slots * cells
    n_tile = grid.n_tile
    n_chunk = -(-channels // LANES)
    per_group = channels // GROUPS
    per_owner, run, cols = master.shape
    pairs = per_owner // 2
    block_total = block_order.shape[0]
    half = block_total // 2
    width = up_to(run, 16)

    live = (jnp.arange(slots) < tile_count[position]).astype(F32)
    mask = (land_mask.astype(F32) * live[:, None, None]).reshape(slots, cells)
    mask_lanes = jnp.broadcast_to(mask[:, :, None], (slots, cells, LANES))
    flat_mask = mask_lanes.reshape(rows, LANES)
    taps = jnp.broadcast_to(small_params[:50, None, :], (50, 8, channels))

    weights_float = cell_weight.astype(F32)
    sample_weight = weights_float[sample] * weights_float.shape[0] / jnp.sum(weights_float)
    weight_lanes = jnp.broadcast_to(sample_weight, (8, LANES))
    weight_row = jnp.broadcast_to(sample_weight, (1, LANES))

    low_master = jnp.pad(pack_pairs(master.astype(BF)), ((0, 0), (0, width - run), (0, 0)))
    rims = rims_of_input(inputs, mask_lanes)
    halos, weights, all_neighbours, conv_out, sums, d_branch, d_branch_t, d_out_bias = exchange_forward(
        grid,
        rims,
        low_master,
        neighbours,
        inputs,
        mask_lanes,
        taps,
        cotangent.reshape(rows, channels),
        flat_mask,
        weight_row,
        width,
    )

    sums = jnp.sum(sums, axis=(0, 2))
    occupied = jnp.broadcast_to(jnp.sum(mask), (1, channels))
    sums = tile_total(grid, jnp.concatenate([sums, occupied], 0), 5)
    counted = sums[2, 0] * per_group
    by_group = sums[:2].reshape(2, GROUPS, per_group).sum(2)
    group_mean = by_group[0] / counted
    variance = by_group[1] / counted - group_mean * group_mean
    inv_std = jnp.repeat(lax.rsqrt(variance + epsilon), per_group)
    mean = jnp.repeat(group_mean, per_group)
    gain, shift = small_params[50], small_params[51]
    norm_coefs = jnp.stack([inv_std, mean * inv_std, gain, shift])

    def shaped_body(v_ref, c_ref):
        normed = v_ref[...] * c_ref[0:1] - c_ref[1:2]
        return normed * c_ref[2:3] + c_ref[3:4]

    flat_conv = conv_out.reshape(rows, channels)
    shaped, shaped_t, _ = arrange(
        shaped_body,
        (flat_conv, norm_coefs),
        lambda step: [
            pl.BlockSpec((step, channels), lambda i: (i, 0)),
            pl.BlockSpec((4, channels), lambda i: (0, 0)),
        ],
        rows,
        channels,
        n_tile,
        width,
        "arrange_shaped",
    )

    block_ids = jnp.arange(block_total, dtype=jnp.int32)
    inverse = jnp.sum(
        jnp.where(block_order[None, :] == block_ids[:, None], block_ids[None, :], 0), axis=1
    ).astype(jnp.int32)
    hidden_bias = small_params[53:57].reshape(half, 1, cols)
    branch, d_shaped, grads, d_hidden = feed_forward(
        inverse, shaped, shaped_t, d_branch, d_branch_t, hidden_bias, weights, n_tile * width
    )
    block_output, d_shaped, d_sums = close_out(
        branch, d_shaped, inputs.reshape(rows, channels), flat_conv, flat_mask, small_params[52:53], n_tile, run
    )

    d_shift = d_sums[0, 0]
    d_gain = inv_std * (d_sums[1, 0] - mean * d_shift)
    parts = tile_total(grid, jnp.stack([gain * d_shift, gain * d_gain]), 6)
    parts = jnp.repeat(parts.reshape(2, GROUPS, per_group).sum(2) / counted, per_group, axis=1)
    grad_coefs = jnp.stack(
        [
            inv_std * gain,
            inv_std * (parts[0] - mean * inv_std * parts[1]),
            inv_std * inv_std * parts[1],
        ]
    )
    d_conv, grad_rims = conv_gradient(
        d_shaped.reshape(slots, cells, channels),
        conv_out,
        mask_lanes,
        jnp.broadcast_to(grad_coefs[:, None, :], (3, 8, channels)),
        side,
    )
    small = jnp.concatenate([d_gain[None], d_shift[None], d_out_bias, d_hidden.reshape(4, channels)], 0)
    grad_halos, owned, d_small = exchange_backward(
        grid, grad_rims, grads, all_neighbours, inputs, mask_lanes, d_conv, halos, small
    )

    correction = 1.0 - jnp.power(F32(decay_rate), step_count[0].astype(F32))

    first_new, second_new, change = rotate(
        owned, left_basis, column_basis, moment_one, moment_two, correction, grid, width
    )
    input_grad, change = conv_backward(
        grid, d_conv, grad_halos, cotangent, mask_lanes, taps, weight_lanes, change
    )
    change = unpack_pairs(change[:, :run])
    d_small = d_small[: small_params.shape[0], :channels]
    small_one = decay_rate * small_first + (1.0 - decay_rate) * d_small
    small_two = decay_rate * small_second + (1.0 - decay_rate) * d_small * d_small
    new_small = small_params - small_rate * (small_one / correction) / (
        jnp.sqrt(small_two / correction) + adam_eps
    )
    new_master = master - 0.5 / math.sqrt(channels) * change
    return (
        block_output.reshape((1,) + inputs.shape),
        input_grad.reshape((1,) + inputs.shape),
        new_master,
        new_master.astype(BF),
        first_new,
        second_new,
        new_small,
        small_one,
        small_two,
    )


def solution(mesh):
    grid = Grid(mesh.shape["tile"], mesh.shape["opt"])

    def step(*args):
        return per_device(grid, *args)

    return jax.shard_map(
        step,
        mesh=mesh,
        in_specs=(
            P("opt", "tile", None, None, None),
            P("opt", "tile", None, None, None),
            P("opt", "tile", None),
            P("opt", "tile", None),
            P("opt", "tile", None),
            P("opt", None, "tile"),
            P("opt", None, None),
            P(),
            P(),
            P(),
            P("tile", None, None),
            P(),
            P("tile", None),
            P(),
            P(),
            P(),
        ),
        out_specs=(
            P("opt", "tile", None, None, None),
            P("opt", "tile", None, None, None),
            P("opt", "tile", None),
            P("opt", "tile", None),
            P("opt", "tile", None),
            P("opt", "tile", None),
            P(),
            P(),
            P(),
        ),
        check_vma=False,
    )
```

```python
import math

import jax
import jax.numpy as jnp
from jax import lax
from jax.experimental import pallas as pl
from jax.experimental.pallas import tpu as pltpu
from jax.sharding import PartitionSpec as P

GROUPS = 16
LANES = 128
RIM = 3
PITCH = 40
BF = jnp.bfloat16
F32 = jnp.float32

highest = lax.Precision.HIGHEST
epsilon = 1e-05
adam_eps = 1e-08
decay_rate = 0.5
small_rate = 0.05
ROOT = 0.7978845608028654
CUBE = 0.044715


class Grid:
    def __init__(self, n_tile, n_opt):
        b = n_tile // 4
        self.n_tile, self.n_opt = n_tile, n_opt
        self.size = {"a": 4, "b": b, "x": n_opt // 2, "c": 2}

    def own(self):
        t, o = lax.axis_index("tile"), lax.axis_index("opt")
        b = self.size["b"]
        return {"a": t // b, "b": t % b, "x": o // 2, "c": o % 2}

    def at(self, place):
        return place["a"] * self.size["b"] + place["b"], place["x"] * 2 + place["c"]

    def partners(self, dims):
        own = self.own()
        found = []
        for dim in dims:
            if dim == "tile":
                t, o = self.at(own)
                found += [(t ^ k, o) for k in range(1, self.n_tile)]
            else:
                found += [self.beside(own, dim, k) for k in range(1, self.size[dim])]
        return found

    def beside(self, own, dim, k):
        return self.at({**own, dim: own[dim] ^ k})


def meet(devices):
    barrier = pltpu.get_barrier_semaphore()
    for device in devices:
        pl.semaphore_signal(barrier, inc=1, device_id=device, device_id_type=pl.DeviceIdType.MESH)
    pl.semaphore_wait(barrier, len(devices))


class Copies:
    def __init__(self, send_sems, recv_sems):
        self.sems = send_sems, recv_sems
        self.used = 0

    def make(self, src, dst, device):
        i = self.used
        self.used += 1
        return pltpu.make_async_remote_copy(
            src_ref=src,
            dst_ref=dst,
            send_sem=self.sems[0].at[i],
            recv_sem=self.sems[1].at[i],
            device_id=device,
            device_id_type=pl.DeviceIdType.MESH,
        )

    def start(self, src, dst, device):
        copy = self.make(src, dst, device)
        copy.start()
        return copy


def remote_params(number, mib):
    return pltpu.CompilerParams(collective_id=number, has_side_effects=True, vmem_limit_bytes=mib << 20)


def add_rows(target, sources, rows, step=16):
    @pl.loop(0, rows // step)
    def _(i):
        at = pl.ds(pl.multiple_of(i * step, step), step)
        total = target[at, :].astype(F32)
        for source in sources:
            total = total + source[at, :].astype(F32)
        target[at, :] = total.astype(BF)


def store_rims(src, outs, slot, side):
    outs[0, slot, 0] = src[pl.ds(0, RIM * side), :].astype(BF)
    outs[0, slot, 1] = src[pl.ds((side - RIM) * side, RIM * side), :].astype(BF)
    for e in range(RIM):
        rows = pl.ds(e * side, side)
        outs[0, slot, 2, rows] = src[pl.ds(e, side, stride=side), :].astype(BF)
        outs[0, slot, 3, rows] = src[pl.ds(side - RIM + e, side, stride=side), :].astype(BF)


def rims_of_input(inputs, mask_lanes):
    slots, side, _, channels = inputs.shape
    n_chunk = -(-channels // LANES)

    def kernel(x_ref, m_ref, o_ref, cells):
        for s in range(slots):
            for i in range(side):
                cells[pl.ds(i * side, side), :] = (
                    x_ref[s, i].astype(F32) * m_ref[s, pl.ds(i * side, side), :]
                )
            store_rims(cells, o_ref, s, side)

    return pl.pallas_call(
        kernel,
        grid=(n_chunk,),
        in_specs=[
            pl.BlockSpec((slots, side, side, LANES), lambda c: (0, 0, 0, c)),
            pl.BlockSpec((slots, side * side, LANES), lambda c: (0, 0, 0)),
        ],
        out_specs=pl.BlockSpec((1, slots, 4, RIM * side, LANES), lambda c: (c, 0, 0, 0, 0)),
        out_shape=jax.ShapeDtypeStruct((n_chunk, slots, 4, RIM * side, LANES), BF),
        scratch_shapes=[pltpu.VMEM((side * side, LANES), F32)],
        compiler_params=pltpu.CompilerParams(vmem_limit_bytes=32 << 20),
        name="rims_of_input",
    )(inputs, mask_lanes)


class HaloExchange:
    def __init__(self, grid, n_chunk, slots, side):
        self.grid, self.n_chunk, self.slots, self.side = grid, n_chunk, slots, side
        self.count = 2 * (grid.n_tile - 1)

    def scratch(self):
        n, s, band = self.grid.n_tile, self.slots, RIM * self.side
        return [
            pltpu.VMEM((n, s, 4, band, LANES), BF),
            pltpu.VMEM((n, s, 5, band, LANES), BF),
            pltpu.SemaphoreType.DMA((2,)),
        ]

    def halo_shape(self):
        return jax.ShapeDtypeStruct((self.n_chunk, self.slots, 5, RIM * self.side, LANES), BF)

    def plan(self, copies, rims, arrived, picked, halos, local):
        t, o = self.grid.at(self.grid.own())
        self.t, self.arrived, self.picked = t, arrived, picked
        own_chunk = jnp.minimum(t, self.n_chunk - 1)
        self.first, self.second = [], []
        for k in range(1, self.grid.n_tile):
            to = t ^ k
            source = jnp.minimum(to, self.n_chunk - 1)
            self.first.append((to, copies.make(rims.at[source], arrived.at[t], (to, o))))
            self.second.append((to, copies.make(picked.at[to], halos.at[own_chunk], (to, o))))
        self.own_copy = pltpu.make_async_copy(rims.at[own_chunk], arrived.at[t], local.at[0])
        self.back_copy = pltpu.make_async_copy(picked.at[t], halos.at[own_chunk], local.at[1])

    def send_rims(self):
        for to, copy in self.first:

            @pl.when(to < self.n_chunk)
            def _():
                copy.start()

        self.own_copy.start()

    def pick_and_send(self, neighbours):
        grid, slots, side = self.grid, self.slots, self.side
        t, arrived, picked = self.t, self.arrived, self.picked
        self.own_copy.wait()
        for _, copy in self.first:

            @pl.when(t < self.n_chunk)
            def _():
                copy.wait_recv()

        @pl.when(t < self.n_chunk)
        def _():
            @pl.loop(0, grid.n_tile * slots)
            def _(d):
                def rim(direction, which):
                    slot = neighbours(d, direction)
                    at = jnp.maximum(slot, 0)
                    value = arrived[at // slots, at % slots, which].astype(F32)
                    return jnp.where(slot >= 0, value, 0.0)

                to_tile, to_slot = d // slots, d % slots
                for to, (direction, which) in enumerate(((1, 1), (6, 0), (3, 3), (4, 2))):
                    picked[to_tile, to_slot, to] = rim(direction, which).astype(BF)
                rows = []
                for direction, which, first in ((0, 1, side - RIM), (2, 1, 0), (5, 0, side - RIM), (7, 0, 0)):
                    value = rim(direction, which)
                    rows += [value[e * side + first : e * side + first + RIM] for e in range(RIM)]
                    rows.append(jnp.zeros((16 - RIM * RIM, LANES), F32))
                rows.append(jnp.zeros((RIM * side - 64, LANES), F32))
                picked[to_tile, to_slot, 4] = jnp.concatenate(rows, 0).astype(BF)

        for _, copy in self.second:

            @pl.when(t < self.n_chunk)
            def _():
                copy.start()

        @pl.when(t < self.n_chunk)
        def _():
            self.back_copy.start()

    def finish(self):
        t = self.t

        @pl.when(t < self.n_chunk)
        def _():
            self.back_copy.wait()

        for to, copy in self.first:

            @pl.when(to < self.n_chunk)
            def _():
                copy.wait_send()

        for to, copy in self.second:

            @pl.when(to < self.n_chunk)
            def _():
                copy.wait_recv()

            @pl.when(t < self.n_chunk)
            def _():
                copy.wait_send()


class WeightGather:
    def __init__(self, grid, pairs, width):
        self.grid, self.pairs, self.width = grid, pairs, width
        self.count = pairs * (grid.n_tile * grid.n_opt + 2)

    def plan(self, copies, packed, gathered, local):
        grid, width = self.grid, self.width
        own = grid.own()
        self.middle = (own["a"] == 1) | (own["a"] == 2)

        def place(m, rel):
            t, o = grid.at({d: own[d] ^ rel.get(d, 0) for d in own})
            return gathered.at[m, o, pl.ds(pl.multiple_of(t * width, width), width)]

        def send(m, rel, dim, k):
            source = packed.at[m] if not rel else place(m, rel)
            return copies.make(source, place(m, rel), grid.beside(own, dim, k))

        self.keeps = [pltpu.make_async_copy(packed.at[m], place(m, {}), local.at[m]) for m in range(self.pairs)]
        self.first, self.chain, self.onward, arrivals = [], {}, {}, []
        for m in range(self.pairs):
            self.chain["near", m] = send(m, {}, "a", 1)
            self.chain["over", m] = send(m, {}, "a", 3)
            self.chain["over2", m] = send(m, {"a": 1}, "a", 3)
            self.chain["out", m] = send(m, {"a": 3}, "a", 1)
            self.chain["out2", m] = send(m, {"a": 2}, "a", 1)
            order = ("x", "b", "c") if m % 2 == 0 else ("b", "x", "c")

            def spread(rel, left):
                self.onward[m, tuple(rel.items())] = sends = []
                for i, dim in enumerate(left):
                    for k in range(1, grid.size[dim]):
                        copy = send(m, rel, dim, k)
                        sends.append(copy)
                        child = {**rel, dim: k}
                        arrivals.append((m, child, copy))
                        spread(child, left[i + 1 :])

            for k in range(4):
                spread({"a": k} if k else {}, order)

        def waves(turn):
            found = [[] for _ in range(6)]
            for m, rel, copy in arrivals:
                found[turn[rel.get("a", 0)] + ("x" in rel) + ("b" in rel)].append((m, rel, copy))
            return [sorted(wave, key=lambda e: "c" in e[1]) for wave in found]

        self.sides = {True: waves({0: 0, 1: 1, 3: 2, 2: 3}), False: waves({0: 0, 1: 1, 2: 2, 3: 3})}

    def start(self):
        for copy in self.keeps:
            copy.start()
        for m in range(self.pairs):
            self.chain["near", m].start()

            @pl.when(self.middle)
            def _():
                self.chain["over", m].start()

            self.pass_on(m, {})

    def pass_on(self, m, rel):
        for copy in self.onward[m, tuple(rel.items())]:
            copy.start()

    def run(self, wave):
        along = {True: {1: ("near", 1, "over2"), 2: ("over", 3, "out"), 3: ("over2", 2, "out2")}}
        along[False] = {1: ("near", 1, None), 2: ("out", 2, None), 3: ("out2", 3, None)}
        for side in (True, False):

            @pl.when(self.middle == side)
            def _():
                if wave in along[side]:
                    came, k, goes = along[side][wave]
                    for m in range(self.pairs):
                        self.chain[came, m].wait_recv()
                        if goes is not None:
                            self.chain[goes, m].start()
                        self.pass_on(m, {"a": k})
                for m, rel, copy in self.sides[side][wave]:
                    copy.wait_recv()
                    self.pass_on(m, rel)

    def finish(self):
        for copy in self.keeps:
            copy.wait()
        for m in range(self.pairs):
            self.chain["near", m].wait_send()

            @pl.when(self.middle)
            def _():
                for name in ("over", "over2", "out", "out2"):
                    self.chain[name, m].wait_send()

        for sends in self.onward.values():
            for copy in sends:
                copy.wait_send()


def exchange_forward(grid, rims, packed, neighbours, inputs, mask_lanes, taps, cotangent, flat_mask, weight_row, width):
    n_chunk, slots, _, band, _ = rims.shape
    side, channels = inputs.shape[1], inputs.shape[3]
    cells = side * side
    pairs, _, cols = packed.shape
    n_tile = grid.n_tile
    rows = slots * cells
    block = row_block(rows)
    early = rows // block
    halo = HaloExchange(grid, n_chunk, slots, side)
    gather = WeightGather(grid, pairs, packed.shape[1])
    total = halo.count + gather.count + n_tile - 1
    last = early + n_chunk * slots

    def kernel(
        r_ref, p_ref, n_ref, x_ref, m_ref, t_ref, g_ref, f_ref, l_ref,
        halo_ref, w_ref, nbr_ref, conv_ref, sum_ref, gap_ref, turned_ref, bias_ref,
        arrived, picked, local, landed, table, pad, send, recv, locals_w, locals_n,
    ):
        step = pl.program_id(0)
        t, o = grid.at(grid.own())
        copies = Copies(send, recv)
        halo.plan(copies, r_ref, arrived, picked, landed, local)
        gather.plan(copies, p_ref, w_ref, locals_w)
        tables = [copies.make(n_ref, nbr_ref.at[t], (t ^ k, o)) for k in range(1, n_tile)]
        keep = pltpu.make_async_copy(n_ref, nbr_ref.at[t], locals_n.at[0])
        load = pltpu.make_async_copy(nbr_ref, table, locals_n.at[1])
        halo_out = pltpu.make_async_copy(landed, halo_ref, locals_n.at[0])

        @pl.when(step == 0)
        def _():
            meet(grid.partners(("tile", "x", "c")))
            for copy in tables:
                copy.start()
            keep.start()
            halo.send_rims()
            gather.start()

        @pl.when((step > 0) & (step <= early))
        def _():
            value = f_ref[:, :1] * (l_ref[:, :1] * g_ref[...].astype(F32))
            arranged(value, gap_ref, turned_ref, bias_ref, step == 1, n_tile, width)

        @pl.when(step == early)
        def _():
            keep.wait()
            for copy in tables:
                copy.wait()
            load.start()
            load.wait()
            gather.run(0)
            halo.pick_and_send(lambda d, k: table[d // slots, d % slots, k])
            gather.run(1)
            gather.run(2)
            halo.finish()
            halo_out.start()

        for i in range(3):

            @pl.when(step == min(last, early + 3 + 4 * i))
            def _():
                gather.run(3 + i)

        @pl.when(step > early)
        def _():
            at = step - early - 1
            conv_step(
                x_ref, m_ref, t_ref, lambda k: landed[at // slots, at % slots, k].astype(F32), conv_ref, sum_ref, pad, side
            )

        @pl.when(step == last)
        def _():
            gather.finish()
            halo_out.wait()

    conv_at = lambda i: jnp.maximum(i - early - 1, 0)
    row_at = lambda i: jnp.clip(i - 1, 0, early - 1)
    any_space = pl.BlockSpec(memory_space=pl.ANY)
    return pl.pallas_call(
        kernel,
        grid=(last + 1,),
        in_specs=[any_space] * 3
        + [
            pl.BlockSpec((1, side, side, LANES), lambda i: (conv_at(i) % slots, 0, 0, conv_at(i) // slots)),
            pl.BlockSpec((1, cells, LANES), lambda i: (conv_at(i) % slots, 0, 0)),
            pl.BlockSpec((50, 8, LANES), lambda i: (0, 0, conv_at(i) // slots)),
            pl.BlockSpec((block, channels), lambda i: (row_at(i), 0)),
            pl.BlockSpec((block, LANES), lambda i: (row_at(i), 0)),
            pl.BlockSpec((1, LANES), lambda i: (0, 0)),
        ],
        out_specs=[any_space] * 3
        + [
            pl.BlockSpec((1, cells, LANES), lambda i: (conv_at(i) % slots, 0, conv_at(i) // slots)),
            pl.BlockSpec((1, 2, 8, LANES), lambda i: (conv_at(i) % slots, 0, 0, conv_at(i) // slots)),
            pl.BlockSpec((block, n_tile * width), lambda i: (row_at(i), 0)),
            pl.BlockSpec((channels, block), lambda i: (0, row_at(i))),
            pl.BlockSpec((1, channels), lambda i: (0, 0)),
        ],
        out_shape=[
            halo.halo_shape(),
            jax.ShapeDtypeStruct((pairs, grid.n_opt, n_tile * packed.shape[1], cols), BF),
            jax.ShapeDtypeStruct((n_tile,) + neighbours.shape, jnp.int32),
            jax.ShapeDtypeStruct((slots, cells, channels), F32),
            jax.ShapeDtypeStruct((slots, 2, 8, channels), F32),
            jax.ShapeDtypeStruct((rows, n_tile * width), BF),
            jax.ShapeDtypeStruct((channels, rows), BF),
            jax.ShapeDtypeStruct((1, channels), F32),
        ],
        scratch_shapes=halo.scratch()
        + [
            pltpu.VMEM(halo.halo_shape().shape, BF),
            pltpu.SMEM((n_tile,) + neighbours.shape, jnp.int32),
            pltpu.VMEM(((side + 2 * RIM) * PITCH, LANES), F32),
            pltpu.SemaphoreType.DMA((total,)),
            pltpu.SemaphoreType.DMA((total,)),
            pltpu.SemaphoreType.DMA((pairs,)),
            pltpu.SemaphoreType.DMA((2,)),
        ],
        compiler_params=remote_params(1, 63),
        name="exchange_forward",
    )(rims, packed, neighbours, inputs, mask_lanes, taps, cotangent, flat_mask, weight_row)


def exchange_backward(grid, rims, grads, neighbours, inputs, mask_lanes, d_conv, halos, small):
    n_chunk, slots, _, band, _ = rims.shape
    side, channels = inputs.shape[1], inputs.shape[3]
    side_b, side_x = grid.size["b"], grid.size["x"]
    _, blocks, rows, cols = grads.shape
    pairs = blocks // side_x
    part = rows // side_b
    side_a = grid.size["a"]
    piece = part // side_a
    halo = HaloExchange(grid, n_chunk, slots, side)
    hops = [(dim, 1 << i) for dim in ("c", "x", "b", "a") for i in range((grid.size[dim] - 1).bit_length())]
    total = len(hops) + 1 + halo.count + blocks + side_a * pairs * side_x * side_b * 2
    total += pairs * (side_a - 1 + 5 + side_a * (side_b - 1))
    last = n_chunk * slots - 1
    small_rows = small.shape[0]
    small_shape = (up_to(50 + small_rows, 16), n_chunk * LANES)

    def kernel(
        r_ref, g_ref, n_ref, x_ref, m_ref, d_ref, h_ref, s_ref, halo_ref, o_ref, t_ref,
        arrived, picked, local, here, core, far, across, pad, sums, got, mine, heard, send, recv, load_sems,
    ):
        own = grid.own()
        own_x, own_b, own_c = own["x"], own["b"], own["c"]
        step = pl.program_id(0) * slots + pl.program_id(1)
        copies = Copies(send, recv)
        halo.plan(copies, r_ref, arrived, picked, halo_ref, local)
        order = [(k, m) for m in range(pairs) for k in range(1, side_x)]
        order += [(0, m) for m in range(pairs - 1, -1, -1)]
        index = lambda k, m: (own_x ^ k) * pairs + m
        own_a = own["a"]
        row_of = lambda a, b: pl.ds(pl.multiple_of((b * side_a + a) * piece, 16), piece)
        part_row = lambda a: pl.ds(pl.multiple_of(a * piece, 16), piece)
        turns = [*range(side_a - 1, 0, -1), 0]
        cores, loads = [], []
        for i, (k, m) in enumerate(order):
            at = index(k, m)
            cores.append(copies.make(g_ref.at[1 - own_c, at], core.at[at], grid.beside(own, "c", 1)))
            loads.append(pltpu.make_async_copy(g_ref.at[own_c, at], here.at[at], load_sems.at[i]))
        one, two, one_adds, two_adds = {}, {}, {}, {}
        for m in range(pairs):
            for k in turns:
                a = own_a ^ k
                mine_at = here.at[index(0, m), row_of(a, own_b)]
                across_x = lambda q, b: (
                    copies.make(
                        here.at[index(q, m), row_of(a, b)], far.at[q - 1, m, row_of(a, b)], grid.beside(own, "x", q)
                    )
                )
                across_b = lambda q, j: (
                    copies.make(
                        here.at[index(q, m), row_of(a, own_b ^ j)],
                        across.at[j - 1, index(q, m), part_row(a)],
                        grid.beside(own, "b", j),
                    )
                )
                from_x = lambda b: [far.at[q - 1, m, row_of(a, b)] for q in range(1, side_x)]
                from_b = lambda q: [across.at[j - 1, index(q, m), part_row(a)] for j in range(1, side_b)]
                if m % 2 == 0:
                    one[k, m] = [across_x(q, b) for q in range(1, side_x) for b in range(side_b)]
                    one_adds[k, m] = [(here.at[index(0, m), row_of(a, b)], from_x(b)) for b in range(side_b)]
                    two[k, m] = [across_b(0, j) for j in range(1, side_b)]
                    two_adds[k, m] = [(mine_at, from_b(0))]
                else:
                    one[k, m] = [across_b(q, j) for q in range(side_x) for j in range(1, side_b)]
                    one_adds[k, m] = [(here.at[index(q, m), row_of(a, own_b)], from_b(q)) for q in range(side_x)]
                    two[k, m] = [across_x(q, own_b) for q in range(1, side_x)]
                    two_adds[k, m] = [(mine_at, from_x(own_b))]

        to_a, back_a, back_b, keeps = {}, {}, {}, []
        for m in range(pairs):
            at = index(0, m)
            done = here.at[at, row_of(own_a, own_b)]
            place = o_ref.at[m, row_of(own_a, own_b)]
            keeps.append(pltpu.make_async_copy(done, place, load_sems.at[m]))
            for k in range(1, side_a):
                to = grid.beside(own, "a", k)
                to_a[k, m] = copies.make(here.at[at, row_of(own_a ^ k, own_b)], got.at[m, k - 1], to)
            got_at = lambda k: o_ref.at[m, row_of(own_a ^ k, own_b)]
            beside_a = lambda k: grid.beside(own, "a", k)
            back_a["near", m] = copies.make(done, place, beside_a(1))
            back_a["over", m] = copies.make(done, place, beside_a(3))
            back_a["over2", m] = copies.make(got_at(1), got_at(1), beside_a(3))
            back_a["out", m] = copies.make(got_at(3), got_at(3), beside_a(1))
            back_a["out2", m] = copies.make(got_at(2), got_at(2), beside_a(1))
            for k in range(side_a):
                for j in range(1, side_b):
                    came = o_ref.at[m, row_of(own_a ^ k, own_b)]
                    back_b[k, j, m] = copies.make(done if k == 0 else came, came, grid.beside(own, "b", j))
        middle = (own_a == 1) | (own_a == 2)
        lines = small_shape[0] // 2
        own_half = pl.ds(pl.multiple_of(own_c * lines, 8), lines)
        other_half = pl.ds(pl.multiple_of((1 - own_c) * lines, 8), lines)
        hop_copies = [copies.make(mine.at[other_half], heard.at[0], grid.beside(own, "c", 1))]
        hop_copies += [
            copies.make(mine.at[own_half], heard.at[i], grid.beside(own, dim, k))
            for i, (dim, k) in enumerate(hops)
            if i > 0
        ]
        hop_copies.append(copies.make(mine.at[own_half], heard.at[len(hops)], grid.beside(own, "c", 1)))

        def hop(i):
            if 0 < i <= len(hops):
                hop_copies[i - 1].wait()
                mine[own_half, :] = mine[own_half, :] + heard[i - 1]
            if i <= len(hops):
                hop_copies[i].start()
            else:
                hop_copies[i - 1].wait()

        def start(found):
            for copy in found:
                copy.start()

        def wait(found):
            for copy in found:
                copy.wait()

        @pl.when(step == 0)
        def _():
            meet(grid.partners(("tile", "x", "c")))
            halo.send_rims()
            mine[...] = jnp.zeros_like(mine)
            start(cores)
            start(loads)

        add_taps(x_ref, m_ref, d_ref, h_ref, mine, pad, sums, slots, side)

        ready = {}
        for i, (k, m) in enumerate(order):
            ready[m] = max(ready.get(m, 0), i) if m % 2 == 1 or k > 0 else ready.get(m, 0)
        for i, (k, m) in enumerate(order):

            @pl.when(step == min(last, 3 + 2 * i))
            def _():
                loads[i].wait()
                cores[i].wait()
                at = index(k, m)
                add_rows(here.at[at], [core.at[at]], rows)
                for n in range(pairs):
                    if ready[n] == i:
                        start(one[turns[0], n])
                        start(one[turns[1], n])

        @pl.when(step == last)
        def _():
            halo.pick_and_send(lambda d, k: n_ref[d // slots, d % slots, k])
            mine[pl.ds(50, small_rows), pl.ds(0, channels)] = s_ref[...]
            for i in range(side_a + 1):
                hop(i)
                for m in range(pairs):
                    if i < side_a:
                        k = turns[i]
                        wait(one[k, m])
                        if i + 2 < side_a:
                            start(one[turns[i + 2], m])
                        for target, sources in one_adds[k, m]:
                            add_rows(target, sources, piece)
                        start(two[k, m])
                for m in range(pairs):
                    if i > 0:
                        k = turns[i - 1]
                        wait(two[k, m])
                        for target, sources in two_adds[k, m]:
                            add_rows(target, sources, piece)
                        if k > 0:
                            to_a[k, m].start()
            for m in range(pairs):
                wait(to_a[k, m] for k in range(1, side_a))
                done = here.at[index(0, m), row_of(own_a, own_b)]
                add_rows(done, [got.at[m, k] for k in range(side_a - 1)], piece)
                keeps[m].start()
                back_a["near", m].start()

                @pl.when(middle)
                def _():
                    back_a["over", m].start()

                start(back_b[0, j, m] for j in range(1, side_b))

            def arrive(came, k, onward):
                for m in range(pairs):
                    back_a[came, m].wait_recv()
                    if onward is not None:
                        back_a[onward, m].start()
                    start(back_b[k, j, m] for j in range(1, side_b))

            for m in range(pairs):
                back_a["near", m].wait_recv()

                @pl.when(middle)
                def _():
                    back_a["over2", m].start()

                start(back_b[1, j, m] for j in range(1, side_b))

            @pl.when(middle)
            def _():
                arrive("over", 3, "out")
                arrive("over2", 2, "out2")

            @pl.when(~middle)
            def _():
                arrive("out", 2, None)
                arrive("out2", 3, None)

            for i in range(side_a + 1, len(hops) + 2):
                hop(i)
            halo.finish()
            t_ref[own_half, :] = mine[own_half, :]
            t_ref[other_half, :] = heard[len(hops)]
            for m in range(pairs):
                keeps[m].wait()
                back_a["near", m].wait_send()

                @pl.when(middle)
                def _():
                    for name in ("over", "over2", "out", "out2"):
                        back_a[name, m].wait_send()

            wait(back_b.values())

    any_space = pl.BlockSpec(memory_space=pl.ANY)
    cells = side * side
    return pl.pallas_call(
        kernel,
        grid=(n_chunk, slots),
        in_specs=[
            any_space,
            any_space,
            pl.BlockSpec(memory_space=pltpu.SMEM),
            pl.BlockSpec((1, side, side, LANES), lambda c, s: (s, 0, 0, c)),
            pl.BlockSpec((1, cells, LANES), lambda c, s: (s, 0, 0)),
            pl.BlockSpec((1, cells, LANES), lambda c, s: (s, 0, c)),
            halo_block(halos),
            pl.BlockSpec(small.shape, lambda c, s: (0, 0)),
        ],
        out_specs=[any_space, any_space, pl.BlockSpec(small_shape, lambda c, s: (0, 0))],
        out_shape=[
            halo.halo_shape(),
            jax.ShapeDtypeStruct((pairs, rows, cols), BF),
            jax.ShapeDtypeStruct(small_shape, F32),
        ],
        scratch_shapes=halo.scratch()
        + [
            pltpu.VMEM((blocks, rows, cols), BF),
            pltpu.VMEM((blocks, rows, cols), BF),
            pltpu.VMEM((side_x - 1, pairs, rows, cols), BF),
            pltpu.VMEM((side_b - 1, blocks, part, cols), BF),
            pltpu.VMEM(((side + 2 * RIM) * PITCH, LANES), F32),
            pltpu.VMEM((50, 8, LANES), F32),
            pltpu.VMEM((pairs, side_a - 1, piece, cols), BF),
            pltpu.VMEM(small_shape, F32),
            pltpu.VMEM((len(hops) + 1, small_shape[0] // 2, small_shape[1]), F32),
            pltpu.SemaphoreType.DMA((total,)),
            pltpu.SemaphoreType.DMA((total,)),
            pltpu.SemaphoreType.DMA((blocks,)),
        ],
        compiler_params=remote_params(2, 60),
        name="exchange_backward",
    )(rims, grads, neighbours, inputs, mask_lanes, d_conv, halos, small)


def tile_total(grid, value, number):
    n_tile = grid.n_tile

    def kernel(v_ref, o_ref, got, send, recv):
        t, o = grid.at(grid.own())
        meet(grid.partners(("tile",)))
        copies = Copies(send, recv)
        got[t] = v_ref[...]
        sent = [copies.start(v_ref, got.at[t], (t ^ k, o)) for k in range(1, n_tile)]
        for copy in sent:
            copy.wait()
        total = got[0]
        for i in range(1, n_tile):
            total = total + got[i]
        o_ref[...] = total

    whole = pl.BlockSpec(memory_space=pltpu.VMEM)
    return pl.pallas_call(
        kernel,
        in_specs=[whole],
        out_specs=whole,
        out_shape=jax.ShapeDtypeStruct(value.shape, F32),
        scratch_shapes=[
            pltpu.VMEM((n_tile,) + value.shape, F32),
            pltpu.SemaphoreType.DMA((n_tile - 1,)),
            pltpu.SemaphoreType.DMA((n_tile - 1,)),
        ],
        compiler_params=remote_params(number, 16),
        name="tile_total",
    )(value)


def fill_halo(pad, halo, side):
    last = side + RIM
    up, down, left, right, corner = (halo(k) for k in range(5))
    for e in range(RIM):
        rows = slice(e * side, e * side + side)
        pad[pl.ds(e * PITCH + 8, side), :] = up[rows]
        pad[pl.ds((last + e) * PITCH + 8, side), :] = down[rows]
        pad[pl.ds(RIM * PITCH + 8 - RIM + e, side, stride=PITCH), :] = left[rows]
        pad[pl.ds(RIM * PITCH + 8 + side + e, side, stride=PITCH), :] = right[rows]
    places = ((0, 8 - RIM), (0, 8 + side), (last, 8 - RIM), (last, 8 + side))
    for k, (row, col) in enumerate(places):
        for e in range(RIM):
            at = 16 * k + RIM * e
            pad[pl.ds((row + e) * PITCH + col, RIM), :] = corner[at : at + RIM]


def conv_pass(pad, side, weight, emit):
    for block in range(side // 8):
        sums = [None] * side
        for b in range(7):
            taps = [weight(a, b) for a in range(7)]
            for r in range(side + 2 * RIM):
                cells = pad[pl.ds(r * PITCH + 8 - RIM + b + 8 * block, 8), :]
                for a in range(7):
                    i = r - a
                    if 0 <= i < side:
                        term = taps[a] * cells
                        sums[i] = term if sums[i] is None else sums[i] + term
        emit(block, sums)


def halo_block(halos):
    return pl.BlockSpec((1, 1) + halos.shape[2:], lambda c, s: (c, s, 0, 0, 0))


def conv_step(x_ref, m_ref, w_ref, halo, o_ref, s_ref, pad, side):
    for i in range(side):
        pad[pl.ds((i + RIM) * PITCH + 8, side), :] = x_ref[0, i].astype(F32) * m_ref[0, pl.ds(i * side, side), :]
    fill_halo(pad, halo, side)
    bias = w_ref[49]
    totals = [jnp.zeros((8, LANES), F32), jnp.zeros((8, LANES), F32)]

    def emit(block, sums):
        for i in range(side):
            value = sums[i] + bias
            rows = pl.ds(i * side + 8 * block, 8)
            o_ref[0, rows, :] = value
            weighted = m_ref[0, rows, :] * value
            totals[0] = totals[0] + weighted
            totals[1] = totals[1] + weighted * value

    conv_pass(pad, side, lambda a, b: w_ref[7 * a + b], emit)
    s_ref[0, 0], s_ref[0, 1] = totals


def conv_gradient(d_shaped, conv_out, mask_lanes, coefs, side):
    slots, cells, channels = d_shaped.shape
    n_chunk = -(-channels // LANES)

    def kernel(d_ref, v_ref, m_ref, c_ref, o_ref, r_ref, held):
        one, two, three = c_ref[0, :1], c_ref[1, :1], c_ref[2, :1]
        for s in range(slots):
            value = d_ref[s] * one - m_ref[s] * (two + three * v_ref[s])
            o_ref[s] = value
            held[...] = value
            store_rims(held, r_ref, s, side)

    piece = (slots, 4, RIM * side, LANES)
    block = pl.BlockSpec((slots, cells, LANES), lambda c: (0, 0, c))
    return pl.pallas_call(
        kernel,
        grid=(n_chunk,),
        in_specs=[
            block,
            block,
            pl.BlockSpec((slots, cells, LANES), lambda c: (0, 0, 0)),
            pl.BlockSpec((3, 8, LANES), lambda c: (0, 0, c)),
        ],
        out_specs=[block, pl.BlockSpec((1,) + piece, lambda c: (c, 0, 0, 0, 0))],
        scratch_shapes=[pltpu.VMEM((cells, LANES), F32)],
        out_shape=[
            jax.ShapeDtypeStruct((slots, cells, channels), F32),
            jax.ShapeDtypeStruct((n_chunk,) + piece, BF),
        ],
        compiler_params=pltpu.CompilerParams(vmem_limit_bytes=32 << 20),
        name="conv_gradient",
    )(d_shaped, conv_out, mask_lanes, coefs)


def add_taps(x_ref, m_ref, d_ref, h_ref, o_ref, pad, sums, slots, side):
    slot = pl.program_id(1)
    for i in range(side):
        pad[pl.ds((i + RIM) * PITCH + 8, side), :] = x_ref[0, i].astype(F32) * m_ref[0, pl.ds(i * side, side), :]
    fill_halo(pad, lambda k: h_ref[0, 0, k].astype(F32), side)

    @pl.when(slot == 0)
    def _():
        sums[...] = jnp.zeros_like(sums)

    for block in range(side // 8):
        grads = [d_ref[0, pl.ds(i * side + 8 * block, 8), :] for i in range(side)]
        total = grads[0]
        for i in range(1, side):
            total = total + grads[i]
        sums[49] += total
        for b in range(7):
            taps = [None] * 7
            for r in range(side + 2 * RIM):
                window = pad[pl.ds(r * PITCH + 8 - RIM + b + 8 * block, 8), :]
                for a in range(7):
                    i = r - a
                    if 0 <= i < side:
                        term = window * grads[i]
                        taps[a] = term if taps[a] is None else taps[a] + term
            for a in range(7):
                sums[7 * a + b] += taps[a]

    @pl.when(slot == slots - 1)
    def _():
        at = pl.multiple_of(pl.program_id(0) * LANES, LANES)
        o_ref[pl.ds(0, 50), pl.ds(at, LANES)] = jnp.sum(sums[...], axis=1)


def conv_backward(grid, d_conv, halos, cotangent, mask_lanes, taps, weight_lanes, change):
    slots, side, _, channels = cotangent.shape
    n_chunk = halos.shape[0]
    cells = side * side
    pairs, rows, cols = change.shape
    side_a, side_b = grid.size["a"], grid.size["b"]
    part = rows // side_b
    piece = part // side_a
    total = pairs * (side_a * (side_b - 1) + (side_a - 1))
    last = n_chunk * slots - 1

    def kernel(
        d_ref, g_ref, m_ref, w_ref, l_ref, h_ref, c_ref, o_ref, change_ref,
        pad, mine, from_b, from_a, send, recv, load_sems,
    ):
        own = grid.own()
        step = pl.program_id(0) * slots + pl.program_id(1)
        copies = Copies(send, recv)
        own_a, own_b = own["a"], own["b"]
        half = lambda b: pl.ds(pl.multiple_of(b * part, 16), part)
        row_of = lambda a, b: pl.ds(pl.multiple_of((b * side_a + a) * piece, 16), piece)
        part_row = lambda a: pl.ds(pl.multiple_of(a * piece, 16), piece)
        turns = [*range(side_a - 1, 0, -1), 0]
        firsts, seconds, loads = {}, {}, []
        for m in range(pairs):
            for k in turns:
                a = own_a ^ k
                firsts[k, m] = [
                    copies.make(
                        c_ref.at[m, row_of(a, own_b ^ j)], from_b.at[j - 1, m, part_row(a)], grid.beside(own, "b", j)
                    )
                    for j in range(1, side_b)
                ]
                if k > 0:
                    seconds[k, m] = copies.make(
                        mine.at[m, part_row(a)], from_a.at[k - 1, m], grid.beside(own, "a", k)
                    )
            loads.append(pltpu.make_async_copy(c_ref.at[m, half(own_b)], mine.at[m], load_sems.at[m]))

        @pl.when(step == 0)
        def _():
            meet(grid.partners(("a", "b")))
            for load in loads:
                load.start()
            for k in turns:
                for m in range(pairs):
                    for copy in firsts[k, m]:
                        copy.start()

        for i in range(side):
            pad[pl.ds((i + RIM) * PITCH + 8, side), :] = d_ref[0, pl.ds(i * side, side), :]
        fill_halo(pad, lambda k: h_ref[0, 0, k].astype(F32), side)
        weight = l_ref[...]

        def emit(block, sums):
            for i in range(side):
                at = pl.ds(i * side + 8 * block, 8)
                scaled = weight * g_ref[0, i, pl.ds(8 * block, 8), :].astype(F32)
                o_ref[0, at, :] = m_ref[0, at, :] * (scaled + sums[i])

        conv_pass(pad, side, lambda a, b: w_ref[7 * (6 - a) + 6 - b], emit)

        for i, k in enumerate(turns):

            @pl.when(step == min(last, 5 + 4 * i))
            def _():
                for m in range(pairs):
                    if i == 0:
                        loads[m].wait()
                    for copy in firsts[k, m]:
                        copy.wait()
                    rows_here = part_row(own_a ^ k)
                    sources = [from_b.at[j, m, rows_here] for j in range(side_b - 1)]
                    add_rows(mine.at[m, rows_here], sources, piece)
                    if k > 0:
                        seconds[k, m].start()

        @pl.when(step == last)
        def _():
            for m in range(pairs):
                for k in range(1, side_a):
                    seconds[k, m].wait()
                value = mine[m, part_row(own_a)].astype(F32)
                for k in range(side_a - 1):
                    value = value + from_a[k, m].astype(F32)
                change_ref[m] = value

    return pl.pallas_call(
        kernel,
        grid=(n_chunk, slots),
        in_specs=[
            pl.BlockSpec((1, cells, LANES), lambda c, s: (s, 0, c)),
            pl.BlockSpec((1, side, side, LANES), lambda c, s: (s, 0, 0, c)),
            pl.BlockSpec((1, cells, LANES), lambda c, s: (s, 0, 0)),
            pl.BlockSpec((50, 8, LANES), lambda c, s: (0, 0, c)),
            pl.BlockSpec((8, LANES), lambda c, s: (0, 0)),
            halo_block(halos),
            pl.BlockSpec(memory_space=pl.ANY),
        ],
        out_specs=[
            pl.BlockSpec((1, cells, LANES), lambda c, s: (s, 0, c)),
            pl.BlockSpec((pairs, piece, cols), lambda c, s: (0, 0, 0)),
        ],
        scratch_shapes=[
            pltpu.VMEM(((side + 2 * RIM) * PITCH, LANES), F32),
            pltpu.VMEM((pairs, part, cols), BF),
            pltpu.VMEM((side_b - 1, pairs, part, cols), BF),
            pltpu.VMEM((side_a - 1, pairs, piece, cols), BF),
            pltpu.SemaphoreType.DMA((total,)),
            pltpu.SemaphoreType.DMA((total,)),
            pltpu.SemaphoreType.DMA((pairs,)),
        ],
        out_shape=[
            jax.ShapeDtypeStruct((slots, cells, channels), F32),
            jax.ShapeDtypeStruct((pairs, piece, cols), F32),
        ],
        compiler_params=remote_params(4, 48),
        name="conv_backward",
    )(d_conv, cotangent, mask_lanes, taps, weight_lanes, halos, change)


def spread_lanes(value, parts, width):
    rows, channels = value.shape
    run = channels // parts
    if run == width:
        return value
    gap = jnp.zeros((rows, width - run), value.dtype)
    pieces = []
    for t in range(parts):
        pieces += [value[:, t * run : (t + 1) * run], gap]
    return jnp.concatenate(pieces, 1)


def close_lanes(value, parts, run):
    width = value.shape[1] // parts
    if run == width:
        return value
    return jnp.concatenate([value[:, t * width : t * width + run] for t in range(parts)], 1)


def row_block(rows):
    return 3 * LANES if rows % (3 * LANES) == 0 else LANES


def arranged(value, gap_ref, turned_ref, sum_ref, first, parts, width):
    low = value.astype(BF).astype(F32)
    gap_ref[...] = spread_lanes(low, parts, width).astype(BF)
    turned_ref[...] = low.T.astype(BF)

    @pl.when(first)
    def _():
        sum_ref[...] = jnp.zeros_like(sum_ref)

    sum_ref[...] += jnp.sum(low, axis=0, keepdims=True)


def arrange(body, args, specs, rows, channels, parts, width, name):
    step = row_block(rows)

    def kernel(*refs):
        given, (gap_ref, turned_ref, sum_ref) = refs[: len(args)], refs[len(args) :]
        arranged(body(*given), gap_ref, turned_ref, sum_ref, pl.program_id(0) == 0, parts, width)

    return pl.pallas_call(
        kernel,
        grid=(rows // step,),
        in_specs=specs(step),
        out_specs=[
            pl.BlockSpec((step, parts * width), lambda i: (i, 0)),
            pl.BlockSpec((channels, step), lambda i: (0, i)),
            pl.BlockSpec((1, channels), lambda i: (0, 0)),
        ],
        out_shape=[
            jax.ShapeDtypeStruct((rows, parts * width), BF),
            jax.ShapeDtypeStruct((channels, rows), BF),
            jax.ShapeDtypeStruct((1, channels), F32),
        ],
        compiler_params=pltpu.CompilerParams(vmem_limit_bytes=48 << 20),
        name=name,
    )(*args)


def feed_forward(inverse, shaped, shaped_t, d_branch, d_branch_t, hidden_bias, weights, grad_rows):
    rows, depth = shaped.shape
    channels = shaped_t.shape[0]
    half, _, cols = hidden_bias.shape
    pairs, owners = weights.shape[:2]
    per_owner = 2 * pairs
    tile_rows = 3 * LANES if rows % (3 * LANES) == 0 else LANES

    def kernel(inv_ref, s_ref, st_ref, d_ref, dt_ref, hb_ref, w_ref, branch_ref, ds_ref, grad_ref, bias_ref, *scratch):
        packed, first, second, act, dpre, grads, sems, out_sem = scratch
        step = pl.program_id(0)

        def where(slot):
            owner, inside = slot // per_owner, slot % per_owner
            return owner, inside // 2, inside % 2

        def fetch(h, buffer):
            copies = []
            for which in range(2):
                owner, pair, _ = where(inv_ref[h + which * half])
                copies.append(
                    pltpu.make_async_copy(w_ref.at[pair, owner], packed.at[buffer, which], sems.at[buffer, which])
                )
            return copies

        @pl.when(step == 0)
        def _():
            for copy in fetch(0, 0):
                copy.start()
            if grad_rows > channels:
                rest = grad_rows - channels
                grads[:, :, pl.ds(channels, rest), :] = jnp.zeros(grads.shape[:2] + (rest, 2 * cols), BF)

        @pl.when(step + 1 < half)
        def _():
            for copy in fetch(step + 1, (step + 1) % 2):
                copy.start()

        now = step % 2
        slots = [where(inv_ref[step + which * half]) for which in range(2)]
        waits = fetch(step, now)
        for which, held in enumerate((first, second)):
            waits[which].wait()
            for parity in range(2):

                @pl.when(slots[which][2] == parity)
                def _():
                    held[...] = packed[now, which, :, parity * cols : (parity + 1) * cols]

        hidden = hb_ref[0]

        @pl.when(step == 0)
        def _():
            branch_ref[...] = jnp.zeros_like(branch_ref)
            ds_ref[...] = jnp.zeros_like(ds_ref)

        total = jnp.zeros((1, cols), F32)
        across = (((1,), (1,)), ((), ()))
        for i in range(rows // tile_rows):
            at = pl.ds(i * tile_rows, tile_rows)
            pre = jnp.dot(s_ref[at, :], first[...], preferred_element_type=F32) + hidden
            d_act = jnp.dot(d_ref[at, :], second[...], preferred_element_type=F32)
            square = pre * pre
            bend = jnp.tanh(ROOT * pre * (1.0 + CUBE * square))
            half_up = 0.5 * (1.0 + bend)
            low = (pre * half_up).astype(BF)
            slope = half_up + (0.5 * ROOT) * pre * (1.0 - bend * bend) * (1.0 + (3.0 * CUBE) * square)
            back = (d_act * slope).astype(BF)
            act[at, :] = low
            dpre[at, :] = back
            total = total + jnp.sum(back.astype(F32), axis=0, keepdims=True)
            out_add = lax.dot_general(low, second[...], across, preferred_element_type=F32)
            in_add = lax.dot_general(back, first[...], across, preferred_element_type=F32)

            branch_ref[at, :] += out_add
            ds_ref[at, :] += in_add

        bias_ref[0] = total
        for which, (left, right) in enumerate(((st_ref, dpre), (dt_ref, act))):
            owner, pair, half_of_pair = slots[which]
            value = jnp.dot(left[...], right[...], preferred_element_type=F32).astype(BF)
            for parity in range(2):

                @pl.when(half_of_pair == parity)
                def _():
                    at = (owner // 2) * pairs + pair
                    grads[owner % 2, at, pl.ds(0, channels), parity * cols : (parity + 1) * cols] = value

        @pl.when(step == half - 1)
        def _():
            out = pltpu.make_async_copy(grads, grad_ref, out_sem.at[0])
            out.start()
            out.wait()

    whole = lambda *shape: pl.BlockSpec(shape, lambda h, *_: (0,) * len(shape))
    line = pl.BlockSpec((1, 1, cols), lambda h, *_: (h, 0, 0))
    grad_shape = (2, owners // 2 * pairs, grad_rows, 2 * cols)
    return pl.pallas_call(
        kernel,
        grid_spec=pltpu.PrefetchScalarGridSpec(
            num_scalar_prefetch=1,
            grid=(half,),
            in_specs=[
                whole(rows, depth),
                whole(channels, rows),
                whole(rows, depth),
                whole(channels, rows),
                line,
                pl.BlockSpec(memory_space=pl.ANY),
            ],
            out_specs=[whole(rows, depth), whole(rows, depth), pl.BlockSpec(memory_space=pl.ANY), line],
            scratch_shapes=[
                pltpu.VMEM((2, 2, depth, 2 * cols), BF),
                pltpu.VMEM((depth, cols), BF),
                pltpu.VMEM((depth, cols), BF),
                pltpu.VMEM((rows, cols), BF),
                pltpu.VMEM((rows, cols), BF),
                pltpu.VMEM(grad_shape, BF),
                pltpu.SemaphoreType.DMA((2, 2)),
                pltpu.SemaphoreType.DMA((1,)),
            ],
        ),
        out_shape=[
            jax.ShapeDtypeStruct((rows, depth), F32),
            jax.ShapeDtypeStruct((rows, depth), F32),
            jax.ShapeDtypeStruct(grad_shape, BF),
            jax.ShapeDtypeStruct((half, 1, cols), F32),
        ],
        cost_estimate=pl.CostEstimate(
            flops=12 * rows * channels * half * cols, bytes_accessed=40 << 20, transcendentals=rows * half * cols
        ),
        compiler_params=pltpu.CompilerParams(vmem_limit_bytes=63 << 20),
        name="feed_forward",
    )(inverse, shaped, shaped_t, d_branch, d_branch_t, hidden_bias, weights)


def close_out(branch, d_shaped, inputs, conv_out, mask_lanes, out_bias, parts, run):
    rows, channels = inputs.shape
    depth = branch.shape[1]
    step = row_block(rows)

    def kernel(b_ref, d_ref, x_ref, v_ref, m_ref, o_ref, out_ref, ds_ref, sum_ref):
        branch_here = close_lanes(b_ref[...], parts, run) + o_ref[...]
        out_ref[...] = (m_ref[:, :1] * (x_ref[...].astype(F32) + branch_here)).astype(BF)
        grads = close_lanes(d_ref[...], parts, run)
        ds_ref[...] = grads

        @pl.when(pl.program_id(0) == 0)
        def _():
            sum_ref[...] = jnp.zeros_like(sum_ref)

        sum_ref[0] += jnp.sum(grads, axis=0, keepdims=True)
        sum_ref[1] += jnp.sum(grads * v_ref[...], axis=0, keepdims=True)

    line = lambda n: pl.BlockSpec((step, n), lambda i: (i, 0))
    return pl.pallas_call(
        kernel,
        grid=(rows // step,),
        in_specs=[
            line(depth),
            line(depth),
            line(channels),
            line(channels),
            line(LANES),
            pl.BlockSpec((1, channels), lambda i: (0, 0)),
        ],
        out_specs=[line(channels), line(channels), pl.BlockSpec((2, 1, channels), lambda i: (0, 0, 0))],
        out_shape=[
            jax.ShapeDtypeStruct((rows, channels), BF),
            jax.ShapeDtypeStruct((rows, channels), F32),
            jax.ShapeDtypeStruct((2, 1, channels), F32),
        ],
        compiler_params=pltpu.CompilerParams(vmem_limit_bytes=60 << 20),
        name="close_out",
    )(branch, d_shaped, inputs, conv_out, mask_lanes, out_bias)


def halves(value):
    high = value.astype(BF)
    return high, (value - high.astype(F32)).astype(BF)


def product(left, right, contract):
    dims = (contract, ((), ()))
    total = None
    for i, a in enumerate(left):
        for j, b in enumerate(right):
            if i + j < 2:
                term = lax.dot_general(a, b, dims, preferred_element_type=F32)
                total = term if total is None else total + term
    return total


def rotate(owned, left_basis, column_basis, moment_one, moment_two, correction, grid, width):
    slots, channels, run = left_basis.shape
    cols = column_basis.shape[1]
    pairs = slots // 2
    side_a, side_b = grid.size["a"], grid.size["b"]
    n_tile = grid.n_tile

    def kernel(f_ref, g_ref, l_ref, c_ref, one_ref, two_ref, first_ref, second_ref, o_ref):
        factor = f_ref[0]
        changes = []
        for p in range(2):
            grad = g_ref[0, pl.ds(0, channels), p * cols : (p + 1) * cols]
            left = halves(l_ref[p])
            column = halves(c_ref[p])
            rotated = product(left, (grad,), ((0,), (0,)))
            rotated = product(halves(rotated), column, ((1,), (0,)))
            first = decay_rate * one_ref[p] + (1.0 - decay_rate) * rotated
            second = decay_rate * two_ref[p] + (1.0 - decay_rate) * rotated * rotated
            first_ref[p] = first
            second_ref[p] = second
            direction = first * factor / (jnp.sqrt(second * factor) + adam_eps)
            turned = product(halves(direction), column, ((1,), (1,)))
            changes.append(product(left, halves(turned), ((1,), (0,))))
        change = jnp.concatenate(changes, 1)
        gap = jnp.zeros((width - run, 2 * cols), F32)
        for t in range(n_tile):
            piece = jnp.concatenate([change[t * run : (t + 1) * run], gap], 0)
            place = (t % side_b) * side_a + t // side_b
            o_ref[0, pl.ds(place * width, width), :] = piece.astype(BF)

    pair = lambda *shape: pl.BlockSpec(shape, lambda m: (m,) + (0,) * (len(shape) - 1))
    return pl.pallas_call(
        kernel,
        grid=(pairs,),
        in_specs=[
            pl.BlockSpec(memory_space=pltpu.SMEM),
            pair(1, owned.shape[1], 2 * cols),
            pair(2, channels, run),
            pair(2, cols, cols),
            pair(2, run, cols),
            pair(2, run, cols),
        ],
        out_specs=[pair(2, run, cols), pair(2, run, cols), pair(1, n_tile * width, 2 * cols)],
        out_shape=[
            jax.ShapeDtypeStruct(moment_one.shape, F32),
            jax.ShapeDtypeStruct(moment_one.shape, F32),
            jax.ShapeDtypeStruct((pairs, n_tile * width, 2 * cols), BF),
        ],
        compiler_params=pltpu.CompilerParams(vmem_limit_bytes=60 << 20),
        name="rotate",
    )(1.0 / correction.reshape(1), owned, left_basis, column_basis, moment_one, moment_two)


def up_to(value, unit):
    return -(-value // unit) * unit


def pack_pairs(value):
    slots, rows, cols = value.shape
    return value.reshape(slots // 2, 2, rows, cols).transpose(0, 2, 1, 3).reshape(slots // 2, rows, 2 * cols)


def unpack_pairs(value):
    pairs, rows, cols = value.shape
    return value.reshape(pairs, rows, 2, cols // 2).transpose(0, 2, 1, 3).reshape(2 * pairs, rows, cols // 2)


def per_device(
    grid,
    inputs,
    cotangent,
    master,
    moment_one,
    moment_two,
    left_basis,
    column_basis,
    small_params,
    small_first,
    small_second,
    land_mask,
    tile_count,
    neighbours,
    block_order,
    cell_weight,
    step_count,
):
    position = lax.axis_index("tile")
    sample = lax.axis_index("opt")
    inputs, cotangent = inputs[0], cotangent[0]
    slots, side, _, channels = inputs.shape
    cells = side * side
    rows = slots * cells
    n_tile = grid.n_tile
    n_chunk = -(-channels // LANES)
    per_group = channels // GROUPS
    per_owner, run, cols = master.shape
    pairs = per_owner // 2
    block_total = block_order.shape[0]
    half = block_total // 2
    width = up_to(run, 16)

    live = (jnp.arange(slots) < tile_count[position]).astype(F32)
    mask = (land_mask.astype(F32) * live[:, None, None]).reshape(slots, cells)
    mask_lanes = jnp.broadcast_to(mask[:, :, None], (slots, cells, LANES))
    flat_mask = mask_lanes.reshape(rows, LANES)
    taps = jnp.broadcast_to(small_params[:50, None, :], (50, 8, channels))

    weights_float = cell_weight.astype(F32)
    sample_weight = weights_float[sample] * weights_float.shape[0] / jnp.sum(weights_float)
    weight_lanes = jnp.broadcast_to(sample_weight, (8, LANES))
    weight_row = jnp.broadcast_to(sample_weight, (1, LANES))

    low_master = jnp.pad(pack_pairs(master.astype(BF)), ((0, 0), (0, width - run), (0, 0)))
    rims = rims_of_input(inputs, mask_lanes)
    halos, weights, all_neighbours, conv_out, sums, d_branch, d_branch_t, d_out_bias = exchange_forward(
        grid,
        rims,
        low_master,
        neighbours,
        inputs,
        mask_lanes,
        taps,
        cotangent.reshape(rows, channels),
        flat_mask,
        weight_row,
        width,
    )

    sums = jnp.sum(sums, axis=(0, 2))
    occupied = jnp.broadcast_to(jnp.sum(mask), (1, channels))
    sums = tile_total(grid, jnp.concatenate([sums, occupied], 0), 5)
    counted = sums[2, 0] * per_group
    by_group = sums[:2].reshape(2, GROUPS, per_group).sum(2)
    group_mean = by_group[0] / counted
    variance = by_group[1] / counted - group_mean * group_mean
    inv_std = jnp.repeat(lax.rsqrt(variance + epsilon), per_group)
    mean = jnp.repeat(group_mean, per_group)
    gain, shift = small_params[50], small_params[51]
    norm_coefs = jnp.stack([inv_std, mean * inv_std, gain, shift])

    def shaped_body(v_ref, c_ref):
        normed = v_ref[...] * c_ref[0:1] - c_ref[1:2]
        return normed * c_ref[2:3] + c_ref[3:4]

    flat_conv = conv_out.reshape(rows, channels)
    shaped, shaped_t, _ = arrange(
        shaped_body,
        (flat_conv, norm_coefs),
        lambda step: [
            pl.BlockSpec((step, channels), lambda i: (i, 0)),
            pl.BlockSpec((4, channels), lambda i: (0, 0)),
        ],
        rows,
        channels,
        n_tile,
        width,
        "arrange_shaped",
    )

    block_ids = jnp.arange(block_total, dtype=jnp.int32)
    inverse = jnp.sum(
        jnp.where(block_order[None, :] == block_ids[:, None], block_ids[None, :], 0), axis=1
    ).astype(jnp.int32)
    hidden_bias = small_params[53:57].reshape(half, 1, cols)
    branch, d_shaped, grads, d_hidden = feed_forward(
        inverse, shaped, shaped_t, d_branch, d_branch_t, hidden_bias, weights, n_tile * width
    )
    block_output, d_shaped, d_sums = close_out(
        branch, d_shaped, inputs.reshape(rows, channels), flat_conv, flat_mask, small_params[52:53], n_tile, run
    )

    d_shift = d_sums[0, 0]
    d_gain = inv_std * (d_sums[1, 0] - mean * d_shift)
    parts = tile_total(grid, jnp.stack([gain * d_shift, gain * d_gain]), 6)
    parts = jnp.repeat(parts.reshape(2, GROUPS, per_group).sum(2) / counted, per_group, axis=1)
    grad_coefs = jnp.stack(
        [
            inv_std * gain,
            inv_std * (parts[0] - mean * inv_std * parts[1]),
            inv_std * inv_std * parts[1],
        ]
    )
    d_conv, grad_rims = conv_gradient(
        d_shaped.reshape(slots, cells, channels),
        conv_out,
        mask_lanes,
        jnp.broadcast_to(grad_coefs[:, None, :], (3, 8, channels)),
        side,
    )
    small = jnp.concatenate([d_gain[None], d_shift[None], d_out_bias, d_hidden.reshape(4, channels)], 0)
    grad_halos, owned, d_small = exchange_backward(
        grid, grad_rims, grads, all_neighbours, inputs, mask_lanes, d_conv, halos, small
    )

    correction = 1.0 - jnp.power(F32(decay_rate), step_count[0].astype(F32))

    first_new, second_new, change = rotate(
        owned, left_basis, column_basis, moment_one, moment_two, correction, grid, width
    )
    input_grad, change = conv_backward(
        grid, d_conv, grad_halos, cotangent, mask_lanes, taps, weight_lanes, change
    )
    change = unpack_pairs(change[:, :run])
    d_small = d_small[: small_params.shape[0], :channels]
    small_one = decay_rate * small_first + (1.0 - decay_rate) * d_small
    small_two = decay_rate * small_second + (1.0 - decay_rate) * d_small * d_small
    new_small = small_params - small_rate * (small_one / correction) / (
        jnp.sqrt(small_two / correction) + adam_eps
    )
    new_master = master - 0.5 / math.sqrt(channels) * change
    return (
        block_output.reshape((1,) + inputs.shape),
        input_grad.reshape((1,) + inputs.shape),
        new_master,
        new_master.astype(BF),
        first_new,
        second_new,
        new_small,
        small_one,
        small_two,
    )


def solution(mesh):
    grid = Grid(mesh.shape["tile"], mesh.shape["opt"])

    def step(*args):
        return per_device(grid, *args)

    return jax.shard_map(
        step,
        mesh=mesh,
        in_specs=(
            P("opt", "tile", None, None, None),
            P("opt", "tile", None, None, None),
            P("opt", "tile", None),
            P("opt", "tile", None),
            P("opt", "tile", None),
            P("opt", None, "tile"),
            P("opt", None, None),
            P(),
            P(),
            P(),
            P("tile", None, None),
            P(),
            P("tile", None),
            P(),
            P(),
            P(),
        ),
        out_specs=(
            P("opt", "tile", None, None, None),
            P("opt", "tile", None, None, None),
            P("opt", "tile", None),
            P("opt", "tile", None),
            P("opt", "tile", None),
            P("opt", "tile", None),
            P(),
            P(),
            P(),
        ),
        check_vma=False,
    )
```
